32 devices in a mesh: section: 8 (over y, x, core), ep: 4 (over z).
Axes of the slice: x: 2, y: 2, z: 4, core: 2. Of those that a mesh axis runs over, the one named last changes fastest.
Arguments:
- grad_out: bfloat16 [8, 2048, 2048], P('section', 'ep'), may hold values from -0.125 to 0.125
- router_weights: bfloat16 [8, 2048, 8], P('section', 'ep'), may hold values from 0.049804688 to 0.29882812
- expert_ids: int32 [8, 2048, 8], P('section', 'ep'), may hold values from 0 to 127, all different within a row; in each aligned block of 512 rows (0 to 511, 512 to 1023, ..., all dimensions but the last counted through in order) at most 64 rows name the same one
- hidden: bfloat16 [8, 4, 768, 256], P('section', 'ep'), may hold values from -6 to 6
- master: float32 [8, 4, 768, 1024], P('section', 'ep'), may hold values from -0.25 to 0.25
- moment: bfloat16 [8, 4, 768, 1024], P('section', 'ep'), may hold values from -0.049804688 to 0.049804688
- second: bfloat16 [8, 4, 768, 1024], P('section', 'ep'), may hold values from 0.0019989014 to 0.019897461
Outputs:
- update: float32 [8, 4, 768, 1024], P('section', 'ep')
- router_grad: float32 [8, 2048, 8], P('section', 'ep')
The draws below stay inside these ranges and needn't reach their ends.
Inputs may be any that keep to these rules, and one draw needn't show every extreme that they name: `expert_ids`: in the rows of one device (aligned blocks of 512 rows) no expert is named by more than 64 rows, a bound that some block reaches.
All inputs are finite; a program needn't handle non-finite values.
Results may differ from the reference program's by a relative error of at most 0.0029.
Values may be sent and summed in bfloat16 or wider, within the bound.
No kernel may reach another device: no remote copies, remote signals or barrier semaphores. Data moves between devices by JAX's collectives and lax.ppermute only.
A program may use at most 128 MiB of HBM per device.

```python
import math
import jax
import jax.numpy as jnp
import numpy as np
from jax import lax

D = 2048
DH = 1024
HID = 768
EXPERTS = 128
TOP = 8
TOK_DEV = 512
CAP = 64
SLOTS = 256
TOKENS = 2048
N_SECTION = 8
N_EP = 4


def levels(key, shape, shards, low, top_value):
    level = 1.0
    for axis_at, parts in shards:
        heights = jax.random.uniform(jax.random.fold_in(jax.random.fold_in(key, 6), axis_at), (parts,), jnp.float32, low / len(shards), top_value / len(shards))
        level = level * jnp.repeat(jnp.exp(heights), shape[axis_at] // parts).reshape((-1,) + (1,) * (len(shape) - 1 - axis_at))
    return level


def routed_block(key, own, number, rows, count, top, limit, slope):
    ranking = jax.random.permutation(key, count)
    packed, ordinary = portions_of(count, rows * top, limit, slope, True), portions_of(count, rows * top, limit, slope, False)
    places = jnp.arange(count)

    def named(lengths, turn):
        used = int((lengths > 0).sum())
        fixed = max(1, used // 4)
        passed = fixed + (places - fixed + turn * (used - fixed)) % max(1, count - fixed)
        return jnp.zeros((count,), jnp.int32).at[ranking[jnp.where(places < fixed, places, passed)]].set(jnp.asarray(lengths, jnp.int32))

    lengths = jnp.where(number % 4 == 0, named(packed, number // 4), named(ordinary, number - number // 4 - 1))
    mixed = jax.random.permutation(jax.random.fold_in(own, 3), count)
    giver, taker = mixed[0:count // 2 * 2:2], mixed[1:count // 2 * 2:2]
    margin = jnp.minimum(lengths[giver] - 1, limit - lengths[taker]) // 2
    margin = jnp.where((giver == ranking[0]) | (taker == ranking[0]) | (lengths[taker] == 0), 0, jnp.maximum(margin, 0))
    passed = jax.random.randint(jax.random.fold_in(own, 4), (count // 2,), 0, 1 << 20) % (margin + 1)
    lengths = lengths.at[giver].add(-passed).at[taker].add(passed)
    items = jnp.searchsorted(jnp.cumsum(lengths), jnp.arange(rows * top), side="right").astype(jnp.int32)
    listing = items.reshape(top, rows).T
    listing = listing[jax.random.permutation(jax.random.fold_in(own, 1), rows)]
    turn = jax.random.randint(jax.random.fold_in(own, 2), (rows, 1), 0, top)
    return jnp.take_along_axis(listing, (jnp.arange(top)[None, :] + turn) % top, axis=1)


def portions_of(amount, total, bound, slope, full):
    loads = [(1 << 20) // math.isqrt(grade ** slope) + 1 for grade in range(1, amount + 1)]
    largest = bound if full else min(bound, max(-(-total // amount), total * loads[0] // sum(loads)))
    least = 1 if total - largest >= amount - 1 else 0
    given, rest = [largest] + [least] * (amount - 1), total - largest - least * (amount - 1)
    while rest > 0:
        candidates = [i for i in range(1, amount) if given[i] < largest] or [i for i in range(1, amount) if given[i] < bound]
        whole, remaining = sum([loads[i] for i in candidates]), rest
        for i in candidates:
            addition = min(bound - given[i], max(1, remaining * loads[i] // whole), rest)
            given[i] = given[i] + addition
            rest = rest - addition
    return np.array(given)


def noise(key, extent, deviation, reach, pieces=(), kind=jnp.bfloat16):
    result = jax.random.normal(key, extent, jnp.float32) * deviation
    if len(pieces) > 0:
        result = levels(key, extent, pieces, -0.22, 0.18) * result
    return jnp.clip(result, min=-reach, max=reach).astype(kind)


def setup_inputs(seed: int = 0) -> dict:
    arg_keys = jax.random.split(jax.random.key(seed), 8)
    grad_out = noise(arg_keys[0], (N_SECTION, TOKENS, D), (D ** -0.5), 0.125, ((0, 8), (1, 4)))
    router_weights = jnp.clip(0.049804688 + 0.24902344 * jax.random.uniform(arg_keys[1], (N_SECTION, TOKENS, TOP), jnp.float32) ** levels(arg_keys[1], (N_SECTION, TOKENS, TOP), ((0, 8), (1, 4)), -0.2, 0.2), 0.049804688, 0.29882812).astype(jnp.bfloat16)
    expert_ids_keys = jax.random.split(jax.random.fold_in(arg_keys[2], 1), N_SECTION * TOKENS // TOK_DEV)
    expert_ids_turns = jax.random.permutation(jax.random.fold_in(arg_keys[2], 3), N_SECTION * TOKENS // TOK_DEV)
    expert_ids = jax.vmap(lambda own, number: routed_block(jax.random.fold_in(arg_keys[2], 2), own, number, TOK_DEV, EXPERTS, TOP, CAP, 1))(expert_ids_keys, expert_ids_turns).reshape((N_SECTION, TOKENS, TOP))
    hidden = noise(arg_keys[3], (N_SECTION, N_EP, HID, SLOTS), 1.0, 6.0, ((0, 8), (1, 4)))
    master = jnp.clip(jax.random.uniform(arg_keys[4], (N_SECTION, N_EP, HID, DH), jnp.float32, -0.25, 0.25) * levels(arg_keys[4], (N_SECTION, N_EP, HID, DH), ((0, 8), (1, 4)), -0.4, 0.0), -0.25, 0.25)
    moment = jnp.clip(jax.random.uniform(arg_keys[5], (N_SECTION, N_EP, HID, DH), jnp.float32, -0.049804688, 0.049804688) * levels(arg_keys[5], (N_SECTION, N_EP, HID, DH), ((0, 8), (1, 4)), -0.4, 0.0), -0.049804688, 0.049804688).astype(jnp.bfloat16)
    second = jnp.clip(jnp.exp(math.log(0.019897461) - 2.2979944 * jax.random.uniform(arg_keys[6], (N_SECTION, N_EP, HID, DH), jnp.float32) ** levels(arg_keys[6], (N_SECTION, N_EP, HID, DH), ((0, 8), (1, 4)), -0.2, 0.2)), 0.0019989014, 0.019897461).astype(jnp.bfloat16)
    return {"grad_out": grad_out, "router_weights": router_weights, "expert_ids": expert_ids, "hidden": hidden, "master": master, "moment": moment, "second": second}


beta_first = 0.9
beta_second = 0.95
adam_eps = 1e-08
decay_rate = 0.1
first_fix = 1.0 - 0.9 ** 10
second_fix = 1.0 - 0.95 ** 10

def slot_ranks(routes, count):
    onehot = (routes[:, :, None] == jnp.arange(count, dtype=jnp.int32)[None, None, :]).astype(jnp.int32)
    per_token = lax.optimization_barrier(jnp.sum(onehot, axis=1))
    before = jnp.cumsum(per_token, axis=0, dtype=jnp.int32) - per_token
    return lax.optimization_barrier(jnp.sum(before[:, None, :] * onehot, axis=2)).astype(jnp.int32)

def adam_update(total, param, first, second_moment):
    first_new = beta_first * first + (1.0 - beta_first) * total
    second_new = beta_second * second_moment + (1.0 - beta_second) * total * total
    return first_new / first_fix / (jnp.sqrt(second_new / second_fix) + adam_eps) + decay_rate * param

def one_expert(items):
    hid_block, weight, row_block, weight_block = items
    scaled = (hid_block.astype(jnp.float32) * weight_block[None, :].astype(jnp.float32)).astype(jnp.bfloat16)
    grad = jnp.dot(scaled, row_block, preferred_element_type=jnp.float32)
    proj = jnp.einsum('rd,hd->hr', row_block, weight, preferred_element_type=jnp.float32)
    score = lax.optimization_barrier(jnp.sum(hid_block.astype(jnp.float32) * proj, axis=0))
    return (grad, score)

def section_pass(grads_section, weights_section, routes_section, hidden_section, full):
    routes_block = routes_section.reshape(N_EP, TOK_DEV, TOP)
    slots = jax.vmap(lambda block: slot_ranks(block, N_EP))(routes_block)
    source = jnp.arange(N_EP, dtype=jnp.int32)[:, None, None]
    flying = routes_block < N_EP
    flat = jnp.where(flying, (routes_block * N_EP + source) * CAP + slots, N_EP * SLOTS).reshape(-1).astype(jnp.int32)
    token = (source * TOK_DEV + jnp.arange(TOK_DEV, dtype=jnp.int32)[None, :, None] + jnp.zeros_like(routes_block)).reshape(-1)
    rows = jnp.zeros((N_EP * SLOTS, D), grads_section.dtype).at[flat].set(grads_section[token], mode='drop')
    slot_weight = jnp.zeros((N_EP * SLOTS,), weights_section.dtype).at[flat].set(weights_section.reshape(-1), mode='drop')
    grad, score = lax.map(one_expert, (hidden_section, full, rows.reshape(N_EP, SLOTS, D), slot_weight.reshape(N_EP, SLOTS)))
    picked = score.reshape(-1)[jnp.minimum(flat, N_EP * SLOTS - 1)]
    router = jnp.where(flying.reshape(-1), picked, jnp.zeros_like(picked)).reshape(TOKENS, TOP)
    return (grad, router)

def reference(grad_out, router_weights, expert_ids, hidden, master, moment, second):

    def take(array, index):
        return lax.dynamic_index_in_dim(array, index, 0, keepdims=False)

    def pair_pass(low):
        high = (low + N_SECTION // 2).astype(jnp.int32)
        low_master = take(master, low)
        high_master = take(master, high)
        full = jnp.concatenate([low_master, high_master], -1).astype(jnp.bfloat16)
        grad_low, router_low = section_pass(take(grad_out, low), take(router_weights, low), take(expert_ids, low), take(hidden, low), full)
        grad_high, router_high = section_pass(take(grad_out, high), take(router_weights, high), take(expert_ids, high), take(hidden, high), full)
        total_low = grad_low[..., :DH] + grad_high[..., :DH]
        total_high = grad_low[..., DH:] + grad_high[..., DH:]
        up_low = adam_update(total_low, low_master, take(moment, low).astype(jnp.float32), take(second, low).astype(jnp.float32))
        up_high = adam_update(total_high, high_master, take(moment, high).astype(jnp.float32), take(second, high).astype(jnp.float32))
        return (up_low, up_high, router_low, router_high)
    lows, highs, router_lows, router_highs = lax.map(pair_pass, jnp.arange(N_SECTION // 2, dtype=jnp.int32))
    update = jnp.concatenate([lows, highs], 0)
    router = jnp.concatenate([router_lows, router_highs], 0)
    return (update, router)
```

```python
import functools

import jax
import jax.numpy as jnp
from jax import lax
from jax.experimental import pallas as pl
from jax.experimental.pallas import tpu as pltpu
from jax.sharding import PartitionSpec as P

beta_first = 0.9
beta_second = 0.95
adam_eps = 1e-08
decay_rate = 0.1
first_fix = 1.0 - 0.9**10
second_fix = 1.0 - 0.95**10

LANES = 128
TILE = 16
VMEM_BYTES = 48 * 1024 * 1024
F32 = jnp.float32
BF16 = jnp.bfloat16


def params(**kwargs):
    return pltpu.CompilerParams(vmem_limit_bytes=VMEM_BYTES, **kwargs)


def vmem_specs(count):
    return [pl.BlockSpec(memory_space=pltpu.VMEM) for _ in range(count)]


def own_half():
    sections = lax.axis_size("section")
    return jnp.where(lax.axis_index("section") < sections // 2, 0, 1).astype(jnp.int32)


def route_kernel(group, cap, ids_ref, weight_ref, grads_ref, slots_ref, *rest):
    chunks, (held, sems) = rest[: 2 * group], rest[2 * group :]
    tokens, half = held.shape[1], held.shape[2]
    me = lax.axis_index("ep").astype(jnp.int32)
    mine = own_half()
    copies = []
    for turn in range(2):
        side = 1 - mine if turn == 0 else mine
        columns = pl.ds(pl.multiple_of(side * half, half), half)
        copy = pltpu.make_async_copy(grads_ref.at[:, columns], held.at[turn], sems.at[turn])
        copy.start()
        copies.append(copy)
    ids = ids_ref[...]
    weights = weight_ref[...].astype(F32)
    members, scales = [], []
    for k in range(group):
        named = ids == (me ^ k)
        members.append(jnp.sum(jnp.where(named, 1.0, 0.0), axis=0, keepdims=True))
        scales.append(jnp.sum(jnp.where(named, weights, 0.0), axis=0, keepdims=True))
    member = jnp.concatenate(
        members + [jnp.zeros((-group % TILE, tokens), F32)] if group % TILE else members, axis=0
    )
    earlier = lax.broadcasted_iota(jnp.int32, (tokens, tokens), 0)
    later = lax.broadcasted_iota(jnp.int32, (tokens, tokens), 1)
    ahead = jnp.where(earlier < later, 1.0, 0.0).astype(BF16)
    before = jnp.dot(member.astype(BF16), ahead, preferred_element_type=F32)
    slots = jnp.where(member > 0.5, before, -1.0)
    slots_ref[...] = slots
    place = lax.broadcasted_iota(jnp.int32, (cap, tokens), 0).astype(F32)
    picks = [
        jnp.where(place == slots[k : k + 1, :], 1.0, 0.0).astype(BF16) for k in range(group)
    ]
    base = me * cap
    tile_row = lax.broadcasted_iota(jnp.int32, (TILE, LANES), 0)
    tile_lane = lax.broadcasted_iota(jnp.int32, (TILE, LANES), 1)
    kept = (tile_row * LANES + tile_lane >= base) & (tile_row * LANES + tile_lane < base + cap)
    data_rows = half // LANES * cap
    for k in range(group):
        spread = jnp.broadcast_to(scales[k], (TILE, tokens)).astype(BF16)
        doubled = jnp.concatenate([picks[k]] * (LANES // cap), axis=0)
        tile = lax.dot_general(
            spread, doubled, (((1,), (1,)), ((), ())), preferred_element_type=F32
        )
        tile = jnp.where(kept, tile, 0.0).astype(BF16)
        for turn in range(2):
            chunks[turn * group + k][data_rows:, :] = tile
    pick = jnp.concatenate(picks, axis=0)
    step = min(half, 2 * LANES)
    for turn in range(2):
        copies[turn].wait()
        for column in range(0, half, step):
            block = jnp.dot(
                pick, held[turn, :, column : column + step], preferred_element_type=F32
            ).astype(BF16)
            for k in range(group):
                for part in range(step // LANES):
                    at = (column // LANES + part) * cap
                    chunks[turn * group + k][at : at + cap, :] = block[
                        k * cap : (k + 1) * cap, part * LANES : (part + 1) * LANES
                    ]


def inner_kernel(own_ref, other_ref, master_ref, inner_ref):
    weights = master_ref[...].astype(BF16)
    slots = own_ref.shape[1]
    for at, ref in ((0, own_ref), (slots, other_ref)):
        inner_ref[at : at + slots, :] = lax.dot_general(
            ref[...], weights, (((0,), (0,)), ((), ())), preferred_element_type=F32
        )


def score_kernel(group, cap, inner_ref, *rest):
    chunks, outs = rest[: 2 * group], rest[2 * group :]
    slots = group * cap
    blocks = inner_ref.shape[1] // LANES
    me = lax.axis_index("ep").astype(jnp.int32)
    for k in range(group):
        sums = []
        for side in range(2):
            start = pl.multiple_of(side * slots + (me ^ k) * cap, cap)
            total = jnp.zeros((cap, LANES), F32)
            for block in range(blocks):
                rows = chunks[side * group + k][block * cap : (block + 1) * cap, :].astype(F32)
                total += rows * inner_ref[
                    pl.ds(start, cap), block * LANES : (block + 1) * LANES
                ]
            sums.append(total)
        both = jnp.concatenate(sums, axis=0)
        line = jnp.sum(both.T, axis=0, keepdims=True)
        outs[k][...] = jnp.broadcast_to(line, outs[k].shape)


def update_kernel(
    group, cap, own_ref, other_ref, master_ref, moment_ref, second_ref, *rest
):
    chunks, (update_ref, rows, scales) = rest[: 2 * group], rest[2 * group :]
    slots = group * cap
    half = rows.shape[1]
    data_rows = half // LANES * cap
    me = lax.axis_index("ep").astype(jnp.int32)

    @pl.when(pl.program_id(0) == 0)
    def _():
        for side in range(2):
            tile = jnp.zeros((TILE, LANES), F32)
            for k in range(group):
                chunk = chunks[side * group + k]
                tile += chunk[data_rows:, :].astype(F32)
                start = pl.multiple_of(side * slots + (me ^ k) * cap, cap)
                for block in range(half // LANES):
                    rows[pl.ds(start, cap), block * LANES : (block + 1) * LANES] = chunk[
                        block * cap : (block + 1) * cap, :
                    ]
            scales[side] = tile

    parts = []
    for side, ref in enumerate((own_ref, other_ref)):
        for part in range(slots // LANES):
            hidden = ref[:, part * LANES : (part + 1) * LANES].astype(F32)
            parts.append((hidden * scales[side, part : part + 1, :]).astype(BF16))
    scaled = jnp.concatenate(parts, axis=1)
    total = jnp.dot(scaled, rows[...], preferred_element_type=F32)
    first = beta_first * moment_ref[...].astype(F32) + (1.0 - beta_first) * total
    second = beta_second * second_ref[...].astype(F32) + (1.0 - beta_second) * total * total
    update_ref[...] = (first * (1.0 / first_fix)) / (
        jnp.sqrt(second * (1.0 / second_fix)) + adam_eps
    ) + decay_rate * master_ref[...]


def combine_kernel(group, cap, ids_ref, slots_ref, *rest):
    own, other, out_ref = rest[:group], rest[group : 2 * group], rest[2 * group]
    tokens = ids_ref.shape[1]
    me = lax.axis_index("ep").astype(jnp.int32)
    lane = lax.broadcasted_iota(jnp.int32, (1, LANES), 1)
    lines = [
        jnp.where(lane < cap, own[k][0:1, :], other[k][0:1, :]) for k in range(group)
    ]
    lines.append(jnp.zeros((LANES - group, LANES), F32))
    columns = jnp.concatenate(lines, axis=0).T
    columns = columns[:cap] + columns[cap : 2 * cap]
    place = lax.broadcasted_iota(jnp.int32, (cap, tokens), 0).astype(F32)
    ids = ids_ref[...]
    result = jnp.zeros(ids.shape, F32)
    for k in range(group):
        at_slot = jnp.where(place == slots_ref[k : k + 1, :], columns[:, k : k + 1], 0.0)
        chosen = jnp.sum(at_slot, axis=0, keepdims=True)
        result = jnp.where(ids == (me ^ k), chosen, result)
    out_ref[...] = result


def moved(array, flip, step):
    sections, group = lax.axis_size("section"), lax.axis_size("ep")
    pairs = []
    for s in range(sections):
        target = (s + sections // 2) % sections if flip else s
        for e in range(group):
            pairs.append((s * group + e, target * group + (e ^ step)))
    return lax.ppermute(array, ("section", "ep"), pairs)


def cost(flops, touched):
    return pl.CostEstimate(flops=int(flops), bytes_accessed=int(touched), transcendentals=0)


def local(grad_out, router_weights, expert_ids, hidden, master, moment, second):
    group = lax.axis_size("ep")
    tokens, width = grad_out.shape[1:]
    top = expert_ids.shape[2]
    hid, slots = hidden.shape[2:]
    half = master.shape[3]
    cap = slots // group
    ids = expert_ids[0].T
    weights = router_weights[0].T
    own_hidden = hidden[0, 0]
    param = master[0, 0]
    other_hidden = moved(own_hidden, True, 0)

    chunk_shape = jax.ShapeDtypeStruct((half // LANES * cap + TILE, LANES), BF16)
    slot_rows = group + -group % TILE
    routed = pl.pallas_call(
        functools.partial(route_kernel, group, cap),
        out_shape=[jax.ShapeDtypeStruct((slot_rows, tokens), F32)] + [chunk_shape] * (2 * group),
        in_specs=vmem_specs(2) + [pl.BlockSpec(memory_space=pl.ANY)],
        out_specs=vmem_specs(1 + 2 * group),
        scratch_shapes=[
            pltpu.VMEM((2, tokens, half), BF16),
            pltpu.SemaphoreType.DMA((2,)),
        ],
        compiler_params=params(),
        cost_estimate=cost(2 * slots * tokens * width, 2 * (tokens + slots) * width),
        name="route",
    )(ids, weights, grad_out[0])
    slot_of, sent = routed[0], routed[1:]
    order = sorted(range(group), key=lambda k: -k)
    arrived = {}
    for k in order:
        for side in (1, 0):
            source = sent[k] if side else sent[group + k]
            arrived[side, k] = source if not side and k == 0 else moved(source, side == 1, k)
    chunks = [arrived[side, k] for side in range(2) for k in range(group)]

    inner = pl.pallas_call(
        inner_kernel,
        out_shape=jax.ShapeDtypeStruct((2 * slots, half), F32),
        in_specs=vmem_specs(3),
        out_specs=vmem_specs(1)[0],
        compiler_params=params(),
        cost_estimate=cost(4 * slots * hid * half, 4 * hid * half + 8 * slots * half),
        name="inner",
    )(own_hidden, other_hidden, param)
    scores = pl.pallas_call(
        functools.partial(score_kernel, group, cap),
        out_shape=[jax.ShapeDtypeStruct((8, LANES), F32)] * group,
        in_specs=vmem_specs(1 + 2 * group),
        out_specs=vmem_specs(group),
        compiler_params=params(),
        cost_estimate=cost(4 * slots * half, 12 * slots * half),
        name="score",
    )(inner, *chunks)
    own_scores = [scores[k] if k == 0 else moved(scores[k], False, k) for k in range(group)]
    other_scores = [moved(scores[k], True, k) for k in range(group)]

    block = LANES
    tile = pl.BlockSpec((block, half), lambda i: (i, 0))
    hidden_tile = pl.BlockSpec((block, slots), lambda i: (i, 0))
    whole = pl.BlockSpec(chunk_shape.shape, lambda i: (0, 0))
    update = pl.pallas_call(
        functools.partial(update_kernel, group, cap),
        out_shape=jax.ShapeDtypeStruct((hid, half), F32),
        grid=(hid // block,),
        in_specs=[hidden_tile, hidden_tile, tile, tile, tile] + [whole] * (2 * group),
        out_specs=tile,
        scratch_shapes=[
            pltpu.VMEM((2 * slots, half), BF16),
            pltpu.VMEM((2, TILE, LANES), F32),
        ],
        compiler_params=params(),
        cost_estimate=cost(4 * slots * hid * half, 12 * hid * half + 4 * slots * half),
        name="update",
    )(own_hidden, other_hidden, param, moment[0, 0], second[0, 0], *chunks)
    router = pl.pallas_call(
        functools.partial(combine_kernel, group, cap),
        out_shape=jax.ShapeDtypeStruct((top, tokens), F32),
        in_specs=vmem_specs(2 + 2 * group),
        out_specs=vmem_specs(1)[0],
        compiler_params=params(),
        cost_estimate=cost(4 * slots * tokens, 8 * top * tokens),
        name="combine",
    )(ids, slot_of, *own_scores, *other_scores)
    return (update[None, None], router.T[None])


def solution(mesh):
    placed = (
        P("section", "ep", None),
        P("section", "ep", None),
        P("section", "ep", None),
        P("section", "ep", None, None),
        P("section", "ep", None, None),
        P("section", "ep", None, None),
        P("section", "ep", None, None),
    )
    return jax.shard_map(
        local,
        mesh=mesh,
        in_specs=placed,
        out_specs=(P("section", "ep", None, None), P("section", "ep", None)),
        check_vma=False,
    )
```

```python
import functools

import jax
import jax.numpy as jnp
from jax import lax
from jax.experimental import pallas as pl
from jax.experimental.pallas import tpu as pltpu
from jax.sharding import PartitionSpec as P

beta_first = 0.9
beta_second = 0.95
adam_eps = 1e-08
decay_rate = 0.1
first_fix = 1.0 - 0.9**10
second_fix = 1.0 - 0.95**10

LANES = 128
TILE = 16
VMEM_BYTES = 48 * 1024 * 1024
F32 = jnp.float32
BF16 = jnp.bfloat16


def params():
    return pltpu.CompilerParams(vmem_limit_bytes=VMEM_BYTES)


def cost(flops, touched):
    return pl.CostEstimate(flops=int(flops), bytes_accessed=int(touched), transcendentals=0)


def specs(space, count):
    return [pl.BlockSpec(memory_space=space) for _ in range(count)]


def ep_index():
    return lax.axis_index("ep").astype(jnp.int32)


def own_half():
    sections = lax.axis_size("section")
    return jnp.where(lax.axis_index("section") < sections // 2, 0, 1).astype(jnp.int32)


def start_grads(grads_hbm, held, sems):
    half = held.shape[2]
    mine = own_half()
    copies = []
    for side in range(2):
        column = pl.multiple_of((1 - mine if side else mine) * half, half)
        copies.append(
            pltpu.make_async_copy(
                grads_hbm.at[:, pl.ds(column, half)], held.at[side], sems.at[side]
            )
        )
        copies[-1].start()
    return copies


def pick_rows(slots, k, cap):
    place = lax.broadcasted_iota(jnp.int32, (cap, slots.shape[1]), 0).astype(F32)
    return jnp.where(place == slots[k : k + 1, :], 1.0, 0.0).astype(BF16)


def fill_chunks(steps, cap, pick, held, copies, tiles, chunks):
    half = held.shape[2]
    data_rows = half // LANES * cap
    step = min(half, 2 * LANES)
    for side in range(2):
        for at, k in enumerate(steps):
            chunks[side * len(steps) + at][data_rows:, :] = tiles[k]
        copies[side].wait()
        for column in range(0, half, step):
            block = jnp.dot(
                pick, held[side, :, column : column + step], preferred_element_type=F32
            ).astype(BF16)
            for at in range(len(steps)):
                chunk = chunks[side * len(steps) + at]
                for part in range(step // LANES):
                    top = (column // LANES + part) * cap
                    chunk[top : top + cap, :] = block[
                        at * cap : (at + 1) * cap, part * LANES : (part + 1) * LANES
                    ]


def route_kernel(
    steps, group, cap, ids_hbm, weight_hbm, grads_hbm, slots_ref, tiles_ref, *rest
):
    chunks = rest[: 2 * len(steps)]
    ids_ref, weight_ref, held, sems = rest[2 * len(steps) :]
    tokens = held.shape[1]
    me = ep_index()
    small = [
        pltpu.make_async_copy(ids_hbm, ids_ref, sems.at[2]),
        pltpu.make_async_copy(weight_hbm, weight_ref, sems.at[3]),
    ]
    for copy in small:
        copy.start()
    copies = start_grads(grads_hbm, held, sems)
    earlier = lax.broadcasted_iota(jnp.int32, (tokens, tokens), 0)
    later = lax.broadcasted_iota(jnp.int32, (tokens, tokens), 1)
    ahead = jnp.where(earlier < later, 1.0, 0.0).astype(BF16)
    for copy in small:
        copy.wait()
    ids = ids_ref[...]
    weights = weight_ref[...].astype(F32)
    members, scales = [], []
    for k in range(group):
        named = ids == (me ^ k)
        members.append(jnp.sum(jnp.where(named, 1.0, 0.0), axis=0, keepdims=True))
        scales.append(jnp.sum(jnp.where(named, weights, 0.0), axis=0, keepdims=True))
    if group % TILE:
        members.append(jnp.zeros((-group % TILE, tokens), F32))
    member = jnp.concatenate(members, axis=0)
    before = jnp.dot(member.astype(BF16), ahead, preferred_element_type=F32)
    slots = jnp.where(member > 0.5, before, -1.0)
    slots_ref[...] = slots
    picks = [pick_rows(slots, k, cap) for k in range(group)]
    base = me * cap
    tile_row = lax.broadcasted_iota(jnp.int32, (TILE, LANES), 0)
    tile_lane = lax.broadcasted_iota(jnp.int32, (TILE, LANES), 1)
    spot = tile_row * LANES + tile_lane
    kept = (spot >= base) & (spot < base + cap)
    tiles = []
    for k in range(group):
        spread = jnp.broadcast_to(scales[k], (TILE, tokens)).astype(BF16)
        doubled = jnp.concatenate([picks[k]] * (LANES // cap), axis=0)
        tile = lax.dot_general(
            spread, doubled, (((1,), (1,)), ((), ())), preferred_element_type=F32
        )
        tiles.append(jnp.where(kept, tile, 0.0).astype(BF16))
        tiles_ref[k] = tiles[k]
    pick = jnp.concatenate([picks[k] for k in steps], axis=0)
    fill_chunks(steps, cap, pick, held, copies, tiles, chunks)


def later_kernel(steps, cap, slots_ref, tiles_ref, grads_hbm, *rest):
    chunks, (held, sems) = rest[-2 - 2 * len(steps) : -2], rest[-2:]
    copies = start_grads(grads_hbm, held, sems)
    slots = slots_ref[...]
    pick = jnp.concatenate([pick_rows(slots, k, cap) for k in steps], axis=0)
    fill_chunks(steps, cap, pick, held, copies, tiles_ref, chunks)


def inner_kernel(own_ref, other_ref, master_ref, inner_ref):
    weights = master_ref[...].astype(BF16)
    slots = own_ref.shape[1]
    for at, ref in ((0, own_ref), (slots, other_ref)):
        inner_ref[at : at + slots, :] = lax.dot_general(
            ref[...], weights, (((0,), (0,)), ((), ())), preferred_element_type=F32
        )


def score_kernel(items, group, cap, inner_ref, *rest):
    chunks, outs = rest[: len(items)], rest[-len(items) :]
    blocks = inner_ref.shape[1] // LANES
    me = ep_index()
    sums = []
    for (side, k), chunk in zip(items, chunks):
        start = pl.multiple_of(side * group * cap + (me ^ k) * cap, cap)
        total = jnp.zeros((cap, LANES), F32)
        for block in range(blocks):
            rows = chunk[block * cap : (block + 1) * cap, :].astype(F32)
            total += rows * inner_ref[pl.ds(start, cap), block * LANES : (block + 1) * LANES]
        sums.append(total)
    fold = LANES // cap
    for at in range(0, len(items), fold):
        some = sums[at : at + fold]
        if len(some) < fold:
            some.append(jnp.zeros(((fold - len(some)) * cap, LANES), F32))
        line = jnp.sum(jnp.concatenate(some, axis=0).T, axis=0, keepdims=True)
        for out in outs[at : at + fold]:
            out[...] = jnp.broadcast_to(line, out.shape)


def update_kernel(
    group, cap, own_ref, other_ref, master_ref, moment_ref, second_ref, *rest
):
    chunks = rest[: 2 * group]
    update_hbm, rows, scaled, total, update, sems = rest[2 * group :]
    slots = group * cap
    hid, half = update.shape
    data_rows = half // LANES * cap
    me = ep_index()
    for side in range(2):
        tile = jnp.zeros((TILE, LANES), F32)
        for k in range(group):
            chunk = chunks[side * group + k]
            tile += chunk[data_rows : data_rows + TILE, :].astype(F32)
            start = pl.multiple_of(side * slots + (me ^ k) * cap, cap)
            for block in range(half // LANES):
                rows[pl.ds(start, cap), block * LANES : (block + 1) * LANES] = chunk[
                    block * cap : (block + 1) * cap, :
                ]
        for part in range(slots // LANES):
            lanes = slice(part * LANES, (part + 1) * LANES)
            line = tile[part : part + 1, :]
            at = side * slots + part * LANES
            for top in range(0, hid, LANES):
                hidden = (own_ref, other_ref)[side][top : top + LANES, lanes]
                scaled[top : top + LANES, at : at + LANES] = (
                    hidden.astype(F32) * line
                ).astype(BF16)
    step = min(half, 2 * LANES)
    piece = 32

    def multiply(turn):
        total[turn % 2] = jnp.dot(
            scaled[...], rows[:, turn * step : (turn + 1) * step], preferred_element_type=F32
        )

    def adam(turn):
        columns = slice(turn * step, (turn + 1) * step)
        for top in range(0, hid, piece):
            lines = slice(top, top + piece)
            grad = total[turn % 2, lines, :]
            first = moment_ref[lines, columns].astype(F32) * (beta_first / first_fix) + grad * (
                (1.0 - beta_first) / first_fix
            )
            square = second_ref[lines, columns].astype(F32) * (beta_second / second_fix) + (
                grad * grad
            ) * ((1.0 - beta_second) / second_fix)
            root = square * lax.rsqrt(square) + adam_eps
            update[lines, columns] = (
                first * pl.reciprocal(root, approx=True) + decay_rate * master_ref[lines, columns]
            )

    copies = []
    multiply(0)
    for turn in range(half // step):
        if turn + 1 < half // step:
            multiply(turn + 1)
        adam(turn)
        columns = slice(turn * step, (turn + 1) * step)
        copies.append(
            pltpu.make_async_copy(update.at[:, columns], update_hbm.at[:, columns], sems.at[turn])
        )
        copies[-1].start()
    for copy in copies:
        copy.wait()


def combine_kernel(places, group, cap, ids_ref, slots_ref, *rest):
    scores, out_ref = rest[:-1], rest[-1]
    tokens = ids_ref.shape[1]
    me = ep_index()
    lines = [ref[0:1, :] for ref in scores]
    lines.append(jnp.zeros((LANES - len(lines), LANES), F32))
    columns = jnp.concatenate(lines, axis=0).T
    place = lax.broadcasted_iota(jnp.int32, (cap, tokens), 0).astype(F32)
    ids = ids_ref[...]
    result = jnp.zeros(ids.shape, F32)
    for k in range(group):
        score = 0.0
        for side in range(2):
            at = places[side * group + k]
            score += columns[at : at + cap, side * group + k : side * group + k + 1]
        chosen = jnp.sum(
            jnp.where(place == slots_ref[k : k + 1, :], score, 0.0), axis=0, keepdims=True
        )
        result = jnp.where(ids == (me ^ k), chosen, result)
    out_ref[...] = result


def moved(array, side, step):
    if (side, step) == (0, 0):
        return array
    sections, group = lax.axis_size("section"), lax.axis_size("ep")
    pairs = []
    for s in range(sections):
        target = (s + side * (sections // 2)) % sections
        for e in range(group):
            pairs.append((s * group + e, target * group + (e ^ step)))
    return lax.ppermute(array, ("section", "ep"), pairs)


def local(grad_out, router_weights, expert_ids, hidden, master, moment, second):
    group = lax.axis_size("ep")
    tokens, width = grad_out.shape[1:]
    top = expert_ids.shape[2]
    hid, slots = hidden.shape[2:]
    half = master.shape[3]
    cap = slots // group
    ids = expert_ids[0].T
    own_hidden = hidden[0, 0]
    param = master[0, 0]
    other_hidden = moved(own_hidden, 1, 0)

    far = group // 2
    steps = [k for k in range(1, group) if k != far]
    later_steps = [0, far]
    chunk = jax.ShapeDtypeStruct((half // LANES * cap + TILE, LANES), BF16)
    slot_rows = group + -group % TILE
    grads = pltpu.with_memory_space_constraint(grad_out[0], pltpu.HBM)
    held = pltpu.VMEM((2, tokens, half), BF16)
    routed = pl.pallas_call(
        functools.partial(route_kernel, steps, group, cap),
        out_shape=[
            jax.ShapeDtypeStruct((slot_rows, tokens), F32),
            jax.ShapeDtypeStruct((group, TILE, LANES), BF16),
        ]
        + [chunk] * (2 * len(steps)),
        in_specs=specs(pltpu.HBM, 3),
        out_specs=specs(pltpu.VMEM, 2 + 2 * len(steps)),
        scratch_shapes=[
            pltpu.VMEM((top, tokens), jnp.int32),
            pltpu.VMEM((top, tokens), BF16),
            held,
            pltpu.SemaphoreType.DMA((4,)),
        ],
        compiler_params=params(),
        cost_estimate=cost(2 * slots * tokens * width, 2 * (tokens + slots) * width),
        name="route",
    )(
        pltpu.with_memory_space_constraint(ids, pltpu.HBM),
        pltpu.with_memory_space_constraint(router_weights[0].T, pltpu.HBM),
        grads,
    )
    slot_of, tiles = routed[:2]
    arrived = {}
    for at in reversed(range(len(steps))):
        for side in range(2):
            sent = routed[2 + side * len(steps) + at]
            arrived[side, steps[at]] = moved(sent, side, steps[at])
    routed = pl.pallas_call(
        functools.partial(later_kernel, later_steps, cap),
        out_shape=[chunk] * (2 * len(later_steps)),
        in_specs=specs(pltpu.VMEM, 2) + specs(pltpu.HBM, 1) + specs(pl.ANY, 2),
        out_specs=specs(pltpu.VMEM, 2 * len(later_steps)),
        scratch_shapes=[held, pltpu.SemaphoreType.DMA((2,))],
        compiler_params=params(),
        cost_estimate=cost(2 * slots * tokens * width, 2 * (tokens + slots) * width),
        name="later",
    )(slot_of, tiles, grads, arrived[0, 1], arrived[1, 1])
    for at, k in ((1, far), (0, 0)):
        for side in range(2):
            arrived[side, k] = moved(routed[side * len(later_steps) + at], side, k)
    chunks = [arrived[side, k] for side in range(2) for k in range(group)]

    inner = pl.pallas_call(
        inner_kernel,
        out_shape=jax.ShapeDtypeStruct((2 * slots, half), F32),
        in_specs=specs(pltpu.VMEM, 3),
        out_specs=specs(pltpu.VMEM, 1)[0],
        compiler_params=params(),
        cost_estimate=cost(4 * slots * hid * half, 4 * hid * half + 8 * slots * half),
        name="inner",
    )(own_hidden, other_hidden, param)

    every = [(side, k) for side in range(2) for k in range(group)]
    last_items = [(0, far), (1, far)]
    waves = [[(0, 0)]]
    for k in steps + [0]:
        for side in range(2):
            if (side, k) != (0, 0):
                if len(waves[-1]) == (4 if len(waves) == 1 else 3):
                    waves.append([])
                waves[-1].append((side, k))
    returned, places = {}, {}
    for items in waves + [last_items]:
        done = list(returned.values())
        lines = pl.pallas_call(
            functools.partial(score_kernel, items, group, cap),
            out_shape=[jax.ShapeDtypeStruct((8, LANES), F32)] * len(items),
            in_specs=specs(pltpu.VMEM, 1 + len(items)) + specs(pl.ANY, len(done)),
            out_specs=specs(pltpu.VMEM, len(items)),
            compiler_params=params(),
            cost_estimate=cost(2 * len(items) * cap * half, 6 * len(items) * cap * half),
            name="score",
        )(inner, *[arrived[item] for item in items], *done)
        for at, (item, line) in enumerate(zip(items, lines)):
            returned[item] = moved(line, *item)
            places[item] = at * cap % LANES

    step = min(half, 2 * LANES)
    update = pl.pallas_call(
        functools.partial(update_kernel, group, cap),
        out_shape=jax.ShapeDtypeStruct((hid, half), F32),
        in_specs=specs(pltpu.VMEM, 5 + 2 * group),
        out_specs=specs(pltpu.HBM, 1)[0],
        scratch_shapes=[
            pltpu.VMEM((2 * slots, half), BF16),
            pltpu.VMEM((hid, 2 * slots), BF16),
            pltpu.VMEM((2, hid, step), F32),
            pltpu.VMEM((hid, half), F32),
            pltpu.SemaphoreType.DMA((half // step,)),
        ],
        compiler_params=params(),
        cost_estimate=cost(4 * slots * hid * half, 12 * hid * half + 4 * slots * half),
        name="update",
    )(own_hidden, other_hidden, param, moment[0, 0], second[0, 0], *chunks)
    router = pl.pallas_call(
        functools.partial(combine_kernel, [places[item] for item in every], group, cap),
        out_shape=jax.ShapeDtypeStruct((top, tokens), F32),
        in_specs=specs(pltpu.VMEM, 2 + 2 * group),
        out_specs=specs(pltpu.VMEM, 1)[0],
        compiler_params=params(),
        cost_estimate=cost(4 * slots * tokens, 8 * top * tokens),
        name="combine",
    )(ids, slot_of, *[returned[item] for item in every])
    return (update[None, None], router.T[None])


def solution(mesh):
    placed = (
        P("section", "ep", None),
        P("section", "ep", None),
        P("section", "ep", None),
        P("section", "ep", None, None),
        P("section", "ep", None, None),
        P("section", "ep", None, None),
        P("section", "ep", None, None),
    )
    return jax.shard_map(
        local,
        mesh=mesh,
        in_specs=placed,
        out_specs=(P("section", "ep", None, None), P("section", "ep", None)),
        check_vma=False,
    )
```

```python
import functools

import jax
import jax.numpy as jnp
from jax import lax
from jax.experimental import pallas as pl
from jax.experimental.pallas import tpu as pltpu
from jax.sharding import PartitionSpec as P

beta_first = 0.9
beta_second = 0.95
adam_eps = 1e-08
decay_rate = 0.1
first_fix = 1.0 - 0.9**10
second_fix = 1.0 - 0.95**10

LANES = 128
TILE = 16
VMEM_BYTES = 48 * 1024 * 1024
F32 = jnp.float32
BF16 = jnp.bfloat16


def params():
    return pltpu.CompilerParams(vmem_limit_bytes=VMEM_BYTES)


def cost(flops, touched):
    return pl.CostEstimate(flops=int(flops), bytes_accessed=int(touched), transcendentals=0)


def specs(space, count):
    return [pl.BlockSpec(memory_space=space) for _ in range(count)]


def ep_index():
    return lax.axis_index("ep").astype(jnp.int32)


def own_half():
    return lax.axis_index("pair").astype(jnp.int32)


def start_grads(grads_hbm, held, sems):
    half = held.shape[2]
    mine = own_half()
    copies = []
    for side in range(2):
        column = pl.multiple_of((1 - mine if side else mine) * half, half)
        copies.append(
            pltpu.make_async_copy(
                grads_hbm.at[:, pl.ds(column, half)], held.at[side], sems.at[side]
            )
        )
        copies[-1].start()
    return copies


def pick_rows(slots, k, cap):
    place = lax.broadcasted_iota(jnp.int32, (cap, slots.shape[1]), 0).astype(F32)
    return jnp.where(place == slots[k : k + 1, :], 1.0, 0.0).astype(BF16)


def fill_chunks(steps, cap, pick, held, copies, tiles, chunks):
    half = held.shape[2]
    data_rows = half // LANES * cap
    step = min(half, 2 * LANES)
    for side in range(2):
        for at, k in enumerate(steps):
            chunks[side * len(steps) + at][data_rows:, :] = tiles[k]
        copies[side].wait()
        for column in range(0, half, step):
            block = jnp.dot(
                pick, held[side, :, column : column + step], preferred_element_type=F32
            ).astype(BF16)
            for at in range(len(steps)):
                chunk = chunks[side * len(steps) + at]
                for part in range(step // LANES):
                    top = (column // LANES + part) * cap
                    chunk[top : top + cap, :] = block[
                        at * cap : (at + 1) * cap, part * LANES : (part + 1) * LANES
                    ]


def route_kernel(
    steps, group, cap, ids_hbm, weight_hbm, grads_hbm, slots_ref, *rest
):
    chunks = rest[: 2 * len(steps)]
    ids_ref, weight_ref, held, sems = rest[2 * len(steps) :]
    tokens = held.shape[1]
    me = ep_index()
    small = [
        pltpu.make_async_copy(ids_hbm, ids_ref, sems.at[2]),
        pltpu.make_async_copy(weight_hbm, weight_ref, sems.at[3]),
    ]
    for copy in small:
        copy.start()
    copies = start_grads(grads_hbm, held, sems)
    earlier = lax.broadcasted_iota(jnp.int32, (tokens, tokens), 0)
    later = lax.broadcasted_iota(jnp.int32, (tokens, tokens), 1)
    ahead = jnp.where(earlier < later, 1.0, 0.0).astype(BF16)
    for copy in small:
        copy.wait()
    ids = ids_ref[...]
    weights = weight_ref[...].astype(F32)
    members, scales = [], []
    for k in range(group):
        named = ids == (me ^ k)
        members.append(jnp.sum(jnp.where(named, 1.0, 0.0), axis=0, keepdims=True))
        scales.append(jnp.sum(jnp.where(named, weights, 0.0), axis=0, keepdims=True))
    if group % TILE:
        members.append(jnp.zeros((-group % TILE, tokens), F32))
    member = jnp.concatenate(members, axis=0)
    before = jnp.dot(member.astype(BF16), ahead, preferred_element_type=F32)
    slots = jnp.where(member > 0.5, before, -1.0)
    slots_ref[...] = slots
    picks = [pick_rows(slots, k, cap) for k in range(group)]
    base = me * cap
    tile_row = lax.broadcasted_iota(jnp.int32, (TILE, LANES), 0)
    tile_lane = lax.broadcasted_iota(jnp.int32, (TILE, LANES), 1)
    spot = tile_row * LANES + tile_lane
    kept = (spot >= base) & (spot < base + cap)
    tiles = []
    for k in range(group):
        spread = jnp.broadcast_to(scales[k], (TILE, tokens)).astype(BF16)
        doubled = jnp.concatenate([picks[k]] * (LANES // cap), axis=0)
        tile = lax.dot_general(
            spread, doubled, (((1,), (1,)), ((), ())), preferred_element_type=F32
        )
        tiles.append(jnp.where(kept, tile, 0.0).astype(BF16))
    pick = jnp.concatenate([picks[k] for k in steps], axis=0)
    fill_chunks(steps, cap, pick, held, copies, tiles, chunks)


def inner_kernel(own_ref, other_ref, master_ref, inner_ref):
    weights = master_ref[...].astype(BF16)
    slots = own_ref.shape[1]
    for at, ref in ((0, own_ref), (slots, other_ref)):
        inner_ref[at : at + slots, :] = lax.dot_general(
            ref[...], weights, (((0,), (0,)), ((), ())), preferred_element_type=F32
        )


def score_kernel(group, cap, inner_ref, *rest):
    chunks, out_ref = rest[:-1], rest[-1]
    blocks = inner_ref.shape[1] // LANES
    me = ep_index()
    mine = own_half()
    for k in range(group):
        sums = []
        for side in range(2):
            start = pl.multiple_of(side * group * cap + (me ^ k) * cap, cap)
            total = jnp.zeros((cap, LANES), F32)
            for block in range(blocks):
                rows = chunks[side * group + k][block * cap : (block + 1) * cap, :].astype(F32)
                total += rows * inner_ref[pl.ds(start, cap), block * LANES : (block + 1) * LANES]
            sums.append(total)
        both = jnp.concatenate(sums, axis=0)
        line = jnp.sum(both.T, axis=0, keepdims=True)
        for side in range(2):
            out_ref[(mine ^ side) * group + (me ^ k)] = jnp.broadcast_to(line, out_ref.shape[1:])


def update_kernel(
    group, cap, own_ref, other_ref, master_ref, moment_ref, second_ref, *rest
):
    chunks = rest[: 2 * group]
    update_hbm, rows, scaled, total, update, sems = rest[2 * group :]
    slots = group * cap
    hid, half = update.shape
    data_rows = half // LANES * cap
    me = ep_index()
    for side in range(2):
        tile = jnp.zeros((TILE, LANES), F32)
        for k in range(group):
            chunk = chunks[side * group + k]
            tile += chunk[data_rows : data_rows + TILE, :].astype(F32)
            start = pl.multiple_of(side * slots + (me ^ k) * cap, cap)
            for block in range(half // LANES):
                rows[pl.ds(start, cap), block * LANES : (block + 1) * LANES] = chunk[
                    block * cap : (block + 1) * cap, :
                ]
        for part in range(slots // LANES):
            lanes = slice(part * LANES, (part + 1) * LANES)
            line = tile[part : part + 1, :]
            at = side * slots + part * LANES
            for top in range(0, hid, LANES):
                hidden = (own_ref, other_ref)[side][top : top + LANES, lanes]
                scaled[top : top + LANES, at : at + LANES] = (
                    hidden.astype(F32) * line
                ).astype(BF16)
    step = min(half, 2 * LANES)
    piece = 32

    def multiply(turn):
        total[turn % 2] = jnp.dot(
            scaled[...], rows[:, turn * step : (turn + 1) * step], preferred_element_type=F32
        )

    def adam(turn):
        columns = slice(turn * step, (turn + 1) * step)
        for top in range(0, hid, piece):
            lines = slice(top, top + piece)
            grad = total[turn % 2, lines, :]
            first = moment_ref[lines, columns].astype(F32) * (beta_first / first_fix) + grad * (
                (1.0 - beta_first) / first_fix
            )
            square = second_ref[lines, columns].astype(F32) * (beta_second / second_fix) + (
                grad * grad
            ) * ((1.0 - beta_second) / second_fix)
            root = square * lax.rsqrt(square) + adam_eps
            update[lines, columns] = (
                first * pl.reciprocal(root, approx=True) + decay_rate * master_ref[lines, columns]
            )

    copies = []
    multiply(0)
    for turn in range(half // step):
        if turn + 1 < half // step:
            multiply(turn + 1)
        adam(turn)
        columns = slice(turn * step, (turn + 1) * step)
        copies.append(
            pltpu.make_async_copy(update.at[:, columns], update_hbm.at[:, columns], sems.at[turn])
        )
        copies[-1].start()
    for copy in copies:
        copy.wait()


def combine_kernel(group, cap, ids_ref, slots_ref, score_ref, out_ref):
    tokens = ids_ref.shape[1]
    me = ep_index()
    mine = own_half()
    lane = lax.broadcasted_iota(jnp.int32, (1, LANES), 1)
    lines = []
    for k in range(group):
        own = score_ref[mine * group + (me ^ k)][0:1, :]
        other = score_ref[(1 - mine) * group + (me ^ k)][0:1, :]
        lines.append(jnp.where(lane < cap, own, other))
    lines.append(jnp.zeros((LANES - group, LANES), F32))
    columns = jnp.concatenate(lines, axis=0).T
    columns = columns[:cap] + columns[cap : 2 * cap]
    place = lax.broadcasted_iota(jnp.int32, (cap, tokens), 0).astype(F32)
    ids = ids_ref[...]
    result = jnp.zeros(ids.shape, F32)
    for k in range(group):
        at_slot = jnp.where(place == slots_ref[k : k + 1, :], columns[:, k : k + 1], 0.0)
        result = jnp.where(ids == (me ^ k), jnp.sum(at_slot, axis=0, keepdims=True), result)
    out_ref[...] = result


def moved(array, side, step):
    group = lax.axis_size("ep")
    pairs = [
        (p * group + e, (p ^ side) * group + (e ^ step)) for p in range(2) for e in range(group)
    ]
    return lax.ppermute(array, ("pair", "ep"), pairs)


def local(grad_out, router_weights, expert_ids, hidden, master, moment, second):
    group = lax.axis_size("ep")
    tokens, width = grad_out.shape[1:]
    top = expert_ids.shape[2]
    hid, slots = hidden.shape[2:]
    half = master.shape[3]
    cap = slots // group
    ids = expert_ids[0].T
    own_hidden = hidden[0, 0]
    param = master[0, 0]
    other_hidden = moved(own_hidden, 1, 0)

    steps = list(range(group))
    chunk = jax.ShapeDtypeStruct((half // LANES * cap + TILE, LANES), BF16)
    routed = pl.pallas_call(
        functools.partial(route_kernel, steps, group, cap),
        out_shape=[jax.ShapeDtypeStruct((group + -group % TILE, tokens), F32)]
        + [chunk] * (2 * group),
        in_specs=specs(pltpu.HBM, 3),
        out_specs=specs(pltpu.VMEM, 1 + 2 * group),
        scratch_shapes=[
            pltpu.VMEM((top, tokens), jnp.int32),
            pltpu.VMEM((top, tokens), BF16),
            pltpu.VMEM((2, tokens, half), BF16),
            pltpu.SemaphoreType.DMA((4,)),
        ],
        compiler_params=params(),
        cost_estimate=cost(2 * slots * tokens * width, 2 * (tokens + slots) * width),
        name="route",
    )(
        pltpu.with_memory_space_constraint(ids, pltpu.HBM),
        pltpu.with_memory_space_constraint(router_weights[0].T, pltpu.HBM),
        pltpu.with_memory_space_constraint(grad_out[0], pltpu.HBM),
    )
    slot_of, sent = routed[0], routed[1:]
    arrived = {(0, 0): sent[0]}
    by_distance = list(range(group - 1, 1, -1))
    order = [(0, 1)] + [(side, k) for k in by_distance for side in range(2)] + [(1, 1), (1, 0)]
    for side, k in order:
        arrived[side, k] = moved(sent[side * group + k], side, k)
    chunks = [arrived[side, k] for side in range(2) for k in range(group)]

    inner = pl.pallas_call(
        inner_kernel,
        out_shape=jax.ShapeDtypeStruct((2 * slots, half), F32),
        in_specs=specs(pltpu.VMEM, 3),
        out_specs=specs(pltpu.VMEM, 1)[0],
        compiler_params=params(),
        cost_estimate=cost(4 * slots * hid * half, 4 * hid * half + 8 * slots * half),
        name="inner",
    )(own_hidden, other_hidden, param)

    scores = pl.pallas_call(
        functools.partial(score_kernel, group, cap),
        out_shape=jax.ShapeDtypeStruct((2 * group, 8, LANES), F32),
        in_specs=specs(pltpu.VMEM, 1 + 2 * group),
        out_specs=specs(pltpu.VMEM, 1)[0],
        compiler_params=params(),
        cost_estimate=cost(4 * slots * half, 12 * slots * half),
        name="score",
    )(inner, *chunks)
    returned = lax.all_to_all(scores, ("pair", "ep"), split_axis=0, concat_axis=0, tiled=True)

    step = min(half, 2 * LANES)
    update = pl.pallas_call(
        functools.partial(update_kernel, group, cap),
        out_shape=jax.ShapeDtypeStruct((hid, half), F32),
        in_specs=specs(pltpu.VMEM, 5 + 2 * group),
        out_specs=specs(pltpu.HBM, 1)[0],
        scratch_shapes=[
            pltpu.VMEM((2 * slots, half), BF16),
            pltpu.VMEM((hid, 2 * slots), BF16),
            pltpu.VMEM((2, hid, step), F32),
            pltpu.VMEM((hid, half), F32),
            pltpu.SemaphoreType.DMA((half // step,)),
        ],
        compiler_params=params(),
        cost_estimate=cost(4 * slots * hid * half, 12 * hid * half + 4 * slots * half),
        name="update",
    )(own_hidden, other_hidden, param, moment[0, 0], second[0, 0], *chunks)
    router = pl.pallas_call(
        functools.partial(combine_kernel, group, cap),
        out_shape=jax.ShapeDtypeStruct((top, tokens), F32),
        in_specs=specs(pltpu.VMEM, 3),
        out_specs=specs(pltpu.VMEM, 1)[0],
        compiler_params=params(),
        cost_estimate=cost(4 * slots * tokens, 8 * top * tokens),
        name="combine",
    )(ids, slot_of, returned)
    return (update[None, None], router.T[None])


def solution(mesh):
    sections, group = mesh.devices.shape
    split = jax.sharding.Mesh(
        mesh.devices.reshape(2, sections // 2, group), ("pair", "rest", "ep")
    )
    section = ("pair", "rest")
    rows = P(section, "ep", None)
    blocks = P(section, "ep", None, None)
    return jax.shard_map(
        local,
        mesh=split,
        in_specs=(rows, rows, rows, blocks, blocks, blocks, blocks),
        out_specs=(blocks, rows),
        check_vma=False,
    )
```

```python
import functools

import jax
import jax.numpy as jnp
from jax import lax
from jax.experimental import pallas as pl
from jax.experimental.pallas import tpu as pltpu
from jax.sharding import PartitionSpec as P

beta_first = 0.9
beta_second = 0.95
adam_eps = 1e-08
decay_rate = 0.1
first_fix = 1.0 - 0.9**10
second_fix = 1.0 - 0.95**10

LANES = 128
TILE = 16
VMEM_BYTES = 32 * 1024 * 1024
F32 = jnp.float32
BF16 = jnp.bfloat16


def params():
    return pltpu.CompilerParams(vmem_limit_bytes=VMEM_BYTES)


def cost(flops, touched):
    return pl.CostEstimate(flops=int(flops), bytes_accessed=int(touched), transcendentals=0)


def specs(space, count):
    return [pl.BlockSpec(memory_space=space) for _ in range(count)]


def ep_index():
    return lax.axis_index("ep").astype(jnp.int32)


def own_half():
    return lax.axis_index("pair").astype(jnp.int32)


def start_grads(grads_hbm, held, sems):
    half = held.shape[2]
    mine = own_half()
    copies = []
    for side in range(2):
        column = pl.multiple_of((1 - mine if side else mine) * half, half)
        copies.append(
            pltpu.make_async_copy(
                grads_hbm.at[:, pl.ds(column, half)], held.at[side], sems.at[side]
            )
        )
        copies[-1].start()
    return copies


def pick_rows(slots, k, cap):
    place = lax.broadcasted_iota(jnp.int32, (cap, slots.shape[1]), 0).astype(F32)
    return jnp.where(place == slots[k : k + 1, :], 1.0, 0.0).astype(BF16)


def fill_chunks(group, cap, pick, held, copies, tiles, chunks):
    half = held.shape[2]
    data_rows = half // LANES * cap
    step = min(half, 2 * LANES)
    for side in range(2):
        for k in range(group):
            chunks[side, k][data_rows:, :] = tiles[k]
        copies[side].wait()
        for column in range(0, half, step):
            block = jnp.dot(
                pick, held[side, :, column : column + step], preferred_element_type=F32
            ).astype(BF16)
            for k in range(group):
                for part in range(step // LANES):
                    top = (column // LANES + part) * cap
                    chunks[side, k][top : top + cap, :] = block[
                        k * cap : (k + 1) * cap, part * LANES : (part + 1) * LANES
                    ]


def route_kernel(
    items, group, cap, ids_hbm, weight_hbm, grads_hbm, slots_ref, *rest
):
    chunks = dict(zip(items, rest))
    ids_ref, weight_ref, held, sems = rest[len(items) :]
    tokens = held.shape[1]
    me = ep_index()
    small = [
        pltpu.make_async_copy(ids_hbm, ids_ref, sems.at[2]),
        pltpu.make_async_copy(weight_hbm, weight_ref, sems.at[3]),
    ]
    for copy in small:
        copy.start()
    copies = start_grads(grads_hbm, held, sems)
    earlier = lax.broadcasted_iota(jnp.int32, (tokens, tokens), 0)
    later = lax.broadcasted_iota(jnp.int32, (tokens, tokens), 1)
    ahead = jnp.where(earlier < later, 1.0, 0.0).astype(BF16)
    for copy in small:
        copy.wait()
    ids = ids_ref[...]
    weights = weight_ref[...].astype(F32)
    members, scales = [], []
    for k in range(group):
        named = ids == (me ^ k)
        members.append(jnp.sum(jnp.where(named, 1.0, 0.0), axis=0, keepdims=True))
        scales.append(jnp.sum(jnp.where(named, weights, 0.0), axis=0, keepdims=True))
    if group % TILE:
        members.append(jnp.zeros((-group % TILE, tokens), F32))
    member = jnp.concatenate(members, axis=0)
    before = jnp.dot(member.astype(BF16), ahead, preferred_element_type=F32)
    slots = jnp.where(member > 0.5, before, -1.0)
    slots_ref[...] = slots
    picks = [pick_rows(slots, k, cap) for k in range(group)]
    base = me * cap
    tile_row = lax.broadcasted_iota(jnp.int32, (TILE, LANES), 0)
    tile_lane = lax.broadcasted_iota(jnp.int32, (TILE, LANES), 1)
    spot = tile_row * LANES + tile_lane
    kept = (spot >= base) & (spot < base + cap)
    tiles = []
    for k in range(group):
        spread = jnp.broadcast_to(scales[k], (TILE, tokens)).astype(BF16)
        doubled = jnp.concatenate([picks[k]] * (LANES // cap), axis=0)
        tile = lax.dot_general(
            spread, doubled, (((1,), (1,)), ((), ())), preferred_element_type=F32
        )
        tiles.append(jnp.where(kept, tile, 0.0).astype(BF16))
    pick = jnp.concatenate(picks, axis=0)
    fill_chunks(group, cap, pick, held, copies, tiles, chunks)


def inner_kernel(own_ref, other_ref, master_ref, inner_ref):
    weights = master_ref[...].astype(BF16)
    slots = own_ref.shape[1]
    for at, ref in ((0, own_ref), (slots, other_ref)):
        inner_ref[at : at + slots, :] = lax.dot_general(
            ref[...], weights, (((0,), (0,)), ((), ())), preferred_element_type=F32
        )


def score_kernel(group, cap, inner_ref, *rest):
    chunks, out_ref = rest[:-1], rest[-1]
    blocks = inner_ref.shape[1] // LANES
    me = ep_index()
    row = lax.broadcasted_iota(jnp.int32, out_ref.shape, 0)
    result = jnp.zeros(out_ref.shape, F32)
    for k in range(group):
        sums = []
        for side in range(2):
            start = pl.multiple_of(side * group * cap + (me ^ k) * cap, cap)
            total = jnp.zeros((cap, LANES), F32)
            for block in range(blocks):
                rows = chunks[side * group + k][block * cap : (block + 1) * cap, :].astype(F32)
                total += rows * inner_ref[pl.ds(start, cap), block * LANES : (block + 1) * LANES]
            sums.append(total)
        both = jnp.concatenate(sums, axis=0)
        line = jnp.sum(both.T, axis=0, keepdims=True)
        result = jnp.where(row == (me ^ k), line, result)
    out_ref[...] = result


def update_kernel(
    group, cap, own_ref, other_ref, master_ref, moment_hbm, second_hbm, *rest
):
    chunks = rest[: 2 * group]
    update_hbm, rows, scaled, total, update, moment_ref, second_ref, sems = rest[2 * group :]
    loads = [
        pltpu.make_async_copy(moment_hbm, moment_ref, sems.at[0]),
        pltpu.make_async_copy(second_hbm, second_ref, sems.at[1]),
    ]
    for load in loads:
        load.start()
    slots = group * cap
    hid, half = update.shape
    data_rows = half // LANES * cap
    me = ep_index()
    for side in range(2):
        tile = jnp.zeros((TILE, LANES), F32)
        for k in range(group):
            chunk = chunks[side * group + k]
            tile += chunk[data_rows : data_rows + TILE, :].astype(F32)
            start = pl.multiple_of(side * slots + (me ^ k) * cap, cap)
            for block in range(half // LANES):
                rows[pl.ds(start, cap), block * LANES : (block + 1) * LANES] = chunk[
                    block * cap : (block + 1) * cap, :
                ]
        for part in range(slots // LANES):
            lanes = slice(part * LANES, (part + 1) * LANES)
            line = tile[part : part + 1, :]
            at = side * slots + part * LANES
            for top in range(0, hid, LANES):
                hidden = (own_ref, other_ref)[side][top : top + LANES, lanes]
                scaled[top : top + LANES, at : at + LANES] = (
                    hidden.astype(F32) * line
                ).astype(BF16)
    step = min(half, 2 * LANES)
    piece = 32

    def multiply(turn):
        total[turn % 2] = jnp.dot(
            scaled[...], rows[:, turn * step : (turn + 1) * step], preferred_element_type=F32
        )

    def adam(turn):
        columns = slice(turn * step, (turn + 1) * step)
        for top in range(0, hid, piece):
            lines = slice(top, top + piece)
            grad = total[turn % 2, lines, :]
            first = moment_ref[lines, columns].astype(F32) * (beta_first / first_fix) + grad * (
                (1.0 - beta_first) / first_fix
            )
            square = second_ref[lines, columns].astype(F32) * (beta_second / second_fix) + (
                grad * grad
            ) * ((1.0 - beta_second) / second_fix)
            root = square * lax.rsqrt(square) + adam_eps
            update[lines, columns] = (
                first * pl.reciprocal(root, approx=True) + decay_rate * master_ref[lines, columns]
            )

    copies = []
    multiply(0)
    for load in loads:
        load.wait()
    for turn in range(half // step):
        if turn + 1 < half // step:
            multiply(turn + 1)
        adam(turn)
        columns = slice(turn * step, (turn + 1) * step)
        copies.append(
            pltpu.make_async_copy(update.at[:, columns], update_hbm.at[:, columns], sems.at[2 + turn])
        )
        copies[-1].start()
    for copy in copies:
        copy.wait()


def combine_kernel(group, cap, ids_ref, slots_ref, score_ref, out_ref):
    tokens = ids_ref.shape[1]
    me = ep_index()
    mine = own_half()
    row = lax.broadcasted_iota(jnp.int32, score_ref.shape[1:], 0)
    lane = lax.broadcasted_iota(jnp.int32, (1, LANES), 1)
    lines = []
    for k in range(group):
        sides = [
            jnp.sum(
                jnp.where(row == me, score_ref[(mine ^ side) * group + (me ^ k)], 0.0),
                axis=0,
                keepdims=True,
            )
            for side in range(2)
        ]
        lines.append(jnp.where(lane < cap, sides[0], sides[1]))
    lines.append(jnp.zeros((LANES - group, LANES), F32))
    columns = jnp.concatenate(lines, axis=0).T
    columns = columns[:cap] + columns[cap : 2 * cap]
    place = lax.broadcasted_iota(jnp.int32, (cap, tokens), 0).astype(F32)
    ids = ids_ref[...]
    result = jnp.zeros(ids.shape, F32)
    for k in range(group):
        at_slot = jnp.where(place == slots_ref[k : k + 1, :], columns[:, k : k + 1], 0.0)
        result = jnp.where(ids == (me ^ k), jnp.sum(at_slot, axis=0, keepdims=True), result)
    out_ref[...] = result


def moved(array, side, step):
    if (side, step) == (0, 0):
        return array
    group = lax.axis_size("ep")
    pairs = [
        (p * group + e, (p ^ side) * group + (e ^ step)) for p in range(2) for e in range(group)
    ]
    return lax.ppermute(array, ("pair", "ep"), pairs)


def local(grad_out, router_weights, expert_ids, hidden, master, moment, second):
    group = lax.axis_size("ep")
    tokens, width = grad_out.shape[1:]
    top = expert_ids.shape[2]
    hid, slots = hidden.shape[2:]
    half = master.shape[3]
    cap = slots // group
    ids = expert_ids[0].T
    own_hidden = hidden[0, 0]
    param = master[0, 0]
    other_hidden = moved(own_hidden, 1, 0)

    order = [(0, 1)] + [(side, k) for k in range(group - 1, 1, -1) for side in range(2)]
    order += [(1, 1), (1, 0), (0, 0)]
    chunk = jax.ShapeDtypeStruct((half // LANES * cap + TILE, LANES), BF16)
    routed = pl.pallas_call(
        functools.partial(route_kernel, order, group, cap),
        out_shape=[jax.ShapeDtypeStruct((group + -group % TILE, tokens), F32)]
        + [chunk] * (2 * group),
        in_specs=specs(pltpu.HBM, 3),
        out_specs=specs(pltpu.VMEM, 1 + 2 * group),
        scratch_shapes=[
            pltpu.VMEM((top, tokens), jnp.int32),
            pltpu.VMEM((top, tokens), BF16),
            pltpu.VMEM((2, tokens, half), BF16),
            pltpu.SemaphoreType.DMA((4,)),
        ],
        compiler_params=params(),
        cost_estimate=cost(2 * slots * tokens * width, 2 * (tokens + slots) * width),
        name="route",
    )(
        pltpu.with_memory_space_constraint(ids, pltpu.HBM),
        pltpu.with_memory_space_constraint(router_weights[0].T, pltpu.HBM),
        pltpu.with_memory_space_constraint(grad_out[0], pltpu.HBM),
    )
    slot_of = routed[0]
    arrived = {item: moved(sent, *item) for item, sent in zip(order, routed[1:])}
    chunks = [arrived[side, k] for side in range(2) for k in range(group)]

    inner = pl.pallas_call(
        inner_kernel,
        out_shape=jax.ShapeDtypeStruct((2 * slots, half), F32),
        in_specs=specs(pltpu.VMEM, 3),
        out_specs=specs(pltpu.VMEM, 1)[0],
        compiler_params=params(),
        cost_estimate=cost(4 * slots * hid * half, 4 * hid * half + 8 * slots * half),
        name="inner",
    )(own_hidden, other_hidden, param)

    scores = pl.pallas_call(
        functools.partial(score_kernel, group, cap),
        out_shape=jax.ShapeDtypeStruct((group + -group % 8, LANES), F32),
        in_specs=specs(pltpu.VMEM, 1 + 2 * group),
        out_specs=specs(pltpu.VMEM, 1)[0],
        compiler_params=params(),
        cost_estimate=cost(4 * slots * half, 12 * slots * half),
        name="score",
    )(inner, *chunks)
    returned = lax.all_gather(scores, ("pair", "ep"), axis=0, tiled=False)

    step = min(half, 2 * LANES)
    update = pl.pallas_call(
        functools.partial(update_kernel, group, cap),
        out_shape=jax.ShapeDtypeStruct((hid, half), F32),
        in_specs=specs(pltpu.VMEM, 3) + specs(pltpu.HBM, 2) + specs(pltpu.VMEM, 2 * group),
        out_specs=specs(pltpu.HBM, 1)[0],
        scratch_shapes=[
            pltpu.VMEM((2 * slots, half), BF16),
            pltpu.VMEM((hid, 2 * slots), BF16),
            pltpu.VMEM((2, hid, step), F32),
            pltpu.VMEM((hid, half), F32),
            pltpu.VMEM((hid, half), BF16),
            pltpu.VMEM((hid, half), BF16),
            pltpu.SemaphoreType.DMA((2 + half // step,)),
        ],
        compiler_params=params(),
        cost_estimate=cost(4 * slots * hid * half, 12 * hid * half + 4 * slots * half),
        name="update",
    )(
        own_hidden,
        other_hidden,
        param,
        pltpu.with_memory_space_constraint(moment[0, 0], pltpu.HBM),
        pltpu.with_memory_space_constraint(second[0, 0], pltpu.HBM),
        *chunks,
    )
    router = pl.pallas_call(
        functools.partial(combine_kernel, group, cap),
        out_shape=jax.ShapeDtypeStruct((top, tokens), F32),
        in_specs=specs(pltpu.VMEM, 3),
        out_specs=specs(pltpu.VMEM, 1)[0],
        compiler_params=params(),
        cost_estimate=cost(4 * slots * tokens, 8 * top * tokens),
        name="combine",
    )(ids, slot_of, returned)
    return (update[None, None], router.T[None])


def solution(mesh):
    sections, group = mesh.devices.shape
    split = jax.sharding.Mesh(
        mesh.devices.reshape(2, sections // 2, group), ("pair", "rest", "ep")
    )
    section = ("pair", "rest")
    rows = P(section, "ep", None)
    blocks = P(section, "ep", None, None)
    return jax.shard_map(
        local,
        mesh=split,
        in_specs=(rows, rows, rows, blocks, blocks, blocks, blocks),
        out_specs=(blocks, rows),
        check_vma=False,
    )
```

```python
import functools

import jax
import jax.numpy as jnp
from jax import lax
from jax.experimental import pallas as pl
from jax.experimental.pallas import tpu as pltpu
from jax.sharding import PartitionSpec as P

beta_first = 0.9
beta_second = 0.95
adam_eps = 1e-08
decay_rate = 0.1
first_fix = 1.0 - 0.9**10
second_fix = 1.0 - 0.95**10

LANES = 128
TILE = 16
VMEM_BYTES = 32 * 1024 * 1024
F32 = jnp.float32
BF16 = jnp.bfloat16


def params():
    return pltpu.CompilerParams(vmem_limit_bytes=VMEM_BYTES)


def cost(flops, touched):
    return pl.CostEstimate(flops=int(flops), bytes_accessed=int(touched), transcendentals=0)


def specs(space, count):
    return [pl.BlockSpec(memory_space=space) for _ in range(count)]


def ep_index():
    return lax.axis_index("ep").astype(jnp.int32)


def own_half():
    return lax.axis_index("pair").astype(jnp.int32)


def start_grads(grads_hbm, held, sems):
    half = held.shape[2]
    mine = own_half()
    copies = []
    for side in range(2):
        column = pl.multiple_of((1 - mine if side else mine) * half, half)
        copies.append(
            pltpu.make_async_copy(
                grads_hbm.at[:, pl.ds(column, half)], held.at[side], sems.at[side]
            )
        )
        copies[-1].start()
    return copies


def pick_rows(slots, k, cap):
    place = lax.broadcasted_iota(jnp.int32, (cap, slots.shape[1]), 0).astype(F32)
    return jnp.where(place == slots[k : k + 1, :], 1.0, 0.0).astype(BF16)


def fill_chunks(group, cap, pick, held, copies, tiles, chunks):
    half = held.shape[2]
    data_rows = half // LANES * cap
    step = min(half, 2 * LANES)
    for side in range(2):
        for k in range(group):
            chunks[side, k][data_rows:, :] = tiles[k]
        copies[side].wait()
        for column in range(0, half, step):
            block = jnp.dot(
                pick, held[side, :, column : column + step], preferred_element_type=F32
            ).astype(BF16)
            for k in range(group):
                for part in range(step // LANES):
                    top = (column // LANES + part) * cap
                    chunks[side, k][top : top + cap, :] = block[
                        k * cap : (k + 1) * cap, part * LANES : (part + 1) * LANES
                    ]


def route_kernel(
    items, group, cap, ids_hbm, weight_hbm, grads_hbm, slots_ref, *rest
):
    chunks = dict(zip(items, rest))
    ids_ref, weight_ref, held, sems = rest[len(items) :]
    tokens = held.shape[1]
    me = ep_index()
    small = [
        pltpu.make_async_copy(ids_hbm, ids_ref, sems.at[2]),
        pltpu.make_async_copy(weight_hbm, weight_ref, sems.at[3]),
    ]
    for copy in small:
        copy.start()
    copies = start_grads(grads_hbm, held, sems)
    earlier = lax.broadcasted_iota(jnp.int32, (tokens, tokens), 0)
    later = lax.broadcasted_iota(jnp.int32, (tokens, tokens), 1)
    ahead = jnp.where(earlier < later, 1.0, 0.0).astype(BF16)
    for copy in small:
        copy.wait()
    ids = ids_ref[...]
    weights = weight_ref[...].astype(F32)
    members, scales = [], []
    for k in range(group):
        named = ids == (me ^ k)
        members.append(jnp.sum(jnp.where(named, 1.0, 0.0), axis=0, keepdims=True))
        scales.append(jnp.sum(jnp.where(named, weights, 0.0), axis=0, keepdims=True))
    if group % TILE:
        members.append(jnp.zeros((-group % TILE, tokens), F32))
    member = jnp.concatenate(members, axis=0)
    before = jnp.dot(member.astype(BF16), ahead, preferred_element_type=F32)
    slots = jnp.where(member > 0.5, before, -1.0)
    slots_ref[...] = slots
    picks = [pick_rows(slots, k, cap) for k in range(group)]
    base = me * cap
    tile_row = lax.broadcasted_iota(jnp.int32, (TILE, LANES), 0)
    tile_lane = lax.broadcasted_iota(jnp.int32, (TILE, LANES), 1)
    spot = tile_row * LANES + tile_lane
    kept = (spot >= base) & (spot < base + cap)
    tiles = []
    for k in range(group):
        spread = jnp.broadcast_to(scales[k], (TILE, tokens)).astype(BF16)
        doubled = jnp.concatenate([picks[k]] * (LANES // cap), axis=0)
        tile = lax.dot_general(
            spread, doubled, (((1,), (1,)), ((), ())), preferred_element_type=F32
        )
        tiles.append(jnp.where(kept, tile, 0.0).astype(BF16))
    pick = jnp.concatenate(picks, axis=0)
    fill_chunks(group, cap, pick, held, copies, tiles, chunks)


def inner_kernel(own_ref, other_ref, master_ref, inner_ref):
    weights = master_ref[...].astype(BF16)
    slots = own_ref.shape[1]
    for at, ref in ((0, own_ref), (slots, other_ref)):
        inner_ref[at : at + slots, :] = lax.dot_general(
            ref[...], weights, (((0,), (0,)), ((), ())), preferred_element_type=F32
        )


def score_kernel(items, group, cap, inner_ref, *rest):
    chunks, out_ref = dict(zip(items, rest)), rest[-1]
    blocks = inner_ref.shape[1] // LANES
    me = ep_index()
    mine = own_half()
    for k in range(group):
        sums = []
        for side in range(2):
            start = pl.multiple_of(side * group * cap + (me ^ k) * cap, cap)
            total = jnp.zeros((cap, LANES), F32)
            for block in range(blocks):
                rows = chunks[side, k][block * cap : (block + 1) * cap, :].astype(F32)
                total += rows * inner_ref[pl.ds(start, cap), block * LANES : (block + 1) * LANES]
            sums.append(total)
        both = jnp.concatenate(sums, axis=0)
        line = jnp.sum(both.T, axis=0, keepdims=True)
        for side in range(2):
            out_ref[(mine ^ side) * group + (me ^ k)] = jnp.broadcast_to(line, out_ref.shape[1:])


def update_kernel(
    items, group, cap, own_ref, other_ref, master_ref, moment_hbm, second_hbm, *rest
):
    chunks = dict(zip(items, rest))
    update_hbm, rows, scaled, total, update, moment_ref, second_ref, sems = rest[2 * group :]
    loads = [
        pltpu.make_async_copy(moment_hbm, moment_ref, sems.at[0]),
        pltpu.make_async_copy(second_hbm, second_ref, sems.at[1]),
    ]
    for load in loads:
        load.start()
    slots = group * cap
    hid, half = update.shape
    data_rows = half // LANES * cap
    me = ep_index()
    for side in range(2):
        tile = jnp.zeros((TILE, LANES), F32)
        for k in range(group):
            chunk = chunks[side, k]
            tile += chunk[data_rows : data_rows + TILE, :].astype(F32)
            start = pl.multiple_of(side * slots + (me ^ k) * cap, cap)
            for block in range(half // LANES):
                rows[pl.ds(start, cap), block * LANES : (block + 1) * LANES] = chunk[
                    block * cap : (block + 1) * cap, :
                ]
        for part in range(slots // LANES):
            lanes = slice(part * LANES, (part + 1) * LANES)
            line = tile[part : part + 1, :]
            at = side * slots + part * LANES
            for top in range(0, hid, LANES):
                hidden = (own_ref, other_ref)[side][top : top + LANES, lanes]
                scaled[top : top + LANES, at : at + LANES] = (
                    hidden.astype(F32) * line
                ).astype(BF16)
    step = min(half, 2 * LANES)
    piece = 32

    def multiply(turn):
        total[turn % 2] = jnp.dot(
            scaled[...], rows[:, turn * step : (turn + 1) * step], preferred_element_type=F32
        )

    def adam(turn):
        columns = slice(turn * step, (turn + 1) * step)
        for top in range(0, hid, piece):
            lines = slice(top, top + piece)
            grad = total[turn % 2, lines, :]
            first = moment_ref[lines, columns].astype(F32) * (beta_first / first_fix) + grad * (
                (1.0 - beta_first) / first_fix
            )
            square = second_ref[lines, columns].astype(F32) * (beta_second / second_fix) + (
                grad * grad
            ) * ((1.0 - beta_second) / second_fix)
            root = square * lax.rsqrt(square) + adam_eps
            update[lines, columns] = (
                first * pl.reciprocal(root, approx=True) + decay_rate * master_ref[lines, columns]
            )

    copies = []
    multiply(0)
    for load in loads:
        load.wait()
    for turn in range(half // step):
        if turn + 1 < half // step:
            multiply(turn + 1)
        adam(turn)
        columns = slice(turn * step, (turn + 1) * step)
        copies.append(
            pltpu.make_async_copy(update.at[:, columns], update_hbm.at[:, columns], sems.at[2 + turn])
        )
        copies[-1].start()
    for copy in copies:
        copy.wait()


def combine_kernel(group, cap, ids_ref, slots_ref, score_ref, out_ref):
    tokens = ids_ref.shape[1]
    me = ep_index()
    mine = own_half()
    lane = lax.broadcasted_iota(jnp.int32, (1, LANES), 1)
    lines = []
    for k in range(group):
        own = score_ref[mine * group + (me ^ k)][0:1, :]
        other = score_ref[(1 - mine) * group + (me ^ k)][0:1, :]
        lines.append(jnp.where(lane < cap, own, other))
    lines.append(jnp.zeros((LANES - group, LANES), F32))
    columns = jnp.concatenate(lines, axis=0).T
    columns = columns[:cap] + columns[cap : 2 * cap]
    place = lax.broadcasted_iota(jnp.int32, (cap, tokens), 0).astype(F32)
    ids = ids_ref[...]
    result = jnp.zeros(ids.shape, F32)
    for k in range(group):
        at_slot = jnp.where(place == slots_ref[k : k + 1, :], columns[:, k : k + 1], 0.0)
        result = jnp.where(ids == (me ^ k), jnp.sum(at_slot, axis=0, keepdims=True), result)
    out_ref[...] = result


def moved(array, side, step):
    if (side, step) == (0, 0):
        return array
    group = lax.axis_size("ep")
    pairs = [
        (p * group + e, (p ^ side) * group + (e ^ step)) for p in range(2) for e in range(group)
    ]
    return lax.ppermute(array, ("pair", "ep"), pairs)


def local(grad_out, router_weights, expert_ids, hidden, master, moment, second):
    group = lax.axis_size("ep")
    tokens, width = grad_out.shape[1:]
    top = expert_ids.shape[2]
    hid, slots = hidden.shape[2:]
    half = master.shape[3]
    cap = slots // group
    ids = expert_ids[0].T
    own_hidden = hidden[0, 0]
    param = master[0, 0]
    other_hidden = moved(own_hidden, 1, 0)

    order = [(0, 1)] + [(side, k) for k in range(group - 1, 1, -1) for side in range(2)]
    order += [(1, 1), (1, 0), (0, 0)]
    chunk = jax.ShapeDtypeStruct((half // LANES * cap + TILE, LANES), BF16)
    routed = pl.pallas_call(
        functools.partial(route_kernel, order, group, cap),
        out_shape=[jax.ShapeDtypeStruct((group + -group % TILE, tokens), F32)]
        + [chunk] * (2 * group),
        in_specs=specs(pltpu.HBM, 3),
        out_specs=specs(pltpu.VMEM, 1 + 2 * group),
        scratch_shapes=[
            pltpu.VMEM((top, tokens), jnp.int32),
            pltpu.VMEM((top, tokens), BF16),
            pltpu.VMEM((2, tokens, half), BF16),
            pltpu.SemaphoreType.DMA((4,)),
        ],
        compiler_params=params(),
        cost_estimate=cost(2 * slots * tokens * width, 2 * (tokens + slots) * width),
        name="route",
    )(
        pltpu.with_memory_space_constraint(ids, pltpu.HBM),
        pltpu.with_memory_space_constraint(router_weights[0].T, pltpu.HBM),
        pltpu.with_memory_space_constraint(grad_out[0], pltpu.HBM),
    )
    slot_of = routed[0]
    arrived = {item: moved(sent, *item) for item, sent in zip(order, routed[1:])}
    chunks = [arrived[item] for item in order]

    inner = pl.pallas_call(
        inner_kernel,
        out_shape=jax.ShapeDtypeStruct((2 * slots, half), F32),
        in_specs=specs(pltpu.VMEM, 3),
        out_specs=specs(pltpu.VMEM, 1)[0],
        compiler_params=params(),
        cost_estimate=cost(4 * slots * hid * half, 4 * hid * half + 8 * slots * half),
        name="inner",
    )(own_hidden, other_hidden, param)

    scores = pl.pallas_call(
        functools.partial(score_kernel, order, group, cap),
        out_shape=jax.ShapeDtypeStruct((2 * group, 8, LANES), F32),
        in_specs=specs(pltpu.VMEM, 1 + 2 * group),
        out_specs=specs(pltpu.VMEM, 1)[0],
        compiler_params=params(),
        cost_estimate=cost(4 * slots * half, 12 * slots * half),
        name="score",
    )(inner, *chunks)
    returned = lax.all_to_all(scores, ("pair", "ep"), split_axis=0, concat_axis=0, tiled=True)

    step = min(half, 2 * LANES)
    update = pl.pallas_call(
        functools.partial(update_kernel, order, group, cap),
        out_shape=jax.ShapeDtypeStruct((hid, half), F32),
        in_specs=specs(pltpu.VMEM, 3) + specs(pltpu.HBM, 2) + specs(pltpu.VMEM, 2 * group),
        out_specs=specs(pltpu.HBM, 1)[0],
        scratch_shapes=[
            pltpu.VMEM((2 * slots, half), BF16),
            pltpu.VMEM((hid, 2 * slots), BF16),
            pltpu.VMEM((2, hid, step), F32),
            pltpu.VMEM((hid, half), F32),
            pltpu.VMEM((hid, half), BF16),
            pltpu.VMEM((hid, half), BF16),
            pltpu.SemaphoreType.DMA((2 + half // step,)),
        ],
        compiler_params=params(),
        cost_estimate=cost(4 * slots * hid * half, 12 * hid * half + 4 * slots * half),
        name="update",
    )(
        own_hidden,
        other_hidden,
        param,
        pltpu.with_memory_space_constraint(moment[0, 0], pltpu.HBM),
        pltpu.with_memory_space_constraint(second[0, 0], pltpu.HBM),
        *chunks,
    )
    router = pl.pallas_call(
        functools.partial(combine_kernel, group, cap),
        out_shape=jax.ShapeDtypeStruct((top, tokens), F32),
        in_specs=specs(pltpu.VMEM, 3),
        out_specs=specs(pltpu.VMEM, 1)[0],
        compiler_params=params(),
        cost_estimate=cost(4 * slots * tokens, 8 * top * tokens),
        name="combine",
    )(ids, slot_of, returned)
    return (update[None, None], router.T[None])


def solution(mesh):
    sections, group = mesh.devices.shape
    split = jax.sharding.Mesh(
        mesh.devices.reshape(2, sections // 2, group), ("pair", "rest", "ep")
    )
    section = ("pair", "rest")
    rows = P(section, "ep", None)
    blocks = P(section, "ep", None, None)
    return jax.shard_map(
        local,
        mesh=split,
        in_specs=(rows, rows, rows, blocks, blocks, blocks, blocks),
        out_specs=(blocks, rows),
        check_vma=False,
    )
```

```python
import functools

import jax
import jax.numpy as jnp
from jax import lax
from jax.experimental import pallas as pl
from jax.experimental.pallas import tpu as pltpu
from jax.sharding import PartitionSpec as P

beta_first = 0.9
beta_second = 0.95
adam_eps = 1e-08
decay_rate = 0.1
first_fix = 1.0 - 0.9**10
second_fix = 1.0 - 0.95**10

LANES = 128
TILE = 16
VMEM_BYTES = 32 * 1024 * 1024
F32 = jnp.float32
BF16 = jnp.bfloat16


def params():
    return pltpu.CompilerParams(vmem_limit_bytes=VMEM_BYTES)


def cost(flops, touched):
    return pl.CostEstimate(flops=int(flops), bytes_accessed=int(touched), transcendentals=0)


def specs(space, count):
    return [pl.BlockSpec(memory_space=space) for _ in range(count)]


def ep_index():
    return lax.axis_index("ep").astype(jnp.int32)


def own_half():
    return lax.axis_index("pair").astype(jnp.int32)


def start_grads(grads_hbm, held, sems):
    half = held.shape[2]
    mine = own_half()
    copies = []
    for side in range(2):
        column = pl.multiple_of((1 - mine if side else mine) * half, half)
        copies.append(
            pltpu.make_async_copy(
                grads_hbm.at[:, pl.ds(column, half)], held.at[side], sems.at[side]
            )
        )
        copies[-1].start()
    return copies


def pick_rows(slots, k, cap):
    place = lax.broadcasted_iota(jnp.int32, (cap, slots.shape[1]), 0).astype(F32)
    return jnp.where(place == slots[k : k + 1, :], 1.0, 0.0).astype(BF16)


def fill_chunks(group, cap, pick, held, copies, tiles, chunks):
    half = held.shape[2]
    data_rows = half // LANES * cap
    step = min(half, 2 * LANES)
    for side in range(2):
        for k in range(group):
            chunks[side, k][data_rows:, :] = tiles[k]
        copies[side].wait()
        for column in range(0, half, step):
            block = jnp.dot(
                pick, held[side, :, column : column + step], preferred_element_type=F32
            ).astype(BF16)
            for k in range(group):
                for part in range(step // LANES):
                    top = (column // LANES + part) * cap
                    chunks[side, k][top : top + cap, :] = block[
                        k * cap : (k + 1) * cap, part * LANES : (part + 1) * LANES
                    ]


def route_kernel(
    items, group, cap, ids_hbm, weight_hbm, grads_hbm, slots_ref, *rest
):
    chunks = dict(zip(items, rest))
    ids_ref, weight_ref, held, sems = rest[len(items) :]
    tokens = held.shape[1]
    me = ep_index()
    small = [
        pltpu.make_async_copy(ids_hbm, ids_ref, sems.at[2]),
        pltpu.make_async_copy(weight_hbm, weight_ref, sems.at[3]),
    ]
    for copy in small:
        copy.start()
    copies = start_grads(grads_hbm, held, sems)
    earlier = lax.broadcasted_iota(jnp.int32, (tokens, tokens), 0)
    later = lax.broadcasted_iota(jnp.int32, (tokens, tokens), 1)
    ahead = jnp.where(earlier < later, 1.0, 0.0).astype(BF16)
    for copy in small:
        copy.wait()
    ids = ids_ref[...]
    weights = weight_ref[...].astype(F32)
    members, scales = [], []
    for k in range(group):
        named = ids == (me ^ k)
        members.append(jnp.sum(jnp.where(named, 1.0, 0.0), axis=0, keepdims=True))
        scales.append(jnp.sum(jnp.where(named, weights, 0.0), axis=0, keepdims=True))
    if group % TILE:
        members.append(jnp.zeros((-group % TILE, tokens), F32))
    member = jnp.concatenate(members, axis=0)
    before = jnp.dot(member.astype(BF16), ahead, preferred_element_type=F32)
    slots = jnp.where(member > 0.5, before, -1.0)
    slots_ref[...] = slots
    picks = [pick_rows(slots, k, cap) for k in range(group)]
    base = me * cap
    tile_row = lax.broadcasted_iota(jnp.int32, (TILE, LANES), 0)
    tile_lane = lax.broadcasted_iota(jnp.int32, (TILE, LANES), 1)
    spot = tile_row * LANES + tile_lane
    kept = (spot >= base) & (spot < base + cap)
    tiles = []
    for k in range(group):
        spread = jnp.broadcast_to(scales[k], (TILE, tokens)).astype(BF16)
        doubled = jnp.concatenate([picks[k]] * (LANES // cap), axis=0)
        tile = lax.dot_general(
            spread, doubled, (((1,), (1,)), ((), ())), preferred_element_type=F32
        )
        tiles.append(jnp.where(kept, tile, 0.0).astype(BF16))
    pick = jnp.concatenate(picks, axis=0)
    fill_chunks(group, cap, pick, held, copies, tiles, chunks)


def inner_kernel(own_ref, other_ref, master_ref, inner_ref):
    weights = master_ref[...].astype(BF16)
    slots = own_ref.shape[1]
    for at, ref in ((0, own_ref), (slots, other_ref)):
        inner_ref[at : at + slots, :] = lax.dot_general(
            ref[...], weights, (((0,), (0,)), ((), ())), preferred_element_type=F32
        )


def score_kernel(items, group, cap, inner_ref, *rest):
    chunks = dict(zip(items, rest))
    score_ref, rows_ref, scales_ref = rest[len(items) :]
    blocks = inner_ref.shape[1] // LANES
    me = ep_index()
    mine = own_half()
    scales = [jnp.zeros((TILE, LANES), F32)] * 2
    for k in range(group):
        sums = []
        for side in range(2):
            chunk = chunks[side, k]
            scales[side] += chunk[blocks * cap :, :].astype(F32)
            start = pl.multiple_of(side * group * cap + (me ^ k) * cap, cap)
            total = jnp.zeros((cap, LANES), F32)
            for block in range(blocks):
                columns = slice(block * LANES, (block + 1) * LANES)
                rows = chunk[block * cap : (block + 1) * cap, :]
                rows_ref[pl.ds(start, cap), columns] = rows
                total += rows.astype(F32) * inner_ref[pl.ds(start, cap), columns]
            sums.append(total)
        both = jnp.concatenate(sums, axis=0)
        line = jnp.sum(both.T, axis=0, keepdims=True)
        for side in range(2):
            score_ref[(mine ^ side) * group + (me ^ k)] = jnp.broadcast_to(
                line, score_ref.shape[1:]
            )
    for side in range(2):
        scales_ref[side] = scales[side]


def update_kernel(
    own_ref, other_ref, rows, scales_ref, master_hbm, moment_hbm, second_hbm, update_hbm, *rest
):
    master_ref, moment_ref, second_ref, scaled, total, update, sems = rest
    hid, half = update.shape
    slots = own_ref.shape[1]
    step = total.shape[2]
    piece = 2 * TILE
    turns = half // step
    loads = []
    for turn in range(turns):
        columns = slice(turn * step, (turn + 1) * step)
        loads.append(
            [
                pltpu.make_async_copy(src.at[:, columns], dst.at[:, columns], sems.at[turn, at])
                for at, (src, dst) in enumerate(
                    (
                        (master_hbm, master_ref),
                        (moment_hbm, moment_ref),
                        (second_hbm, second_ref),
                    )
                )
            ]
        )
        for load in loads[-1]:
            load.start()
    for side, ref in enumerate((own_ref, other_ref)):
        for part in range(slots // LANES):
            lanes = slice(part * LANES, (part + 1) * LANES)
            line = scales_ref[side, part : part + 1, :]
            at = side * slots + part * LANES
            for top in range(0, hid, LANES):
                scaled[top : top + LANES, at : at + LANES] = (
                    ref[top : top + LANES, lanes].astype(F32) * line
                ).astype(BF16)

    def multiply(turn):
        total[turn % 2] = jnp.dot(
            scaled[...], rows[:, turn * step : (turn + 1) * step], preferred_element_type=F32
        )

    def moments(turn, lines):
        columns = slice(turn * step, (turn + 1) * step)
        grad = total[turn % 2, lines, :]
        first = moment_ref[lines, columns].astype(F32) * (beta_first / first_fix) + grad * (
            (1.0 - beta_first) / first_fix
        )
        square = second_ref[lines, columns].astype(F32) * (beta_second / second_fix) + (
            grad * grad
        ) * ((1.0 - beta_second) / second_fix)
        return first, square, lax.rsqrt(square)

    def inverse(first, square, root):
        return first, pl.reciprocal(square * root + adam_eps, approx=True)

    def finish(turn, lines, first, scale):
        columns = slice(turn * step, (turn + 1) * step)
        update[lines, columns] = first * scale + decay_rate * master_ref[lines, columns]

    copies = []
    multiply(0)
    for turn in range(turns):
        if turn + 1 < turns:
            multiply(turn + 1)
        for load in loads[turn]:
            load.wait()
        pieces = [slice(top, top + piece) for top in range(0, hid, piece)]
        held = {}
        for at in range(len(pieces) + 2):
            if at < len(pieces):
                held[at, 0] = moments(turn, pieces[at])
            if 0 <= at - 1 < len(pieces):
                held[at - 1, 1] = inverse(*held.pop((at - 1, 0)))
            if at >= 2:
                finish(turn, pieces[at - 2], *held.pop((at - 2, 1)))
        columns = slice(turn * step, (turn + 1) * step)
        copies.append(
            pltpu.make_async_copy(
                update.at[:, columns], update_hbm.at[:, columns], sems.at[turn, 3]
            )
        )
        copies[-1].start()
    for copy in copies:
        copy.wait()


def combine_kernel(group, cap, ids_ref, slots_ref, score_ref, out_ref):
    tokens = ids_ref.shape[1]
    me = ep_index()
    mine = own_half()
    lane = lax.broadcasted_iota(jnp.int32, (1, LANES), 1)
    lines = []
    for k in range(group):
        own = score_ref[mine * group + (me ^ k)][0:1, :]
        other = score_ref[(1 - mine) * group + (me ^ k)][0:1, :]
        lines.append(jnp.where(lane < cap, own, other))
    lines.append(jnp.zeros((LANES - group, LANES), F32))
    columns = jnp.concatenate(lines, axis=0).T
    columns = columns[:cap] + columns[cap : 2 * cap]
    place = lax.broadcasted_iota(jnp.int32, (cap, tokens), 0).astype(F32)
    ids = ids_ref[...]
    result = jnp.zeros(ids.shape, F32)
    for k in range(group):
        at_slot = jnp.where(place == slots_ref[k : k + 1, :], columns[:, k : k + 1], 0.0)
        result = jnp.where(ids == (me ^ k), jnp.sum(at_slot, axis=0, keepdims=True), result)
    out_ref[...] = result


def moved(array, side, step):
    if (side, step) == (0, 0):
        return array
    group = lax.axis_size("ep")
    pairs = [
        (p * group + e, (p ^ side) * group + (e ^ step)) for p in range(2) for e in range(group)
    ]
    return lax.ppermute(array, ("pair", "ep"), pairs)


def local(grad_out, router_weights, expert_ids, hidden, master, moment, second):
    group = lax.axis_size("ep")
    tokens, width = grad_out.shape[1:]
    top = expert_ids.shape[2]
    hid, slots = hidden.shape[2:]
    half = master.shape[3]
    cap = slots // group
    ids = expert_ids[0].T
    own_hidden = hidden[0, 0]
    param = master[0, 0]
    other_hidden = moved(own_hidden, 1, 0)

    order = [(side, k) for side in range(2) for k in range(group)]
    chunk = jax.ShapeDtypeStruct((half // LANES * cap + TILE, LANES), BF16)
    routed = pl.pallas_call(
        functools.partial(route_kernel, order, group, cap),
        out_shape=[jax.ShapeDtypeStruct((group + -group % TILE, tokens), F32)]
        + [chunk] * (2 * group),
        in_specs=specs(pltpu.HBM, 3),
        out_specs=specs(pltpu.VMEM, 1 + 2 * group),
        scratch_shapes=[
            pltpu.VMEM((top, tokens), jnp.int32),
            pltpu.VMEM((top, tokens), BF16),
            pltpu.VMEM((2, tokens, half), BF16),
            pltpu.SemaphoreType.DMA((4,)),
        ],
        compiler_params=params(),
        cost_estimate=cost(2 * slots * tokens * width, 2 * (tokens + slots) * width),
        name="route",
    )(
        pltpu.with_memory_space_constraint(ids, pltpu.HBM),
        pltpu.with_memory_space_constraint(router_weights[0].T, pltpu.HBM),
        pltpu.with_memory_space_constraint(grad_out[0], pltpu.HBM),
    )
    slot_of = routed[0]
    arrived = {item: moved(sent, *item) for item, sent in zip(order, routed[1:])}
    chunks = [arrived[item] for item in order]

    inner = pl.pallas_call(
        inner_kernel,
        out_shape=jax.ShapeDtypeStruct((2 * slots, half), F32),
        in_specs=specs(pltpu.VMEM, 3),
        out_specs=specs(pltpu.VMEM, 1)[0],
        compiler_params=params(),
        cost_estimate=cost(4 * slots * hid * half, 4 * hid * half + 8 * slots * half),
        name="inner",
    )(own_hidden, other_hidden, param)

    scores, placed, scales = pl.pallas_call(
        functools.partial(score_kernel, order, group, cap),
        out_shape=[
            jax.ShapeDtypeStruct((2 * group, 8, LANES), F32),
            jax.ShapeDtypeStruct((2 * slots, half), BF16),
            jax.ShapeDtypeStruct((2, TILE, LANES), F32),
        ],
        in_specs=specs(pltpu.VMEM, 1 + 2 * group),
        out_specs=specs(pltpu.VMEM, 3),
        compiler_params=params(),
        cost_estimate=cost(4 * slots * half, 12 * slots * half),
        name="score",
    )(inner, *chunks)
    returned = lax.all_to_all(scores, ("pair", "ep"), split_axis=0, concat_axis=0, tiled=True)

    step = min(half, 2 * LANES)
    update = pl.pallas_call(
        update_kernel,
        out_shape=jax.ShapeDtypeStruct((hid, half), F32),
        in_specs=specs(pltpu.VMEM, 4) + specs(pltpu.HBM, 3),
        out_specs=specs(pltpu.HBM, 1)[0],
        scratch_shapes=[
            pltpu.VMEM((hid, half), F32),
            pltpu.VMEM((hid, half), BF16),
            pltpu.VMEM((hid, half), BF16),
            pltpu.VMEM((hid, 2 * slots), BF16),
            pltpu.VMEM((2, hid, step), F32),
            pltpu.VMEM((hid, half), F32),
            pltpu.SemaphoreType.DMA((half // step, 4)),
        ],
        compiler_params=params(),
        cost_estimate=cost(4 * slots * hid * half, 12 * hid * half + 4 * slots * half),
        name="update",
    )(
        own_hidden,
        other_hidden,
        placed,
        scales,
        *[
            pltpu.with_memory_space_constraint(array[0, 0], pltpu.HBM)
            for array in (master, moment, second)
        ],
    )
    router = pl.pallas_call(
        functools.partial(combine_kernel, group, cap),
        out_shape=jax.ShapeDtypeStruct((top, tokens), F32),
        in_specs=specs(pltpu.VMEM, 3),
        out_specs=specs(pltpu.VMEM, 1)[0],
        compiler_params=params(),
        cost_estimate=cost(4 * slots * tokens, 8 * top * tokens),
        name="combine",
    )(ids, slot_of, returned)
    return (update[None, None], router.T[None])


def solution(mesh):
    sections, group = mesh.devices.shape
    split = jax.sharding.Mesh(
        mesh.devices.reshape(2, sections // 2, group), ("pair", "rest", "ep")
    )
    section = ("pair", "rest")
    rows = P(section, "ep", None)
    blocks = P(section, "ep", None, None)
    return jax.shard_map(
        local,
        mesh=split,
        in_specs=(rows, rows, rows, blocks, blocks, blocks, blocks),
        out_specs=(blocks, rows),
        check_vma=False,
    )
```

```python
import functools

import jax
import jax.numpy as jnp
from jax import lax
from jax.experimental import pallas as pl
from jax.experimental.pallas import tpu as pltpu
from jax.sharding import PartitionSpec as P

beta_first = 0.9
beta_second = 0.95
adam_eps = 1e-08
decay_rate = 0.1
first_fix = 1.0 - 0.9**10
second_fix = 1.0 - 0.95**10

LANES = 128
TILE = 16
VMEM_BYTES = 32 * 1024 * 1024
F32 = jnp.float32
BF16 = jnp.bfloat16


def params():
    return pltpu.CompilerParams(vmem_limit_bytes=VMEM_BYTES)


def cost(flops, touched):
    return pl.CostEstimate(flops=int(flops), bytes_accessed=int(touched), transcendentals=0)


def specs(space, count):
    return [pl.BlockSpec(memory_space=space) for _ in range(count)]


def ep_index():
    return lax.axis_index("ep").astype(jnp.int32)


def own_half():
    return lax.axis_index("pair").astype(jnp.int32)


def start_grads(grads_hbm, held, sems):
    half = held.shape[2]
    mine = own_half()
    copies = []
    for side in range(2):
        column = pl.multiple_of((1 - mine if side else mine) * half, half)
        copies.append(
            pltpu.make_async_copy(
                grads_hbm.at[:, pl.ds(column, half)], held.at[side], sems.at[side]
            )
        )
        copies[-1].start()
    return copies


def pick_rows(slots, k, cap):
    place = lax.broadcasted_iota(jnp.int32, (cap, slots.shape[1]), 0).astype(F32)
    return jnp.where(place == slots[k : k + 1, :], 1.0, 0.0).astype(BF16)


def fill_chunks(group, cap, pick, held, copies, tiles, chunks):
    half = held.shape[2]
    data_rows = half // LANES * cap
    step = min(half, 2 * LANES)
    for side in range(2):
        for k in range(group):
            chunks[side, k][data_rows:, :] = tiles[k]
        copies[side].wait()
        for column in range(0, half, step):
            block = jnp.dot(
                pick, held[side, :, column : column + step], preferred_element_type=F32
            ).astype(BF16)
            for k in range(group):
                for part in range(step // LANES):
                    top = (column // LANES + part) * cap
                    chunks[side, k][top : top + cap, :] = block[
                        k * cap : (k + 1) * cap, part * LANES : (part + 1) * LANES
                    ]


def route_kernel(
    items, group, cap, ids_hbm, weight_hbm, grads_hbm, slots_ref, *rest
):
    chunks = dict(zip(items, rest))
    ids_ref, weight_ref, held, sems = rest[len(items) :]
    tokens = held.shape[1]
    me = ep_index()
    small = [
        pltpu.make_async_copy(ids_hbm, ids_ref, sems.at[2]),
        pltpu.make_async_copy(weight_hbm, weight_ref, sems.at[3]),
    ]
    for copy in small:
        copy.start()
    copies = start_grads(grads_hbm, held, sems)
    earlier = lax.broadcasted_iota(jnp.int32, (tokens, tokens), 0)
    later = lax.broadcasted_iota(jnp.int32, (tokens, tokens), 1)
    ahead = jnp.where(earlier < later, 1.0, 0.0).astype(BF16)
    for copy in small:
        copy.wait()
    ids = ids_ref[...]
    weights = weight_ref[...].astype(F32)
    members, scales = [], []
    for k in range(group):
        named = ids == (me ^ k)
        members.append(jnp.sum(jnp.where(named, 1.0, 0.0), axis=0, keepdims=True))
        scales.append(jnp.sum(jnp.where(named, weights, 0.0), axis=0, keepdims=True))
    if group % TILE:
        members.append(jnp.zeros((-group % TILE, tokens), F32))
    member = jnp.concatenate(members, axis=0)
    before = jnp.dot(member.astype(BF16), ahead, preferred_element_type=F32)
    slots = jnp.where(member > 0.5, before, -1.0)
    slots_ref[...] = slots
    picks = [pick_rows(slots, k, cap) for k in range(group)]
    base = me * cap
    tile_row = lax.broadcasted_iota(jnp.int32, (TILE, LANES), 0)
    tile_lane = lax.broadcasted_iota(jnp.int32, (TILE, LANES), 1)
    spot = tile_row * LANES + tile_lane
    kept = (spot >= base) & (spot < base + cap)
    tiles = []
    for k in range(group):
        spread = jnp.broadcast_to(scales[k], (TILE, tokens)).astype(BF16)
        doubled = jnp.concatenate([picks[k]] * (LANES // cap), axis=0)
        tile = lax.dot_general(
            spread, doubled, (((1,), (1,)), ((), ())), preferred_element_type=F32
        )
        tiles.append(jnp.where(kept, tile, 0.0).astype(BF16))
    pick = jnp.concatenate(picks, axis=0)
    fill_chunks(group, cap, pick, held, copies, tiles, chunks)


def inner_kernel(own_ref, other_ref, master_ref, inner_ref):
    weights = master_ref[...].astype(BF16)
    slots = own_ref.shape[1]
    for at, ref in ((0, own_ref), (slots, other_ref)):
        inner_ref[at : at + slots, :] = lax.dot_general(
            ref[...], weights, (((0,), (0,)), ((), ())), preferred_element_type=F32
        )


def score_kernel(items, group, cap, inner_ref, *rest):
    chunks = dict(zip(items, rest))
    score_ref, rows_ref, scales_ref = rest[len(items) :]
    blocks = inner_ref.shape[1] // LANES
    me = ep_index()
    line_of = lax.broadcasted_iota(jnp.int32, score_ref.shape, 0)
    scores = jnp.zeros(score_ref.shape, F32)
    scales = [jnp.zeros((TILE, LANES), F32)] * 2
    for k in range(group):
        sums = []
        for side in range(2):
            chunk = chunks[side, k]
            scales[side] += chunk[blocks * cap :, :].astype(F32)
            start = pl.multiple_of(side * group * cap + (me ^ k) * cap, cap)
            total = jnp.zeros((cap, LANES), F32)
            for block in range(blocks):
                columns = slice(block * LANES, (block + 1) * LANES)
                rows = chunk[block * cap : (block + 1) * cap, :]
                rows_ref[pl.ds(start, cap), columns] = rows
                total += rows.astype(F32) * inner_ref[pl.ds(start, cap), columns]
            sums.append(total)
        both = jnp.concatenate(sums, axis=0)
        line = jnp.sum(both.T, axis=0, keepdims=True)
        scores = jnp.where(line_of == (me ^ k), line, scores)
    score_ref[...] = scores
    for side in range(2):
        scales_ref[side] = scales[side]


def merge_kernel(cap, own_ref, other_ref, out_ref):
    out_ref[...] = own_ref[...] + pltpu.roll(other_ref[...], LANES - cap, axis=1)


def update_rows(blocks, operands, scaled, total, update, finished):
    own_ref, other_ref, rows, scales_ref, master_ref, moment_ref, second_ref = operands
    slots = own_ref.shape[1]
    half = rows.shape[1]
    step = min(half, 4 * LANES)

    def multiply(at):
        block = blocks[at]
        for side, ref in enumerate((own_ref, other_ref)):
            for part in range(slots // LANES):
                lanes = slice(part * LANES, (part + 1) * LANES)
                column = side * slots + part * LANES
                scaled[at % 2, :, column : column + LANES] = (
                    ref[block, lanes].astype(F32) * scales_ref[side, part : part + 1, :]
                ).astype(BF16)
        total[at % 2] = jnp.dot(scaled[at % 2], rows[...], preferred_element_type=F32)

    def moments(at, top, columns):
        lines = slice(blocks[at].start + top, blocks[at].start + top + TILE)
        grad = total[at % 2, top : top + TILE, columns]
        first = moment_ref[lines, columns].astype(F32) * (beta_first / first_fix) + grad * (
            (1.0 - beta_first) / first_fix
        )
        square = second_ref[lines, columns].astype(F32) * (beta_second / second_fix) + (
            grad * grad
        ) * ((1.0 - beta_second) / second_fix)
        return first, square, lax.rsqrt(square)

    def inverse(first, square, root):
        return first, pl.reciprocal(square * root + adam_eps, approx=True)

    def finish(at, top, columns, first, scale):
        lines = slice(blocks[at].start + top, blocks[at].start + top + TILE)
        place = slice(lines.start - blocks[0].start, lines.stop - blocks[0].start)
        update[place, columns] = first * scale + decay_rate * master_ref[lines, columns]

    multiply(0)
    for at, block in enumerate(blocks):
        if at + 1 < len(blocks):
            multiply(at + 1)
        pieces = [
            (top, slice(column, column + step))
            for top in range(0, block.stop - block.start, TILE)
            for column in range(0, half, step)
        ]
        held = {}
        for turn in range(len(pieces) + 2):
            if turn < len(pieces):
                held[turn, 0] = moments(at, *pieces[turn])
            if 0 <= turn - 1 < len(pieces):
                held[turn - 1, 1] = inverse(*held.pop((turn - 1, 0)))
            if turn >= 2:
                finish(at, *pieces[turn - 2], *held.pop((turn - 2, 1)))
        finished(at)


def first_update_kernel(blocks, *refs):
    scaled, total = refs[-2:]
    update_rows(blocks, refs[:7], scaled, total, refs[7], lambda at: None)


def last_update_kernel(blocks, *refs):
    earlier, _, update_hbm, scaled, total, update, sems = refs[7:]
    above = earlier.shape[0]
    copies = [
        pltpu.make_async_copy(earlier, update_hbm.at[:above, :], sems.at[len(blocks)])
    ]
    copies[0].start()

    def finished(at):
        block = blocks[at]
        copies.append(
            pltpu.make_async_copy(
                update.at[block.start - above : block.stop - above, :],
                update_hbm.at[block, :],
                sems.at[at],
            )
        )
        copies[-1].start()

    update_rows(blocks, refs[:7], scaled, total, update, finished)
    for copy in copies:
        copy.wait()


def combine_kernel(group, cap, ids_ref, slots_ref, *rest):
    scores, out_ref = rest[:-1], rest[-1]
    tokens = ids_ref.shape[1]
    me = ep_index()
    row = lax.broadcasted_iota(jnp.int32, scores[0].shape, 0)
    lines = [
        jnp.sum(jnp.where(row == me, ref[...], 0.0), axis=0, keepdims=True) for ref in scores
    ]
    lines.append(jnp.zeros((LANES - group, LANES), F32))
    columns = jnp.concatenate(lines, axis=0).T
    place = lax.broadcasted_iota(jnp.int32, (cap, tokens), 0).astype(F32)
    ids = ids_ref[...]
    result = jnp.zeros(ids.shape, F32)
    for k in range(group):
        at_slot = jnp.where(place == slots_ref[k : k + 1, :], columns[:cap, k : k + 1], 0.0)
        result = jnp.where(ids == (me ^ k), jnp.sum(at_slot, axis=0, keepdims=True), result)
    out_ref[...] = result


def moved(array, side, step):
    if (side, step) == (0, 0):
        return array
    group = lax.axis_size("ep")
    pairs = [
        (p * group + e, (p ^ side) * group + (e ^ step)) for p in range(2) for e in range(group)
    ]
    return lax.ppermute(array, ("pair", "ep"), pairs)


def local(grad_out, router_weights, expert_ids, hidden, master, moment, second):
    group = lax.axis_size("ep")
    tokens, width = grad_out.shape[1:]
    top = expert_ids.shape[2]
    hid, slots = hidden.shape[2:]
    half = master.shape[3]
    cap = slots // group
    ids = expert_ids[0].T
    own_hidden = hidden[0, 0]
    param = master[0, 0]
    other_hidden = moved(own_hidden, 1, 0)

    order = [(side, k) for side in range(2) for k in range(group)]
    chunk = jax.ShapeDtypeStruct((half // LANES * cap + TILE, LANES), BF16)
    routed = pl.pallas_call(
        functools.partial(route_kernel, order, group, cap),
        out_shape=[jax.ShapeDtypeStruct((group + -group % TILE, tokens), F32)]
        + [chunk] * (2 * group),
        in_specs=specs(pltpu.HBM, 3),
        out_specs=specs(pltpu.VMEM, 1 + 2 * group),
        scratch_shapes=[
            pltpu.VMEM((top, tokens), jnp.int32),
            pltpu.VMEM((top, tokens), BF16),
            pltpu.VMEM((2, tokens, half), BF16),
            pltpu.SemaphoreType.DMA((4,)),
        ],
        compiler_params=params(),
        cost_estimate=cost(2 * slots * tokens * width, 2 * (tokens + slots) * width),
        name="route",
    )(
        pltpu.with_memory_space_constraint(ids, pltpu.HBM),
        pltpu.with_memory_space_constraint(router_weights[0].T, pltpu.HBM),
        pltpu.with_memory_space_constraint(grad_out[0], pltpu.HBM),
    )
    slot_of = routed[0]
    arrived = {item: moved(sent, *item) for item, sent in zip(order, routed[1:])}
    chunks = [arrived[item] for item in order]

    inner = pl.pallas_call(
        inner_kernel,
        out_shape=jax.ShapeDtypeStruct((2 * slots, half), F32),
        in_specs=specs(pltpu.VMEM, 3),
        out_specs=specs(pltpu.VMEM, 1)[0],
        compiler_params=params(),
        cost_estimate=cost(4 * slots * hid * half, 4 * hid * half + 8 * slots * half),
        name="inner",
    )(own_hidden, other_hidden, param)

    scores, placed, scales = pl.pallas_call(
        functools.partial(score_kernel, order, group, cap),
        out_shape=[
            jax.ShapeDtypeStruct((group + -group % 8, LANES), F32),
            jax.ShapeDtypeStruct((2 * slots, half), BF16),
            jax.ShapeDtypeStruct((2, TILE, LANES), F32),
        ],
        in_specs=specs(pltpu.VMEM, 1 + 2 * group),
        out_specs=specs(pltpu.VMEM, 3),
        compiler_params=params(),
        cost_estimate=cost(4 * slots * half, 12 * slots * half),
        name="score",
    )(inner, *chunks)
    other_scores = moved(scores, 1, 0)
    block = min(hid, 2 * LANES)
    blocks = [slice(top, top + block) for top in range(0, hid, block)]
    operands = (own_hidden, other_hidden, placed, scales, param, moment[0, 0], second[0, 0])
    scratch = [
        pltpu.VMEM((2, block, 2 * slots), BF16),
        pltpu.VMEM((2, block, half), F32),
    ]
    earlier = pl.pallas_call(
        functools.partial(first_update_kernel, blocks[:1]),
        out_shape=jax.ShapeDtypeStruct((block, half), F32),
        in_specs=specs(pltpu.VMEM, 7),
        out_specs=specs(pltpu.VMEM, 1)[0],
        scratch_shapes=scratch,
        compiler_params=params(),
        cost_estimate=cost(4 * slots * block * half, 12 * block * half),
        name="first_update",
    )(*operands)
    full_scores = pl.pallas_call(
        functools.partial(merge_kernel, cap),
        out_shape=jax.ShapeDtypeStruct(scores.shape, F32),
        in_specs=specs(pltpu.VMEM, 2),
        out_specs=specs(pltpu.VMEM, 1)[0],
        compiler_params=params(),
        name="merge",
    )(scores, other_scores)
    returned = [moved(full_scores, 0, k) for k in range(group)]
    update = pl.pallas_call(
        functools.partial(last_update_kernel, blocks[1:]),
        out_shape=jax.ShapeDtypeStruct((hid, half), F32),
        in_specs=specs(pltpu.VMEM, 8) + specs(pl.ANY, 1),
        out_specs=specs(pltpu.HBM, 1)[0],
        scratch_shapes=scratch
        + [
            pltpu.VMEM((hid - block, half), F32),
            pltpu.SemaphoreType.DMA((len(blocks),)),
        ],
        compiler_params=params(),
        cost_estimate=cost(4 * slots * (hid - block) * half, 12 * hid * half),
        name="last_update",
    )(*operands, earlier, full_scores)
    router = pl.pallas_call(
        functools.partial(combine_kernel, group, cap),
        out_shape=jax.ShapeDtypeStruct((top, tokens), F32),
        in_specs=specs(pltpu.VMEM, 2 + group),
        out_specs=specs(pltpu.VMEM, 1)[0],
        compiler_params=params(),
        cost_estimate=cost(4 * slots * tokens, 8 * top * tokens),
        name="combine",
    )(ids, slot_of, *returned)
    return (update[None, None], router.T[None])


def solution(mesh):
    sections, group = mesh.devices.shape
    split = jax.sharding.Mesh(
        mesh.devices.reshape(2, sections // 2, group), ("pair", "rest", "ep")
    )
    section = ("pair", "rest")
    rows = P(section, "ep", None)
    blocks = P(section, "ep", None, None)
    return jax.shard_map(
        local,
        mesh=split,
        in_specs=(rows, rows, rows, blocks, blocks, blocks, blocks),
        out_specs=(blocks, rows),
        check_vma=False,
    )
```

```python
import functools

import jax
import jax.numpy as jnp
from jax import lax
from jax.experimental import pallas as pl
from jax.experimental.pallas import tpu as pltpu
from jax.sharding import PartitionSpec as P

beta_first = 0.9
beta_second = 0.95
adam_eps = 1e-08
decay_rate = 0.1
first_fix = 1.0 - 0.9**10
second_fix = 1.0 - 0.95**10

LANES = 128
TILE = 16
VMEM_BYTES = 32 * 1024 * 1024
F32 = jnp.float32
BF16 = jnp.bfloat16


def params():
    return pltpu.CompilerParams(vmem_limit_bytes=VMEM_BYTES)


def cost(flops, touched):
    return pl.CostEstimate(flops=int(flops), bytes_accessed=int(touched), transcendentals=0)


def specs(space, count):
    return [pl.BlockSpec(memory_space=space) for _ in range(count)]


def ep_index():
    return lax.axis_index("ep").astype(jnp.int32)


def own_half():
    return lax.axis_index("pair").astype(jnp.int32)


def start_grads(grads_hbm, held, sems):
    half = held.shape[2]
    mine = own_half()
    copies = []
    for side in range(2):
        column = pl.multiple_of((1 - mine if side else mine) * half, half)
        copies.append(
            pltpu.make_async_copy(
                grads_hbm.at[:, pl.ds(column, half)], held.at[side], sems.at[side]
            )
        )
        copies[-1].start()
    return copies


def pick_rows(slots, k, cap):
    place = lax.broadcasted_iota(jnp.int32, (cap, slots.shape[1]), 0).astype(F32)
    return jnp.where(place == slots[k : k + 1, :], 1.0, 0.0).astype(BF16)


def fill_chunks(group, cap, pick, held, copies, tiles, chunks):
    half = held.shape[2]
    data_rows = half // LANES * cap
    step = min(half, 2 * LANES)
    for side in range(2):
        for k in range(group):
            chunks[side, k][data_rows:, :] = tiles[k]
        copies[side].wait()
        for column in range(0, half, step):
            block = jnp.dot(
                pick, held[side, :, column : column + step], preferred_element_type=F32
            ).astype(BF16)
            for k in range(group):
                for part in range(step // LANES):
                    top = (column // LANES + part) * cap
                    chunks[side, k][top : top + cap, :] = block[
                        k * cap : (k + 1) * cap, part * LANES : (part + 1) * LANES
                    ]


def route_kernel(
    items, group, cap, ids_hbm, weight_hbm, grads_hbm, slots_ref, *rest
):
    chunks = dict(zip(items, rest))
    ids_ref, weight_ref, held, sems = rest[len(items) :]
    tokens = held.shape[1]
    me = ep_index()
    small = [
        pltpu.make_async_copy(ids_hbm, ids_ref, sems.at[2]),
        pltpu.make_async_copy(weight_hbm, weight_ref, sems.at[3]),
    ]
    for copy in small:
        copy.start()
    copies = start_grads(grads_hbm, held, sems)
    earlier = lax.broadcasted_iota(jnp.int32, (tokens, tokens), 0)
    later = lax.broadcasted_iota(jnp.int32, (tokens, tokens), 1)
    ahead = jnp.where(earlier < later, 1.0, 0.0).astype(BF16)
    for copy in small:
        copy.wait()
    ids = ids_ref[...]
    weights = weight_ref[...].astype(F32)
    members, scales = [], []
    for k in range(group):
        named = ids == (me ^ k)
        members.append(jnp.sum(jnp.where(named, 1.0, 0.0), axis=0, keepdims=True))
        scales.append(jnp.sum(jnp.where(named, weights, 0.0), axis=0, keepdims=True))
    if group % TILE:
        members.append(jnp.zeros((-group % TILE, tokens), F32))
    member = jnp.concatenate(members, axis=0)
    before = jnp.dot(member.astype(BF16), ahead, preferred_element_type=F32)
    slots = jnp.where(member > 0.5, before, -1.0)
    slots_ref[...] = slots
    picks = [pick_rows(slots, k, cap) for k in range(group)]
    base = me * cap
    tile_row = lax.broadcasted_iota(jnp.int32, (TILE, LANES), 0)
    tile_lane = lax.broadcasted_iota(jnp.int32, (TILE, LANES), 1)
    spot = tile_row * LANES + tile_lane
    kept = (spot >= base) & (spot < base + cap)
    tiles = []
    for k in range(group):
        spread = jnp.broadcast_to(scales[k], (TILE, tokens)).astype(BF16)
        doubled = jnp.concatenate([picks[k]] * (LANES // cap), axis=0)
        tile = lax.dot_general(
            spread, doubled, (((1,), (1,)), ((), ())), preferred_element_type=F32
        )
        tiles.append(jnp.where(kept, tile, 0.0).astype(BF16))
    pick = jnp.concatenate(picks, axis=0)
    fill_chunks(group, cap, pick, held, copies, tiles, chunks)


def inner_kernel(own_ref, other_ref, master_hbm, inner_ref, master_ref, sems):
    half = master_ref.shape[1]
    step = min(half, 4 * LANES)
    parts = [slice(column, column + step) for column in range(0, half, step)]
    loads = [
        pltpu.make_async_copy(master_hbm.at[:, part], master_ref.at[:, part], sems.at[at])
        for at, part in enumerate(parts)
    ]
    for load in loads:
        load.start()
    slots = own_ref.shape[1]
    for load, part in zip(loads, parts):
        load.wait()
        weights = master_ref[:, part].astype(BF16)
        for at, ref in ((0, own_ref), (slots, other_ref)):
            inner_ref[at : at + slots, part] = lax.dot_general(
                ref[...], weights, (((0,), (0,)), ((), ())), preferred_element_type=F32
            )


def score_chunks(steps, group, cap, chunks, inner_ref, score_ref):
    blocks = inner_ref.shape[1] // LANES
    me = ep_index()
    line_of = lax.broadcasted_iota(jnp.int32, score_ref.shape, 0)
    scores = jnp.zeros(score_ref.shape, F32)
    for k in steps:
        sums = []
        for side in range(2):
            start = pl.multiple_of(side * group * cap + (me ^ k) * cap, cap)
            total = jnp.zeros((cap, LANES), F32)
            for block in range(blocks):
                rows = chunks[side, k][block * cap : (block + 1) * cap, :].astype(F32)
                total += rows * inner_ref[pl.ds(start, cap), block * LANES : (block + 1) * LANES]
            sums.append(total)
        both = jnp.concatenate(sums, axis=0)
        line = jnp.sum(both.T, axis=0, keepdims=True)
        scores = jnp.where(line_of == (me ^ k), line, scores)
    score_ref[...] = scores


def place_chunks(items, group, cap, chunks, rows_ref):
    blocks = rows_ref.shape[1] // LANES
    me = ep_index()
    scales = [jnp.zeros((TILE, LANES), F32)] * 2
    for side, k in items:
        chunk = chunks[side, k]
        start = pl.multiple_of(side * group * cap + (me ^ k) * cap, cap)
        for block in range(blocks):
            rows_ref[pl.ds(start, cap), block * LANES : (block + 1) * LANES] = chunk[
                block * cap : (block + 1) * cap, :
            ]
        scales[side] += chunk[blocks * cap :, :].astype(F32)
    return scales


def score_kernel(items, steps, group, cap, inner_ref, *rest):
    score_ref = rest[-1]
    score_chunks(steps, group, cap, dict(zip(items, rest)), inner_ref, score_ref)


def merge_kernel(group, local_ref, *rest):
    out_ref = rest[-1]
    row = lax.broadcasted_iota(jnp.int32, out_ref.shape, 0)
    me = ep_index()
    table = jnp.zeros(out_ref.shape, F32)
    for k, ref in enumerate((local_ref,) + rest[:-1]):
        line = jnp.sum(jnp.where(row == me, ref[...], 0.0), axis=0, keepdims=True)
        table = jnp.where(row == k, line, table)
    out_ref[...] = table


def update_rows(blocks, operands, scaled, total, update, finished):
    own_ref, other_ref, rows, scales_ref, master_ref, moment_ref, second_ref = operands
    slots = own_ref.shape[1]
    half = rows.shape[1]
    step = min(half, 4 * LANES)

    def multiply(at):
        block = blocks[at]
        for side, ref in enumerate((own_ref, other_ref)):
            for part in range(slots // LANES):
                lanes = slice(part * LANES, (part + 1) * LANES)
                column = side * slots + part * LANES
                scaled[at % 2, :, column : column + LANES] = (
                    ref[block, lanes].astype(F32) * scales_ref[side, part : part + 1, :]
                ).astype(BF16)
        total[at % 2] = jnp.dot(scaled[at % 2], rows[...], preferred_element_type=F32)

    def moments(at, top, columns):
        lines = slice(blocks[at].start + top, blocks[at].start + top + TILE)
        grad = total[at % 2, top : top + TILE, columns]
        first = moment_ref[lines, columns].astype(F32) * (beta_first / first_fix) + grad * (
            (1.0 - beta_first) / first_fix
        )
        square = second_ref[lines, columns].astype(F32) * (beta_second / second_fix) + (
            grad * grad
        ) * ((1.0 - beta_second) / second_fix)
        return first, square, lax.rsqrt(square)

    def inverse(first, square, root):
        return first, pl.reciprocal(square * root + adam_eps, approx=True)

    def finish(at, top, columns, first, scale):
        lines = slice(blocks[at].start + top, blocks[at].start + top + TILE)
        place = slice(lines.start - blocks[0].start, lines.stop - blocks[0].start)
        update[place, columns] = first * scale + decay_rate * master_ref[lines, columns]

    multiply(0)
    for at, block in enumerate(blocks):
        if at + 1 < len(blocks):
            multiply(at + 1)
        pieces = [
            (top, slice(column, column + step))
            for top in range(0, block.stop - block.start, TILE)
            for column in range(0, half, step)
        ]
        held = {}
        for turn in range(len(pieces) + 2):
            if turn < len(pieces):
                held[turn, 0] = moments(at, *pieces[turn])
            if 0 <= turn - 1 < len(pieces):
                held[turn - 1, 1] = inverse(*held.pop((turn - 1, 0)))
            if turn >= 2:
                finish(at, *pieces[turn - 2], *held.pop((turn - 2, 1)))
        finished(at)


def first_update_kernel(blocks, items, group, cap, *refs):
    chunks, operands = dict(zip(items, refs)), refs[len(items) : len(items) + 5]
    update, rows, scales_ref, scaled, total = refs[len(items) + 5 :]
    scales = place_chunks(items, group, cap, chunks, rows)
    for side in range(2):
        scales_ref[side] = scales[side]
    operands = operands[:2] + (rows, scales_ref) + operands[2:]
    update_rows(blocks, operands, scaled, total, update, lambda at: None)


def last_update_kernel(blocks, *refs):
    earlier, _, update_hbm, scaled, total, update, sems = refs[7:]
    above = earlier.shape[0]
    copies = [
        pltpu.make_async_copy(earlier, update_hbm.at[:above, :], sems.at[len(blocks)])
    ]
    copies[0].start()

    def finished(at):
        block = blocks[at]
        copies.append(
            pltpu.make_async_copy(
                update.at[block.start - above : block.stop - above, :],
                update_hbm.at[block, :],
                sems.at[at],
            )
        )
        copies[-1].start()

    update_rows(blocks, refs[:7], scaled, total, update, finished)
    for copy in copies:
        copy.wait()


def combine_kernel(group, cap, ids_ref, slots_ref, own_ref, other_ref, out_ref):
    tokens = ids_ref.shape[1]
    me = ep_index()
    lane = lax.broadcasted_iota(jnp.int32, own_ref.shape, 1)
    lines = jnp.where(lane < cap, own_ref[...], other_ref[...])
    rest = jnp.zeros((LANES - lines.shape[0], LANES), F32)
    columns = jnp.concatenate([lines, rest], axis=0).T
    columns = columns[:cap] + columns[cap : 2 * cap]
    place = lax.broadcasted_iota(jnp.int32, (cap, tokens), 0).astype(F32)
    ids = ids_ref[...]
    result = jnp.zeros(ids.shape, F32)
    for k in range(group):
        at_slot = jnp.where(place == slots_ref[k : k + 1, :], columns[:, k : k + 1], 0.0)
        result = jnp.where(ids == (me ^ k), jnp.sum(at_slot, axis=0, keepdims=True), result)
    out_ref[...] = result


def moved(array, side, step):
    if (side, step) == (0, 0):
        return array
    group = lax.axis_size("ep")
    pairs = [
        (p * group + e, (p ^ side) * group + (e ^ step)) for p in range(2) for e in range(group)
    ]
    return lax.ppermute(array, ("pair", "ep"), pairs)


def local(grad_out, router_weights, expert_ids, hidden, master, moment, second):
    group = lax.axis_size("ep")
    tokens, width = grad_out.shape[1:]
    top = expert_ids.shape[2]
    hid, slots = hidden.shape[2:]
    half = master.shape[3]
    cap = slots // group
    ids = expert_ids[0].T
    own_hidden = hidden[0, 0]
    param = master[0, 0]
    other_hidden = moved(own_hidden, 1, 0)

    far = group // 2
    early = [k for k in range(group) if k != far]
    wide = [k for k in reversed(early) if k > 1]
    order = [(0, 1)] + [(0, k) for k in wide] + [(1, 0)] + [(1, k) for k in wide] + [(1, 1)]
    first_items = [(0, 0)] + order
    last_items = [(0, far), (1, far)]
    order = first_items + last_items
    chunk = jax.ShapeDtypeStruct((half // LANES * cap + TILE, LANES), BF16)
    routed = pl.pallas_call(
        functools.partial(route_kernel, order, group, cap),
        out_shape=[jax.ShapeDtypeStruct((group + -group % TILE, tokens), F32)]
        + [chunk] * (2 * group),
        in_specs=specs(pltpu.HBM, 3),
        out_specs=specs(pltpu.VMEM, 1 + 2 * group),
        scratch_shapes=[
            pltpu.VMEM((top, tokens), jnp.int32),
            pltpu.VMEM((top, tokens), BF16),
            pltpu.VMEM((2, tokens, half), BF16),
            pltpu.SemaphoreType.DMA((4,)),
        ],
        compiler_params=params(),
        cost_estimate=cost(2 * slots * tokens * width, 2 * (tokens + slots) * width),
        name="route",
    )(
        pltpu.with_memory_space_constraint(ids, pltpu.HBM),
        pltpu.with_memory_space_constraint(router_weights[0].T, pltpu.HBM),
        pltpu.with_memory_space_constraint(grad_out[0], pltpu.HBM),
    )
    slot_of = routed[0]
    arrived = {item: moved(sent, *item) for item, sent in zip(order, routed[1:])}
    inner = pl.pallas_call(
        inner_kernel,
        out_shape=jax.ShapeDtypeStruct((2 * slots, half), F32),
        in_specs=specs(pltpu.VMEM, 2) + specs(pltpu.HBM, 1),
        out_specs=specs(pltpu.VMEM, 1)[0],
        scratch_shapes=[
            pltpu.VMEM((hid, half), F32),
            pltpu.SemaphoreType.DMA((half // min(half, 4 * LANES),)),
        ],
        compiler_params=params(),
        cost_estimate=cost(4 * slots * hid * half, 4 * hid * half + 8 * slots * half),
        name="inner",
    )(own_hidden, other_hidden, pltpu.with_memory_space_constraint(param, pltpu.HBM))

    tile = jax.ShapeDtypeStruct((group + -group % 8, LANES), F32)
    returned = {}
    for items, steps in ((first_items, early), (last_items, [far])):
        done = list(returned.values())
        scores = pl.pallas_call(
            functools.partial(score_kernel, items, steps, group, cap),
            out_shape=tile,
            in_specs=specs(pltpu.VMEM, 1 + len(items)) + specs(pl.ANY, len(done)),
            out_specs=specs(pltpu.VMEM, 1)[0],
            compiler_params=params(),
            cost_estimate=cost(2 * len(items) * cap * half, 6 * len(items) * cap * half),
            name="score",
        )(inner, *[arrived[item] for item in items], *done)
        for k in steps:
            returned[k] = moved(scores, 0, k)

    block = min(hid, 2 * LANES)
    blocks = [slice(top, top + block) for top in range(0, hid, block)]
    above = blocks[-1].start
    inputs = (param, moment[0, 0], second[0, 0])
    scratch = [
        pltpu.VMEM((2, block, 2 * slots), BF16),
        pltpu.VMEM((2, block, half), F32),
    ]
    earlier, placed, scales = pl.pallas_call(
        functools.partial(first_update_kernel, blocks[:-1], order, group, cap),
        out_shape=[
            jax.ShapeDtypeStruct((above, half), F32),
            jax.ShapeDtypeStruct((2 * slots, half), BF16),
            jax.ShapeDtypeStruct((2, TILE, LANES), F32),
        ],
        in_specs=specs(pltpu.VMEM, len(order) + 5),
        out_specs=specs(pltpu.VMEM, 3),
        scratch_shapes=scratch,
        compiler_params=params(),
        cost_estimate=cost(4 * slots * above * half, 12 * above * half),
        name="first_update",
    )(*[arrived[item] for item in order], own_hidden, other_hidden, *inputs)
    own_scores = pl.pallas_call(
        functools.partial(merge_kernel, group),
        out_shape=tile,
        in_specs=specs(pltpu.VMEM, group),
        out_specs=specs(pltpu.VMEM, 1)[0],
        compiler_params=params(),
        name="merge",
    )(*[returned[k] for k in range(group)])
    other_scores = moved(own_scores, 1, 0)
    update = pl.pallas_call(
        functools.partial(last_update_kernel, blocks[-1:]),
        out_shape=jax.ShapeDtypeStruct((hid, half), F32),
        in_specs=specs(pltpu.VMEM, 8) + specs(pl.ANY, 1),
        out_specs=specs(pltpu.HBM, 1)[0],
        scratch_shapes=scratch
        + [
            pltpu.VMEM((hid - above, half), F32),
            pltpu.SemaphoreType.DMA((2,)),
        ],
        compiler_params=params(),
        cost_estimate=cost(4 * slots * (hid - above) * half, 12 * hid * half),
        name="last_update",
    )(own_hidden, other_hidden, placed, scales, *inputs, earlier, own_scores)
    router = pl.pallas_call(
        functools.partial(combine_kernel, group, cap),
        out_shape=jax.ShapeDtypeStruct((top, tokens), F32),
        in_specs=specs(pltpu.VMEM, 4),
        out_specs=specs(pltpu.VMEM, 1)[0],
        compiler_params=params(),
        cost_estimate=cost(4 * slots * tokens, 8 * top * tokens),
        name="combine",
    )(ids, slot_of, own_scores, other_scores)
    return (update[None, None], router.T[None])


def solution(mesh):
    sections, group = mesh.devices.shape
    split = jax.sharding.Mesh(
        mesh.devices.reshape(2, sections // 2, group), ("pair", "rest", "ep")
    )
    section = ("pair", "rest")
    rows = P(section, "ep", None)
    blocks = P(section, "ep", None, None)
    return jax.shard_map(
        local,
        mesh=split,
        in_specs=(rows, rows, rows, blocks, blocks, blocks, blocks),
        out_specs=(blocks, rows),
        check_vma=False,
    )
```

```python
import functools

import jax
import jax.numpy as jnp
from jax import lax
from jax.experimental import pallas as pl
from jax.experimental.pallas import tpu as pltpu
from jax.sharding import PartitionSpec as P

beta_first = 0.9
beta_second = 0.95
adam_eps = 1e-08
decay_rate = 0.1
first_fix = 1.0 - 0.9**10
second_fix = 1.0 - 0.95**10

LANES = 128
TILE = 16
VMEM_BYTES = 32 * 1024 * 1024
F32 = jnp.float32
BF16 = jnp.bfloat16


def params():
    return pltpu.CompilerParams(vmem_limit_bytes=VMEM_BYTES)


def cost(flops, touched):
    return pl.CostEstimate(flops=int(flops), bytes_accessed=int(touched), transcendentals=0)


def specs(space, count):
    return [pl.BlockSpec(memory_space=space) for _ in range(count)]


def ep_index():
    return lax.axis_index("ep").astype(jnp.int32)


def own_half():
    return lax.axis_index("pair").astype(jnp.int32)


def start_grads(grads_hbm, held, sems):
    half = held.shape[2]
    mine = own_half()
    copies = []
    for side in range(2):
        column = pl.multiple_of((1 - mine if side else mine) * half, half)
        copies.append(
            pltpu.make_async_copy(
                grads_hbm.at[:, pl.ds(column, half)], held.at[side], sems.at[side]
            )
        )
        copies[-1].start()
    return copies


def pick_rows(slots, k, cap):
    place = lax.broadcasted_iota(jnp.int32, (cap, slots.shape[1]), 0).astype(F32)
    return jnp.where(place == slots[k : k + 1, :], 1.0, 0.0).astype(BF16)


def fill_chunks(steps, cap, picks, held, copies, tiles, chunks):
    half = held.shape[2]
    data_rows = half // LANES * cap
    step = min(half, 2 * LANES)
    pick = jnp.concatenate([picks[k] for k in steps], axis=0)
    for side in range(2):
        for k in steps:
            chunks[side, k][data_rows:, :] = tiles[k]
        copies[side].wait()
        for column in range(0, half, step):
            block = jnp.dot(
                pick, held[side, :, column : column + step], preferred_element_type=F32
            ).astype(BF16)
            for at, k in enumerate(steps):
                for part in range(step // LANES):
                    top = (column // LANES + part) * cap
                    chunks[side, k][top : top + cap, :] = block[
                        at * cap : (at + 1) * cap, part * LANES : (part + 1) * LANES
                    ]


def route_kernel(
    items, steps, group, cap, ids_hbm, weight_hbm, grads_hbm, slots_ref, tiles_ref, *rest
):
    chunks = dict(zip(items, rest))
    ids_ref, weight_ref, held, sems = rest[len(items) :]
    tokens = held.shape[1]
    me = ep_index()
    small = [
        pltpu.make_async_copy(ids_hbm, ids_ref, sems.at[2]),
        pltpu.make_async_copy(weight_hbm, weight_ref, sems.at[3]),
    ]
    for copy in small:
        copy.start()
    copies = start_grads(grads_hbm, held, sems)
    earlier = lax.broadcasted_iota(jnp.int32, (tokens, tokens), 0)
    later = lax.broadcasted_iota(jnp.int32, (tokens, tokens), 1)
    ahead = jnp.where(earlier < later, 1.0, 0.0).astype(BF16)
    for copy in small:
        copy.wait()
    ids = ids_ref[...]
    weights = weight_ref[...].astype(F32)
    members, scales = [], []
    for k in range(group):
        named = ids == (me ^ k)
        members.append(jnp.sum(jnp.where(named, 1.0, 0.0), axis=0, keepdims=True))
        scales.append(jnp.sum(jnp.where(named, weights, 0.0), axis=0, keepdims=True))
    if group % TILE:
        members.append(jnp.zeros((-group % TILE, tokens), F32))
    member = jnp.concatenate(members, axis=0)
    before = jnp.dot(member.astype(BF16), ahead, preferred_element_type=F32)
    slots = jnp.where(member > 0.5, before, -1.0)
    slots_ref[...] = slots
    picks = [pick_rows(slots, k, cap) for k in range(group)]
    base = me * cap
    tile_row = lax.broadcasted_iota(jnp.int32, (TILE, LANES), 0)
    tile_lane = lax.broadcasted_iota(jnp.int32, (TILE, LANES), 1)
    spot = tile_row * LANES + tile_lane
    kept = (spot >= base) & (spot < base + cap)
    tiles = []
    for k in range(group):
        spread = jnp.broadcast_to(scales[k], (TILE, tokens)).astype(BF16)
        doubled = jnp.concatenate([picks[k]] * (LANES // cap), axis=0)
        tile = lax.dot_general(
            spread, doubled, (((1,), (1,)), ((), ())), preferred_element_type=F32
        )
        tiles.append(jnp.where(kept, tile, 0.0).astype(BF16))
        tiles_ref[k] = tiles[k]
    fill_chunks(steps, cap, picks, held, copies, tiles, chunks)


def later_kernel(items, steps, cap, slots_ref, tiles_ref, grads_hbm, _, *rest):
    chunks = dict(zip(items, rest))
    held, sems = rest[len(items) :]
    copies = start_grads(grads_hbm, held, sems)
    slots = slots_ref[...]
    picks = {k: pick_rows(slots, k, cap) for k in steps}
    fill_chunks(steps, cap, picks, held, copies, tiles_ref, chunks)


def inner_kernel(own_ref, other_ref, master_hbm, inner_ref, master_ref, sems):
    half = master_ref.shape[1]
    step = min(half, 4 * LANES)
    parts = [slice(column, column + step) for column in range(0, half, step)]
    loads = [
        pltpu.make_async_copy(master_hbm.at[:, part], master_ref.at[:, part], sems.at[at])
        for at, part in enumerate(parts)
    ]
    for load in loads:
        load.start()
    slots = own_ref.shape[1]
    for load, part in zip(loads, parts):
        load.wait()
        weights = master_ref[:, part].astype(BF16)
        for at, ref in ((0, own_ref), (slots, other_ref)):
            inner_ref[at : at + slots, part] = lax.dot_general(
                ref[...], weights, (((0,), (0,)), ((), ())), preferred_element_type=F32
            )


def score_chunks(steps, group, cap, chunks, inner_ref, score_ref):
    blocks = inner_ref.shape[1] // LANES
    me = ep_index()
    line_of = lax.broadcasted_iota(jnp.int32, score_ref.shape, 0)
    scores = jnp.zeros(score_ref.shape, F32)
    for k in steps:
        sums = []
        for side in range(2):
            start = pl.multiple_of(side * group * cap + (me ^ k) * cap, cap)
            total = jnp.zeros((cap, LANES), F32)
            for block in range(blocks):
                rows = chunks[side, k][block * cap : (block + 1) * cap, :].astype(F32)
                total += rows * inner_ref[pl.ds(start, cap), block * LANES : (block + 1) * LANES]
            sums.append(total)
        both = jnp.concatenate(sums, axis=0)
        line = jnp.sum(both.T, axis=0, keepdims=True)
        scores = jnp.where(line_of == (me ^ k), line, scores)
    score_ref[...] = scores


def place_chunks(items, group, cap, chunks, rows_ref):
    blocks = rows_ref.shape[1] // LANES
    me = ep_index()
    scales = [jnp.zeros((TILE, LANES), F32)] * 2
    for side, k in items:
        chunk = chunks[side, k]
        start = pl.multiple_of(side * group * cap + (me ^ k) * cap, cap)
        for block in range(blocks):
            rows_ref[pl.ds(start, cap), block * LANES : (block + 1) * LANES] = chunk[
                block * cap : (block + 1) * cap, :
            ]
        scales[side] += chunk[blocks * cap :, :].astype(F32)
    return scales


def score_kernel(items, steps, group, cap, inner_ref, *rest):
    score_ref = rest[-1]
    score_chunks(steps, group, cap, dict(zip(items, rest)), inner_ref, score_ref)


def merge_kernel(group, local_ref, *rest):
    out_ref = rest[-1]
    row = lax.broadcasted_iota(jnp.int32, out_ref.shape, 0)
    me = ep_index()
    table = jnp.zeros(out_ref.shape, F32)
    for k, ref in enumerate((local_ref,) + rest[:-1]):
        line = jnp.sum(jnp.where(row == me, ref[...], 0.0), axis=0, keepdims=True)
        table = jnp.where(row == k, line, table)
    out_ref[...] = table


def update_rows(blocks, operands, scaled, total, update, finished):
    own_ref, other_ref, rows, scales_ref, master_ref, moment_ref, second_ref = operands
    slots = own_ref.shape[1]
    half = rows.shape[1]
    step = min(half, 4 * LANES)

    def multiply(at):
        block = blocks[at]
        for side, ref in enumerate((own_ref, other_ref)):
            for part in range(slots // LANES):
                lanes = slice(part * LANES, (part + 1) * LANES)
                column = side * slots + part * LANES
                scaled[at % 2, :, column : column + LANES] = (
                    ref[block, lanes].astype(F32) * scales_ref[side, part : part + 1, :]
                ).astype(BF16)
        total[at % 2] = jnp.dot(scaled[at % 2], rows[...], preferred_element_type=F32)

    def moments(at, top, columns):
        lines = slice(blocks[at].start + top, blocks[at].start + top + TILE)
        grad = total[at % 2, top : top + TILE, columns]
        first = moment_ref[lines, columns].astype(F32) * (beta_first / first_fix) + grad * (
            (1.0 - beta_first) / first_fix
        )
        square = second_ref[lines, columns].astype(F32) * (beta_second / second_fix) + (
            grad * grad
        ) * ((1.0 - beta_second) / second_fix)
        return first, square, lax.rsqrt(square)

    def inverse(first, square, root):
        return first, pl.reciprocal(square * root + adam_eps, approx=True)

    def finish(at, top, columns, first, scale):
        lines = slice(blocks[at].start + top, blocks[at].start + top + TILE)
        place = slice(lines.start - blocks[0].start, lines.stop - blocks[0].start)
        update[place, columns] = first * scale + decay_rate * master_ref[lines, columns]

    multiply(0)
    for at, block in enumerate(blocks):
        if at + 1 < len(blocks):
            multiply(at + 1)
        pieces = [
            (top, slice(column, column + step))
            for top in range(0, block.stop - block.start, TILE)
            for column in range(0, half, step)
        ]
        held = {}
        for turn in range(len(pieces) + 2):
            if turn < len(pieces):
                held[turn, 0] = moments(at, *pieces[turn])
            if 0 <= turn - 1 < len(pieces):
                held[turn - 1, 1] = inverse(*held.pop((turn - 1, 0)))
            if turn >= 2:
                finish(at, *pieces[turn - 2], *held.pop((turn - 2, 1)))
        finished(at)


def first_update_kernel(blocks, items, group, cap, *refs):
    chunks, operands = dict(zip(items, refs)), refs[len(items) : len(items) + 5]
    update, rows, scales_ref, scaled, total = refs[len(items) + 5 :]
    scales = place_chunks(items, group, cap, chunks, rows)
    for side in range(2):
        scales_ref[side] = scales[side]
    operands = operands[:2] + (rows, scales_ref) + operands[2:]
    update_rows(blocks, operands, scaled, total, update, lambda at: None)


def last_update_kernel(blocks, *refs):
    earlier, _, update_hbm, scaled, total, update, sems = refs[7:]
    above = earlier.shape[0]
    copies = [
        pltpu.make_async_copy(earlier, update_hbm.at[:above, :], sems.at[len(blocks)])
    ]
    copies[0].start()

    def finished(at):
        block = blocks[at]
        copies.append(
            pltpu.make_async_copy(
                update.at[block.start - above : block.stop - above, :],
                update_hbm.at[block, :],
                sems.at[at],
            )
        )
        copies[-1].start()

    update_rows(blocks, refs[:7], scaled, total, update, finished)
    for copy in copies:
        copy.wait()


def combine_kernel(group, cap, ids_ref, slots_ref, own_ref, other_ref, out_ref):
    tokens = ids_ref.shape[1]
    me = ep_index()
    lane = lax.broadcasted_iota(jnp.int32, own_ref.shape, 1)
    lines = jnp.where(lane < cap, own_ref[...], other_ref[...])
    rest = jnp.zeros((LANES - lines.shape[0], LANES), F32)
    columns = jnp.concatenate([lines, rest], axis=0).T
    columns = columns[:cap] + columns[cap : 2 * cap]
    place = lax.broadcasted_iota(jnp.int32, (cap, tokens), 0).astype(F32)
    ids = ids_ref[...]
    result = jnp.zeros(ids.shape, F32)
    for k in range(group):
        at_slot = jnp.where(place == slots_ref[k : k + 1, :], columns[:, k : k + 1], 0.0)
        result = jnp.where(ids == (me ^ k), jnp.sum(at_slot, axis=0, keepdims=True), result)
    out_ref[...] = result


def moved(array, side, step):
    if (side, step) == (0, 0):
        return array
    group = lax.axis_size("ep")
    pairs = [
        (p * group + e, (p ^ side) * group + (e ^ step)) for p in range(2) for e in range(group)
    ]
    return lax.ppermute(array, ("pair", "ep"), pairs)


def local(grad_out, router_weights, expert_ids, hidden, master, moment, second):
    group = lax.axis_size("ep")
    tokens, width = grad_out.shape[1:]
    top = expert_ids.shape[2]
    hid, slots = hidden.shape[2:]
    half = master.shape[3]
    cap = slots // group
    ids = expert_ids[0].T
    own_hidden = hidden[0, 0]
    param = master[0, 0]
    other_hidden = moved(own_hidden, 1, 0)

    far = group // 2
    early = [k for k in range(1, group) if k != far]
    late = [0, far]
    first_items = [(side, k) for side in range(2) for k in reversed(early)]
    last_items = [(0, far), (1, far), (1, 0), (0, 0)]
    order = first_items + last_items
    chunk = jax.ShapeDtypeStruct((half // LANES * cap + TILE, LANES), BF16)
    grads = pltpu.with_memory_space_constraint(grad_out[0], pltpu.HBM)
    held = pltpu.VMEM((2, tokens, half), BF16)
    routed = pl.pallas_call(
        functools.partial(route_kernel, first_items, early, group, cap),
        out_shape=[
            jax.ShapeDtypeStruct((group + -group % TILE, tokens), F32),
            jax.ShapeDtypeStruct((group, TILE, LANES), BF16),
        ]
        + [chunk] * len(first_items),
        in_specs=specs(pltpu.HBM, 3),
        out_specs=specs(pltpu.VMEM, 2 + len(first_items)),
        scratch_shapes=[
            pltpu.VMEM((top, tokens), jnp.int32),
            pltpu.VMEM((top, tokens), BF16),
            held,
            pltpu.SemaphoreType.DMA((4,)),
        ],
        compiler_params=params(),
        cost_estimate=cost(2 * slots * tokens * width, 2 * (tokens + slots) * width),
        name="route",
    )(
        pltpu.with_memory_space_constraint(ids, pltpu.HBM),
        pltpu.with_memory_space_constraint(router_weights[0].T, pltpu.HBM),
        grads,
    )
    slot_of, tiles = routed[:2]
    arrived = {item: moved(sent, *item) for item, sent in zip(first_items, routed[2:])}

    inner = pl.pallas_call(
        inner_kernel,
        out_shape=jax.ShapeDtypeStruct((2 * slots, half), F32),
        in_specs=specs(pltpu.VMEM, 2) + specs(pltpu.HBM, 1),
        out_specs=specs(pltpu.VMEM, 1)[0],
        scratch_shapes=[
            pltpu.VMEM((hid, half), F32),
            pltpu.SemaphoreType.DMA((half // min(half, 4 * LANES),)),
        ],
        compiler_params=params(),
        cost_estimate=cost(4 * slots * hid * half, 4 * hid * half + 8 * slots * half),
        name="inner",
    )(own_hidden, other_hidden, pltpu.with_memory_space_constraint(param, pltpu.HBM))

    routed = pl.pallas_call(
        functools.partial(later_kernel, last_items, late, cap),
        out_shape=[chunk] * len(last_items),
        in_specs=specs(pltpu.VMEM, 2) + specs(pltpu.HBM, 1) + specs(pl.ANY, 1),
        out_specs=specs(pltpu.VMEM, len(last_items)),
        scratch_shapes=[held, pltpu.SemaphoreType.DMA((2,))],
        compiler_params=params(),
        cost_estimate=cost(2 * slots * tokens * width, 2 * (tokens + slots) * width),
        name="later",
    )(slot_of, tiles, grads, inner)
    arrived |= {item: moved(sent, *item) for item, sent in zip(last_items, routed)}

    tile = jax.ShapeDtypeStruct((group + -group % 8, LANES), F32)
    returned = {}
    for items, steps in ((first_items, early), (last_items, late)):
        done = list(returned.values())
        scores = pl.pallas_call(
            functools.partial(score_kernel, items, steps, group, cap),
            out_shape=tile,
            in_specs=specs(pltpu.VMEM, 1 + len(items)) + specs(pl.ANY, len(done)),
            out_specs=specs(pltpu.VMEM, 1)[0],
            compiler_params=params(),
            cost_estimate=cost(2 * len(items) * cap * half, 6 * len(items) * cap * half),
            name="score",
        )(inner, *[arrived[item] for item in items], *done)
        for k in steps:
            returned[k] = moved(scores, 0, k)

    block = min(hid, 2 * LANES)
    blocks = [slice(top, top + block) for top in range(0, hid, block)]
    above = blocks[-1].start
    inputs = (param, moment[0, 0], second[0, 0])
    scratch = [
        pltpu.VMEM((2, block, 2 * slots), BF16),
        pltpu.VMEM((2, block, half), F32),
    ]
    earlier, placed, scales = pl.pallas_call(
        functools.partial(first_update_kernel, blocks[:-1], order, group, cap),
        out_shape=[
            jax.ShapeDtypeStruct((above, half), F32),
            jax.ShapeDtypeStruct((2 * slots, half), BF16),
            jax.ShapeDtypeStruct((2, TILE, LANES), F32),
        ],
        in_specs=specs(pltpu.VMEM, len(order) + 5),
        out_specs=specs(pltpu.VMEM, 3),
        scratch_shapes=scratch,
        compiler_params=params(),
        cost_estimate=cost(4 * slots * above * half, 12 * above * half),
        name="first_update",
    )(*[arrived[item] for item in order], own_hidden, other_hidden, *inputs)
    own_scores = pl.pallas_call(
        functools.partial(merge_kernel, group),
        out_shape=tile,
        in_specs=specs(pltpu.VMEM, group),
        out_specs=specs(pltpu.VMEM, 1)[0],
        compiler_params=params(),
        name="merge",
    )(*[returned[k] for k in range(group)])
    other_scores = moved(own_scores, 1, 0)
    update = pl.pallas_call(
        functools.partial(last_update_kernel, blocks[-1:]),
        out_shape=jax.ShapeDtypeStruct((hid, half), F32),
        in_specs=specs(pltpu.VMEM, 8) + specs(pl.ANY, 1),
        out_specs=specs(pltpu.HBM, 1)[0],
        scratch_shapes=scratch
        + [
            pltpu.VMEM((hid - above, half), F32),
            pltpu.SemaphoreType.DMA((2,)),
        ],
        compiler_params=params(),
        cost_estimate=cost(4 * slots * (hid - above) * half, 12 * hid * half),
        name="last_update",
    )(own_hidden, other_hidden, placed, scales, *inputs, earlier, own_scores)
    router = pl.pallas_call(
        functools.partial(combine_kernel, group, cap),
        out_shape=jax.ShapeDtypeStruct((top, tokens), F32),
        in_specs=specs(pltpu.VMEM, 4),
        out_specs=specs(pltpu.VMEM, 1)[0],
        compiler_params=params(),
        cost_estimate=cost(4 * slots * tokens, 8 * top * tokens),
        name="combine",
    )(ids, slot_of, own_scores, other_scores)
    return (update[None, None], router.T[None])


def solution(mesh):
    sections, group = mesh.devices.shape
    split = jax.sharding.Mesh(
        mesh.devices.reshape(2, sections // 2, group), ("pair", "rest", "ep")
    )
    section = ("pair", "rest")
    rows = P(section, "ep", None)
    blocks = P(section, "ep", None, None)
    return jax.shard_map(
        local,
        mesh=split,
        in_specs=(rows, rows, rows, blocks, blocks, blocks, blocks),
        out_specs=(blocks, rows),
        check_vma=False,
    )
```

```python
import functools

import jax
import jax.numpy as jnp
from jax import lax
from jax.experimental import pallas as pl
from jax.experimental.pallas import tpu as pltpu
from jax.sharding import PartitionSpec as P

beta_first = 0.9
beta_second = 0.95
adam_eps = 1e-08
decay_rate = 0.1
first_fix = 1.0 - 0.9**10
second_fix = 1.0 - 0.95**10

LANES = 128
TILE = 16
VMEM_BYTES = 32 * 1024 * 1024
F32 = jnp.float32
BF16 = jnp.bfloat16


def params():
    return pltpu.CompilerParams(vmem_limit_bytes=VMEM_BYTES)


def cost(flops, touched):
    return pl.CostEstimate(flops=int(flops), bytes_accessed=int(touched), transcendentals=0)


def specs(space, count):
    return [pl.BlockSpec(memory_space=space) for _ in range(count)]


def ep_index():
    return lax.axis_index("ep").astype(jnp.int32)


def own_half():
    return lax.axis_index("pair").astype(jnp.int32)


def start_grads(grads_hbm, held, sems):
    half = held.shape[2]
    mine = own_half()
    copies = []
    for side in range(2):
        column = pl.multiple_of((1 - mine if side else mine) * half, half)
        copies.append(
            pltpu.make_async_copy(
                grads_hbm.at[:, pl.ds(column, half)], held.at[side], sems.at[side]
            )
        )
        copies[-1].start()
    return copies


def pick_rows(slots, k, cap):
    place = lax.broadcasted_iota(jnp.int32, (cap, slots.shape[1]), 0).astype(F32)
    return jnp.where(place == slots[k : k + 1, :], 1.0, 0.0).astype(BF16)


def fill_chunks(steps, cap, picks, held, copies, tiles, chunks):
    half = held.shape[2]
    data_rows = half // LANES * cap
    step = min(half, 2 * LANES)
    pick = jnp.concatenate([picks[k] for k in steps], axis=0)
    for side in range(2):
        for k in steps:
            chunks[side, k][data_rows:, :] = tiles[k]
        copies[side].wait()
        for column in range(0, half, step):
            block = jnp.dot(
                pick, held[side, :, column : column + step], preferred_element_type=F32
            ).astype(BF16)
            for at, k in enumerate(steps):
                for part in range(step // LANES):
                    top = (column // LANES + part) * cap
                    chunks[side, k][top : top + cap, :] = block[
                        at * cap : (at + 1) * cap, part * LANES : (part + 1) * LANES
                    ]


def route_kernel(
    items, steps, group, cap, ids_hbm, weight_hbm, grads_hbm, slots_ref, tiles_ref, *rest
):
    chunks = dict(zip(items, rest))
    ids_ref, weight_ref, held, sems = rest[len(items) :]
    tokens = held.shape[1]
    me = ep_index()
    small = [
        pltpu.make_async_copy(ids_hbm, ids_ref, sems.at[2]),
        pltpu.make_async_copy(weight_hbm, weight_ref, sems.at[3]),
    ]
    for copy in small:
        copy.start()
    copies = start_grads(grads_hbm, held, sems)
    earlier = lax.broadcasted_iota(jnp.int32, (tokens, tokens), 0)
    later = lax.broadcasted_iota(jnp.int32, (tokens, tokens), 1)
    ahead = jnp.where(earlier < later, 1.0, 0.0).astype(BF16)
    for copy in small:
        copy.wait()
    ids = ids_ref[...]
    weights = weight_ref[...].astype(F32)
    members, scales = [], []
    for k in range(group):
        named = ids == (me ^ k)
        members.append(jnp.sum(jnp.where(named, 1.0, 0.0), axis=0, keepdims=True))
        scales.append(jnp.sum(jnp.where(named, weights, 0.0), axis=0, keepdims=True))
    if group % TILE:
        members.append(jnp.zeros((-group % TILE, tokens), F32))
    member = jnp.concatenate(members, axis=0)
    before = jnp.dot(member.astype(BF16), ahead, preferred_element_type=F32)
    slots = jnp.where(member > 0.5, before, -1.0)
    slots_ref[...] = slots
    picks = [pick_rows(slots, k, cap) for k in range(group)]
    base = me * cap
    tile_row = lax.broadcasted_iota(jnp.int32, (TILE, LANES), 0)
    tile_lane = lax.broadcasted_iota(jnp.int32, (TILE, LANES), 1)
    spot = tile_row * LANES + tile_lane
    kept = (spot >= base) & (spot < base + cap)
    tiles = []
    for k in range(group):
        spread = jnp.broadcast_to(scales[k], (TILE, tokens)).astype(BF16)
        doubled = jnp.concatenate([picks[k]] * (LANES // cap), axis=0)
        tile = lax.dot_general(
            spread, doubled, (((1,), (1,)), ((), ())), preferred_element_type=F32
        )
        tiles.append(jnp.where(kept, tile, 0.0).astype(BF16))
        tiles_ref[k] = tiles[k]
    fill_chunks(steps, cap, picks, held, copies, tiles, chunks)


def later_kernel(
    items, steps, cap, slots_ref, tiles_ref, grads_hbm, own_ref, other_ref, master_hbm, inner_ref, *rest
):
    chunks = dict(zip(items, rest))
    held, master_ref, sems = rest[len(items) :]
    copies = start_grads(grads_hbm, held, sems)
    half = master_ref.shape[1]
    step = min(half, 4 * LANES)
    parts = [slice(column, column + step) for column in range(0, half, step)]
    loads = [
        pltpu.make_async_copy(master_hbm.at[:, part], master_ref.at[:, part], sems.at[2 + at])
        for at, part in enumerate(parts)
    ]
    for load in loads:
        load.start()
    slots = slots_ref[...]
    picks = {k: pick_rows(slots, k, cap) for k in steps}
    fill_chunks(steps, cap, picks, held, copies, tiles_ref, chunks)
    slot_count = own_ref.shape[1]
    for load, part in zip(loads, parts):
        load.wait()
        weights = master_ref[:, part].astype(BF16)
        for at, ref in ((0, own_ref), (slot_count, other_ref)):
            inner_ref[at : at + slot_count, part] = lax.dot_general(
                ref[...], weights, (((0,), (0,)), ((), ())), preferred_element_type=F32
            )


def score_chunks(steps, group, cap, chunks, inner_ref, score_ref):
    blocks = inner_ref.shape[1] // LANES
    me = ep_index()
    line_of = lax.broadcasted_iota(jnp.int32, score_ref.shape, 0)
    scores = jnp.zeros(score_ref.shape, F32)
    for k in steps:
        sums = []
        for side in range(2):
            start = pl.multiple_of(side * group * cap + (me ^ k) * cap, cap)
            total = jnp.zeros((cap, LANES), F32)
            for block in range(blocks):
                rows = chunks[side, k][block * cap : (block + 1) * cap, :].astype(F32)
                total += rows * inner_ref[pl.ds(start, cap), block * LANES : (block + 1) * LANES]
            sums.append(total)
        both = jnp.concatenate(sums, axis=0)
        line = jnp.sum(both.T, axis=0, keepdims=True)
        scores = jnp.where(line_of == (me ^ k), line, scores)
    score_ref[...] = scores


def place_chunks(items, group, cap, chunks, rows_ref):
    blocks = rows_ref.shape[1] // LANES
    me = ep_index()
    scales = [jnp.zeros((TILE, LANES), F32)] * 2
    for side, k in items:
        chunk = chunks[side, k]
        start = pl.multiple_of(side * group * cap + (me ^ k) * cap, cap)
        for block in range(blocks):
            rows_ref[pl.ds(start, cap), block * LANES : (block + 1) * LANES] = chunk[
                block * cap : (block + 1) * cap, :
            ]
        scales[side] += chunk[blocks * cap :, :].astype(F32)
    return scales


def score_kernel(items, steps, group, cap, inner_ref, *rest):
    score_ref = rest[-1]
    score_chunks(steps, group, cap, dict(zip(items, rest)), inner_ref, score_ref)


def merge_kernel(steps, *rest):
    refs, out_ref = rest[:-1], rest[-1]
    row = lax.broadcasted_iota(jnp.int32, out_ref.shape, 0)
    me = ep_index()
    table = jnp.zeros(out_ref.shape, F32)
    for k, ref in zip(steps, refs):
        line = jnp.sum(jnp.where(row == me, ref[...], 0.0), axis=0, keepdims=True)
        table = jnp.where(row == k, line, table)
    out_ref[...] = table


def update_rows(blocks, operands, scaled, total, update, finished):
    own_ref, other_ref, rows, scales_ref, master_ref, moment_ref, second_ref = operands
    slots = own_ref.shape[1]
    half = rows.shape[1]
    step = min(half, 4 * LANES)

    def multiply(at):
        block = blocks[at]
        for side, ref in enumerate((own_ref, other_ref)):
            for part in range(slots // LANES):
                lanes = slice(part * LANES, (part + 1) * LANES)
                column = side * slots + part * LANES
                scaled[at % 2, :, column : column + LANES] = (
                    ref[block, lanes].astype(F32) * scales_ref[side, part : part + 1, :]
                ).astype(BF16)
        total[at % 2] = jnp.dot(scaled[at % 2], rows[...], preferred_element_type=F32)

    def moments(at, top, columns):
        lines = slice(blocks[at].start + top, blocks[at].start + top + TILE)
        grad = total[at % 2, top : top + TILE, columns]
        first = moment_ref[lines, columns].astype(F32) * (beta_first / first_fix) + grad * (
            (1.0 - beta_first) / first_fix
        )
        square = second_ref[lines, columns].astype(F32) * (beta_second / second_fix) + (
            grad * grad
        ) * ((1.0 - beta_second) / second_fix)
        return first, square, lax.rsqrt(square)

    def inverse(first, square, root):
        return first, pl.reciprocal(square * root + adam_eps, approx=True)

    def finish(at, top, columns, first, scale):
        lines = slice(blocks[at].start + top, blocks[at].start + top + TILE)
        place = slice(lines.start - blocks[0].start, lines.stop - blocks[0].start)
        update[place, columns] = first * scale + decay_rate * master_ref[lines, columns]

    multiply(0)
    for at, block in enumerate(blocks):
        if at + 1 < len(blocks):
            multiply(at + 1)
        pieces = [
            (top, slice(column, column + step))
            for top in range(0, block.stop - block.start, TILE)
            for column in range(0, half, step)
        ]
        held = {}
        for turn in range(len(pieces) + 2):
            if turn < len(pieces):
                held[turn, 0] = moments(at, *pieces[turn])
            if 0 <= turn - 1 < len(pieces):
                held[turn - 1, 1] = inverse(*held.pop((turn - 1, 0)))
            if turn >= 2:
                finish(at, *pieces[turn - 2], *held.pop((turn - 2, 1)))
        finished(at)


def update_kernel(items, group, cap, own_ref, other_ref, master_ref, moment_ref, second_ref, *rest):
    chunks = dict(zip(items, rest))
    _, update_hbm, rows, scales_ref, scaled, total, update, sems = rest[len(items) :]
    hid, block = update.shape[0], total.shape[1]
    blocks = [slice(top, top + block) for top in range(0, hid, block)]
    scales = place_chunks(items, group, cap, chunks, rows)
    for side in range(2):
        scales_ref[side] = scales[side]
    copies = []

    def finished(at):
        copies.append(
            pltpu.make_async_copy(
                update.at[blocks[at], :], update_hbm.at[blocks[at], :], sems.at[at]
            )
        )
        copies[-1].start()

    operands = (own_ref, other_ref, rows, scales_ref, master_ref, moment_ref, second_ref)
    update_rows(blocks, operands, scaled, total, update, finished)
    for copy in copies:
        copy.wait()


def combine_kernel(
    far, group, cap, ids_ref, slots_ref, own_ref, other_ref, own_far_ref, other_far_ref, out_ref
):
    tokens = ids_ref.shape[1]
    me = ep_index()
    lane = lax.broadcasted_iota(jnp.int32, own_ref.shape, 1)
    row = lax.broadcasted_iota(jnp.int32, own_ref.shape, 0)
    lines = jnp.where(lane < cap, own_ref[...], other_ref[...])
    last = jnp.where(lane < cap, own_far_ref[...], other_far_ref[...])
    last = jnp.sum(jnp.where(row == me, last, 0.0), axis=0, keepdims=True)
    lines = jnp.where(row == far, last, lines)
    rest = jnp.zeros((LANES - lines.shape[0], LANES), F32)
    columns = jnp.concatenate([lines, rest], axis=0).T
    columns = columns[:cap] + columns[cap : 2 * cap]
    place = lax.broadcasted_iota(jnp.int32, (cap, tokens), 0).astype(F32)
    ids = ids_ref[...]
    result = jnp.zeros(ids.shape, F32)
    for k in range(group):
        at_slot = jnp.where(place == slots_ref[k : k + 1, :], columns[:, k : k + 1], 0.0)
        result = jnp.where(ids == (me ^ k), jnp.sum(at_slot, axis=0, keepdims=True), result)
    out_ref[...] = result


def moved(array, side, step):
    if (side, step) == (0, 0):
        return array
    group = lax.axis_size("ep")
    pairs = [
        (p * group + e, (p ^ side) * group + (e ^ step)) for p in range(2) for e in range(group)
    ]
    return lax.ppermute(array, ("pair", "ep"), pairs)


def local(grad_out, router_weights, expert_ids, hidden, master, moment, second):
    group = lax.axis_size("ep")
    tokens, width = grad_out.shape[1:]
    top = expert_ids.shape[2]
    hid, slots = hidden.shape[2:]
    half = master.shape[3]
    cap = slots // group
    ids = expert_ids[0].T
    own_hidden = hidden[0, 0]
    param = master[0, 0]
    other_hidden = moved(own_hidden, 1, 0)

    far = group // 2
    first = [k for k in range(1, group) if k != far]
    late = [0, far]
    first_items = [(side, k) for side in range(2) for k in reversed(first)]
    last_items = [(0, far), (1, 0), (1, far), (0, 0)]
    order = first_items + last_items
    chunk = jax.ShapeDtypeStruct((half // LANES * cap + TILE, LANES), BF16)
    grads = pltpu.with_memory_space_constraint(grad_out[0], pltpu.HBM)
    held = pltpu.VMEM((2, tokens, half), BF16)
    routed = pl.pallas_call(
        functools.partial(route_kernel, first_items, first, group, cap),
        out_shape=[
            jax.ShapeDtypeStruct((group + -group % TILE, tokens), F32),
            jax.ShapeDtypeStruct((group, TILE, LANES), BF16),
        ]
        + [chunk] * len(first_items),
        in_specs=specs(pltpu.HBM, 3),
        out_specs=specs(pltpu.VMEM, 2 + len(first_items)),
        scratch_shapes=[
            pltpu.VMEM((top, tokens), jnp.int32),
            pltpu.VMEM((top, tokens), BF16),
            held,
            pltpu.SemaphoreType.DMA((4,)),
        ],
        compiler_params=params(),
        cost_estimate=cost(2 * slots * tokens * width, 2 * (tokens + slots) * width),
        name="route",
    )(
        pltpu.with_memory_space_constraint(ids, pltpu.HBM),
        pltpu.with_memory_space_constraint(router_weights[0].T, pltpu.HBM),
        grads,
    )
    slot_of, tiles = routed[:2]
    arrived = {item: moved(sent, *item) for item, sent in zip(first_items, routed[2:])}

    routed = pl.pallas_call(
        functools.partial(later_kernel, last_items, late, cap),
        out_shape=[jax.ShapeDtypeStruct((2 * slots, half), F32)] + [chunk] * len(last_items),
        in_specs=specs(pltpu.VMEM, 2)
        + specs(pltpu.HBM, 1)
        + specs(pltpu.VMEM, 2)
        + specs(pltpu.HBM, 1),
        out_specs=specs(pltpu.VMEM, 1 + len(last_items)),
        scratch_shapes=[
            held,
            pltpu.VMEM((hid, half), F32),
            pltpu.SemaphoreType.DMA((2 + half // min(half, 4 * LANES),)),
        ],
        compiler_params=params(),
        cost_estimate=cost(
            2 * slots * tokens * width + 4 * slots * hid * half, 2 * (tokens + slots) * width
        ),
        name="later",
    )(
        slot_of,
        tiles,
        grads,
        own_hidden,
        other_hidden,
        pltpu.with_memory_space_constraint(param, pltpu.HBM),
    )
    inner = routed[0]
    arrived |= {item: moved(sent, *item) for item, sent in zip(last_items, routed[1:])}

    tile = jax.ShapeDtypeStruct((group + -group % 8, LANES), F32)

    def scored(steps, *after):
        items = [(side, k) for side in range(2) for k in steps]
        return pl.pallas_call(
            functools.partial(score_kernel, items, steps, group, cap),
            out_shape=tile,
            in_specs=specs(pltpu.VMEM, 1 + len(items)) + specs(pl.ANY, len(after)),
            out_specs=specs(pltpu.VMEM, 1)[0],
            compiler_params=params(),
            cost_estimate=cost(2 * len(items) * cap * half, 6 * len(items) * cap * half),
            name="score",
        )(inner, *[arrived[item] for item in items], *after)

    early = [0] + first
    early_scores = scored(early)
    own_scores = pl.pallas_call(
        functools.partial(merge_kernel, early),
        out_shape=tile,
        in_specs=specs(pltpu.VMEM, len(early)),
        out_specs=specs(pltpu.VMEM, 1)[0],
        compiler_params=params(),
        name="merge",
    )(*[moved(early_scores, 0, k) for k in early])
    other_scores = moved(own_scores, 1, 0)
    late_scores = scored([far], own_scores)
    far_scores = [moved(late_scores, side, far) for side in range(2)]

    block = min(hid, 2 * LANES)
    update = pl.pallas_call(
        functools.partial(update_kernel, order, group, cap),
        out_shape=jax.ShapeDtypeStruct((hid, half), F32),
        in_specs=specs(pltpu.VMEM, 5 + len(order)) + specs(pl.ANY, 1),
        out_specs=specs(pltpu.HBM, 1)[0],
        scratch_shapes=[
            pltpu.VMEM((2 * slots, half), BF16),
            pltpu.VMEM((2, TILE, LANES), F32),
            pltpu.VMEM((2, block, 2 * slots), BF16),
            pltpu.VMEM((2, block, half), F32),
            pltpu.VMEM((hid, half), F32),
            pltpu.SemaphoreType.DMA((hid // block,)),
        ],
        compiler_params=params(),
        cost_estimate=cost(4 * slots * hid * half, 12 * hid * half),
        name="update",
    )(
        own_hidden,
        other_hidden,
        param,
        moment[0, 0],
        second[0, 0],
        *[arrived[item] for item in order],
        late_scores,
    )
    router = pl.pallas_call(
        functools.partial(combine_kernel, far, group, cap),
        out_shape=jax.ShapeDtypeStruct((top, tokens), F32),
        in_specs=specs(pltpu.VMEM, 6),
        out_specs=specs(pltpu.VMEM, 1)[0],
        compiler_params=params(),
        cost_estimate=cost(4 * slots * tokens, 8 * top * tokens),
        name="combine",
    )(ids, slot_of, own_scores, other_scores, *far_scores)
    return (update[None, None], router.T[None])


def solution(mesh):
    sections, group = mesh.devices.shape
    split = jax.sharding.Mesh(
        mesh.devices.reshape(2, sections // 2, group), ("pair", "rest", "ep")
    )
    section = ("pair", "rest")
    rows = P(section, "ep", None)
    blocks = P(section, "ep", None, None)
    return jax.shard_map(
        local,
        mesh=split,
        in_specs=(rows, rows, rows, blocks, blocks, blocks, blocks),
        out_specs=(blocks, rows),
        check_vma=False,
    )
```

```python
import functools

import jax
import jax.numpy as jnp
from jax import lax
from jax.experimental import pallas as pl
from jax.experimental.pallas import tpu as pltpu
from jax.sharding import PartitionSpec as P

beta_first = 0.9
beta_second = 0.95
adam_eps = 1e-08
decay_rate = 0.1
first_fix = 1.0 - 0.9**10
second_fix = 1.0 - 0.95**10

LANES = 128
TILE = 16
VMEM_BYTES = 32 * 1024 * 1024
F32 = jnp.float32
BF16 = jnp.bfloat16


def params():
    return pltpu.CompilerParams(vmem_limit_bytes=VMEM_BYTES)


def cost(flops, touched):
    return pl.CostEstimate(flops=int(flops), bytes_accessed=int(touched), transcendentals=0)


def specs(space, count):
    return [pl.BlockSpec(memory_space=space) for _ in range(count)]


def ep_index():
    return lax.axis_index("ep").astype(jnp.int32)


def own_half():
    return lax.axis_index("pair").astype(jnp.int32)


def start_grads(grads_hbm, held, sems):
    half = held.shape[2]
    mine = own_half()
    copies = []
    for side in range(2):
        column = pl.multiple_of((1 - mine if side else mine) * half, half)
        copies.append(
            pltpu.make_async_copy(
                grads_hbm.at[:, pl.ds(column, half)], held.at[side], sems.at[side]
            )
        )
        copies[-1].start()
    return copies


def pick_rows(slots, k, cap):
    place = lax.broadcasted_iota(jnp.int32, (cap, slots.shape[1]), 0).astype(F32)
    return jnp.where(place == slots[k : k + 1, :], 1.0, 0.0).astype(BF16)


def fill_chunks(steps, cap, picks, held, copies, tiles, chunks):
    half = held.shape[2]
    data_rows = half // LANES * cap
    step = min(half, 2 * LANES)
    pick = jnp.concatenate([picks[k] for k in steps], axis=0)
    for side in range(2):
        for k in steps:
            chunks[side, k][data_rows:, :] = tiles[k]
        copies[side].wait()
        for column in range(0, half, step):
            block = jnp.dot(
                pick, held[side, :, column : column + step], preferred_element_type=F32
            ).astype(BF16)
            for at, k in enumerate(steps):
                for part in range(step // LANES):
                    top = (column // LANES + part) * cap
                    chunks[side, k][top : top + cap, :] = block[
                        at * cap : (at + 1) * cap, part * LANES : (part + 1) * LANES
                    ]


def route_kernel(
    items, steps, group, cap, ids_hbm, weight_hbm, grads_hbm, slots_ref, tiles_ref, *rest
):
    chunks = dict(zip(items, rest))
    ids_ref, weight_ref, held, sems = rest[len(items) :]
    tokens = held.shape[1]
    me = ep_index()
    small = [
        pltpu.make_async_copy(ids_hbm, ids_ref, sems.at[2]),
        pltpu.make_async_copy(weight_hbm, weight_ref, sems.at[3]),
    ]
    for copy in small:
        copy.start()
    copies = start_grads(grads_hbm, held, sems)
    earlier = lax.broadcasted_iota(jnp.int32, (tokens, tokens), 0)
    later = lax.broadcasted_iota(jnp.int32, (tokens, tokens), 1)
    ahead = jnp.where(earlier < later, 1.0, 0.0).astype(BF16)
    for copy in small:
        copy.wait()
    ids = ids_ref[...]
    weights = weight_ref[...].astype(F32)
    members, scales = [], []
    for k in range(group):
        named = ids == (me ^ k)
        members.append(jnp.sum(jnp.where(named, 1.0, 0.0), axis=0, keepdims=True))
        scales.append(jnp.sum(jnp.where(named, weights, 0.0), axis=0, keepdims=True))
    if group % TILE:
        members.append(jnp.zeros((-group % TILE, tokens), F32))
    member = jnp.concatenate(members, axis=0)
    before = jnp.dot(member.astype(BF16), ahead, preferred_element_type=F32)
    slots = jnp.where(member > 0.5, before, -1.0)
    slots_ref[...] = slots
    picks = [pick_rows(slots, k, cap) for k in range(group)]
    base = me * cap
    tile_row = lax.broadcasted_iota(jnp.int32, (TILE, LANES), 0)
    tile_lane = lax.broadcasted_iota(jnp.int32, (TILE, LANES), 1)
    spot = tile_row * LANES + tile_lane
    kept = (spot >= base) & (spot < base + cap)
    tiles = []
    for k in range(group):
        spread = jnp.broadcast_to(scales[k], (TILE, tokens)).astype(BF16)
        doubled = jnp.concatenate([picks[k]] * (LANES // cap), axis=0)
        tile = lax.dot_general(
            spread, doubled, (((1,), (1,)), ((), ())), preferred_element_type=F32
        )
        tiles.append(jnp.where(kept, tile, 0.0).astype(BF16))
        tiles_ref[k] = tiles[k]
    fill_chunks(steps, cap, picks, held, copies, tiles, chunks)


def later_kernel(
    items, steps, cap, slots_ref, tiles_ref, grads_hbm, own_ref, other_ref, master_hbm, inner_ref, *rest
):
    chunks = dict(zip(items, rest))
    held, master_ref, sems = rest[len(items) :]
    copies = start_grads(grads_hbm, held, sems)
    half = master_ref.shape[1]
    step = min(half, 4 * LANES)
    parts = [slice(column, column + step) for column in range(0, half, step)]
    loads = [
        pltpu.make_async_copy(master_hbm.at[:, part], master_ref.at[:, part], sems.at[2 + at])
        for at, part in enumerate(parts)
    ]
    for load in loads:
        load.start()
    slots = slots_ref[...]
    picks = {k: pick_rows(slots, k, cap) for k in steps}
    fill_chunks(steps, cap, picks, held, copies, tiles_ref, chunks)
    slot_count = own_ref.shape[1]
    for load, part in zip(loads, parts):
        load.wait()
        weights = master_ref[:, part].astype(BF16)
        for at, ref in ((0, own_ref), (slot_count, other_ref)):
            inner_ref[at : at + slot_count, part] = lax.dot_general(
                ref[...], weights, (((0,), (0,)), ((), ())), preferred_element_type=F32
            )


def score_chunks(steps, group, cap, chunks, inner_ref, score_ref):
    blocks = inner_ref.shape[1] // LANES
    me = ep_index()
    line_of = lax.broadcasted_iota(jnp.int32, score_ref.shape, 0)
    scores = jnp.zeros(score_ref.shape, F32)
    for k in steps:
        sums = []
        for side in range(2):
            start = pl.multiple_of(side * group * cap + (me ^ k) * cap, cap)
            total = jnp.zeros((cap, LANES), F32)
            for block in range(blocks):
                rows = chunks[side, k][block * cap : (block + 1) * cap, :].astype(F32)
                total += rows * inner_ref[pl.ds(start, cap), block * LANES : (block + 1) * LANES]
            sums.append(total)
        both = jnp.concatenate(sums, axis=0)
        line = jnp.sum(both.T, axis=0, keepdims=True)
        scores = jnp.where(line_of == (me ^ k), line, scores)
    score_ref[...] = scores


def place_chunks(items, group, cap, chunks, rows_ref):
    blocks = rows_ref.shape[1] // LANES
    me = ep_index()
    scales = [jnp.zeros((TILE, LANES), F32)] * 2
    for side, k in items:
        chunk = chunks[side, k]
        start = pl.multiple_of(side * group * cap + (me ^ k) * cap, cap)
        for block in range(blocks):
            rows_ref[pl.ds(start, cap), block * LANES : (block + 1) * LANES] = chunk[
                block * cap : (block + 1) * cap, :
            ]
        scales[side] += chunk[blocks * cap :, :].astype(F32)
    return scales


def score_kernel(items, steps, group, cap, inner_ref, *rest):
    score_ref = rest[-1]
    score_chunks(steps, group, cap, dict(zip(items, rest)), inner_ref, score_ref)


def merge_kernel(steps, *rest):
    refs, out_ref = rest[:-1], rest[-1]
    row = lax.broadcasted_iota(jnp.int32, out_ref.shape, 0)
    me = ep_index()
    table = jnp.zeros(out_ref.shape, F32)
    for k, ref in zip(steps, refs):
        line = jnp.sum(jnp.where(row == me, ref[...], 0.0), axis=0, keepdims=True)
        table = jnp.where(row == k, line, table)
    out_ref[...] = table


def update_rows(blocks, operands, scaled, total, update, finished):
    own_ref, other_ref, rows, scales_ref, master_ref, moment_ref, second_ref = operands
    slots = own_ref.shape[1]
    half = rows.shape[1]
    step = min(half, 4 * LANES)

    def multiply(at):
        block = blocks[at]
        for side, ref in enumerate((own_ref, other_ref)):
            for part in range(slots // LANES):
                lanes = slice(part * LANES, (part + 1) * LANES)
                column = side * slots + part * LANES
                scaled[at % 2, :, column : column + LANES] = (
                    ref[block, lanes].astype(F32) * scales_ref[side, part : part + 1, :]
                ).astype(BF16)
        total[at % 2] = jnp.dot(scaled[at % 2], rows[...], preferred_element_type=F32)

    def moments(at, top, columns):
        lines = slice(blocks[at].start + top, blocks[at].start + top + TILE)
        grad = total[at % 2, top : top + TILE, columns]
        first = moment_ref[lines, columns].astype(F32) * (beta_first / first_fix) + grad * (
            (1.0 - beta_first) / first_fix
        )
        square = second_ref[lines, columns].astype(F32) * (beta_second / second_fix) + (
            grad * grad
        ) * ((1.0 - beta_second) / second_fix)
        return first, square, lax.rsqrt(square)

    def inverse(first, square, root):
        return first, pl.reciprocal(square * root + adam_eps, approx=True)

    def finish(at, top, columns, first, scale):
        lines = slice(blocks[at].start + top, blocks[at].start + top + TILE)
        place = slice(lines.start - blocks[0].start, lines.stop - blocks[0].start)
        update[place, columns] = first * scale + decay_rate * master_ref[lines, columns]

    multiply(0)
    for at, block in enumerate(blocks):
        if at + 1 < len(blocks):
            multiply(at + 1)
        pieces = [
            (top, slice(column, column + step))
            for top in range(0, block.stop - block.start, TILE)
            for column in range(0, half, step)
        ]
        held = {}
        for turn in range(len(pieces) + 2):
            if turn < len(pieces):
                held[turn, 0] = moments(at, *pieces[turn])
            if 0 <= turn - 1 < len(pieces):
                held[turn - 1, 1] = inverse(*held.pop((turn - 1, 0)))
            if turn >= 2:
                finish(at, *pieces[turn - 2], *held.pop((turn - 2, 1)))
        finished(at)


def update_kernel(items, group, cap, own_ref, other_ref, master_ref, moment_ref, second_ref, *rest):
    chunks = dict(zip(items, rest))
    _, update_hbm, rows, scales_ref, scaled, total, update, sems = rest[len(items) :]
    hid, block = update.shape[0], total.shape[1]
    blocks = [slice(top, top + block) for top in range(0, hid, block)]
    scales = place_chunks(items, group, cap, chunks, rows)
    for side in range(2):
        scales_ref[side] = scales[side]
    copies = []

    def finished(at):
        copies.append(
            pltpu.make_async_copy(
                update.at[blocks[at], :], update_hbm.at[blocks[at], :], sems.at[at]
            )
        )
        copies[-1].start()

    operands = (own_ref, other_ref, rows, scales_ref, master_ref, moment_ref, second_ref)
    update_rows(blocks, operands, scaled, total, update, finished)
    for copy in copies:
        copy.wait()


def combine_kernel(
    far, group, cap, ids_ref, slots_ref, own_ref, other_ref, own_far_ref, other_far_ref, out_ref
):
    tokens = ids_ref.shape[1]
    me = ep_index()
    lane = lax.broadcasted_iota(jnp.int32, own_ref.shape, 1)
    row = lax.broadcasted_iota(jnp.int32, own_ref.shape, 0)
    lines = jnp.where(lane < cap, own_ref[...], other_ref[...])
    last = jnp.where(lane < cap, own_far_ref[...], other_far_ref[...])
    last = jnp.sum(jnp.where(row == me, last, 0.0), axis=0, keepdims=True)
    lines = jnp.where(row == far, last, lines)
    rest = jnp.zeros((LANES - lines.shape[0], LANES), F32)
    columns = jnp.concatenate([lines, rest], axis=0).T
    columns = columns[:cap] + columns[cap : 2 * cap]
    place = lax.broadcasted_iota(jnp.int32, (cap, tokens), 0).astype(F32)
    ids = ids_ref[...]
    result = jnp.zeros(ids.shape, F32)
    for k in range(group):
        at_slot = jnp.where(place == slots_ref[k : k + 1, :], columns[:, k : k + 1], 0.0)
        result = jnp.where(ids == (me ^ k), jnp.sum(at_slot, axis=0, keepdims=True), result)
    out_ref[...] = result


def moved(array, side, step):
    if (side, step) == (0, 0):
        return array
    group = lax.axis_size("ep")
    pairs = [
        (p * group + e, (p ^ side) * group + (e ^ step)) for p in range(2) for e in range(group)
    ]
    return lax.ppermute(array, ("pair", "ep"), pairs)


def local(grad_out, router_weights, expert_ids, hidden, master, moment, second):
    group = lax.axis_size("ep")
    tokens, width = grad_out.shape[1:]
    top = expert_ids.shape[2]
    hid, slots = hidden.shape[2:]
    half = master.shape[3]
    cap = slots // group
    ids = expert_ids[0].T
    own_hidden = hidden[0, 0]
    param = master[0, 0]
    other_hidden = moved(own_hidden, 1, 0)

    far = group // 2
    first = [k for k in range(1, group) if k != far]
    late = [0, far]
    first_items = [(side, k) for side in range(2) for k in reversed(first)]
    last_items = [(0, far), (1, 0), (1, far), (0, 0)]
    order = first_items + last_items
    chunk = jax.ShapeDtypeStruct((half // LANES * cap + TILE, LANES), BF16)
    grads = pltpu.with_memory_space_constraint(grad_out[0], pltpu.HBM)
    held = pltpu.VMEM((2, tokens, half), BF16)
    routed = pl.pallas_call(
        functools.partial(route_kernel, first_items, first, group, cap),
        out_shape=[
            jax.ShapeDtypeStruct((group + -group % TILE, tokens), F32),
            jax.ShapeDtypeStruct((group, TILE, LANES), BF16),
        ]
        + [chunk] * len(first_items),
        in_specs=specs(pltpu.HBM, 3),
        out_specs=specs(pltpu.VMEM, 2 + len(first_items)),
        scratch_shapes=[
            pltpu.VMEM((top, tokens), jnp.int32),
            pltpu.VMEM((top, tokens), BF16),
            held,
            pltpu.SemaphoreType.DMA((4,)),
        ],
        compiler_params=params(),
        cost_estimate=cost(2 * slots * tokens * width, 2 * (tokens + slots) * width),
        name="route",
    )(
        pltpu.with_memory_space_constraint(ids, pltpu.HBM),
        pltpu.with_memory_space_constraint(router_weights[0].T, pltpu.HBM),
        grads,
    )
    slot_of, tiles = routed[:2]
    arrived = {item: moved(sent, *item) for item, sent in zip(first_items, routed[2:])}

    routed = pl.pallas_call(
        functools.partial(later_kernel, last_items, late, cap),
        out_shape=[jax.ShapeDtypeStruct((2 * slots, half), F32)] + [chunk] * len(last_items),
        in_specs=specs(pltpu.VMEM, 2)
        + specs(pltpu.HBM, 1)
        + specs(pltpu.VMEM, 2)
        + specs(pltpu.HBM, 1),
        out_specs=specs(pltpu.VMEM, 1 + len(last_items)),
        scratch_shapes=[
            held,
            pltpu.VMEM((hid, half), F32),
            pltpu.SemaphoreType.DMA((2 + half // min(half, 4 * LANES),)),
        ],
        compiler_params=params(),
        cost_estimate=cost(
            2 * slots * tokens * width + 4 * slots * hid * half, 2 * (tokens + slots) * width
        ),
        name="later",
    )(
        slot_of,
        tiles,
        grads,
        own_hidden,
        other_hidden,
        pltpu.with_memory_space_constraint(param, pltpu.HBM),
    )
    inner = routed[0]
    arrived |= {item: moved(sent, *item) for item, sent in zip(last_items, routed[1:])}

    tile = jax.ShapeDtypeStruct((group + -group % 8, LANES), F32)

    def scored(steps, *after):
        items = [(side, k) for side in range(2) for k in steps]
        return pl.pallas_call(
            functools.partial(score_kernel, items, steps, group, cap),
            out_shape=tile,
            in_specs=specs(pltpu.VMEM, 1 + len(items)) + specs(pl.ANY, len(after)),
            out_specs=specs(pltpu.VMEM, 1)[0],
            compiler_params=params(),
            cost_estimate=cost(2 * len(items) * cap * half, 6 * len(items) * cap * half),
            name="score",
        )(inner, *[arrived[item] for item in items], *after)

    first_scores = scored(first)
    returned = [moved(first_scores, 0, k) for k in first]
    own_scores = pl.pallas_call(
        functools.partial(merge_kernel, first + [0]),
        out_shape=tile,
        in_specs=specs(pltpu.VMEM, group - 1),
        out_specs=specs(pltpu.VMEM, 1)[0],
        compiler_params=params(),
        name="merge",
    )(*returned, scored([0]))
    other_scores = moved(own_scores, 1, 0)
    late_scores = scored([far], own_scores)
    far_scores = [moved(late_scores, side, far) for side in range(2)]

    block = min(hid, 2 * LANES)
    update = pl.pallas_call(
        functools.partial(update_kernel, order, group, cap),
        out_shape=jax.ShapeDtypeStruct((hid, half), F32),
        in_specs=specs(pltpu.VMEM, 5 + len(order)) + specs(pl.ANY, 1),
        out_specs=specs(pltpu.HBM, 1)[0],
        scratch_shapes=[
            pltpu.VMEM((2 * slots, half), BF16),
            pltpu.VMEM((2, TILE, LANES), F32),
            pltpu.VMEM((2, block, 2 * slots), BF16),
            pltpu.VMEM((2, block, half), F32),
            pltpu.VMEM((hid, half), F32),
            pltpu.SemaphoreType.DMA((hid // block,)),
        ],
        compiler_params=params(),
        cost_estimate=cost(4 * slots * hid * half, 12 * hid * half),
        name="update",
    )(
        own_hidden,
        other_hidden,
        param,
        moment[0, 0],
        second[0, 0],
        *[arrived[item] for item in order],
        late_scores,
    )
    router = pl.pallas_call(
        functools.partial(combine_kernel, far, group, cap),
        out_shape=jax.ShapeDtypeStruct((top, tokens), F32),
        in_specs=specs(pltpu.VMEM, 6),
        out_specs=specs(pltpu.VMEM, 1)[0],
        compiler_params=params(),
        cost_estimate=cost(4 * slots * tokens, 8 * top * tokens),
        name="combine",
    )(ids, slot_of, own_scores, other_scores, *far_scores)
    return (update[None, None], router.T[None])


def solution(mesh):
    sections, group = mesh.devices.shape
    split = jax.sharding.Mesh(
        mesh.devices.reshape(2, sections // 2, group), ("pair", "rest", "ep")
    )
    section = ("pair", "rest")
    rows = P(section, "ep", None)
    blocks = P(section, "ep", None, None)
    return jax.shard_map(
        local,
        mesh=split,
        in_specs=(rows, rows, rows, blocks, blocks, blocks, blocks),
        out_specs=(blocks, rows),
        check_vma=False,
    )
```

```python
import functools

import jax
import jax.numpy as jnp
from jax import lax
from jax.experimental import pallas as pl
from jax.experimental.pallas import tpu as pltpu
from jax.sharding import PartitionSpec as P

beta_first = 0.9
beta_second = 0.95
adam_eps = 1e-08
decay_rate = 0.1
first_fix = 1.0 - 0.9**10
second_fix = 1.0 - 0.95**10

LANES = 128
TILE = 16
VMEM_BYTES = 32 * 1024 * 1024
F32 = jnp.float32
BF16 = jnp.bfloat16


def params():
    return pltpu.CompilerParams(vmem_limit_bytes=VMEM_BYTES)


def cost(flops, touched):
    return pl.CostEstimate(flops=int(flops), bytes_accessed=int(touched), transcendentals=0)


def specs(space, count):
    return [pl.BlockSpec(memory_space=space) for _ in range(count)]


def ep_index():
    return lax.axis_index("ep").astype(jnp.int32)


def own_half():
    return lax.axis_index("pair").astype(jnp.int32)


def start_grads(grads_hbm, held, sems):
    half = held.shape[2]
    mine = own_half()
    copies = []
    for side in range(2):
        column = pl.multiple_of((1 - mine if side else mine) * half, half)
        copies.append(
            pltpu.make_async_copy(
                grads_hbm.at[:, pl.ds(column, half)], held.at[side], sems.at[side]
            )
        )
        copies[-1].start()
    return copies


def pick_rows(slots, k, cap):
    place = lax.broadcasted_iota(jnp.int32, (cap, slots.shape[1]), 0).astype(F32)
    return jnp.where(place == slots[k : k + 1, :], 1.0, 0.0).astype(BF16)


def fill_chunks(steps, cap, picks, held, copies, tiles, chunks):
    half = held.shape[2]
    data_rows = half // LANES * cap
    step = min(half, 2 * LANES)
    pick = jnp.concatenate([picks[k] for k in steps], axis=0)
    for side in range(2):
        for k in steps:
            chunks[side, k][data_rows:, :] = tiles[k]
        copies[side].wait()
        for column in range(0, half, step):
            block = jnp.dot(
                pick, held[side, :, column : column + step], preferred_element_type=F32
            ).astype(BF16)
            for at, k in enumerate(steps):
                for part in range(step // LANES):
                    top = (column // LANES + part) * cap
                    chunks[side, k][top : top + cap, :] = block[
                        at * cap : (at + 1) * cap, part * LANES : (part + 1) * LANES
                    ]


def route_kernel(
    items, steps, group, cap, ids_hbm, weight_hbm, grads_hbm, slots_ref, tiles_ref, *rest
):
    chunks = dict(zip(items, rest))
    ids_ref, weight_ref, held, sems = rest[len(items) :]
    tokens = held.shape[1]
    me = ep_index()
    small = [
        pltpu.make_async_copy(ids_hbm, ids_ref, sems.at[2]),
        pltpu.make_async_copy(weight_hbm, weight_ref, sems.at[3]),
    ]
    for copy in small:
        copy.start()
    copies = start_grads(grads_hbm, held, sems)
    earlier = lax.broadcasted_iota(jnp.int32, (tokens, tokens), 0)
    later = lax.broadcasted_iota(jnp.int32, (tokens, tokens), 1)
    ahead = jnp.where(earlier < later, 1.0, 0.0).astype(BF16)
    for copy in small:
        copy.wait()
    ids = ids_ref[...]
    weights = weight_ref[...].astype(F32)
    members, scales = [], []
    for k in range(group):
        named = ids == (me ^ k)
        members.append(jnp.sum(jnp.where(named, 1.0, 0.0), axis=0, keepdims=True))
        scales.append(jnp.sum(jnp.where(named, weights, 0.0), axis=0, keepdims=True))
    if group % TILE:
        members.append(jnp.zeros((-group % TILE, tokens), F32))
    member = jnp.concatenate(members, axis=0)
    before = jnp.dot(member.astype(BF16), ahead, preferred_element_type=F32)
    slots = jnp.where(member > 0.5, before, -1.0)
    slots_ref[...] = slots
    picks = [pick_rows(slots, k, cap) for k in range(group)]
    base = me * cap
    tile_row = lax.broadcasted_iota(jnp.int32, (TILE, LANES), 0)
    tile_lane = lax.broadcasted_iota(jnp.int32, (TILE, LANES), 1)
    spot = tile_row * LANES + tile_lane
    kept = (spot >= base) & (spot < base + cap)
    if group % TILE:
        scales.append(jnp.zeros((-group % TILE, tokens), F32))
    rows = jnp.concatenate(scales, axis=0)
    lines = lax.dot_general(
        rows.astype(BF16),
        jnp.concatenate(picks, axis=0),
        (((1,), (1,)), ((), ())),
        preferred_element_type=F32,
    )
    tiles = []
    for k in range(group):
        line = lines[k : k + 1, k * cap : (k + 1) * cap]
        line = jnp.concatenate([line] * (LANES // cap), axis=1)
        tiles.append(jnp.where(kept, line, 0.0).astype(BF16))
        tiles_ref[k] = tiles[k]
    fill_chunks(steps, cap, picks, held, copies, tiles, chunks)


def later_kernel(
    items, steps, cap, slots_ref, tiles_ref, grads_hbm, own_ref, other_ref, master_hbm, inner_ref, *rest
):
    chunks = dict(zip(items, rest))
    held, master_ref, sems = rest[len(items) :]
    copies = start_grads(grads_hbm, held, sems)
    half = master_ref.shape[1]
    step = min(half, 4 * LANES)
    parts = [slice(column, column + step) for column in range(0, half, step)]
    loads = [
        pltpu.make_async_copy(master_hbm.at[:, part], master_ref.at[:, part], sems.at[2 + at])
        for at, part in enumerate(parts)
    ]
    for load in loads:
        load.start()
    slots = slots_ref[...]
    picks = {k: pick_rows(slots, k, cap) for k in steps}
    fill_chunks(steps, cap, picks, held, copies, tiles_ref, chunks)
    slot_count = own_ref.shape[1]
    for load, part in zip(loads, parts):
        load.wait()
        weights = master_ref[:, part].astype(BF16)
        for at, ref in ((0, own_ref), (slot_count, other_ref)):
            inner_ref[at : at + slot_count, part] = lax.dot_general(
                ref[...], weights, (((0,), (0,)), ((), ())), preferred_element_type=F32
            )


def score_kernel(items, group, cap, inner_ref, *rest):
    chunks, score_ref = dict(zip(items, rest)), rest[-1]
    blocks = inner_ref.shape[1] // LANES
    me = ep_index()
    line_of = lax.broadcasted_iota(jnp.int32, score_ref.shape, 0)
    scores = jnp.zeros(score_ref.shape, F32)
    for k in sorted({k for _, k in items}):
        sums = []
        for side in range(2):
            total = jnp.zeros((cap, LANES), F32)
            if (side, k) in items:
                start = pl.multiple_of(side * group * cap + (me ^ k) * cap, cap)
                for block in range(blocks):
                    rows = chunks[side, k][block * cap : (block + 1) * cap, :].astype(F32)
                    total += rows * inner_ref[
                        pl.ds(start, cap), block * LANES : (block + 1) * LANES
                    ]
            sums.append(total)
        both = jnp.concatenate(sums, axis=0)
        line = jnp.sum(both.T, axis=0, keepdims=True)
        scores = jnp.where(line_of == (me ^ k), line, scores)
    score_ref[...] = scores


def place_chunks(items, group, cap, chunks, rows_ref):
    blocks = rows_ref.shape[1] // LANES
    me = ep_index()
    scales = [jnp.zeros((TILE, LANES), F32)] * 2
    for side, k in items:
        chunk = chunks[side, k]
        start = pl.multiple_of(side * group * cap + (me ^ k) * cap, cap)
        for block in range(blocks):
            rows_ref[pl.ds(start, cap), block * LANES : (block + 1) * LANES] = chunk[
                block * cap : (block + 1) * cap, :
            ]
        scales[side] += chunk[blocks * cap :, :].astype(F32)
    return scales


def merge_kernel(steps, *rest):
    refs, out_ref = rest[: len(steps)], rest[-1]
    row = lax.broadcasted_iota(jnp.int32, out_ref.shape, 0)
    me = ep_index()
    table = jnp.zeros(out_ref.shape, F32)
    for k, ref in zip(steps, refs):
        line = jnp.sum(jnp.where(row == me, ref[...], 0.0), axis=0, keepdims=True)
        table = jnp.where(row == k, line, table)
    out_ref[...] = table


def update_rows(blocks, operands, scaled, total, update, finished):
    own_ref, other_ref, rows, scales_ref, master_ref, moment_ref, second_ref = operands
    slots = own_ref.shape[1]
    half = rows.shape[1]
    step = min(half, 4 * LANES)

    def multiply(at):
        block = blocks[at]
        for side, ref in enumerate((own_ref, other_ref)):
            for part in range(slots // LANES):
                lanes = slice(part * LANES, (part + 1) * LANES)
                column = side * slots + part * LANES
                scaled[at % 2, :, column : column + LANES] = (
                    ref[block, lanes].astype(F32) * scales_ref[side, part : part + 1, :]
                ).astype(BF16)
        total[at % 2] = jnp.dot(scaled[at % 2], rows[...], preferred_element_type=F32)

    def moments(at, top, columns):
        lines = slice(blocks[at].start + top, blocks[at].start + top + TILE)
        grad = total[at % 2, top : top + TILE, columns]
        first = moment_ref[lines, columns].astype(F32) * (beta_first / first_fix) + grad * (
            (1.0 - beta_first) / first_fix
        )
        square = second_ref[lines, columns].astype(F32) * (beta_second / second_fix) + (
            grad * grad
        ) * ((1.0 - beta_second) / second_fix)
        return first, square, lax.rsqrt(square)

    def inverse(first, square, root):
        return first, pl.reciprocal(square * root + adam_eps, approx=True)

    def finish(at, top, columns, first, scale):
        lines = slice(blocks[at].start + top, blocks[at].start + top + TILE)
        place = slice(lines.start - blocks[0].start, lines.stop - blocks[0].start)
        update[place, columns] = first * scale + decay_rate * master_ref[lines, columns]

    multiply(0)
    for at, block in enumerate(blocks):
        if at + 1 < len(blocks):
            multiply(at + 1)
        pieces = [
            (top, slice(column, column + step))
            for top in range(0, block.stop - block.start, TILE)
            for column in range(0, half, step)
        ]
        held = {}
        for turn in range(len(pieces) + 2):
            if turn < len(pieces):
                held[turn, 0] = moments(at, *pieces[turn])
            if 0 <= turn - 1 < len(pieces):
                held[turn - 1, 1] = inverse(*held.pop((turn - 1, 0)))
            if turn >= 2:
                finish(at, *pieces[turn - 2], *held.pop((turn - 2, 1)))
        finished(at)


def update_kernel(items, group, cap, own_ref, other_ref, master_ref, moment_ref, second_ref, *rest):
    chunks = dict(zip(items, rest))
    _, update_hbm, rows, scales_ref, scaled, total, update, sems = rest[len(items) :]
    hid, block = update.shape[0], total.shape[1]
    blocks = [slice(top, top + block) for top in range(0, hid, block)]
    scales = place_chunks(items, group, cap, chunks, rows)
    for side in range(2):
        scales_ref[side] = scales[side]
    copies = []

    def finished(at):
        copies.append(
            pltpu.make_async_copy(
                update.at[blocks[at], :], update_hbm.at[blocks[at], :], sems.at[at]
            )
        )
        copies[-1].start()

    operands = (own_ref, other_ref, rows, scales_ref, master_ref, moment_ref, second_ref)
    update_rows(blocks, operands, scaled, total, update, finished)
    for copy in copies:
        copy.wait()


def combine_kernel(
    far, group, cap, ids_ref, slots_ref, own_ref, other_ref, own_far_ref, other_far_ref, out_ref
):
    tokens = ids_ref.shape[1]
    me = ep_index()
    lane = lax.broadcasted_iota(jnp.int32, own_ref.shape, 1)
    row = lax.broadcasted_iota(jnp.int32, own_ref.shape, 0)
    lines = jnp.where(lane < cap, own_ref[...], other_ref[...])
    last = jnp.where(lane < cap, own_far_ref[...], other_far_ref[...])
    last = jnp.sum(jnp.where(row == me, last, 0.0), axis=0, keepdims=True)
    lines = jnp.where(row == far, last, lines)
    rest = jnp.zeros((LANES - lines.shape[0], LANES), F32)
    columns = jnp.concatenate([lines, rest], axis=0).T
    columns = columns[:cap] + columns[cap : 2 * cap]
    place = lax.broadcasted_iota(jnp.int32, (cap, tokens), 0).astype(F32)
    ids = ids_ref[...]
    result = jnp.zeros(ids.shape, F32)
    for k in range(group):
        at_slot = jnp.where(place == slots_ref[k : k + 1, :], columns[:, k : k + 1], 0.0)
        result = jnp.where(ids == (me ^ k), jnp.sum(at_slot, axis=0, keepdims=True), result)
    out_ref[...] = result


def moved(array, side, step):
    if (side, step) == (0, 0):
        return array
    group = lax.axis_size("ep")
    pairs = [
        (p * group + e, (p ^ side) * group + (e ^ step)) for p in range(2) for e in range(group)
    ]
    return lax.ppermute(array, ("pair", "ep"), pairs)


def local(grad_out, router_weights, expert_ids, hidden, master, moment, second):
    group = lax.axis_size("ep")
    tokens, width = grad_out.shape[1:]
    top = expert_ids.shape[2]
    hid, slots = hidden.shape[2:]
    half = master.shape[3]
    cap = slots // group
    ids = expert_ids[0].T
    own_hidden = hidden[0, 0]
    param = master[0, 0]
    other_hidden = moved(own_hidden, 1, 0)

    far = group // 2
    first = [k for k in range(1, group) if k != far]
    late = [0, far]
    first_items = [(side, k) for side in range(2) for k in reversed(first)]
    last_items = [(0, far), (1, far), (1, 0), (0, 0)]
    order = first_items + last_items
    chunk = jax.ShapeDtypeStruct((half // LANES * cap + TILE, LANES), BF16)
    grads = pltpu.with_memory_space_constraint(grad_out[0], pltpu.HBM)
    held = pltpu.VMEM((2, tokens, half), BF16)
    routed = pl.pallas_call(
        functools.partial(route_kernel, first_items, first, group, cap),
        out_shape=[
            jax.ShapeDtypeStruct((group + -group % TILE, tokens), F32),
            jax.ShapeDtypeStruct((group, TILE, LANES), BF16),
        ]
        + [chunk] * len(first_items),
        in_specs=specs(pltpu.HBM, 3),
        out_specs=specs(pltpu.VMEM, 2 + len(first_items)),
        scratch_shapes=[
            pltpu.VMEM((top, tokens), jnp.int32),
            pltpu.VMEM((top, tokens), BF16),
            held,
            pltpu.SemaphoreType.DMA((4,)),
        ],
        compiler_params=params(),
        cost_estimate=cost(2 * slots * tokens * width, 2 * (tokens + slots) * width),
        name="route",
    )(
        pltpu.with_memory_space_constraint(ids, pltpu.HBM),
        pltpu.with_memory_space_constraint(router_weights[0].T, pltpu.HBM),
        grads,
    )
    slot_of, tiles = routed[:2]
    arrived = {item: moved(sent, *item) for item, sent in zip(first_items, routed[2:])}

    routed = pl.pallas_call(
        functools.partial(later_kernel, last_items, late, cap),
        out_shape=[jax.ShapeDtypeStruct((2 * slots, half), F32)] + [chunk] * len(last_items),
        in_specs=specs(pltpu.VMEM, 2)
        + specs(pltpu.HBM, 1)
        + specs(pltpu.VMEM, 2)
        + specs(pltpu.HBM, 1),
        out_specs=specs(pltpu.VMEM, 1 + len(last_items)),
        scratch_shapes=[
            held,
            pltpu.VMEM((hid, half), F32),
            pltpu.SemaphoreType.DMA((2 + half // min(half, 4 * LANES),)),
        ],
        compiler_params=params(),
        cost_estimate=cost(
            2 * slots * tokens * width + 4 * slots * hid * half, 2 * (tokens + slots) * width
        ),
        name="later",
    )(
        slot_of,
        tiles,
        grads,
        own_hidden,
        other_hidden,
        pltpu.with_memory_space_constraint(param, pltpu.HBM),
    )
    inner = routed[0]
    arrived |= {item: moved(sent, *item) for item, sent in zip(last_items, routed[1:])}

    tile = jax.ShapeDtypeStruct((group + -group % 8, LANES), F32)

    def scored(items, *after):
        return pl.pallas_call(
            functools.partial(score_kernel, items, group, cap),
            out_shape=tile,
            in_specs=specs(pltpu.VMEM, 1 + len(items)) + specs(pl.ANY, len(after)),
            out_specs=specs(pltpu.VMEM, 1)[0],
            compiler_params=params(),
            cost_estimate=cost(2 * len(items) * cap * half, 6 * len(items) * cap * half),
            name="score",
        )(inner, *[arrived[item] for item in items], *after)

    first_scores = scored(first_items)
    returned = [moved(first_scores, 0, k) for k in first]
    far_scores = [scored([(0, far)], first_scores)]
    own_scores = pl.pallas_call(
        functools.partial(merge_kernel, first + [0]),
        out_shape=tile,
        in_specs=specs(pltpu.VMEM, group - 1) + specs(pl.ANY, 1),
        out_specs=specs(pltpu.VMEM, 1)[0],
        compiler_params=params(),
        name="merge",
    )(*returned, scored([(0, 0), (1, 0)]), far_scores[0])
    other_scores = moved(own_scores, 1, 0)
    far_scores.append(scored([(1, far)], own_scores))
    last_scores = far_scores[1]
    far_scores = [moved(scores, side, far) for side, scores in enumerate(far_scores)]

    block = min(hid, 2 * LANES)
    update = pl.pallas_call(
        functools.partial(update_kernel, order, group, cap),
        out_shape=jax.ShapeDtypeStruct((hid, half), F32),
        in_specs=specs(pltpu.VMEM, 5 + len(order)) + specs(pl.ANY, 1),
        out_specs=specs(pltpu.HBM, 1)[0],
        scratch_shapes=[
            pltpu.VMEM((2 * slots, half), BF16),
            pltpu.VMEM((2, TILE, LANES), F32),
            pltpu.VMEM((2, block, 2 * slots), BF16),
            pltpu.VMEM((2, block, half), F32),
            pltpu.VMEM((hid, half), F32),
            pltpu.SemaphoreType.DMA((hid // block,)),
        ],
        compiler_params=params(),
        cost_estimate=cost(4 * slots * hid * half, 12 * hid * half),
        name="update",
    )(
        own_hidden,
        other_hidden,
        param,
        moment[0, 0],
        second[0, 0],
        *[arrived[item] for item in order],
        last_scores,
    )
    router = pl.pallas_call(
        functools.partial(combine_kernel, far, group, cap),
        out_shape=jax.ShapeDtypeStruct((top, tokens), F32),
        in_specs=specs(pltpu.VMEM, 6),
        out_specs=specs(pltpu.VMEM, 1)[0],
        compiler_params=params(),
        cost_estimate=cost(4 * slots * tokens, 8 * top * tokens),
        name="combine",
    )(ids, slot_of, own_scores, other_scores, *far_scores)
    return (update[None, None], router.T[None])


def solution(mesh):
    sections, group = mesh.devices.shape
    split = jax.sharding.Mesh(
        mesh.devices.reshape(2, sections // 2, group), ("pair", "rest", "ep")
    )
    section = ("pair", "rest")
    rows = P(section, "ep", None)
    blocks = P(section, "ep", None, None)
    return jax.shard_map(
        local,
        mesh=split,
        in_specs=(rows, rows, rows, blocks, blocks, blocks, blocks),
        out_specs=(blocks, rows),
        check_vma=False,
    )
```

```python
import functools

import jax
import jax.numpy as jnp
from jax import lax
from jax.experimental import pallas as pl
from jax.experimental.pallas import tpu as pltpu
from jax.sharding import PartitionSpec as P

beta_first = 0.9
beta_second = 0.95
adam_eps = 1e-08
decay_rate = 0.1
first_fix = 1.0 - 0.9**10
second_fix = 1.0 - 0.95**10
first_unit = (1.0 - beta_first) / first_fix
second_unit = (1.0 - beta_second) / second_fix

LANES = 128
TILE = 16
VMEM_BYTES = 32 * 1024 * 1024
F32 = jnp.float32
BF16 = jnp.bfloat16


def params():
    return pltpu.CompilerParams(vmem_limit_bytes=VMEM_BYTES)


def cost(flops, touched):
    return pl.CostEstimate(flops=int(flops), bytes_accessed=int(touched), transcendentals=0)


def specs(space, count):
    return [pl.BlockSpec(memory_space=space) for _ in range(count)]


def ep_index():
    return lax.axis_index("ep").astype(jnp.int32)


def own_half():
    return lax.axis_index("pair").astype(jnp.int32)


def start_grads(grads_hbm, held, sems):
    half = held.shape[2]
    mine = own_half()
    copies = []
    for side in range(2):
        column = pl.multiple_of((1 - mine if side else mine) * half, half)
        copies.append(
            pltpu.make_async_copy(
                grads_hbm.at[:, pl.ds(column, half)], held.at[side], sems.at[side]
            )
        )
        copies[-1].start()
    return copies


def pick_rows(slots, k, cap):
    place = lax.broadcasted_iota(jnp.int32, (cap, slots.shape[1]), 0).astype(F32)
    return jnp.where(place == slots[k : k + 1, :], 1.0, 0.0).astype(BF16)


def fill_chunks(steps, cap, picks, held, copies, tiles, chunks):
    half = held.shape[2]
    data_rows = half // LANES * cap
    step = min(half, 2 * LANES)
    pick = jnp.concatenate([picks[k] for k in steps], axis=0)
    for side in range(2):
        for k in steps:
            chunks[side, k][data_rows:, :] = tiles[k]
        copies[side].wait()
        for column in range(0, half, step):
            block = jnp.dot(
                pick, held[side, :, column : column + step], preferred_element_type=F32
            ).astype(BF16)
            for at, k in enumerate(steps):
                for part in range(step // LANES):
                    top = (column // LANES + part) * cap
                    chunks[side, k][top : top + cap, :] = block[
                        at * cap : (at + 1) * cap, part * LANES : (part + 1) * LANES
                    ]


def route_kernel(
    items, steps, group, cap, ids_hbm, weight_hbm, grads_hbm, slots_ref, tiles_ref, *rest
):
    chunks = dict(zip(items, rest))
    ids_ref, weight_ref, held, sems = rest[len(items) :]
    tokens = held.shape[1]
    me = ep_index()
    small = [
        pltpu.make_async_copy(ids_hbm, ids_ref, sems.at[2]),
        pltpu.make_async_copy(weight_hbm, weight_ref, sems.at[3]),
    ]
    for copy in small:
        copy.start()
    copies = start_grads(grads_hbm, held, sems)
    earlier = lax.broadcasted_iota(jnp.int32, (tokens, tokens), 0)
    later = lax.broadcasted_iota(jnp.int32, (tokens, tokens), 1)
    ahead = jnp.where(earlier < later, 1.0, 0.0).astype(BF16)
    for copy in small:
        copy.wait()
    ids = ids_ref[...]
    weights = weight_ref[...].astype(F32)
    members, scales = [], []
    for k in range(group):
        named = ids == (me ^ k)
        members.append(jnp.sum(jnp.where(named, 1.0, 0.0), axis=0, keepdims=True))
        scales.append(jnp.sum(jnp.where(named, weights, 0.0), axis=0, keepdims=True))
    if group % TILE:
        members.append(jnp.zeros((-group % TILE, tokens), F32))
    member = jnp.concatenate(members, axis=0)
    before = jnp.dot(member.astype(BF16), ahead, preferred_element_type=F32)
    slots = jnp.where(member > 0.5, before, -1.0)
    slots_ref[...] = slots
    picks = [pick_rows(slots, k, cap) for k in range(group)]
    base = me * cap
    tile_row = lax.broadcasted_iota(jnp.int32, (TILE, LANES), 0)
    tile_lane = lax.broadcasted_iota(jnp.int32, (TILE, LANES), 1)
    spot = tile_row * LANES + tile_lane
    kept = (spot >= base) & (spot < base + cap)
    if group % TILE:
        scales.append(jnp.zeros((-group % TILE, tokens), F32))
    rows = jnp.concatenate(scales, axis=0)
    lines = lax.dot_general(
        rows.astype(BF16),
        jnp.concatenate(picks, axis=0),
        (((1,), (1,)), ((), ())),
        preferred_element_type=F32,
    )
    tiles = []
    for k in range(group):
        line = lines[k : k + 1, k * cap : (k + 1) * cap]
        line = jnp.concatenate([line] * (LANES // cap), axis=1)
        tiles.append(jnp.where(kept, line, 0.0).astype(BF16))
        tiles_ref[k] = tiles[k]
    fill_chunks(steps, cap, picks, held, copies, tiles, chunks)


def later_kernel(
    items, steps, cap, slots_ref, tiles_ref, grads_hbm, own_ref, other_ref, master_hbm, inner_ref, *rest
):
    chunks = dict(zip(items, rest))
    held, master_ref, sems = rest[len(items) :]
    copies = start_grads(grads_hbm, held, sems)
    half = master_ref.shape[1]
    step = min(half, 4 * LANES)
    parts = [slice(column, column + step) for column in range(0, half, step)]
    loads = [
        pltpu.make_async_copy(master_hbm.at[:, part], master_ref.at[:, part], sems.at[2 + at])
        for at, part in enumerate(parts)
    ]
    for load in loads:
        load.start()
    slots = slots_ref[...]
    picks = {k: pick_rows(slots, k, cap) for k in steps}
    fill_chunks(steps, cap, picks, held, copies, tiles_ref, chunks)
    slot_count = own_ref.shape[1]
    for load, part in zip(loads, parts):
        load.wait()
        weights = master_ref[:, part].astype(BF16)
        for at, ref in ((0, own_ref), (slot_count, other_ref)):
            inner_ref[at : at + slot_count, part] = lax.dot_general(
                ref[...], weights, (((0,), (0,)), ((), ())), preferred_element_type=F32
            )


def score_kernel(items, group, cap, inner_ref, *rest):
    chunks, score_ref = dict(zip(items, rest)), rest[-1]
    blocks = inner_ref.shape[1] // LANES
    me = ep_index()
    line_of = lax.broadcasted_iota(jnp.int32, score_ref.shape, 0)
    scores = jnp.zeros(score_ref.shape, F32)
    for k in sorted({k for _, k in items}):
        sums = []
        for side in range(2):
            total = jnp.zeros((cap, LANES), F32)
            if (side, k) in items:
                start = pl.multiple_of(side * group * cap + (me ^ k) * cap, cap)
                for block in range(blocks):
                    rows = chunks[side, k][block * cap : (block + 1) * cap, :].astype(F32)
                    total += rows * inner_ref[
                        pl.ds(start, cap), block * LANES : (block + 1) * LANES
                    ]
            sums.append(total)
        both = jnp.concatenate(sums, axis=0)
        line = jnp.sum(both.T, axis=0, keepdims=True)
        scores = jnp.where(line_of == (me ^ k), line, scores)
    score_ref[...] = scores


def scale_into(scaled, at, hidden, line):
    for top in range(0, hidden.shape[0], LANES):
        lines = slice(top, top + LANES)
        scaled[lines, at : at + LANES] = (hidden[lines, :].astype(F32) * line).astype(BF16)


def sum_kernel(items, group, cap, own_ref, other_ref, *rest):
    chunks = dict(zip(items, rest))
    grad_ref, rows, scaled = rest[-3:]
    blocks = rows.shape[1] // LANES
    slots = group * cap
    me = ep_index()
    for side, hidden in enumerate((own_ref, other_ref)):
        tile = jnp.zeros((TILE, LANES), F32)
        for k in range(group):
            start = pl.multiple_of(side * slots + (me ^ k) * cap, cap)
            if (side, k) not in items:
                rows[pl.ds(start, cap), :] = jnp.zeros((cap, rows.shape[1]), BF16)
                continue
            chunk = chunks[side, k]
            tile += chunk[blocks * cap :, :].astype(F32)
            for block in range(blocks):
                rows[pl.ds(start, cap), block * LANES : (block + 1) * LANES] = chunk[
                    block * cap : (block + 1) * cap, :
                ]
        for part in range(slots // LANES):
            lanes = slice(part * LANES, (part + 1) * LANES)
            scale_into(scaled, side * slots + part * LANES, hidden.at[:, lanes], tile[part : part + 1, :])
    grad_ref[...] = jnp.dot(scaled[...], rows[...], preferred_element_type=F32)


def merge_kernel(steps, *rest):
    refs, out_ref = rest[: len(steps)], rest[-1]
    row = lax.broadcasted_iota(jnp.int32, out_ref.shape, 0)
    me = ep_index()
    table = jnp.zeros(out_ref.shape, F32)
    for k, ref in zip(steps, refs):
        line = jnp.sum(jnp.where(row == me, ref[...], 0.0), axis=0, keepdims=True)
        table = jnp.where(row == k, line, table)
    out_ref[...] = table


def update_kernel(items, cap, own_ref, other_ref, grad_ref, master_ref, moment_ref, second_ref, *rest):
    chunks = dict(zip(items, rest))
    _, update_hbm, rows, scaled, total, update, sems = rest[len(items) :]
    hid, half = update.shape
    block = total.shape[1]
    width = min(half, 4 * LANES)
    height = block // 2
    data_rows = half // LANES * cap
    rows[...] = jnp.zeros(rows.shape, BF16)
    for at, ((side, k), chunk) in enumerate(chunks.items()):
        slot = (ep_index() ^ k) * cap
        lanes = pl.ds(pl.multiple_of(slot // LANES * LANES, LANES), LANES)
        start = pl.multiple_of(at * LANES + slot % LANES, cap)
        for part in range(half // LANES):
            rows[pl.ds(start, cap), part * LANES : (part + 1) * LANES] = chunk[
                part * cap : (part + 1) * cap, :
            ]
        line = jnp.sum(chunk[data_rows:, :].astype(F32), axis=0, keepdims=True)
        scale_into(scaled, at * LANES, (own_ref, other_ref)[side].at[:, lanes], line)

    def multiply(at):
        total[at % 2] = jnp.dot(
            scaled[at * block : (at + 1) * block, :], rows[...], preferred_element_type=F32
        )

    def moments(at, top, columns):
        lines = slice(at * block + top, at * block + top + TILE)
        grad = total[at % 2, top : top + TILE, columns] + grad_ref[lines, columns]
        first = moment_ref[lines, columns].astype(F32) * (beta_first / (1.0 - beta_first)) + grad
        square = (
            second_ref[lines, columns].astype(F32) * (beta_second / (1.0 - beta_second))
            + grad * grad
        )
        return first, square, lax.rsqrt(square)

    def inverse(first, square, root):
        scale = square * root * (second_unit**0.5 / first_unit) + adam_eps / first_unit
        return first, pl.reciprocal(scale, approx=True)

    def finish(at, top, columns, first, scale):
        lines = slice(at * block + top, at * block + top + TILE)
        update[lines, columns] = first * scale + decay_rate * master_ref[lines, columns]

    copies = []
    multiply(0)
    for at in range(hid // block):
        if at + 1 < hid // block:
            multiply(at + 1)
        pieces = [
            (top, slice(column, column + width))
            for top in range(0, block, TILE)
            for column in range(0, half, width)
        ]
        held = {}
        for turn in range(len(pieces) + 2):
            if turn < len(pieces):
                held[turn, 0] = moments(at, *pieces[turn])
            if 0 <= turn - 1 < len(pieces):
                held[turn - 1, 1] = inverse(*held.pop((turn - 1, 0)))
            if turn >= 2:
                finish(at, *pieces[turn - 2], *held.pop((turn - 2, 1)))
                top, columns = pieces[turn - 2]
                if (top + TILE) % height == 0 and columns.stop == half:
                    lines = slice(at * block + top + TILE - height, at * block + top + TILE)
                    copies.append(
                        pltpu.make_async_copy(
                            update.at[lines, :], update_hbm.at[lines, :], sems.at[len(copies)]
                        )
                    )
                    copies[-1].start()
    for copy in copies:
        copy.wait()


def combine_kernel(
    far, group, cap, ids_ref, slots_ref, own_ref, other_ref, own_far_ref, other_far_ref, out_ref
):
    tokens = ids_ref.shape[1]
    me = ep_index()
    lane = lax.broadcasted_iota(jnp.int32, own_ref.shape, 1)
    row = lax.broadcasted_iota(jnp.int32, own_ref.shape, 0)
    lines = jnp.where(lane < cap, own_ref[...], other_ref[...])
    last = jnp.where(lane < cap, own_far_ref[...], other_far_ref[...])
    last = jnp.sum(jnp.where(row == me, last, 0.0), axis=0, keepdims=True)
    lines = jnp.where(row == far, last, lines)
    rest = jnp.zeros((LANES - lines.shape[0], LANES), F32)
    columns = jnp.concatenate([lines, rest], axis=0).T
    columns = columns[:cap] + columns[cap : 2 * cap]
    place = lax.broadcasted_iota(jnp.int32, (cap, tokens), 0).astype(F32)
    ids = ids_ref[...]
    result = jnp.zeros(ids.shape, F32)
    for k in range(group):
        at_slot = jnp.where(place == slots_ref[k : k + 1, :], columns[:, k : k + 1], 0.0)
        result = jnp.where(ids == (me ^ k), jnp.sum(at_slot, axis=0, keepdims=True), result)
    out_ref[...] = result


def moved(array, side, step):
    if (side, step) == (0, 0):
        return array
    group = lax.axis_size("ep")
    pairs = [
        (p * group + e, (p ^ side) * group + (e ^ step)) for p in range(2) for e in range(group)
    ]
    return lax.ppermute(array, ("pair", "ep"), pairs)


def local(grad_out, router_weights, expert_ids, hidden, master, moment, second):
    group = lax.axis_size("ep")
    tokens, width = grad_out.shape[1:]
    top = expert_ids.shape[2]
    hid, slots = hidden.shape[2:]
    half = master.shape[3]
    cap = slots // group
    ids = expert_ids[0].T
    own_hidden = hidden[0, 0]
    param = master[0, 0]
    other_hidden = moved(own_hidden, 1, 0)

    far = group // 2
    first = [k for k in range(1, group) if k != far]
    late = [0, far]
    first_items = [(side, k) for side in range(2) for k in reversed(first)]
    last_items = [(0, far), (1, far), (1, 0), (0, 0)]
    order = first_items + last_items
    chunk = jax.ShapeDtypeStruct((half // LANES * cap + TILE, LANES), BF16)
    grads = pltpu.with_memory_space_constraint(grad_out[0], pltpu.HBM)
    held = pltpu.VMEM((2, tokens, half), BF16)
    routed = pl.pallas_call(
        functools.partial(route_kernel, first_items, first, group, cap),
        out_shape=[
            jax.ShapeDtypeStruct((group + -group % TILE, tokens), F32),
            jax.ShapeDtypeStruct((group, TILE, LANES), BF16),
        ]
        + [chunk] * len(first_items),
        in_specs=specs(pltpu.HBM, 3),
        out_specs=specs(pltpu.VMEM, 2 + len(first_items)),
        scratch_shapes=[
            pltpu.VMEM((top, tokens), jnp.int32),
            pltpu.VMEM((top, tokens), BF16),
            held,
            pltpu.SemaphoreType.DMA((4,)),
        ],
        compiler_params=params(),
        cost_estimate=cost(2 * slots * tokens * width, 2 * (tokens + slots) * width),
        name="route",
    )(
        pltpu.with_memory_space_constraint(ids, pltpu.HBM),
        pltpu.with_memory_space_constraint(router_weights[0].T, pltpu.HBM),
        grads,
    )
    slot_of, tiles = routed[:2]
    arrived = {item: moved(sent, *item) for item, sent in zip(first_items, routed[2:])}

    routed = pl.pallas_call(
        functools.partial(later_kernel, last_items, late, cap),
        out_shape=[jax.ShapeDtypeStruct((2 * slots, half), F32)] + [chunk] * len(last_items),
        in_specs=specs(pltpu.VMEM, 2)
        + specs(pltpu.HBM, 1)
        + specs(pltpu.VMEM, 2)
        + specs(pltpu.HBM, 1),
        out_specs=specs(pltpu.VMEM, 1 + len(last_items)),
        scratch_shapes=[
            held,
            pltpu.VMEM((hid, half), F32),
            pltpu.SemaphoreType.DMA((2 + half // min(half, 4 * LANES),)),
        ],
        compiler_params=params(),
        cost_estimate=cost(
            2 * slots * tokens * width + 4 * slots * hid * half, 2 * (tokens + slots) * width
        ),
        name="later",
    )(
        slot_of,
        tiles,
        grads,
        own_hidden,
        other_hidden,
        pltpu.with_memory_space_constraint(param, pltpu.HBM),
    )
    inner = routed[0]
    arrived |= {item: moved(sent, *item) for item, sent in zip(last_items, routed[1:])}

    tile = jax.ShapeDtypeStruct((group + -group % 8, LANES), F32)

    def scored(items, *after):
        return pl.pallas_call(
            functools.partial(score_kernel, items, group, cap),
            out_shape=tile,
            in_specs=specs(pltpu.VMEM, 1 + len(items)) + specs(pl.ANY, len(after)),
            out_specs=specs(pltpu.VMEM, 1)[0],
            compiler_params=params(),
            cost_estimate=cost(2 * len(items) * cap * half, 6 * len(items) * cap * half),
            name="score",
        )(inner, *[arrived[item] for item in items], *after)

    first_scores = scored(first_items)
    returned = [moved(first_scores, 0, k) for k in reversed(first)]
    added = [(0, far), (1, far), (1, 0)]
    summed = [item for item in order if item not in added]
    grad = pl.pallas_call(
        functools.partial(sum_kernel, summed, group, cap),
        out_shape=jax.ShapeDtypeStruct((hid, half), F32),
        in_specs=specs(pltpu.VMEM, 2 + len(summed)) + specs(pl.ANY, 1),
        out_specs=specs(pltpu.VMEM, 1)[0],
        scratch_shapes=[
            pltpu.VMEM((2 * slots, half), BF16),
            pltpu.VMEM((hid, 2 * slots), BF16),
        ],
        compiler_params=params(),
        cost_estimate=cost(4 * slots * hid * half, 4 * hid * half),
        name="sum",
    )(own_hidden, other_hidden, *[arrived[item] for item in summed], first_scores)
    far_scores = [scored([(0, far)], grad)]
    own_scores = pl.pallas_call(
        functools.partial(merge_kernel, first[::-1] + [0]),
        out_shape=tile,
        in_specs=specs(pltpu.VMEM, group - 1) + specs(pl.ANY, 1),
        out_specs=specs(pltpu.VMEM, 1)[0],
        compiler_params=params(),
        name="merge",
    )(*returned, scored([(0, 0), (1, 0)]), far_scores[0])
    other_scores = moved(own_scores, 1, 0)
    far_scores.append(scored([(1, far)], own_scores))
    last_scores = far_scores[1]
    far_scores = [moved(scores, side, far) for side, scores in enumerate(far_scores)]

    block = min(hid, 2 * LANES)
    update = pl.pallas_call(
        functools.partial(update_kernel, added, cap),
        out_shape=jax.ShapeDtypeStruct((hid, half), F32),
        in_specs=specs(pltpu.VMEM, 6 + len(added)) + specs(pl.ANY, 1),
        out_specs=specs(pltpu.HBM, 1)[0],
        scratch_shapes=[
            pltpu.VMEM((len(added) * LANES, half), BF16),
            pltpu.VMEM((hid, len(added) * LANES), BF16),
            pltpu.VMEM((2, block, half), F32),
            pltpu.VMEM((hid, half), F32),
            pltpu.SemaphoreType.DMA((2 * hid // block,)),
        ],
        compiler_params=params(),
        cost_estimate=cost(6 * LANES * hid * half, 16 * hid * half),
        name="update",
    )(
        own_hidden,
        other_hidden,
        grad,
        param,
        moment[0, 0],
        second[0, 0],
        *[arrived[item] for item in added],
        last_scores,
    )
    router = pl.pallas_call(
        functools.partial(combine_kernel, far, group, cap),
        out_shape=jax.ShapeDtypeStruct((top, tokens), F32),
        in_specs=specs(pltpu.VMEM, 6),
        out_specs=specs(pltpu.VMEM, 1)[0],
        compiler_params=params(),
        cost_estimate=cost(4 * slots * tokens, 8 * top * tokens),
        name="combine",
    )(ids, slot_of, own_scores, other_scores, *far_scores)
    return (update[None, None], router.T[None])


def solution(mesh):
    sections, group = mesh.devices.shape
    split = jax.sharding.Mesh(
        mesh.devices.reshape(2, sections // 2, group), ("pair", "rest", "ep")
    )
    section = ("pair", "rest")
    rows = P(section, "ep", None)
    blocks = P(section, "ep", None, None)
    return jax.shard_map(
        local,
        mesh=split,
        in_specs=(rows, rows, rows, blocks, blocks, blocks, blocks),
        out_specs=(blocks, rows),
        check_vma=False,
    )
```

```python
import functools

import jax
import jax.numpy as jnp
from jax import lax
from jax.experimental import pallas as pl
from jax.experimental.pallas import tpu as pltpu
from jax.sharding import PartitionSpec as P

beta_first = 0.9
beta_second = 0.95
adam_eps = 1e-08
decay_rate = 0.1
first_fix = 1.0 - 0.9**10
second_fix = 1.0 - 0.95**10
first_unit = (1.0 - beta_first) / first_fix
second_unit = (1.0 - beta_second) / second_fix

LANES = 128
TILE = 16
VMEM_BYTES = 32 * 1024 * 1024
F32 = jnp.float32
BF16 = jnp.bfloat16


def params():
    return pltpu.CompilerParams(vmem_limit_bytes=VMEM_BYTES)


def cost(flops, touched):
    return pl.CostEstimate(flops=int(flops), bytes_accessed=int(touched), transcendentals=0)


def specs(space, count):
    return [pl.BlockSpec(memory_space=space) for _ in range(count)]


def ep_index():
    return lax.axis_index("ep").astype(jnp.int32)


def own_half():
    return lax.axis_index("pair").astype(jnp.int32)


def start_grads(grads_hbm, held, sems):
    half = held.shape[2]
    mine = own_half()
    copies = []
    for side in range(2):
        column = pl.multiple_of((1 - mine if side else mine) * half, half)
        copies.append(
            pltpu.make_async_copy(
                grads_hbm.at[:, pl.ds(column, half)], held.at[side], sems.at[side]
            )
        )
        copies[-1].start()
    return copies


def pick_rows(slots, k, cap):
    place = lax.broadcasted_iota(jnp.int32, (cap, slots.shape[1]), 0).astype(F32)
    return jnp.where(place == slots[k : k + 1, :], 1.0, 0.0).astype(BF16)


def fill_chunks(steps, cap, picks, held, copies, tiles, chunks):
    half = held.shape[2]
    data_rows = half // LANES * cap
    step = min(half, 2 * LANES)
    pick = jnp.concatenate([picks[k] for k in steps], axis=0)
    for side in range(2):
        for k in steps:
            chunks[side, k][data_rows:, :] = tiles[k]
        copies[side].wait()
        for column in range(0, half, step):
            block = jnp.dot(
                pick, held[side, :, column : column + step], preferred_element_type=F32
            ).astype(BF16)
            for at, k in enumerate(steps):
                for part in range(step // LANES):
                    top = (column // LANES + part) * cap
                    chunks[side, k][top : top + cap, :] = block[
                        at * cap : (at + 1) * cap, part * LANES : (part + 1) * LANES
                    ]


def route_kernel(
    items, steps, group, cap, ids_hbm, weight_hbm, grads_hbm, slots_ref, tiles_ref, *rest
):
    chunks = dict(zip(items, rest))
    ids_ref, weight_ref, held, sems = rest[len(items) :]
    tokens = held.shape[1]
    me = ep_index()
    small = [
        pltpu.make_async_copy(ids_hbm, ids_ref, sems.at[2]),
        pltpu.make_async_copy(weight_hbm, weight_ref, sems.at[3]),
    ]
    for copy in small:
        copy.start()
    copies = start_grads(grads_hbm, held, sems)
    earlier = lax.broadcasted_iota(jnp.int32, (tokens, tokens), 0)
    later = lax.broadcasted_iota(jnp.int32, (tokens, tokens), 1)
    ahead = jnp.where(earlier < later, 1.0, 0.0).astype(BF16)
    for copy in small:
        copy.wait()
    ids = ids_ref[...]
    weights = weight_ref[...].astype(F32)
    members, scales = [], []
    for k in range(group):
        named = ids == (me ^ k)
        members.append(jnp.sum(jnp.where(named, 1.0, 0.0), axis=0, keepdims=True))
        scales.append(jnp.sum(jnp.where(named, weights, 0.0), axis=0, keepdims=True))
    if group % TILE:
        members.append(jnp.zeros((-group % TILE, tokens), F32))
    member = jnp.concatenate(members, axis=0)
    before = jnp.dot(member.astype(BF16), ahead, preferred_element_type=F32)
    slots = jnp.where(member > 0.5, before, -1.0)
    slots_ref[...] = slots
    picks = [pick_rows(slots, k, cap) for k in range(group)]
    base = me * cap
    tile_row = lax.broadcasted_iota(jnp.int32, (TILE, LANES), 0)
    tile_lane = lax.broadcasted_iota(jnp.int32, (TILE, LANES), 1)
    spot = tile_row * LANES + tile_lane
    kept = (spot >= base) & (spot < base + cap)
    if group % TILE:
        scales.append(jnp.zeros((-group % TILE, tokens), F32))
    rows = jnp.concatenate(scales, axis=0)
    lines = lax.dot_general(
        rows.astype(BF16),
        jnp.concatenate(picks, axis=0),
        (((1,), (1,)), ((), ())),
        preferred_element_type=F32,
    )
    tiles = []
    for k in range(group):
        line = lines[k : k + 1, k * cap : (k + 1) * cap]
        line = jnp.concatenate([line] * (LANES // cap), axis=1)
        tiles.append(jnp.where(kept, line, 0.0).astype(BF16))
        tiles_ref[k] = tiles[k]
    fill_chunks(steps, cap, picks, held, copies, tiles, chunks)


def later_kernel(
    items, steps, cap, slots_ref, tiles_ref, grads_hbm, own_ref, other_ref, master_hbm, inner_ref, *rest
):
    chunks = dict(zip(items, rest))
    held, master_ref, sems = rest[len(items) :]
    copies = start_grads(grads_hbm, held, sems)
    half = master_ref.shape[1]
    step = min(half, 4 * LANES)
    parts = [slice(column, column + step) for column in range(0, half, step)]
    loads = [
        pltpu.make_async_copy(master_hbm.at[:, part], master_ref.at[:, part], sems.at[2 + at])
        for at, part in enumerate(parts)
    ]
    for load in loads:
        load.start()
    slots = slots_ref[...]
    picks = {k: pick_rows(slots, k, cap) for k in steps}
    fill_chunks(steps, cap, picks, held, copies, tiles_ref, chunks)
    slot_count = own_ref.shape[1]
    for load, part in zip(loads, parts):
        load.wait()
        weights = master_ref[:, part].astype(BF16)
        for at, ref in ((0, own_ref), (slot_count, other_ref)):
            inner_ref[at : at + slot_count, part] = lax.dot_general(
                ref[...], weights, (((0,), (0,)), ((), ())), preferred_element_type=F32
            )


def score_kernel(items, group, cap, inner_ref, *rest):
    chunks, score_ref = dict(zip(items, rest)), rest[-1]
    blocks = inner_ref.shape[1] // LANES
    me = ep_index()
    line_of = lax.broadcasted_iota(jnp.int32, score_ref.shape, 0)
    scores = jnp.zeros(score_ref.shape, F32)
    for k in sorted({k for _, k in items}):
        sums = []
        for side in range(2):
            total = jnp.zeros((cap, LANES), F32)
            if (side, k) in items:
                start = pl.multiple_of(side * group * cap + (me ^ k) * cap, cap)
                for block in range(blocks):
                    rows = chunks[side, k][block * cap : (block + 1) * cap, :].astype(F32)
                    total += rows * inner_ref[
                        pl.ds(start, cap), block * LANES : (block + 1) * LANES
                    ]
            sums.append(total)
        both = jnp.concatenate(sums, axis=0)
        line = jnp.sum(both.T, axis=0, keepdims=True)
        scores = jnp.where(line_of == (me ^ k), line, scores)
    score_ref[...] = scores


def scale_into(scaled, at, hidden, line):
    for top in range(0, hidden.shape[0], LANES):
        lines = slice(top, top + LANES)
        scaled[lines, at : at + LANES] = (hidden[lines, :].astype(F32) * line).astype(BF16)


def sum_kernel(items, group, cap, own_ref, other_ref, *rest):
    chunks = dict(zip(items, rest))
    grad_ref, rows, scaled = rest[-3:]
    blocks = rows.shape[1] // LANES
    slots = group * cap
    me = ep_index()
    for side, hidden in enumerate((own_ref, other_ref)):
        tile = jnp.zeros((TILE, LANES), F32)
        for k in range(group):
            start = pl.multiple_of(side * slots + (me ^ k) * cap, cap)
            if (side, k) not in items:
                rows[pl.ds(start, cap), :] = jnp.zeros((cap, rows.shape[1]), BF16)
                continue
            chunk = chunks[side, k]
            tile += chunk[blocks * cap :, :].astype(F32)
            for block in range(blocks):
                rows[pl.ds(start, cap), block * LANES : (block + 1) * LANES] = chunk[
                    block * cap : (block + 1) * cap, :
                ]
        for part in range(slots // LANES):
            lanes = slice(part * LANES, (part + 1) * LANES)
            scale_into(scaled, side * slots + part * LANES, hidden.at[:, lanes], tile[part : part + 1, :])
    grad_ref[...] = jnp.dot(scaled[...], rows[...], preferred_element_type=F32)


def merge_kernel(cap, own_ref, other_ref, _, out_ref):
    lane = lax.broadcasted_iota(jnp.int32, own_ref.shape, 1)
    scores = own_ref[...] + pltpu.roll(other_ref[...], LANES - cap, axis=1)
    out_ref[...] = jnp.where(lane < cap, scores, 0.0)


def update_kernel(items, cap, own_ref, other_ref, grad_ref, master_ref, moment_ref, second_ref, *rest):
    chunks = dict(zip(items, rest))
    _, update_hbm, rows, scaled, total, update, sems = rest[len(items) :]
    hid, half = update.shape
    block = total.shape[1]
    width = min(half, 4 * LANES)
    height = block // 2
    data_rows = half // LANES * cap
    rows[...] = jnp.zeros(rows.shape, BF16)
    for at, ((side, k), chunk) in enumerate(chunks.items()):
        slot = (ep_index() ^ k) * cap
        lanes = pl.ds(pl.multiple_of(slot // LANES * LANES, LANES), LANES)
        start = pl.multiple_of(at * LANES + slot % LANES, cap)
        for part in range(half // LANES):
            rows[pl.ds(start, cap), part * LANES : (part + 1) * LANES] = chunk[
                part * cap : (part + 1) * cap, :
            ]
        line = jnp.sum(chunk[data_rows:, :].astype(F32), axis=0, keepdims=True)
        scale_into(scaled, at * LANES, (own_ref, other_ref)[side].at[:, lanes], line)

    def multiply(at):
        total[at % 2] = jnp.dot(
            scaled[at * block : (at + 1) * block, :], rows[...], preferred_element_type=F32
        )

    def moments(at, top, columns):
        lines = slice(at * block + top, at * block + top + TILE)
        grad = total[at % 2, top : top + TILE, columns] + grad_ref[lines, columns]
        first = moment_ref[lines, columns].astype(F32) * (beta_first / (1.0 - beta_first)) + grad
        square = (
            second_ref[lines, columns].astype(F32) * (beta_second / (1.0 - beta_second))
            + grad * grad
        )
        return first, square, lax.rsqrt(square)

    def inverse(first, square, root):
        scale = square * root * (second_unit**0.5 / first_unit) + adam_eps / first_unit
        return first, pl.reciprocal(scale, approx=True)

    def finish(at, top, columns, first, scale):
        lines = slice(at * block + top, at * block + top + TILE)
        update[lines, columns] = first * scale + decay_rate * master_ref[lines, columns]

    copies = []
    multiply(0)
    for at in range(hid // block):
        if at + 1 < hid // block:
            multiply(at + 1)
        pieces = [
            (top, slice(column, column + width))
            for top in range(0, block, TILE)
            for column in range(0, half, width)
        ]
        held = {}
        for turn in range(len(pieces) + 2):
            if turn < len(pieces):
                held[turn, 0] = moments(at, *pieces[turn])
            if 0 <= turn - 1 < len(pieces):
                held[turn - 1, 1] = inverse(*held.pop((turn - 1, 0)))
            if turn >= 2:
                finish(at, *pieces[turn - 2], *held.pop((turn - 2, 1)))
                top, columns = pieces[turn - 2]
                if (top + TILE) % height == 0 and columns.stop == half:
                    lines = slice(at * block + top + TILE - height, at * block + top + TILE)
                    copies.append(
                        pltpu.make_async_copy(
                            update.at[lines, :], update_hbm.at[lines, :], sems.at[len(copies)]
                        )
                    )
                    copies[-1].start()
    for copy in copies:
        copy.wait()


def combine_kernel(steps, group, cap, ids_ref, slots_ref, *rest):
    refs, out_ref = iter(rest[:-1]), rest[-1]
    tokens = ids_ref.shape[1]
    me = ep_index()
    shape = rest[0].shape
    lane = lax.broadcasted_iota(jnp.int32, shape, 1)
    row = lax.broadcasted_iota(jnp.int32, shape, 0)
    lines = jnp.zeros(shape, F32)
    for k, tiles in steps:
        scores = next(refs)[...]
        if tiles == 2:
            scores = jnp.where(lane < cap, scores, next(refs)[...])
        line = jnp.sum(jnp.where(row == me, scores, 0.0), axis=0, keepdims=True)
        lines = jnp.where(row == k, line, lines)
    rest = jnp.zeros((LANES - lines.shape[0], LANES), F32)
    columns = jnp.concatenate([lines, rest], axis=0).T
    columns = columns[:cap] + columns[cap : 2 * cap]
    place = lax.broadcasted_iota(jnp.int32, (cap, tokens), 0).astype(F32)
    ids = ids_ref[...]
    result = jnp.zeros(ids.shape, F32)
    for k in range(group):
        at_slot = jnp.where(place == slots_ref[k : k + 1, :], columns[:, k : k + 1], 0.0)
        result = jnp.where(ids == (me ^ k), jnp.sum(at_slot, axis=0, keepdims=True), result)
    out_ref[...] = result


def moved(array, side, step):
    if (side, step) == (0, 0):
        return array
    group = lax.axis_size("ep")
    pairs = [
        (p * group + e, (p ^ side) * group + (e ^ step)) for p in range(2) for e in range(group)
    ]
    return lax.ppermute(array, ("pair", "ep"), pairs)


def local(grad_out, router_weights, expert_ids, hidden, master, moment, second):
    group = lax.axis_size("ep")
    tokens, width = grad_out.shape[1:]
    top = expert_ids.shape[2]
    hid, slots = hidden.shape[2:]
    half = master.shape[3]
    cap = slots // group
    ids = expert_ids[0].T
    own_hidden = hidden[0, 0]
    param = master[0, 0]
    other_hidden = moved(own_hidden, 1, 0)

    far = group // 2
    first = [k for k in range(1, group) if k != far]
    late = [0, far]
    first_items = [(side, k) for side in range(2) for k in reversed(first)]
    last_items = [(0, far), (1, far), (1, 0), (0, 0)]
    order = first_items + last_items
    chunk = jax.ShapeDtypeStruct((half // LANES * cap + TILE, LANES), BF16)
    grads = pltpu.with_memory_space_constraint(grad_out[0], pltpu.HBM)
    held = pltpu.VMEM((2, tokens, half), BF16)
    routed = pl.pallas_call(
        functools.partial(route_kernel, first_items, first, group, cap),
        out_shape=[
            jax.ShapeDtypeStruct((group + -group % TILE, tokens), F32),
            jax.ShapeDtypeStruct((group, TILE, LANES), BF16),
        ]
        + [chunk] * len(first_items),
        in_specs=specs(pltpu.HBM, 3),
        out_specs=specs(pltpu.VMEM, 2 + len(first_items)),
        scratch_shapes=[
            pltpu.VMEM((top, tokens), jnp.int32),
            pltpu.VMEM((top, tokens), BF16),
            held,
            pltpu.SemaphoreType.DMA((4,)),
        ],
        compiler_params=params(),
        cost_estimate=cost(2 * slots * tokens * width, 2 * (tokens + slots) * width),
        name="route",
    )(
        pltpu.with_memory_space_constraint(ids, pltpu.HBM),
        pltpu.with_memory_space_constraint(router_weights[0].T, pltpu.HBM),
        grads,
    )
    slot_of, tiles = routed[:2]
    arrived = {item: moved(sent, *item) for item, sent in zip(first_items, routed[2:])}

    routed = pl.pallas_call(
        functools.partial(later_kernel, last_items, late, cap),
        out_shape=[jax.ShapeDtypeStruct((2 * slots, half), F32)] + [chunk] * len(last_items),
        in_specs=specs(pltpu.VMEM, 2)
        + specs(pltpu.HBM, 1)
        + specs(pltpu.VMEM, 2)
        + specs(pltpu.HBM, 1),
        out_specs=specs(pltpu.VMEM, 1 + len(last_items)),
        scratch_shapes=[
            held,
            pltpu.VMEM((hid, half), F32),
            pltpu.SemaphoreType.DMA((2 + half // min(half, 4 * LANES),)),
        ],
        compiler_params=params(),
        cost_estimate=cost(
            2 * slots * tokens * width + 4 * slots * hid * half, 2 * (tokens + slots) * width
        ),
        name="later",
    )(
        slot_of,
        tiles,
        grads,
        own_hidden,
        other_hidden,
        pltpu.with_memory_space_constraint(param, pltpu.HBM),
    )
    inner = routed[0]
    arrived |= {item: moved(sent, *item) for item, sent in zip(last_items, routed[1:])}

    tile = jax.ShapeDtypeStruct((group + -group % 8, LANES), F32)

    def scored(items, *after):
        return pl.pallas_call(
            functools.partial(score_kernel, items, group, cap),
            out_shape=tile,
            in_specs=specs(pltpu.VMEM, 1 + len(items)) + specs(pl.ANY, len(after)),
            out_specs=specs(pltpu.VMEM, 1)[0],
            compiler_params=params(),
            cost_estimate=cost(2 * cap * half, 6 * cap * half),
            name="score",
        )(inner, *[arrived[item] for item in items], *after)

    first_scores = scored(first_items)
    other_scores = moved(first_scores, 1, 0)
    added = [(0, far), (1, far), (1, 0)]
    summed = [item for item in order if item not in added]
    grad = pl.pallas_call(
        functools.partial(sum_kernel, summed, group, cap),
        out_shape=jax.ShapeDtypeStruct((hid, half), F32),
        in_specs=specs(pltpu.VMEM, 2 + len(summed)) + specs(pl.ANY, 1),
        out_specs=specs(pltpu.VMEM, 1)[0],
        scratch_shapes=[
            pltpu.VMEM((2 * slots, half), BF16),
            pltpu.VMEM((hid, 2 * slots), BF16),
        ],
        compiler_params=params(),
        cost_estimate=cost(4 * slots * hid * half, 4 * hid * half),
        name="sum",
    )(own_hidden, other_hidden, *[arrived[item] for item in summed], first_scores)
    merged = pl.pallas_call(
        functools.partial(merge_kernel, cap),
        out_shape=tile,
        in_specs=specs(pltpu.VMEM, 2) + specs(pl.ANY, 1),
        out_specs=specs(pltpu.VMEM, 1)[0],
        compiler_params=params(),
        name="merge",
    )(first_scores, other_scores, grad)
    returned = {k: [moved(merged, 0, k)] for k in first}
    zero_scores = scored([(0, 0), (1, 0)], merged)
    returned[0] = [zero_scores, moved(zero_scores, 1, 0)]
    own_far = scored([(0, far)], merged)
    last_scores = scored([(1, far)], zero_scores, own_far)
    returned[far] = [moved(own_far, 0, far), moved(last_scores, 1, far)]

    block = min(hid, 2 * LANES)
    update = pl.pallas_call(
        functools.partial(update_kernel, added, cap),
        out_shape=jax.ShapeDtypeStruct((hid, half), F32),
        in_specs=specs(pltpu.VMEM, 6 + len(added)) + specs(pl.ANY, 1),
        out_specs=specs(pltpu.HBM, 1)[0],
        scratch_shapes=[
            pltpu.VMEM((len(added) * LANES, half), BF16),
            pltpu.VMEM((hid, len(added) * LANES), BF16),
            pltpu.VMEM((2, block, half), F32),
            pltpu.VMEM((hid, half), F32),
            pltpu.SemaphoreType.DMA((2 * hid // block,)),
        ],
        compiler_params=params(),
        cost_estimate=cost(6 * LANES * hid * half, 16 * hid * half),
        name="update",
    )(
        own_hidden,
        other_hidden,
        grad,
        param,
        moment[0, 0],
        second[0, 0],
        *[arrived[item] for item in added],
        last_scores,
    )
    shares = [array for arrays in returned.values() for array in arrays]
    router = pl.pallas_call(
        functools.partial(
            combine_kernel, [(k, len(arrays)) for k, arrays in returned.items()], group, cap
        ),
        out_shape=jax.ShapeDtypeStruct((top, tokens), F32),
        in_specs=specs(pltpu.VMEM, 2 + len(shares)),
        out_specs=specs(pltpu.VMEM, 1)[0],
        compiler_params=params(),
        cost_estimate=cost(4 * slots * tokens, 8 * top * tokens),
        name="combine",
    )(ids, slot_of, *shares)
    return (update[None, None], router.T[None])


def solution(mesh):
    sections, group = mesh.devices.shape
    split = jax.sharding.Mesh(
        mesh.devices.reshape(2, sections // 2, group), ("pair", "rest", "ep")
    )
    section = ("pair", "rest")
    rows = P(section, "ep", None)
    blocks = P(section, "ep", None, None)
    return jax.shard_map(
        local,
        mesh=split,
        in_specs=(rows, rows, rows, blocks, blocks, blocks, blocks),
        out_specs=(blocks, rows),
        check_vma=False,
    )
```

```python
import functools

import jax
import jax.numpy as jnp
from jax import lax
from jax.experimental import pallas as pl
from jax.experimental.pallas import tpu as pltpu
from jax.sharding import PartitionSpec as P

beta_first = 0.9
beta_second = 0.95
adam_eps = 1e-08
decay_rate = 0.1
first_fix = 1.0 - 0.9**10
second_fix = 1.0 - 0.95**10
first_unit = (1.0 - beta_first) / first_fix
second_unit = (1.0 - beta_second) / second_fix

LANES = 128
TILE = 16
VMEM_BYTES = 32 * 1024 * 1024
F32 = jnp.float32
BF16 = jnp.bfloat16


def params():
    return pltpu.CompilerParams(vmem_limit_bytes=VMEM_BYTES)


def cost(flops, touched):
    return pl.CostEstimate(flops=int(flops), bytes_accessed=int(touched), transcendentals=0)


def specs(space, count):
    return [pl.BlockSpec(memory_space=space) for _ in range(count)]


def ep_index():
    return lax.axis_index("ep").astype(jnp.int32)


def own_half():
    return lax.axis_index("pair").astype(jnp.int32)


def start_grads(grads_hbm, held, sems):
    half = held.shape[2]
    mine = own_half()
    copies = []
    for side in range(2):
        column = pl.multiple_of((1 - mine if side else mine) * half, half)
        copies.append(
            pltpu.make_async_copy(
                grads_hbm.at[:, pl.ds(column, half)], held.at[side], sems.at[side]
            )
        )
        copies[-1].start()
    return copies


def pick_rows(slots, k, cap):
    place = lax.broadcasted_iota(jnp.int32, (cap, slots.shape[1]), 0).astype(F32)
    return jnp.where(place == slots[k : k + 1, :], 1.0, 0.0).astype(BF16)


def fill_chunks(steps, cap, picks, held, copies, tiles, chunks):
    half = held.shape[2]
    data_rows = half // LANES * cap
    step = min(half, 2 * LANES)
    pick = jnp.concatenate([picks[k] for k in steps], axis=0)
    for side in range(2):
        for k in steps:
            chunks[side, k][data_rows:, :] = tiles[k]
        copies[side].wait()
        for column in range(0, half, step):
            block = jnp.dot(
                pick, held[side, :, column : column + step], preferred_element_type=F32
            ).astype(BF16)
            for at, k in enumerate(steps):
                for part in range(step // LANES):
                    top = (column // LANES + part) * cap
                    chunks[side, k][top : top + cap, :] = block[
                        at * cap : (at + 1) * cap, part * LANES : (part + 1) * LANES
                    ]


def route_kernel(
    items, steps, group, cap, ids_hbm, weight_hbm, grads_hbm, slots_ref, tiles_ref, *rest
):
    chunks = dict(zip(items, rest))
    ids_ref, weight_ref, held, sems = rest[len(items) :]
    tokens = held.shape[1]
    me = ep_index()
    small = [
        pltpu.make_async_copy(ids_hbm, ids_ref, sems.at[2]),
        pltpu.make_async_copy(weight_hbm, weight_ref, sems.at[3]),
    ]
    for copy in small:
        copy.start()
    copies = start_grads(grads_hbm, held, sems)
    earlier = lax.broadcasted_iota(jnp.int32, (tokens, tokens), 0)
    later = lax.broadcasted_iota(jnp.int32, (tokens, tokens), 1)
    ahead = jnp.where(earlier < later, 1.0, 0.0).astype(BF16)
    for copy in small:
        copy.wait()
    ids = ids_ref[...]
    weights = weight_ref[...].astype(F32)
    members, scales = [], []
    for k in range(group):
        named = ids == (me ^ k)
        members.append(jnp.sum(jnp.where(named, 1.0, 0.0), axis=0, keepdims=True))
        scales.append(jnp.sum(jnp.where(named, weights, 0.0), axis=0, keepdims=True))
    if group % TILE:
        members.append(jnp.zeros((-group % TILE, tokens), F32))
    member = jnp.concatenate(members, axis=0)
    before = jnp.dot(member.astype(BF16), ahead, preferred_element_type=F32)
    slots = jnp.where(member > 0.5, before, -1.0)
    slots_ref[...] = slots
    picks = [pick_rows(slots, k, cap) for k in range(group)]
    base = me * cap
    tile_row = lax.broadcasted_iota(jnp.int32, (TILE, LANES), 0)
    tile_lane = lax.broadcasted_iota(jnp.int32, (TILE, LANES), 1)
    spot = tile_row * LANES + tile_lane
    kept = (spot >= base) & (spot < base + cap)
    if group % TILE:
        scales.append(jnp.zeros((-group % TILE, tokens), F32))
    rows = jnp.concatenate(scales, axis=0)
    lines = lax.dot_general(
        rows.astype(BF16),
        jnp.concatenate(picks, axis=0),
        (((1,), (1,)), ((), ())),
        preferred_element_type=F32,
    )
    tiles = []
    for k in range(group):
        line = lines[k : k + 1, k * cap : (k + 1) * cap]
        line = jnp.concatenate([line] * (LANES // cap), axis=1)
        tiles.append(jnp.where(kept, line, 0.0).astype(BF16))
        tiles_ref[k] = tiles[k]
    fill_chunks(steps, cap, picks, held, copies, tiles, chunks)


def later_kernel(
    items, steps, cap, slots_ref, tiles_ref, grads_hbm, own_ref, other_ref, master_hbm, inner_ref, *rest
):
    chunks = dict(zip(items, rest))
    held, master_ref, sems = rest[len(items) :]
    copies = start_grads(grads_hbm, held, sems)
    half = master_ref.shape[1]
    step = min(half, 4 * LANES)
    parts = [slice(column, column + step) for column in range(0, half, step)]
    loads = [
        pltpu.make_async_copy(master_hbm.at[:, part], master_ref.at[:, part], sems.at[2 + at])
        for at, part in enumerate(parts)
    ]
    for load in loads:
        load.start()
    slots = slots_ref[...]
    picks = {k: pick_rows(slots, k, cap) for k in steps}
    fill_chunks(steps, cap, picks, held, copies, tiles_ref, chunks)
    slot_count = own_ref.shape[1]
    for load, part in zip(loads, parts):
        load.wait()
        weights = master_ref[:, part].astype(BF16)
        for at, ref in ((0, own_ref), (slot_count, other_ref)):
            inner_ref[at : at + slot_count, part] = lax.dot_general(
                ref[...], weights, (((0,), (0,)), ((), ())), preferred_element_type=F32
            )


def score_kernel(items, group, cap, inner_ref, *rest):
    chunks, score_ref = dict(zip(items, rest)), rest[-1]
    blocks = inner_ref.shape[1] // LANES
    me = ep_index()
    line_of = lax.broadcasted_iota(jnp.int32, score_ref.shape, 0)
    scores = jnp.zeros(score_ref.shape, F32)
    for k in sorted({k for _, k in items}):
        sums = []
        for side in range(2):
            total = jnp.zeros((cap, LANES), F32)
            if (side, k) in items:
                start = pl.multiple_of(side * group * cap + (me ^ k) * cap, cap)
                for block in range(blocks):
                    rows = chunks[side, k][block * cap : (block + 1) * cap, :].astype(F32)
                    total += rows * inner_ref[
                        pl.ds(start, cap), block * LANES : (block + 1) * LANES
                    ]
            sums.append(total)
        both = jnp.concatenate(sums, axis=0)
        line = jnp.sum(both.T, axis=0, keepdims=True)
        scores = jnp.where(line_of == (me ^ k), line, scores)
    score_ref[...] = scores


def scale_into(scaled, at, hidden, line):
    for top in range(0, hidden.shape[0], LANES):
        lines = slice(top, top + LANES)
        scaled[lines, at : at + LANES] = (hidden[lines, :].astype(F32) * line).astype(BF16)


def sum_kernel(items, group, cap, own_ref, other_ref, *rest):
    chunks = dict(zip(items, rest))
    grad_ref, rows, scaled = rest[-3:]
    blocks = rows.shape[1] // LANES
    slots = group * cap
    me = ep_index()
    for side, hidden in enumerate((own_ref, other_ref)):
        tile = jnp.zeros((TILE, LANES), F32)
        for k in range(group):
            start = pl.multiple_of(side * slots + (me ^ k) * cap, cap)
            if (side, k) not in items:
                rows[pl.ds(start, cap), :] = jnp.zeros((cap, rows.shape[1]), BF16)
                continue
            chunk = chunks[side, k]
            tile += chunk[blocks * cap :, :].astype(F32)
            for block in range(blocks):
                rows[pl.ds(start, cap), block * LANES : (block + 1) * LANES] = chunk[
                    block * cap : (block + 1) * cap, :
                ]
        for part in range(slots // LANES):
            lanes = slice(part * LANES, (part + 1) * LANES)
            scale_into(scaled, side * slots + part * LANES, hidden.at[:, lanes], tile[part : part + 1, :])
    grad_ref[...] = jnp.dot(scaled[...], rows[...], preferred_element_type=F32)


def merge_kernel(cap, own_ref, other_ref, _, out_ref):
    lane = lax.broadcasted_iota(jnp.int32, own_ref.shape, 1)
    scores = own_ref[...] + pltpu.roll(other_ref[...], LANES - cap, axis=1)
    out_ref[...] = jnp.where(lane < cap, scores, 0.0)


def update_kernel(items, cap, own_ref, other_ref, grad_ref, master_ref, moment_ref, second_ref, *rest):
    chunks = dict(zip(items, rest))
    _, update_hbm, rows, scaled, total, update, sems = rest[len(items) :]
    hid, half = update.shape
    block = total.shape[1]
    width = min(half, 4 * LANES)
    height = block // 2
    data_rows = half // LANES * cap
    rows[...] = jnp.zeros(rows.shape, BF16)
    for at, ((side, k), chunk) in enumerate(chunks.items()):
        slot = (ep_index() ^ k) * cap
        lanes = pl.ds(pl.multiple_of(slot // LANES * LANES, LANES), LANES)
        start = pl.multiple_of(at * LANES + slot % LANES, cap)
        for part in range(half // LANES):
            rows[pl.ds(start, cap), part * LANES : (part + 1) * LANES] = chunk[
                part * cap : (part + 1) * cap, :
            ]
        line = jnp.sum(chunk[data_rows:, :].astype(F32), axis=0, keepdims=True)
        scale_into(scaled, at * LANES, (own_ref, other_ref)[side].at[:, lanes], line)

    def multiply(at):
        total[at % 2] = jnp.dot(
            scaled[at * block : (at + 1) * block, :], rows[...], preferred_element_type=F32
        )

    def moments(at, top, columns):
        lines = slice(at * block + top, at * block + top + TILE)
        grad = total[at % 2, top : top + TILE, columns] + grad_ref[lines, columns]
        first = moment_ref[lines, columns].astype(F32) * (beta_first / (1.0 - beta_first)) + grad
        square = (
            second_ref[lines, columns].astype(F32) * (beta_second / (1.0 - beta_second))
            + grad * grad
        )
        return first, square, lax.rsqrt(square)

    def inverse(first, square, root):
        scale = square * root * (second_unit**0.5 / first_unit) + adam_eps / first_unit
        return first, pl.reciprocal(scale, approx=True)

    def finish(at, top, columns, first, scale):
        lines = slice(at * block + top, at * block + top + TILE)
        update[lines, columns] = first * scale + decay_rate * master_ref[lines, columns]

    copies = []
    multiply(0)
    for at in range(hid // block):
        if at + 1 < hid // block:
            multiply(at + 1)
        pieces = [
            (top, slice(column, column + width))
            for top in range(0, block, TILE)
            for column in range(0, half, width)
        ]
        held = {}
        for turn in range(len(pieces) + 2):
            if turn < len(pieces):
                held[turn, 0] = moments(at, *pieces[turn])
            if 0 <= turn - 1 < len(pieces):
                held[turn - 1, 1] = inverse(*held.pop((turn - 1, 0)))
            if turn >= 2:
                finish(at, *pieces[turn - 2], *held.pop((turn - 2, 1)))
                top, columns = pieces[turn - 2]
                if (top + TILE) % height == 0 and columns.stop == half:
                    lines = slice(at * block + top + TILE - height, at * block + top + TILE)
                    copies.append(
                        pltpu.make_async_copy(
                            update.at[lines, :], update_hbm.at[lines, :], sems.at[len(copies)]
                        )
                    )
                    copies[-1].start()
    for copy in copies:
        copy.wait()


def combine_kernel(steps, group, cap, ids_ref, slots_ref, *rest):
    refs, out_ref = iter(rest[:-1]), rest[-1]
    tokens = ids_ref.shape[1]
    me = ep_index()
    shape = rest[0].shape
    lane = lax.broadcasted_iota(jnp.int32, shape, 1)
    row = lax.broadcasted_iota(jnp.int32, shape, 0)
    lines = jnp.zeros(shape, F32)
    for k, tiles in steps:
        scores = next(refs)[...]
        if tiles == 2:
            scores = jnp.where(lane < cap, scores, next(refs)[...])
        line = jnp.sum(jnp.where(row == me, scores, 0.0), axis=0, keepdims=True)
        lines = jnp.where(row == k, line, lines)
    rest = jnp.zeros((LANES - lines.shape[0], LANES), F32)
    columns = jnp.concatenate([lines, rest], axis=0).T
    columns = columns[:cap] + columns[cap : 2 * cap]
    place = lax.broadcasted_iota(jnp.int32, (cap, tokens), 0).astype(F32)
    ids = ids_ref[...]
    result = jnp.zeros(ids.shape, F32)
    for k in range(group):
        at_slot = jnp.where(place == slots_ref[k : k + 1, :], columns[:, k : k + 1], 0.0)
        result = jnp.where(ids == (me ^ k), jnp.sum(at_slot, axis=0, keepdims=True), result)
    out_ref[...] = result


def moved(array, side, step):
    if (side, step) == (0, 0):
        return array
    group = lax.axis_size("ep")
    pairs = [
        (p * group + e, (p ^ side) * group + (e ^ step)) for p in range(2) for e in range(group)
    ]
    return lax.ppermute(array, ("pair", "ep"), pairs)


def local(grad_out, router_weights, expert_ids, hidden, master, moment, second):
    group = lax.axis_size("ep")
    tokens, width = grad_out.shape[1:]
    top = expert_ids.shape[2]
    hid, slots = hidden.shape[2:]
    half = master.shape[3]
    cap = slots // group
    ids = expert_ids[0].T
    own_hidden = hidden[0, 0]
    param = master[0, 0]
    other_hidden = moved(own_hidden, 1, 0)

    far = group // 2
    first = [k for k in range(1, group) if k != far]
    late = [0, far]
    first_items = [(side, k) for side in range(2) for k in reversed(first)]
    last_items = [(0, far), (1, far), (1, 0), (0, 0)]
    order = first_items + last_items
    chunk = jax.ShapeDtypeStruct((half // LANES * cap + TILE, LANES), BF16)
    grads = pltpu.with_memory_space_constraint(grad_out[0], pltpu.HBM)
    held = pltpu.VMEM((2, tokens, half), BF16)
    routed = pl.pallas_call(
        functools.partial(route_kernel, first_items, first, group, cap),
        out_shape=[
            jax.ShapeDtypeStruct((group + -group % TILE, tokens), F32),
            jax.ShapeDtypeStruct((group, TILE, LANES), BF16),
        ]
        + [chunk] * len(first_items),
        in_specs=specs(pltpu.HBM, 3),
        out_specs=specs(pltpu.VMEM, 2 + len(first_items)),
        scratch_shapes=[
            pltpu.VMEM((top, tokens), jnp.int32),
            pltpu.VMEM((top, tokens), BF16),
            held,
            pltpu.SemaphoreType.DMA((4,)),
        ],
        compiler_params=params(),
        cost_estimate=cost(2 * slots * tokens * width, 2 * (tokens + slots) * width),
        name="route",
    )(
        pltpu.with_memory_space_constraint(ids, pltpu.HBM),
        pltpu.with_memory_space_constraint(router_weights[0].T, pltpu.HBM),
        grads,
    )
    slot_of, tiles = routed[:2]
    arrived = {item: moved(sent, *item) for item, sent in zip(first_items, routed[2:])}

    routed = pl.pallas_call(
        functools.partial(later_kernel, last_items, late, cap),
        out_shape=[jax.ShapeDtypeStruct((2 * slots, half), F32)] + [chunk] * len(last_items),
        in_specs=specs(pltpu.VMEM, 2)
        + specs(pltpu.HBM, 1)
        + specs(pltpu.VMEM, 2)
        + specs(pltpu.HBM, 1),
        out_specs=specs(pltpu.VMEM, 1 + len(last_items)),
        scratch_shapes=[
            held,
            pltpu.VMEM((hid, half), F32),
            pltpu.SemaphoreType.DMA((2 + half // min(half, 4 * LANES),)),
        ],
        compiler_params=params(),
        cost_estimate=cost(
            2 * slots * tokens * width + 4 * slots * hid * half, 2 * (tokens + slots) * width
        ),
        name="later",
    )(
        slot_of,
        tiles,
        grads,
        own_hidden,
        other_hidden,
        pltpu.with_memory_space_constraint(param, pltpu.HBM),
    )
    inner = routed[0]
    arrived |= {item: moved(sent, *item) for item, sent in zip(last_items, routed[1:])}

    tile = jax.ShapeDtypeStruct((group + -group % 8, LANES), F32)

    def scored(items, *after):
        return pl.pallas_call(
            functools.partial(score_kernel, items, group, cap),
            out_shape=tile,
            in_specs=specs(pltpu.VMEM, 1 + len(items)) + specs(pl.ANY, len(after)),
            out_specs=specs(pltpu.VMEM, 1)[0],
            compiler_params=params(),
            cost_estimate=cost(2 * cap * half, 6 * cap * half),
            name="score",
        )(inner, *[arrived[item] for item in items], *after)

    first_scores = scored(first_items)
    other_scores = moved(first_scores, 1, 0)
    added = [(0, far), (1, far), (1, 0)]
    summed = [item for item in order if item not in added]
    grad = pl.pallas_call(
        functools.partial(sum_kernel, summed, group, cap),
        out_shape=jax.ShapeDtypeStruct((hid, half), F32),
        in_specs=specs(pltpu.VMEM, 2 + len(summed)) + specs(pl.ANY, 1),
        out_specs=specs(pltpu.VMEM, 1)[0],
        scratch_shapes=[
            pltpu.VMEM((2 * slots, half), BF16),
            pltpu.VMEM((hid, 2 * slots), BF16),
        ],
        compiler_params=params(),
        cost_estimate=cost(4 * slots * hid * half, 4 * hid * half),
        name="sum",
    )(own_hidden, other_hidden, *[arrived[item] for item in summed], first_scores)
    merged = pl.pallas_call(
        functools.partial(merge_kernel, cap),
        out_shape=tile,
        in_specs=specs(pltpu.VMEM, 2) + specs(pl.ANY, 1),
        out_specs=specs(pltpu.VMEM, 1)[0],
        compiler_params=params(),
        name="merge",
    )(first_scores, other_scores, grad)
    returned = {k: [moved(merged, 0, k)] for k in first}
    zero_scores = scored([(0, 0), (1, 0)], merged)
    returned[0] = [zero_scores, moved(zero_scores, 1, 0)]
    own_far = scored([(0, far)], zero_scores)
    last_scores = scored([(1, far)], own_far)
    returned[far] = [moved(own_far, 0, far), moved(last_scores, 1, far)]

    block = min(hid, 2 * LANES)
    update = pl.pallas_call(
        functools.partial(update_kernel, added, cap),
        out_shape=jax.ShapeDtypeStruct((hid, half), F32),
        in_specs=specs(pltpu.VMEM, 6 + len(added)) + specs(pl.ANY, 1),
        out_specs=specs(pltpu.HBM, 1)[0],
        scratch_shapes=[
            pltpu.VMEM((len(added) * LANES, half), BF16),
            pltpu.VMEM((hid, len(added) * LANES), BF16),
            pltpu.VMEM((2, block, half), F32),
            pltpu.VMEM((hid, half), F32),
            pltpu.SemaphoreType.DMA((2 * hid // block,)),
        ],
        compiler_params=params(),
        cost_estimate=cost(6 * LANES * hid * half, 16 * hid * half),
        name="update",
    )(
        own_hidden,
        other_hidden,
        grad,
        param,
        moment[0, 0],
        second[0, 0],
        *[arrived[item] for item in added],
        last_scores,
    )
    shares = [array for arrays in returned.values() for array in arrays]
    router = pl.pallas_call(
        functools.partial(
            combine_kernel, [(k, len(arrays)) for k, arrays in returned.items()], group, cap
        ),
        out_shape=jax.ShapeDtypeStruct((top, tokens), F32),
        in_specs=specs(pltpu.VMEM, 2 + len(shares)),
        out_specs=specs(pltpu.VMEM, 1)[0],
        compiler_params=params(),
        cost_estimate=cost(4 * slots * tokens, 8 * top * tokens),
        name="combine",
    )(ids, slot_of, *shares)
    return (update[None, None], router.T[None])


def solution(mesh):
    sections, group = mesh.devices.shape
    split = jax.sharding.Mesh(
        mesh.devices.reshape(2, sections // 2, group), ("pair", "rest", "ep")
    )
    section = ("pair", "rest")
    rows = P(section, "ep", None)
    blocks = P(section, "ep", None, None)
    return jax.shard_map(
        local,
        mesh=split,
        in_specs=(rows, rows, rows, blocks, blocks, blocks, blocks),
        out_specs=(blocks, rows),
        check_vma=False,
    )
```

```python
import functools

import jax
import jax.numpy as jnp
from jax import lax
from jax.experimental import pallas as pl
from jax.experimental.pallas import tpu as pltpu
from jax.sharding import PartitionSpec as P

beta_first = 0.9
beta_second = 0.95
adam_eps = 1e-08
decay_rate = 0.1
first_fix = 1.0 - 0.9**10
second_fix = 1.0 - 0.95**10
first_unit = (1.0 - beta_first) / first_fix
second_unit = (1.0 - beta_second) / second_fix

LANES = 128
TILE = 16
VMEM_BYTES = 32 * 1024 * 1024
F32 = jnp.float32
BF16 = jnp.bfloat16


def params():
    return pltpu.CompilerParams(vmem_limit_bytes=VMEM_BYTES)


def cost(flops, touched):
    return pl.CostEstimate(flops=int(flops), bytes_accessed=int(touched), transcendentals=0)


def specs(space, count):
    return [pl.BlockSpec(memory_space=space) for _ in range(count)]


def ep_index():
    return lax.axis_index("ep").astype(jnp.int32)


def own_half():
    return lax.axis_index("pair").astype(jnp.int32)


def start_grads(grads_hbm, held, sems):
    half = held.shape[2]
    mine = own_half()
    copies = []
    for side in range(2):
        column = pl.multiple_of((1 - mine if side else mine) * half, half)
        copies.append(
            pltpu.make_async_copy(
                grads_hbm.at[:, pl.ds(column, half)], held.at[side], sems.at[side]
            )
        )
        copies[-1].start()
    return copies


def pick_rows(slots, k, cap):
    place = lax.broadcasted_iota(jnp.int32, (cap, slots.shape[1]), 0).astype(F32)
    return jnp.where(place == slots[k : k + 1, :], 1.0, 0.0).astype(BF16)


def fill_chunks(steps, cap, picks, held, copies, tiles, chunks):
    half = held.shape[2]
    data_rows = half // LANES * cap
    step = min(half, 2 * LANES)
    pick = jnp.concatenate([picks[k] for k in steps], axis=0)
    for side in range(2):
        for k in steps:
            chunks[side, k][data_rows:, :] = tiles[k]
        copies[side].wait()
        for column in range(0, half, step):
            block = jnp.dot(
                pick, held[side, :, column : column + step], preferred_element_type=F32
            ).astype(BF16)
            for at, k in enumerate(steps):
                for part in range(step // LANES):
                    top = (column // LANES + part) * cap
                    chunks[side, k][top : top + cap, :] = block[
                        at * cap : (at + 1) * cap, part * LANES : (part + 1) * LANES
                    ]


def route_kernel(
    items, steps, group, cap, ids_hbm, weight_hbm, grads_hbm, slots_ref, tiles_ref, *rest
):
    chunks = dict(zip(items, rest))
    ids_ref, weight_ref, held, sems = rest[len(items) :]
    tokens = held.shape[1]
    me = ep_index()
    small = [
        pltpu.make_async_copy(ids_hbm, ids_ref, sems.at[2]),
        pltpu.make_async_copy(weight_hbm, weight_ref, sems.at[3]),
    ]
    for copy in small:
        copy.start()
    copies = start_grads(grads_hbm, held, sems)
    earlier = lax.broadcasted_iota(jnp.int32, (tokens, tokens), 0)
    later = lax.broadcasted_iota(jnp.int32, (tokens, tokens), 1)
    ahead = jnp.where(earlier < later, 1.0, 0.0).astype(BF16)
    for copy in small:
        copy.wait()
    ids = ids_ref[...]
    weights = weight_ref[...].astype(F32)
    members, scales = [], []
    for k in range(group):
        named = ids == (me ^ k)
        members.append(jnp.sum(jnp.where(named, 1.0, 0.0), axis=0, keepdims=True))
        scales.append(jnp.sum(jnp.where(named, weights, 0.0), axis=0, keepdims=True))
    if group % TILE:
        members.append(jnp.zeros((-group % TILE, tokens), F32))
    member = jnp.concatenate(members, axis=0)
    before = jnp.dot(member.astype(BF16), ahead, preferred_element_type=F32)
    slots = jnp.where(member > 0.5, before, -1.0)
    slots_ref[...] = slots
    picks = [pick_rows(slots, k, cap) for k in range(group)]
    base = me * cap
    tile_row = lax.broadcasted_iota(jnp.int32, (TILE, LANES), 0)
    tile_lane = lax.broadcasted_iota(jnp.int32, (TILE, LANES), 1)
    spot = tile_row * LANES + tile_lane
    kept = (spot >= base) & (spot < base + cap)
    if group % TILE:
        scales.append(jnp.zeros((-group % TILE, tokens), F32))
    rows = jnp.concatenate(scales, axis=0)
    lines = lax.dot_general(
        rows.astype(BF16),
        jnp.concatenate(picks, axis=0),
        (((1,), (1,)), ((), ())),
        preferred_element_type=F32,
    )
    tiles = []
    for k in range(group):
        line = lines[k : k + 1, k * cap : (k + 1) * cap]
        line = jnp.concatenate([line] * (LANES // cap), axis=1)
        tiles.append(jnp.where(kept, line, 0.0).astype(BF16))
        tiles_ref[k] = tiles[k]
    fill_chunks(steps, cap, picks, held, copies, tiles, chunks)


def later_kernel(
    items, steps, cap, slots_ref, tiles_ref, grads_hbm, own_ref, other_ref, master_hbm, inner_ref, *rest
):
    chunks = dict(zip(items, rest))
    held, master_ref, sems = rest[len(items) :]
    copies = start_grads(grads_hbm, held, sems)
    half = master_ref.shape[1]
    step = min(half, 4 * LANES)
    parts = [slice(column, column + step) for column in range(0, half, step)]
    loads = [
        pltpu.make_async_copy(master_hbm.at[:, part], master_ref.at[:, part], sems.at[2 + at])
        for at, part in enumerate(parts)
    ]
    for load in loads:
        load.start()
    slots = slots_ref[...]
    picks = {k: pick_rows(slots, k, cap) for k in steps}
    fill_chunks(steps, cap, picks, held, copies, tiles_ref, chunks)
    slot_count = own_ref.shape[1]
    for load, part in zip(loads, parts):
        load.wait()
        weights = master_ref[:, part].astype(BF16)
        for at, ref in ((0, own_ref), (slot_count, other_ref)):
            inner_ref[at : at + slot_count, part] = lax.dot_general(
                ref[...], weights, (((0,), (0,)), ((), ())), preferred_element_type=F32
            )


def score_kernel(items, group, cap, inner_ref, *rest):
    chunks, score_ref = dict(zip(items, rest)), rest[-1]
    blocks = inner_ref.shape[1] // LANES
    me = ep_index()
    line_of = lax.broadcasted_iota(jnp.int32, score_ref.shape, 0)
    scores = jnp.zeros(score_ref.shape, F32)
    for k in sorted({k for _, k in items}):
        sums = []
        for side in range(2):
            total = jnp.zeros((cap, LANES), F32)
            if (side, k) in items:
                start = pl.multiple_of(side * group * cap + (me ^ k) * cap, cap)
                for block in range(blocks):
                    rows = chunks[side, k][block * cap : (block + 1) * cap, :].astype(F32)
                    total += rows * inner_ref[
                        pl.ds(start, cap), block * LANES : (block + 1) * LANES
                    ]
            sums.append(total)
        both = jnp.concatenate(sums, axis=0)
        line = jnp.sum(both.T, axis=0, keepdims=True)
        scores = jnp.where(line_of == (me ^ k), line, scores)
    score_ref[...] = scores


def scale_into(scaled, at, hidden, line):
    for top in range(0, hidden.shape[0], LANES):
        lines = slice(top, top + LANES)
        scaled[lines, at : at + LANES] = (hidden[lines, :].astype(F32) * line).astype(BF16)


def sum_kernel(items, group, cap, own_ref, other_ref, *rest):
    chunks = dict(zip(items, rest))
    grad_ref, rows, scaled = rest[-3:]
    blocks = rows.shape[1] // LANES
    slots = group * cap
    me = ep_index()
    for side, hidden in enumerate((own_ref, other_ref)):
        tile = jnp.zeros((TILE, LANES), F32)
        for k in range(group):
            start = pl.multiple_of(side * slots + (me ^ k) * cap, cap)
            if (side, k) not in items:
                rows[pl.ds(start, cap), :] = jnp.zeros((cap, rows.shape[1]), BF16)
                continue
            chunk = chunks[side, k]
            tile += chunk[blocks * cap :, :].astype(F32)
            for block in range(blocks):
                rows[pl.ds(start, cap), block * LANES : (block + 1) * LANES] = chunk[
                    block * cap : (block + 1) * cap, :
                ]
        for part in range(slots // LANES):
            lanes = slice(part * LANES, (part + 1) * LANES)
            scale_into(scaled, side * slots + part * LANES, hidden.at[:, lanes], tile[part : part + 1, :])
    grad_ref[...] = jnp.dot(scaled[...], rows[...], preferred_element_type=F32)


def merge_kernel(cap, own_ref, other_ref, _, out_ref):
    lane = lax.broadcasted_iota(jnp.int32, own_ref.shape, 1)
    scores = own_ref[...] + pltpu.roll(other_ref[...], LANES - cap, axis=1)
    out_ref[...] = jnp.where(lane < cap, scores, 0.0)


def update_kernel(items, cap, own_ref, other_ref, grad_ref, master_ref, moment_ref, second_ref, *rest):
    chunks = dict(zip(items, rest))
    _, update_hbm, rows, scaled, total, update, sems = rest[len(items) :]
    hid, half = update.shape
    block = total.shape[1]
    width = min(half, 4 * LANES)
    height = block // 2
    data_rows = half // LANES * cap
    rows[...] = jnp.zeros(rows.shape, BF16)
    for at, ((side, k), chunk) in enumerate(chunks.items()):
        slot = (ep_index() ^ k) * cap
        lanes = pl.ds(pl.multiple_of(slot // LANES * LANES, LANES), LANES)
        start = pl.multiple_of(at * LANES + slot % LANES, cap)
        for part in range(half // LANES):
            rows[pl.ds(start, cap), part * LANES : (part + 1) * LANES] = chunk[
                part * cap : (part + 1) * cap, :
            ]
        line = jnp.sum(chunk[data_rows:, :].astype(F32), axis=0, keepdims=True)
        scale_into(scaled, at * LANES, (own_ref, other_ref)[side].at[:, lanes], line)

    def multiply(at):
        total[at % 2] = jnp.dot(
            scaled[at * block : (at + 1) * block, :], rows[...], preferred_element_type=F32
        )

    def moments(at, top, columns):
        lines = slice(at * block + top, at * block + top + TILE)
        grad = total[at % 2, top : top + TILE, columns] + grad_ref[lines, columns]
        first = moment_ref[lines, columns].astype(F32) * (beta_first / (1.0 - beta_first)) + grad
        square = (
            second_ref[lines, columns].astype(F32) * (beta_second / (1.0 - beta_second))
            + grad * grad
        )
        return first, square, lax.rsqrt(square)

    def inverse(first, square, root):
        scale = square * root * (second_unit**0.5 / first_unit) + adam_eps / first_unit
        return first, pl.reciprocal(scale, approx=True)

    def finish(at, top, columns, first, scale):
        lines = slice(at * block + top, at * block + top + TILE)
        update[lines, columns] = first * scale + decay_rate * master_ref[lines, columns]

    copies = []
    multiply(0)
    for at in range(hid // block):
        if at + 1 < hid // block:
            multiply(at + 1)
        pieces = [
            (top, slice(column, column + width))
            for top in range(0, block, TILE)
            for column in range(0, half, width)
        ]
        held = {}
        for turn in range(len(pieces) + 2):
            if turn < len(pieces):
                held[turn, 0] = moments(at, *pieces[turn])
            if 0 <= turn - 1 < len(pieces):
                held[turn - 1, 1] = inverse(*held.pop((turn - 1, 0)))
            if turn >= 2:
                finish(at, *pieces[turn - 2], *held.pop((turn - 2, 1)))
                top, columns = pieces[turn - 2]
                if (top + TILE) % height == 0 and columns.stop == half:
                    lines = slice(at * block + top + TILE - height, at * block + top + TILE)
                    copies.append(
                        pltpu.make_async_copy(
                            update.at[lines, :], update_hbm.at[lines, :], sems.at[len(copies)]
                        )
                    )
                    copies[-1].start()
    for copy in copies:
        copy.wait()


def combine_kernel(steps, group, cap, ids_ref, slots_ref, *rest):
    refs, out_ref = iter(rest[:-1]), rest[-1]
    tokens = ids_ref.shape[1]
    me = ep_index()
    shape = rest[0].shape
    lane = lax.broadcasted_iota(jnp.int32, shape, 1)
    row = lax.broadcasted_iota(jnp.int32, shape, 0)
    lines = jnp.zeros(shape, F32)
    for k, tiles in steps:
        scores = next(refs)[...]
        if tiles == 2:
            scores = jnp.where(lane < cap, scores, next(refs)[...])
        line = jnp.sum(jnp.where(row == me, scores, 0.0), axis=0, keepdims=True)
        lines = jnp.where(row == k, line, lines)
    rest = jnp.zeros((LANES - lines.shape[0], LANES), F32)
    columns = jnp.concatenate([lines, rest], axis=0).T
    columns = columns[:cap] + columns[cap : 2 * cap]
    place = lax.broadcasted_iota(jnp.int32, (cap, tokens), 0).astype(F32)
    ids = ids_ref[...]
    result = jnp.zeros(ids.shape, F32)
    for k in range(group):
        at_slot = jnp.where(place == slots_ref[k : k + 1, :], columns[:, k : k + 1], 0.0)
        result = jnp.where(ids == (me ^ k), jnp.sum(at_slot, axis=0, keepdims=True), result)
    out_ref[...] = result


def moved(array, side, step):
    if (side, step) == (0, 0):
        return array
    group = lax.axis_size("ep")
    pairs = [
        (p * group + e, (p ^ side) * group + (e ^ step)) for p in range(2) for e in range(group)
    ]
    return lax.ppermute(array, ("pair", "ep"), pairs)


def local(grad_out, router_weights, expert_ids, hidden, master, moment, second):
    group = lax.axis_size("ep")
    tokens, width = grad_out.shape[1:]
    top = expert_ids.shape[2]
    hid, slots = hidden.shape[2:]
    half = master.shape[3]
    cap = slots // group
    ids = expert_ids[0].T
    own_hidden = hidden[0, 0]
    param = master[0, 0]
    other_hidden = moved(own_hidden, 1, 0)

    far = group // 2
    first = [k for k in range(1, group) if k != far]
    late = [0, far]
    first_items = [(0, k) for k in reversed(first)] + [(1, k) for k in first]
    last_items = [(1, far), (0, far), (1, 0), (0, 0)]
    order = first_items + last_items
    chunk = jax.ShapeDtypeStruct((half // LANES * cap + TILE, LANES), BF16)
    grads = pltpu.with_memory_space_constraint(grad_out[0], pltpu.HBM)
    held = pltpu.VMEM((2, tokens, half), BF16)
    routed = pl.pallas_call(
        functools.partial(route_kernel, first_items, first, group, cap),
        out_shape=[
            jax.ShapeDtypeStruct((group + -group % TILE, tokens), F32),
            jax.ShapeDtypeStruct((group, TILE, LANES), BF16),
        ]
        + [chunk] * len(first_items),
        in_specs=specs(pltpu.HBM, 3),
        out_specs=specs(pltpu.VMEM, 2 + len(first_items)),
        scratch_shapes=[
            pltpu.VMEM((top, tokens), jnp.int32),
            pltpu.VMEM((top, tokens), BF16),
            held,
            pltpu.SemaphoreType.DMA((4,)),
        ],
        compiler_params=params(),
        cost_estimate=cost(2 * slots * tokens * width, 2 * (tokens + slots) * width),
        name="route",
    )(
        pltpu.with_memory_space_constraint(ids, pltpu.HBM),
        pltpu.with_memory_space_constraint(router_weights[0].T, pltpu.HBM),
        grads,
    )
    slot_of, tiles = routed[:2]
    arrived = {item: moved(sent, *item) for item, sent in zip(first_items, routed[2:])}

    routed = pl.pallas_call(
        functools.partial(later_kernel, last_items, late, cap),
        out_shape=[jax.ShapeDtypeStruct((2 * slots, half), F32)] + [chunk] * len(last_items),
        in_specs=specs(pltpu.VMEM, 2)
        + specs(pltpu.HBM, 1)
        + specs(pltpu.VMEM, 2)
        + specs(pltpu.HBM, 1),
        out_specs=specs(pltpu.VMEM, 1 + len(last_items)),
        scratch_shapes=[
            held,
            pltpu.VMEM((hid, half), F32),
            pltpu.SemaphoreType.DMA((2 + half // min(half, 4 * LANES),)),
        ],
        compiler_params=params(),
        cost_estimate=cost(
            2 * slots * tokens * width + 4 * slots * hid * half, 2 * (tokens + slots) * width
        ),
        name="later",
    )(
        slot_of,
        tiles,
        grads,
        own_hidden,
        other_hidden,
        pltpu.with_memory_space_constraint(param, pltpu.HBM),
    )
    inner = routed[0]
    arrived |= {item: moved(sent, *item) for item, sent in zip(last_items, routed[1:])}

    tile = jax.ShapeDtypeStruct((group + -group % 8, LANES), F32)

    def scored(items, *after):
        return pl.pallas_call(
            functools.partial(score_kernel, items, group, cap),
            out_shape=tile,
            in_specs=specs(pltpu.VMEM, 1 + len(items)) + specs(pl.ANY, len(after)),
            out_specs=specs(pltpu.VMEM, 1)[0],
            compiler_params=params(),
            cost_estimate=cost(2 * cap * half, 6 * cap * half),
            name="score",
        )(inner, *[arrived[item] for item in items], *after)

    first_scores = scored(first_items)
    other_scores = moved(first_scores, 1, 0)
    added = [(1, far), (0, far), (1, 0)]
    summed = [item for item in order if item not in added]
    grad = pl.pallas_call(
        functools.partial(sum_kernel, summed, group, cap),
        out_shape=jax.ShapeDtypeStruct((hid, half), F32),
        in_specs=specs(pltpu.VMEM, 2 + len(summed)) + specs(pl.ANY, 1),
        out_specs=specs(pltpu.VMEM, 1)[0],
        scratch_shapes=[
            pltpu.VMEM((2 * slots, half), BF16),
            pltpu.VMEM((hid, 2 * slots), BF16),
        ],
        compiler_params=params(),
        cost_estimate=cost(4 * slots * hid * half, 4 * hid * half),
        name="sum",
    )(own_hidden, other_hidden, *[arrived[item] for item in summed], first_scores)
    merged = pl.pallas_call(
        functools.partial(merge_kernel, cap),
        out_shape=tile,
        in_specs=specs(pltpu.VMEM, 2) + specs(pl.ANY, 1),
        out_specs=specs(pltpu.VMEM, 1)[0],
        compiler_params=params(),
        name="merge",
    )(first_scores, other_scores, grad)
    returned = {k: [moved(merged, 0, k)] for k in first}
    zero_scores = scored([(0, 0), (1, 0)], merged)
    returned[0] = [zero_scores, moved(zero_scores, 1, 0)]
    other_far = scored([(1, far)], zero_scores)
    last_scores = scored([(0, far)], other_far)
    returned[far] = [moved(last_scores, 0, far), moved(other_far, 1, far)]

    block = min(hid, 2 * LANES)
    update = pl.pallas_call(
        functools.partial(update_kernel, added, cap),
        out_shape=jax.ShapeDtypeStruct((hid, half), F32),
        in_specs=specs(pltpu.VMEM, 6 + len(added)) + specs(pl.ANY, 1),
        out_specs=specs(pltpu.HBM, 1)[0],
        scratch_shapes=[
            pltpu.VMEM((len(added) * LANES, half), BF16),
            pltpu.VMEM((hid, len(added) * LANES), BF16),
            pltpu.VMEM((2, block, half), F32),
            pltpu.VMEM((hid, half), F32),
            pltpu.SemaphoreType.DMA((2 * hid // block,)),
        ],
        compiler_params=params(),
        cost_estimate=cost(6 * LANES * hid * half, 16 * hid * half),
        name="update",
    )(
        own_hidden,
        other_hidden,
        grad,
        param,
        moment[0, 0],
        second[0, 0],
        *[arrived[item] for item in added],
        last_scores,
    )
    shares = [array for arrays in returned.values() for array in arrays]
    router = pl.pallas_call(
        functools.partial(
            combine_kernel, [(k, len(arrays)) for k, arrays in returned.items()], group, cap
        ),
        out_shape=jax.ShapeDtypeStruct((top, tokens), F32),
        in_specs=specs(pltpu.VMEM, 2 + len(shares)),
        out_specs=specs(pltpu.VMEM, 1)[0],
        compiler_params=params(),
        cost_estimate=cost(4 * slots * tokens, 8 * top * tokens),
        name="combine",
    )(ids, slot_of, *shares)
    return (update[None, None], router.T[None])


def solution(mesh):
    sections, group = mesh.devices.shape
    split = jax.sharding.Mesh(
        mesh.devices.reshape(2, sections // 2, group), ("pair", "rest", "ep")
    )
    section = ("pair", "rest")
    rows = P(section, "ep", None)
    blocks = P(section, "ep", None, None)
    return jax.shard_map(
        local,
        mesh=split,
        in_specs=(rows, rows, rows, blocks, blocks, blocks, blocks),
        out_specs=(blocks, rows),
        check_vma=False,
    )
```

```python
import functools

import jax
import jax.numpy as jnp
from jax import lax
from jax.experimental import pallas as pl
from jax.experimental.pallas import tpu as pltpu
from jax.sharding import PartitionSpec as P

beta_first = 0.9
beta_second = 0.95
adam_eps = 1e-08
decay_rate = 0.1
first_fix = 1.0 - 0.9**10
second_fix = 1.0 - 0.95**10
first_unit = (1.0 - beta_first) / first_fix
second_unit = (1.0 - beta_second) / second_fix

LANES = 128
TILE = 16
VMEM_BYTES = 32 * 1024 * 1024
F32 = jnp.float32
BF16 = jnp.bfloat16


def params():
    return pltpu.CompilerParams(vmem_limit_bytes=VMEM_BYTES)


def cost(flops, touched):
    return pl.CostEstimate(flops=int(flops), bytes_accessed=int(touched), transcendentals=0)


def specs(space, count):
    return [pl.BlockSpec(memory_space=space) for _ in range(count)]


def ep_index():
    return lax.axis_index("ep").astype(jnp.int32)


def own_half():
    return lax.axis_index("pair").astype(jnp.int32)


def start_grads(grads_hbm, held, sems):
    half = held.shape[2]
    mine = own_half()
    copies = []
    for side in range(2):
        column = pl.multiple_of((1 - mine if side else mine) * half, half)
        copies.append(
            pltpu.make_async_copy(
                grads_hbm.at[:, pl.ds(column, half)], held.at[side], sems.at[side]
            )
        )
        copies[-1].start()
    return copies


def pick_rows(slots, k, cap):
    place = lax.broadcasted_iota(jnp.int32, (cap, slots.shape[1]), 0).astype(F32)
    return jnp.where(place == slots[k : k + 1, :], 1.0, 0.0).astype(BF16)


def fill_chunks(steps, cap, picks, held, copies, tiles, chunks):
    half = held.shape[2]
    data_rows = half // LANES * cap
    step = min(half, 2 * LANES)
    pick = jnp.concatenate([picks[k] for k in steps], axis=0)
    for side in range(2):
        for k in steps:
            chunks[side, k][data_rows:, :] = tiles[k]
        copies[side].wait()
        for column in range(0, half, step):
            block = jnp.dot(
                pick, held[side, :, column : column + step], preferred_element_type=F32
            ).astype(BF16)
            for at, k in enumerate(steps):
                for part in range(step // LANES):
                    top = (column // LANES + part) * cap
                    chunks[side, k][top : top + cap, :] = block[
                        at * cap : (at + 1) * cap, part * LANES : (part + 1) * LANES
                    ]


def route_kernel(
    items, steps, group, cap, ids_hbm, weight_hbm, grads_hbm, slots_ref, tiles_ref, *rest
):
    chunks = dict(zip(items, rest))
    ids_ref, weight_ref, held, sems = rest[len(items) :]
    tokens = held.shape[1]
    me = ep_index()
    small = [
        pltpu.make_async_copy(ids_hbm, ids_ref, sems.at[2]),
        pltpu.make_async_copy(weight_hbm, weight_ref, sems.at[3]),
    ]
    for copy in small:
        copy.start()
    copies = start_grads(grads_hbm, held, sems)
    earlier = lax.broadcasted_iota(jnp.int32, (tokens, tokens), 0)
    later = lax.broadcasted_iota(jnp.int32, (tokens, tokens), 1)
    ahead = jnp.where(earlier < later, 1.0, 0.0).astype(BF16)
    for copy in small:
        copy.wait()
    ids = ids_ref[...]
    weights = weight_ref[...].astype(F32)
    members, scales = [], []
    for k in range(group):
        named = ids == (me ^ k)
        members.append(jnp.sum(jnp.where(named, 1.0, 0.0), axis=0, keepdims=True))
        scales.append(jnp.sum(jnp.where(named, weights, 0.0), axis=0, keepdims=True))
    if group % TILE:
        members.append(jnp.zeros((-group % TILE, tokens), F32))
    member = jnp.concatenate(members, axis=0)
    before = jnp.dot(member.astype(BF16), ahead, preferred_element_type=F32)
    slots = jnp.where(member > 0.5, before, -1.0)
    slots_ref[...] = slots
    picks = [pick_rows(slots, k, cap) for k in range(group)]
    base = me * cap
    tile_row = lax.broadcasted_iota(jnp.int32, (TILE, LANES), 0)
    tile_lane = lax.broadcasted_iota(jnp.int32, (TILE, LANES), 1)
    spot = tile_row * LANES + tile_lane
    kept = (spot >= base) & (spot < base + cap)
    if group % TILE:
        scales.append(jnp.zeros((-group % TILE, tokens), F32))
    rows = jnp.concatenate(scales, axis=0)
    lines = lax.dot_general(
        rows.astype(BF16),
        jnp.concatenate(picks, axis=0),
        (((1,), (1,)), ((), ())),
        preferred_element_type=F32,
    )
    tiles = []
    for k in range(group):
        line = lines[k : k + 1, k * cap : (k + 1) * cap]
        line = jnp.concatenate([line] * (LANES // cap), axis=1)
        tiles.append(jnp.where(kept, line, 0.0).astype(BF16))
        tiles_ref[k] = tiles[k]
    fill_chunks(steps, cap, picks, held, copies, tiles, chunks)


def later_kernel(
    items, steps, cap, slots_ref, tiles_ref, grads_hbm, own_ref, other_ref, master_hbm, inner_ref, *rest
):
    chunks = dict(zip(items, rest))
    held, master_ref, sems = rest[len(items) :]
    copies = start_grads(grads_hbm, held, sems)
    half = master_ref.shape[1]
    step = min(half, 4 * LANES)
    parts = [slice(column, column + step) for column in range(0, half, step)]
    loads = [
        pltpu.make_async_copy(master_hbm.at[:, part], master_ref.at[:, part], sems.at[2 + at])
        for at, part in enumerate(parts)
    ]
    for load in loads:
        load.start()
    slots = slots_ref[...]
    picks = {k: pick_rows(slots, k, cap) for k in steps}
    fill_chunks(steps, cap, picks, held, copies, tiles_ref, chunks)
    slot_count = own_ref.shape[1]
    for load, part in zip(loads, parts):
        load.wait()
        weights = master_ref[:, part].astype(BF16)
        for at, ref in ((0, own_ref), (slot_count, other_ref)):
            inner_ref[at : at + slot_count, part] = lax.dot_general(
                ref[...], weights, (((0,), (0,)), ((), ())), preferred_element_type=F32
            )


def score_kernel(items, group, cap, inner_ref, *rest):
    chunks, score_ref = dict(zip(items, rest)), rest[-1]
    blocks = inner_ref.shape[1] // LANES
    me = ep_index()
    line_of = lax.broadcasted_iota(jnp.int32, score_ref.shape, 0)
    scores = jnp.zeros(score_ref.shape, F32)
    for k in sorted({k for _, k in items}):
        sums = []
        for side in range(2):
            total = jnp.zeros((cap, LANES), F32)
            if (side, k) in items:
                start = pl.multiple_of(side * group * cap + (me ^ k) * cap, cap)
                for block in range(blocks):
                    rows = chunks[side, k][block * cap : (block + 1) * cap, :].astype(F32)
                    total += rows * inner_ref[
                        pl.ds(start, cap), block * LANES : (block + 1) * LANES
                    ]
            sums.append(total)
        both = jnp.concatenate(sums, axis=0)
        line = jnp.sum(both.T, axis=0, keepdims=True)
        scores = jnp.where(line_of == (me ^ k), line, scores)
    score_ref[...] = scores


def scale_into(scaled, at, hidden, line):
    for top in range(0, hidden.shape[0], LANES):
        lines = slice(top, top + LANES)
        scaled[lines, at : at + LANES] = (hidden[lines, :].astype(F32) * line).astype(BF16)


def sum_kernel(items, group, cap, own_ref, other_ref, *rest):
    chunks = dict(zip(items, rest))
    grad_ref, rows, scaled = rest[-3:]
    blocks = rows.shape[1] // LANES
    slots = group * cap
    me = ep_index()
    for side, hidden in enumerate((own_ref, other_ref)):
        tile = jnp.zeros((TILE, LANES), F32)
        for k in range(group):
            start = pl.multiple_of(side * slots + (me ^ k) * cap, cap)
            if (side, k) not in items:
                rows[pl.ds(start, cap), :] = jnp.zeros((cap, rows.shape[1]), BF16)
                continue
            chunk = chunks[side, k]
            tile += chunk[blocks * cap :, :].astype(F32)
            for block in range(blocks):
                rows[pl.ds(start, cap), block * LANES : (block + 1) * LANES] = chunk[
                    block * cap : (block + 1) * cap, :
                ]
        for part in range(slots // LANES):
            lanes = slice(part * LANES, (part + 1) * LANES)
            scale_into(scaled, side * slots + part * LANES, hidden.at[:, lanes], tile[part : part + 1, :])
    grad_ref[...] = jnp.dot(scaled[...], rows[...], preferred_element_type=F32)


def merge_kernel(cap, own_ref, other_ref, _, out_ref):
    lane = lax.broadcasted_iota(jnp.int32, own_ref.shape, 1)
    scores = own_ref[...] + pltpu.roll(other_ref[...], LANES - cap, axis=1)
    out_ref[...] = jnp.where(lane < cap, scores, 0.0)


def update_kernel(items, cap, own_ref, other_ref, grad_ref, master_ref, moment_ref, second_ref, *rest):
    chunks = dict(zip(items, rest))
    _, update_hbm, rows, scaled, total, update, sems = rest[len(items) :]
    hid, half = update.shape
    block = total.shape[1]
    width = min(half, 4 * LANES)
    height = block // 2
    data_rows = half // LANES * cap
    rows[...] = jnp.zeros(rows.shape, BF16)
    for at, ((side, k), chunk) in enumerate(chunks.items()):
        slot = (ep_index() ^ k) * cap
        lanes = pl.ds(pl.multiple_of(slot // LANES * LANES, LANES), LANES)
        start = pl.multiple_of(at * LANES + slot % LANES, cap)
        for part in range(half // LANES):
            rows[pl.ds(start, cap), part * LANES : (part + 1) * LANES] = chunk[
                part * cap : (part + 1) * cap, :
            ]
        line = jnp.sum(chunk[data_rows:, :].astype(F32), axis=0, keepdims=True)
        scale_into(scaled, at * LANES, (own_ref, other_ref)[side].at[:, lanes], line)

    def multiply(at):
        total[at % 2] = jnp.dot(
            scaled[at * block : (at + 1) * block, :], rows[...], preferred_element_type=F32
        )

    def moments(at, top, columns):
        lines = slice(at * block + top, at * block + top + TILE)
        grad = total[at % 2, top : top + TILE, columns] + grad_ref[lines, columns]
        first = moment_ref[lines, columns].astype(F32) * (beta_first / (1.0 - beta_first)) + grad
        square = (
            second_ref[lines, columns].astype(F32) * (beta_second / (1.0 - beta_second))
            + grad * grad
        )
        return first, square, lax.rsqrt(square)

    def inverse(first, square, root):
        scale = square * root * (second_unit**0.5 / first_unit) + adam_eps / first_unit
        return first, pl.reciprocal(scale, approx=True)

    def finish(at, top, columns, first, scale):
        lines = slice(at * block + top, at * block + top + TILE)
        update[lines, columns] = first * scale + decay_rate * master_ref[lines, columns]

    copies = []
    multiply(0)
    for at in range(hid // block):
        if at + 1 < hid // block:
            multiply(at + 1)
        pieces = [
            (top, slice(column, column + width))
            for top in range(0, block, TILE)
            for column in range(0, half, width)
        ]
        held = {}
        for turn in range(len(pieces) + 2):
            if turn < len(pieces):
                held[turn, 0] = moments(at, *pieces[turn])
            if 0 <= turn - 1 < len(pieces):
                held[turn - 1, 1] = inverse(*held.pop((turn - 1, 0)))
            if turn >= 2:
                finish(at, *pieces[turn - 2], *held.pop((turn - 2, 1)))
                top, columns = pieces[turn - 2]
                if (top + TILE) % height == 0 and columns.stop == half:
                    lines = slice(at * block + top + TILE - height, at * block + top + TILE)
                    copies.append(
                        pltpu.make_async_copy(
                            update.at[lines, :], update_hbm.at[lines, :], sems.at[len(copies)]
                        )
                    )
                    copies[-1].start()
    for copy in copies:
        copy.wait()


def combine_kernel(steps, group, cap, ids_ref, slots_ref, *rest):
    refs, out_ref = iter(rest[:-1]), rest[-1]
    tokens = ids_ref.shape[1]
    me = ep_index()
    shape = rest[0].shape
    lane = lax.broadcasted_iota(jnp.int32, shape, 1)
    row = lax.broadcasted_iota(jnp.int32, shape, 0)
    lines = jnp.zeros(shape, F32)
    for k, tiles in steps:
        scores = next(refs)[...]
        if tiles == 2:
            scores = jnp.where(lane < cap, scores, next(refs)[...])
        line = jnp.sum(jnp.where(row == me, scores, 0.0), axis=0, keepdims=True)
        lines = jnp.where(row == k, line, lines)
    rest = jnp.zeros((LANES - lines.shape[0], LANES), F32)
    columns = jnp.concatenate([lines, rest], axis=0).T
    columns = columns[:cap] + columns[cap : 2 * cap]
    place = lax.broadcasted_iota(jnp.int32, (cap, tokens), 0).astype(F32)
    ids = ids_ref[...]
    result = jnp.zeros(ids.shape, F32)
    for k in range(group):
        at_slot = jnp.where(place == slots_ref[k : k + 1, :], columns[:, k : k + 1], 0.0)
        result = jnp.where(ids == (me ^ k), jnp.sum(at_slot, axis=0, keepdims=True), result)
    out_ref[...] = result


def moved(array, side, step):
    if (side, step) == (0, 0):
        return array
    group = lax.axis_size("ep")
    pairs = [
        (p * group + e, (p ^ side) * group + (e ^ step)) for p in range(2) for e in range(group)
    ]
    return lax.ppermute(array, ("pair", "ep"), pairs)


def local(grad_out, router_weights, expert_ids, hidden, master, moment, second):
    group = lax.axis_size("ep")
    tokens, width = grad_out.shape[1:]
    top = expert_ids.shape[2]
    hid, slots = hidden.shape[2:]
    half = master.shape[3]
    cap = slots // group
    ids = expert_ids[0].T
    own_hidden = hidden[0, 0]
    param = master[0, 0]
    other_hidden = moved(own_hidden, 1, 0)

    far = group // 2
    first = [k for k in range(1, group) if k != far]
    late = [0, far]
    first_items = [(side, k) for side in range(2) for k in reversed(first)]
    last_items = [(1, far), (0, far), (1, 0), (0, 0)]
    order = first_items + last_items
    chunk = jax.ShapeDtypeStruct((half // LANES * cap + TILE, LANES), BF16)
    grads = pltpu.with_memory_space_constraint(grad_out[0], pltpu.HBM)
    held = pltpu.VMEM((2, tokens, half), BF16)
    routed = pl.pallas_call(
        functools.partial(route_kernel, first_items, first, group, cap),
        out_shape=[
            jax.ShapeDtypeStruct((group + -group % TILE, tokens), F32),
            jax.ShapeDtypeStruct((group, TILE, LANES), BF16),
        ]
        + [chunk] * len(first_items),
        in_specs=specs(pltpu.HBM, 3),
        out_specs=specs(pltpu.VMEM, 2 + len(first_items)),
        scratch_shapes=[
            pltpu.VMEM((top, tokens), jnp.int32),
            pltpu.VMEM((top, tokens), BF16),
            held,
            pltpu.SemaphoreType.DMA((4,)),
        ],
        compiler_params=params(),
        cost_estimate=cost(2 * slots * tokens * width, 2 * (tokens + slots) * width),
        name="route",
    )(
        pltpu.with_memory_space_constraint(ids, pltpu.HBM),
        pltpu.with_memory_space_constraint(router_weights[0].T, pltpu.HBM),
        grads,
    )
    slot_of, tiles = routed[:2]
    arrived = {item: moved(sent, *item) for item, sent in zip(first_items, routed[2:])}

    routed = pl.pallas_call(
        functools.partial(later_kernel, last_items, late, cap),
        out_shape=[jax.ShapeDtypeStruct((2 * slots, half), F32)] + [chunk] * len(last_items),
        in_specs=specs(pltpu.VMEM, 2)
        + specs(pltpu.HBM, 1)
        + specs(pltpu.VMEM, 2)
        + specs(pltpu.HBM, 1),
        out_specs=specs(pltpu.VMEM, 1 + len(last_items)),
        scratch_shapes=[
            held,
            pltpu.VMEM((hid, half), F32),
            pltpu.SemaphoreType.DMA((2 + half // min(half, 4 * LANES),)),
        ],
        compiler_params=params(),
        cost_estimate=cost(
            2 * slots * tokens * width + 4 * slots * hid * half, 2 * (tokens + slots) * width
        ),
        name="later",
    )(
        slot_of,
        tiles,
        grads,
        own_hidden,
        other_hidden,
        pltpu.with_memory_space_constraint(param, pltpu.HBM),
    )
    inner = routed[0]
    arrived |= {item: moved(sent, *item) for item, sent in zip(last_items, routed[1:])}

    tile = jax.ShapeDtypeStruct((group + -group % 8, LANES), F32)

    def scored(items, *after):
        return pl.pallas_call(
            functools.partial(score_kernel, items, group, cap),
            out_shape=tile,
            in_specs=specs(pltpu.VMEM, 1 + len(items)) + specs(pl.ANY, len(after)),
            out_specs=specs(pltpu.VMEM, 1)[0],
            compiler_params=params(),
            cost_estimate=cost(2 * cap * half, 6 * cap * half),
            name="score",
        )(inner, *[arrived[item] for item in items], *after)

    first_scores = scored(first_items)
    other_scores = moved(first_scores, 1, 0)
    added = [(1, far), (0, far), (1, 0)]
    summed = [item for item in order if item not in added]
    grad = pl.pallas_call(
        functools.partial(sum_kernel, summed, group, cap),
        out_shape=jax.ShapeDtypeStruct((hid, half), F32),
        in_specs=specs(pltpu.VMEM, 2 + len(summed)) + specs(pl.ANY, 1),
        out_specs=specs(pltpu.VMEM, 1)[0],
        scratch_shapes=[
            pltpu.VMEM((2 * slots, half), BF16),
            pltpu.VMEM((hid, 2 * slots), BF16),
        ],
        compiler_params=params(),
        cost_estimate=cost(4 * slots * hid * half, 4 * hid * half),
        name="sum",
    )(own_hidden, other_hidden, *[arrived[item] for item in summed], first_scores)
    merged = pl.pallas_call(
        functools.partial(merge_kernel, cap),
        out_shape=tile,
        in_specs=specs(pltpu.VMEM, 2) + specs(pl.ANY, 1),
        out_specs=specs(pltpu.VMEM, 1)[0],
        compiler_params=params(),
        name="merge",
    )(first_scores, other_scores, grad)
    returned = {k: [moved(merged, 0, k)] for k in first}
    zero_scores = scored([(0, 0), (1, 0)], merged)
    returned[0] = [zero_scores, moved(zero_scores, 1, 0)]
    other_far = scored([(1, far)], zero_scores)
    last_scores = scored([(0, far)], other_far)
    returned[far] = [moved(last_scores, 0, far), moved(other_far, 1, far)]

    block = min(hid, 2 * LANES)
    update = pl.pallas_call(
        functools.partial(update_kernel, added, cap),
        out_shape=jax.ShapeDtypeStruct((hid, half), F32),
        in_specs=specs(pltpu.VMEM, 6 + len(added)) + specs(pl.ANY, 1),
        out_specs=specs(pltpu.HBM, 1)[0],
        scratch_shapes=[
            pltpu.VMEM((len(added) * LANES, half), BF16),
            pltpu.VMEM((hid, len(added) * LANES), BF16),
            pltpu.VMEM((2, block, half), F32),
            pltpu.VMEM((hid, half), F32),
            pltpu.SemaphoreType.DMA((2 * hid // block,)),
        ],
        compiler_params=params(),
        cost_estimate=cost(6 * LANES * hid * half, 16 * hid * half),
        name="update",
    )(
        own_hidden,
        other_hidden,
        grad,
        param,
        moment[0, 0],
        second[0, 0],
        *[arrived[item] for item in added],
        last_scores,
    )
    shares = [array for arrays in returned.values() for array in arrays]
    router = pl.pallas_call(
        functools.partial(
            combine_kernel, [(k, len(arrays)) for k, arrays in returned.items()], group, cap
        ),
        out_shape=jax.ShapeDtypeStruct((top, tokens), F32),
        in_specs=specs(pltpu.VMEM, 2 + len(shares)),
        out_specs=specs(pltpu.VMEM, 1)[0],
        compiler_params=params(),
        cost_estimate=cost(4 * slots * tokens, 8 * top * tokens),
        name="combine",
    )(ids, slot_of, *shares)
    return (update[None, None], router.T[None])


def solution(mesh):
    sections, group = mesh.devices.shape
    split = jax.sharding.Mesh(
        mesh.devices.reshape(2, sections // 2, group), ("pair", "rest", "ep")
    )
    section = ("pair", "rest")
    rows = P(section, "ep", None)
    blocks = P(section, "ep", None, None)
    return jax.shard_map(
        local,
        mesh=split,
        in_specs=(rows, rows, rows, blocks, blocks, blocks, blocks),
        out_specs=(blocks, rows),
        check_vma=False,
    )
```

```python
import functools

import jax
import jax.numpy as jnp
from jax import lax
from jax.experimental import pallas as pl
from jax.experimental.pallas import tpu as pltpu
from jax.sharding import PartitionSpec as P

beta_first = 0.9
beta_second = 0.95
adam_eps = 1e-08
decay_rate = 0.1
first_fix = 1.0 - 0.9**10
second_fix = 1.0 - 0.95**10
first_unit = (1.0 - beta_first) / first_fix
second_unit = (1.0 - beta_second) / second_fix

LANES = 128
TILE = 16
VMEM_BYTES = 32 * 1024 * 1024
F32 = jnp.float32
BF16 = jnp.bfloat16


def params():
    return pltpu.CompilerParams(vmem_limit_bytes=VMEM_BYTES)


def cost(flops, touched):
    return pl.CostEstimate(flops=int(flops), bytes_accessed=int(touched), transcendentals=0)


def specs(space, count):
    return [pl.BlockSpec(memory_space=space) for _ in range(count)]


def ep_index():
    return lax.axis_index("ep").astype(jnp.int32)


def own_half():
    return lax.axis_index("pair").astype(jnp.int32)


def start_grads(grads_hbm, held, sems):
    half = held.shape[2]
    mine = own_half()
    copies = []
    for side in range(2):
        column = pl.multiple_of((1 - mine if side else mine) * half, half)
        copies.append(
            pltpu.make_async_copy(
                grads_hbm.at[:, pl.ds(column, half)], held.at[side], sems.at[side]
            )
        )
        copies[-1].start()
    return copies


def pick_rows(slots, k, cap):
    place = lax.broadcasted_iota(jnp.int32, (cap, slots.shape[1]), 0).astype(F32)
    return jnp.where(place == slots[k : k + 1, :], 1.0, 0.0).astype(BF16)


def fill_chunks(steps, cap, picks, held, copies, tiles, chunks):
    half = held.shape[2]
    data_rows = half // LANES * cap
    step = min(half, 2 * LANES)
    pick = jnp.concatenate([picks[k] for k in steps], axis=0)
    for side in range(2):
        for k in steps:
            chunks[side, k][data_rows:, :] = tiles[k]
        copies[side].wait()
        for column in range(0, half, step):
            block = jnp.dot(
                pick, held[side, :, column : column + step], preferred_element_type=F32
            ).astype(BF16)
            for at, k in enumerate(steps):
                for part in range(step // LANES):
                    top = (column // LANES + part) * cap
                    chunks[side, k][top : top + cap, :] = block[
                        at * cap : (at + 1) * cap, part * LANES : (part + 1) * LANES
                    ]


def route_kernel(
    items, steps, group, cap, ids_hbm, weight_hbm, grads_hbm, slots_ref, tiles_ref, *rest
):
    chunks = dict(zip(items, rest))
    ids_ref, weight_ref, held, sems = rest[len(items) :]
    tokens = held.shape[1]
    me = ep_index()
    small = [
        pltpu.make_async_copy(ids_hbm, ids_ref, sems.at[2]),
        pltpu.make_async_copy(weight_hbm, weight_ref, sems.at[3]),
    ]
    for copy in small:
        copy.start()
    copies = start_grads(grads_hbm, held, sems)
    earlier = lax.broadcasted_iota(jnp.int32, (tokens, tokens), 0)
    later = lax.broadcasted_iota(jnp.int32, (tokens, tokens), 1)
    ahead = jnp.where(earlier < later, 1.0, 0.0).astype(BF16)
    for copy in small:
        copy.wait()
    ids = ids_ref[...]
    weights = weight_ref[...].astype(F32)
    members, scales = [], []
    for k in range(group):
        named = ids == (me ^ k)
        members.append(jnp.sum(jnp.where(named, 1.0, 0.0), axis=0, keepdims=True))
        scales.append(jnp.sum(jnp.where(named, weights, 0.0), axis=0, keepdims=True))
    if group % TILE:
        members.append(jnp.zeros((-group % TILE, tokens), F32))
    member = jnp.concatenate(members, axis=0)
    before = jnp.dot(member.astype(BF16), ahead, preferred_element_type=F32)
    slots = jnp.where(member > 0.5, before, -1.0)
    slots_ref[...] = slots
    picks = [pick_rows(slots, k, cap) for k in range(group)]
    base = me * cap
    tile_row = lax.broadcasted_iota(jnp.int32, (TILE, LANES), 0)
    tile_lane = lax.broadcasted_iota(jnp.int32, (TILE, LANES), 1)
    spot = tile_row * LANES + tile_lane
    kept = (spot >= base) & (spot < base + cap)
    if group % TILE:
        scales.append(jnp.zeros((-group % TILE, tokens), F32))
    rows = jnp.concatenate(scales, axis=0)
    lines = lax.dot_general(
        rows.astype(BF16),
        jnp.concatenate(picks, axis=0),
        (((1,), (1,)), ((), ())),
        preferred_element_type=F32,
    )
    tiles = []
    for k in range(group):
        line = lines[k : k + 1, k * cap : (k + 1) * cap]
        line = jnp.concatenate([line] * (LANES // cap), axis=1)
        tiles.append(jnp.where(kept, line, 0.0).astype(BF16))
        tiles_ref[k] = tiles[k]
    fill_chunks(steps, cap, picks, held, copies, tiles, chunks)


def later_kernel(
    items, steps, cap, slots_ref, tiles_ref, grads_hbm, own_ref, other_ref, master_hbm, inner_ref, *rest
):
    chunks = dict(zip(items, rest))
    held, master_ref, sems = rest[len(items) :]
    copies = start_grads(grads_hbm, held, sems)
    half = master_ref.shape[1]
    step = min(half, 4 * LANES)
    parts = [slice(column, column + step) for column in range(0, half, step)]
    loads = [
        pltpu.make_async_copy(master_hbm.at[:, part], master_ref.at[:, part], sems.at[2 + at])
        for at, part in enumerate(parts)
    ]
    for load in loads:
        load.start()
    slots = slots_ref[...]
    picks = {k: pick_rows(slots, k, cap) for k in steps}
    fill_chunks(steps, cap, picks, held, copies, tiles_ref, chunks)
    slot_count = own_ref.shape[1]
    for load, part in zip(loads, parts):
        load.wait()
        weights = master_ref[:, part].astype(BF16)
        for at, ref in ((0, own_ref), (slot_count, other_ref)):
            inner_ref[at : at + slot_count, part] = lax.dot_general(
                ref[...], weights, (((0,), (0,)), ((), ())), preferred_element_type=F32
            )


def score_kernel(items, group, cap, inner_ref, *rest):
    chunks, score_ref = dict(zip(items, rest)), rest[-1]
    blocks = inner_ref.shape[1] // LANES
    me = ep_index()
    line_of = lax.broadcasted_iota(jnp.int32, score_ref.shape, 0)
    scores = jnp.zeros(score_ref.shape, F32)
    for k in sorted({k for _, k in items}):
        sums = []
        for side in range(2):
            total = jnp.zeros((cap, LANES), F32)
            if (side, k) in items:
                start = pl.multiple_of(side * group * cap + (me ^ k) * cap, cap)
                for block in range(blocks):
                    rows = chunks[side, k][block * cap : (block + 1) * cap, :].astype(F32)
                    total += rows * inner_ref[
                        pl.ds(start, cap), block * LANES : (block + 1) * LANES
                    ]
            sums.append(total)
        both = jnp.concatenate(sums, axis=0)
        line = jnp.sum(both.T, axis=0, keepdims=True)
        scores = jnp.where(line_of == (me ^ k), line, scores)
    score_ref[...] = scores


def scale_into(scaled, at, hidden, line):
    for top in range(0, hidden.shape[0], LANES):
        lines = slice(top, top + LANES)
        scaled[lines, at : at + LANES] = (hidden[lines, :].astype(F32) * line).astype(BF16)


def sum_kernel(items, group, cap, own_ref, other_ref, *rest):
    chunks = dict(zip(items, rest))
    grad_ref, rows, scaled = rest[-3:]
    blocks = rows.shape[1] // LANES
    slots = group * cap
    me = ep_index()
    for side, hidden in enumerate((own_ref, other_ref)):
        tile = jnp.zeros((TILE, LANES), F32)
        for k in range(group):
            start = pl.multiple_of(side * slots + (me ^ k) * cap, cap)
            if (side, k) not in items:
                rows[pl.ds(start, cap), :] = jnp.zeros((cap, rows.shape[1]), BF16)
                continue
            chunk = chunks[side, k]
            tile += chunk[blocks * cap :, :].astype(F32)
            for block in range(blocks):
                rows[pl.ds(start, cap), block * LANES : (block + 1) * LANES] = chunk[
                    block * cap : (block + 1) * cap, :
                ]
        for part in range(slots // LANES):
            lanes = slice(part * LANES, (part + 1) * LANES)
            scale_into(scaled, side * slots + part * LANES, hidden.at[:, lanes], tile[part : part + 1, :])
    grad_ref[...] = jnp.dot(scaled[...], rows[...], preferred_element_type=F32)


def merge_kernel(cap, own_ref, other_ref, _, out_ref):
    lane = lax.broadcasted_iota(jnp.int32, own_ref.shape, 1)
    scores = own_ref[...] + pltpu.roll(other_ref[...], LANES - cap, axis=1)
    out_ref[...] = jnp.where(lane < cap, scores, 0.0)


def update_kernel(items, cap, own_ref, other_ref, grad_ref, master_ref, moment_ref, second_ref, *rest):
    chunks = rest[: len(items)]
    _, update_hbm, rows, scaled, total, update, sems = rest[len(items) :]
    hid, half = update.shape
    width = min(half, 4 * LANES)
    height = LANES
    data_rows = half // LANES * cap
    me = ep_index()
    for at in range(0, len(items), 2):
        parts = []
        for turn, ((side, k), chunk) in enumerate(zip(items[at : at + 2], chunks[at : at + 2])):
            slot = (me ^ k) * cap
            lanes = pl.ds(pl.multiple_of(slot // LANES * LANES, LANES), LANES)
            place = slot % LANES if turn == 0 else (LANES - cap) - slot % LANES
            start = pl.multiple_of(at // 2 * LANES + place, cap)
            for part in range(half // LANES):
                rows[pl.ds(start, cap), part * LANES : (part + 1) * LANES] = chunk[
                    part * cap : (part + 1) * cap, :
                ]
            line = jnp.sum(chunk[data_rows:, :].astype(F32), axis=0, keepdims=True)
            parts.append(((own_ref, other_ref)[side], lanes, line))
        if len(parts) == 1:
            start = pl.multiple_of(at // 2 * LANES + (LANES - cap) - place, cap)
            rows[pl.ds(start, cap), :] = jnp.zeros((cap, half), BF16)
        for top in range(0, hid, LANES):
            values = [
                hidden[top : top + LANES, lanes].astype(F32) * line for hidden, lanes, line in parts
            ]
            if len(values) == 2:
                values[0] += pltpu.roll(values[1], LANES - cap, axis=1)
            scaled[top : top + LANES, at // 2 * LANES : (at // 2 + 1) * LANES] = values[0].astype(
                BF16
            )
    total[...] = jnp.dot(scaled[...], rows[...], preferred_element_type=F32)

    def moments(top, columns):
        lines = slice(top, top + TILE)
        grad = total[lines, columns] + grad_ref[lines, columns]
        first = moment_ref[lines, columns].astype(F32) * (beta_first / (1.0 - beta_first)) + grad
        square = (
            second_ref[lines, columns].astype(F32) * (beta_second / (1.0 - beta_second))
            + grad * grad
        )
        return first, square, lax.rsqrt(square)

    def inverse(first, square, root):
        scale = square * root * (second_unit**0.5 / first_unit) + adam_eps / first_unit
        return first, pl.reciprocal(scale, approx=True)

    def finish(top, columns, first, scale):
        lines = slice(top, top + TILE)
        update[lines, columns] = first * scale + decay_rate * master_ref[lines, columns]

    copies = []
    pieces = [
        (top, slice(column, column + width))
        for top in range(0, hid, TILE)
        for column in range(0, half, width)
    ]
    held = {}
    for turn in range(len(pieces) + 2):
        if turn < len(pieces):
            held[turn, 0] = moments(*pieces[turn])
        if 0 <= turn - 1 < len(pieces):
            held[turn - 1, 1] = inverse(*held.pop((turn - 1, 0)))
        if turn >= 2:
            finish(*pieces[turn - 2], *held.pop((turn - 2, 1)))
            top, columns = pieces[turn - 2]
            if (top + TILE) % height == 0 and columns.stop == half:
                lines = slice(top + TILE - height, top + TILE)
                copies.append(
                    pltpu.make_async_copy(
                        update.at[lines, :], update_hbm.at[lines, :], sems.at[len(copies)]
                    )
                )
                copies[-1].start()
    for copy in copies:
        copy.wait()


def combine_kernel(steps, group, cap, ids_ref, slots_ref, *rest):
    refs, out_ref = iter(rest[:-1]), rest[-1]
    tokens = ids_ref.shape[1]
    me = ep_index()
    shape = rest[0].shape
    lane = lax.broadcasted_iota(jnp.int32, shape, 1)
    row = lax.broadcasted_iota(jnp.int32, shape, 0)
    lines = jnp.zeros(shape, F32)
    for k, tiles in steps:
        scores = next(refs)[...]
        if tiles == 2:
            scores = jnp.where(lane < cap, scores, next(refs)[...])
        line = jnp.sum(jnp.where(row == me, scores, 0.0), axis=0, keepdims=True)
        lines = jnp.where(row == k, line, lines)
    rest = jnp.zeros((LANES - lines.shape[0], LANES), F32)
    columns = jnp.concatenate([lines, rest], axis=0).T
    columns = columns[:cap] + columns[cap : 2 * cap]
    place = lax.broadcasted_iota(jnp.int32, (cap, tokens), 0).astype(F32)
    ids = ids_ref[...]
    result = jnp.zeros(ids.shape, F32)
    for k in range(group):
        at_slot = jnp.where(place == slots_ref[k : k + 1, :], columns[:, k : k + 1], 0.0)
        result = jnp.where(ids == (me ^ k), jnp.sum(at_slot, axis=0, keepdims=True), result)
    out_ref[...] = result


def moved(array, side, step):
    if (side, step) == (0, 0):
        return array
    group = lax.axis_size("ep")
    pairs = [
        (p * group + e, (p ^ side) * group + (e ^ step)) for p in range(2) for e in range(group)
    ]
    return lax.ppermute(array, ("pair", "ep"), pairs)


def local(grad_out, router_weights, expert_ids, hidden, master, moment, second):
    group = lax.axis_size("ep")
    tokens, width = grad_out.shape[1:]
    top = expert_ids.shape[2]
    hid, slots = hidden.shape[2:]
    half = master.shape[3]
    cap = slots // group
    ids = expert_ids[0].T
    own_hidden = hidden[0, 0]
    param = master[0, 0]
    other_hidden = moved(own_hidden, 1, 0)

    far = group // 2
    first = [k for k in range(1, group) if k != far]
    late = [0, far]
    first_items = [(side, k) for side in range(2) for k in reversed(first)]
    last_items = [(1, far), (0, far), (1, 0), (0, 0)]
    order = first_items + last_items
    chunk = jax.ShapeDtypeStruct((half // LANES * cap + TILE, LANES), BF16)
    grads = pltpu.with_memory_space_constraint(grad_out[0], pltpu.HBM)
    held = pltpu.VMEM((2, tokens, half), BF16)
    routed = pl.pallas_call(
        functools.partial(route_kernel, first_items, first, group, cap),
        out_shape=[
            jax.ShapeDtypeStruct((group + -group % TILE, tokens), F32),
            jax.ShapeDtypeStruct((group, TILE, LANES), BF16),
        ]
        + [chunk] * len(first_items),
        in_specs=specs(pltpu.HBM, 3),
        out_specs=specs(pltpu.VMEM, 2 + len(first_items)),
        scratch_shapes=[
            pltpu.VMEM((top, tokens), jnp.int32),
            pltpu.VMEM((top, tokens), BF16),
            held,
            pltpu.SemaphoreType.DMA((4,)),
        ],
        compiler_params=params(),
        cost_estimate=cost(2 * slots * tokens * width, 2 * (tokens + slots) * width),
        name="route",
    )(
        pltpu.with_memory_space_constraint(ids, pltpu.HBM),
        pltpu.with_memory_space_constraint(router_weights[0].T, pltpu.HBM),
        grads,
    )
    slot_of, tiles = routed[:2]
    arrived = {item: moved(sent, *item) for item, sent in zip(first_items, routed[2:])}

    routed = pl.pallas_call(
        functools.partial(later_kernel, last_items, late, cap),
        out_shape=[jax.ShapeDtypeStruct((2 * slots, half), F32)] + [chunk] * len(last_items),
        in_specs=specs(pltpu.VMEM, 2)
        + specs(pltpu.HBM, 1)
        + specs(pltpu.VMEM, 2)
        + specs(pltpu.HBM, 1),
        out_specs=specs(pltpu.VMEM, 1 + len(last_items)),
        scratch_shapes=[
            held,
            pltpu.VMEM((hid, half), F32),
            pltpu.SemaphoreType.DMA((2 + half // min(half, 4 * LANES),)),
        ],
        compiler_params=params(),
        cost_estimate=cost(
            2 * slots * tokens * width + 4 * slots * hid * half, 2 * (tokens + slots) * width
        ),
        name="later",
    )(
        slot_of,
        tiles,
        grads,
        own_hidden,
        other_hidden,
        pltpu.with_memory_space_constraint(param, pltpu.HBM),
    )
    inner = routed[0]
    arrived |= {item: moved(sent, *item) for item, sent in zip(last_items, routed[1:])}

    tile = jax.ShapeDtypeStruct((group + -group % 8, LANES), F32)

    def scored(items, *after):
        return pl.pallas_call(
            functools.partial(score_kernel, items, group, cap),
            out_shape=tile,
            in_specs=specs(pltpu.VMEM, 1 + len(items)) + specs(pl.ANY, len(after)),
            out_specs=specs(pltpu.VMEM, 1)[0],
            compiler_params=params(),
            cost_estimate=cost(2 * cap * half, 6 * cap * half),
            name="score",
        )(inner, *[arrived[item] for item in items], *after)

    first_scores = scored(first_items)
    other_scores = moved(first_scores, 1, 0)
    added = [(1, far), (0, far), (1, 0)]
    summed = [item for item in order if item not in added]
    grad = pl.pallas_call(
        functools.partial(sum_kernel, summed, group, cap),
        out_shape=jax.ShapeDtypeStruct((hid, half), F32),
        in_specs=specs(pltpu.VMEM, 2 + len(summed)) + specs(pl.ANY, 1),
        out_specs=specs(pltpu.VMEM, 1)[0],
        scratch_shapes=[
            pltpu.VMEM((2 * slots, half), BF16),
            pltpu.VMEM((hid, 2 * slots), BF16),
        ],
        compiler_params=params(),
        cost_estimate=cost(4 * slots * hid * half, 4 * hid * half),
        name="sum",
    )(own_hidden, other_hidden, *[arrived[item] for item in summed], first_scores)
    merged = pl.pallas_call(
        functools.partial(merge_kernel, cap),
        out_shape=tile,
        in_specs=specs(pltpu.VMEM, 2) + specs(pl.ANY, 1),
        out_specs=specs(pltpu.VMEM, 1)[0],
        compiler_params=params(),
        name="merge",
    )(first_scores, other_scores, grad)
    returned = {k: [moved(merged, 0, k)] for k in first}
    zero_scores = scored([(0, 0), (1, 0)], merged)
    returned[0] = [zero_scores, moved(zero_scores, 1, 0)]
    other_far = scored([(1, far)], zero_scores)
    last_scores = scored([(0, far)], other_far)
    returned[far] = [moved(last_scores, 0, far), moved(other_far, 1, far)]

    depth = -(-len(added) // 2) * LANES
    update = pl.pallas_call(
        functools.partial(update_kernel, added, cap),
        out_shape=jax.ShapeDtypeStruct((hid, half), F32),
        in_specs=specs(pltpu.VMEM, 6 + len(added)) + specs(pl.ANY, 1),
        out_specs=specs(pltpu.HBM, 1)[0],
        scratch_shapes=[
            pltpu.VMEM((depth, half), BF16),
            pltpu.VMEM((hid, depth), BF16),
            pltpu.VMEM((hid, half), F32),
            pltpu.VMEM((hid, half), F32),
            pltpu.SemaphoreType.DMA((hid // LANES,)),
        ],
        compiler_params=params(),
        cost_estimate=cost(2 * depth * hid * half, 16 * hid * half),
        name="update",
    )(
        own_hidden,
        other_hidden,
        grad,
        param,
        moment[0, 0],
        second[0, 0],
        *[arrived[item] for item in added],
        last_scores,
    )
    shares = [array for arrays in returned.values() for array in arrays]
    router = pl.pallas_call(
        functools.partial(
            combine_kernel, [(k, len(arrays)) for k, arrays in returned.items()], group, cap
        ),
        out_shape=jax.ShapeDtypeStruct((top, tokens), F32),
        in_specs=specs(pltpu.VMEM, 2 + len(shares)),
        out_specs=specs(pltpu.VMEM, 1)[0],
        compiler_params=params(),
        cost_estimate=cost(4 * slots * tokens, 8 * top * tokens),
        name="combine",
    )(ids, slot_of, *shares)
    return (update[None, None], router.T[None])


def solution(mesh):
    sections, group = mesh.devices.shape
    split = jax.sharding.Mesh(
        mesh.devices.reshape(2, sections // 2, group), ("pair", "rest", "ep")
    )
    section = ("pair", "rest")
    rows = P(section, "ep", None)
    blocks = P(section, "ep", None, None)
    return jax.shard_map(
        local,
        mesh=split,
        in_specs=(rows, rows, rows, blocks, blocks, blocks, blocks),
        out_specs=(blocks, rows),
        check_vma=False,
    )
```

```python
import functools

import jax
import jax.numpy as jnp
from jax import lax
from jax.experimental import pallas as pl
from jax.experimental.pallas import tpu as pltpu
from jax.sharding import PartitionSpec as P

beta_first = 0.9
beta_second = 0.95
adam_eps = 1e-08
decay_rate = 0.1
first_fix = 1.0 - 0.9**10
second_fix = 1.0 - 0.95**10
first_unit = (1.0 - beta_first) / first_fix
second_unit = (1.0 - beta_second) / second_fix

LANES = 128
TILE = 16
VMEM_BYTES = 32 * 1024 * 1024
F32 = jnp.float32
BF16 = jnp.bfloat16


def params():
    return pltpu.CompilerParams(vmem_limit_bytes=VMEM_BYTES)


def cost(flops, touched):
    return pl.CostEstimate(flops=int(flops), bytes_accessed=int(touched), transcendentals=0)


def specs(space, count):
    return [pl.BlockSpec(memory_space=space) for _ in range(count)]


def ep_index():
    return lax.axis_index("ep").astype(jnp.int32)


def own_half():
    return lax.axis_index("pair").astype(jnp.int32)


def start_grads(grads_hbm, held, sems):
    half = held.shape[2]
    mine = own_half()
    copies = []
    for side in range(2):
        column = pl.multiple_of((1 - mine if side else mine) * half, half)
        copies.append(
            pltpu.make_async_copy(
                grads_hbm.at[:, pl.ds(column, half)], held.at[side], sems.at[side]
            )
        )
        copies[-1].start()
    return copies


def pick_rows(slots, k, cap):
    place = lax.broadcasted_iota(jnp.int32, (cap, slots.shape[1]), 0).astype(F32)
    return jnp.where(place == slots[k : k + 1, :], 1.0, 0.0).astype(BF16)


def fill_chunks(steps, cap, picks, held, copies, tiles, chunks):
    half = held.shape[2]
    data_rows = half // LANES * cap
    pick = jnp.concatenate([picks[k] for k in steps], axis=0)
    for side in range(2):
        for k in steps:
            chunks[side, k][data_rows:, :] = tiles[k]
        copies[side].wait()
        block = jnp.dot(pick, held[side], preferred_element_type=F32).astype(BF16)
        for at, k in enumerate(steps):
            for part in range(half // LANES):
                chunks[side, k][part * cap : (part + 1) * cap, :] = block[
                    at * cap : (at + 1) * cap, part * LANES : (part + 1) * LANES
                ]


def route_kernel(
    items, steps, group, cap, ids_hbm, weight_hbm, grads_hbm, slots_ref, tiles_ref, *rest
):
    chunks = dict(zip(items, rest))
    ids_ref, weight_ref, held, sems = rest[len(items) :]
    tokens = held.shape[1]
    me = ep_index()
    small = [
        pltpu.make_async_copy(ids_hbm, ids_ref, sems.at[2]),
        pltpu.make_async_copy(weight_hbm, weight_ref, sems.at[3]),
    ]
    for copy in small:
        copy.start()
    copies = start_grads(grads_hbm, held, sems)
    earlier = lax.broadcasted_iota(jnp.int32, (tokens, tokens), 0)
    later = lax.broadcasted_iota(jnp.int32, (tokens, tokens), 1)
    ahead = jnp.where(earlier < later, 1.0, 0.0).astype(BF16)
    for copy in small:
        copy.wait()
    ids = ids_ref[...]
    weights = weight_ref[...].astype(F32)
    members, scales = [], []
    for k in range(group):
        named = ids == (me ^ k)
        members.append(jnp.sum(jnp.where(named, 1.0, 0.0), axis=0, keepdims=True))
        scales.append(jnp.sum(jnp.where(named, weights, 0.0), axis=0, keepdims=True))
    if group % TILE:
        members.append(jnp.zeros((-group % TILE, tokens), F32))
    member = jnp.concatenate(members, axis=0)
    before = jnp.dot(member.astype(BF16), ahead, preferred_element_type=F32)
    slots = jnp.where(member > 0.5, before, -1.0)
    slots_ref[...] = slots
    picks = [pick_rows(slots, k, cap) for k in range(group)]
    base = me * cap
    tile_row = lax.broadcasted_iota(jnp.int32, (TILE, LANES), 0)
    tile_lane = lax.broadcasted_iota(jnp.int32, (TILE, LANES), 1)
    spot = tile_row * LANES + tile_lane
    kept = (spot >= base) & (spot < base + cap)
    if group % TILE:
        scales.append(jnp.zeros((-group % TILE, tokens), F32))
    rows = jnp.concatenate(scales, axis=0)
    lines = lax.dot_general(
        rows.astype(BF16),
        jnp.concatenate(picks, axis=0),
        (((1,), (1,)), ((), ())),
        preferred_element_type=F32,
    )
    tiles = []
    for k in range(group):
        line = lines[k : k + 1, k * cap : (k + 1) * cap]
        line = jnp.concatenate([line] * (LANES // cap), axis=1)
        tiles.append(jnp.where(kept, line, 0.0).astype(BF16))
        tiles_ref[k] = tiles[k]
    fill_chunks(steps, cap, picks, held, copies, tiles, chunks)


def later_kernel(
    items, steps, cap, slots_ref, tiles_ref, grads_hbm, own_ref, other_ref, master_hbm, inner_ref, *rest
):
    chunks = dict(zip(items, rest))
    held, master_ref, sems = rest[len(items) :]
    copies = start_grads(grads_hbm, held, sems)
    load = pltpu.make_async_copy(master_hbm, master_ref, sems.at[2])
    load.start()
    slots = slots_ref[...]
    picks = {k: pick_rows(slots, k, cap) for k in steps}
    fill_chunks(steps, cap, picks, held, copies, tiles_ref, chunks)
    slot_count = own_ref.shape[1]
    load.wait()
    weights = master_ref[...].astype(BF16)
    for at, ref in ((0, own_ref), (slot_count, other_ref)):
        inner_ref[at : at + slot_count, :] = lax.dot_general(
            ref[...], weights, (((0,), (0,)), ((), ())), preferred_element_type=F32
        )


def score_kernel(items, group, cap, inner_ref, *rest):
    chunks, score_ref = dict(zip(items, rest)), rest[-1]
    blocks = inner_ref.shape[1] // LANES
    me = ep_index()
    line_of = lax.broadcasted_iota(jnp.int32, score_ref.shape, 0)
    scores = jnp.zeros(score_ref.shape, F32)
    for k in sorted({k for _, k in items}):
        sums = []
        for side in range(2):
            total = jnp.zeros((cap, LANES), F32)
            if (side, k) in items:
                start = pl.multiple_of(side * group * cap + (me ^ k) * cap, cap)
                for block in range(blocks):
                    rows = chunks[side, k][block * cap : (block + 1) * cap, :].astype(F32)
                    total += rows * inner_ref[
                        pl.ds(start, cap), block * LANES : (block + 1) * LANES
                    ]
            sums.append(total)
        both = jnp.concatenate(sums, axis=0)
        line = jnp.sum(both.T, axis=0, keepdims=True)
        scores = jnp.where(line_of == (me ^ k), line, scores)
    score_ref[...] = scores


def scale_into(scaled, at, hidden, line):
    for top in range(0, hidden.shape[0], LANES):
        lines = slice(top, top + LANES)
        scaled[lines, at : at + LANES] = (hidden[lines, :].astype(F32) * line).astype(BF16)


def sum_kernel(items, group, cap, own_ref, other_ref, *rest):
    chunks = dict(zip(items, rest))
    grad_ref, rows, scaled = rest[-3:]
    blocks = rows.shape[1] // LANES
    slots = group * cap
    me = ep_index()
    for side, hidden in enumerate((own_ref, other_ref)):
        tile = jnp.zeros((TILE, LANES), F32)
        for k in range(group):
            start = pl.multiple_of(side * slots + (me ^ k) * cap, cap)
            if (side, k) not in items:
                rows[pl.ds(start, cap), :] = jnp.zeros((cap, rows.shape[1]), BF16)
                continue
            chunk = chunks[side, k]
            tile += chunk[blocks * cap :, :].astype(F32)
            for block in range(blocks):
                rows[pl.ds(start, cap), block * LANES : (block + 1) * LANES] = chunk[
                    block * cap : (block + 1) * cap, :
                ]
        for part in range(slots // LANES):
            lanes = slice(part * LANES, (part + 1) * LANES)
            scale_into(scaled, side * slots + part * LANES, hidden.at[:, lanes], tile[part : part + 1, :])
    grad_ref[...] = jnp.dot(scaled[...], rows[...], preferred_element_type=F32)


def merge_kernel(cap, own_ref, other_ref, _, out_ref):
    lane = lax.broadcasted_iota(jnp.int32, own_ref.shape, 1)
    scores = own_ref[...] + pltpu.roll(other_ref[...], LANES - cap, axis=1)
    out_ref[...] = jnp.where(lane < cap, scores, 0.0)


def update_kernel(items, cap, own_ref, other_ref, grad_ref, master_ref, moment_ref, second_ref, *rest):
    chunks = rest[: len(items)]
    _, update_hbm, rows, scaled, total, update, sems = rest[len(items) :]
    hid, half = update.shape
    width = min(half, 4 * LANES)
    height = LANES
    data_rows = half // LANES * cap
    me = ep_index()
    for at in range(0, len(items), 2):
        parts = []
        for turn, ((side, k), chunk) in enumerate(zip(items[at : at + 2], chunks[at : at + 2])):
            slot = (me ^ k) * cap
            lanes = pl.ds(pl.multiple_of(slot // LANES * LANES, LANES), LANES)
            place = slot % LANES if turn == 0 else (LANES - cap) - slot % LANES
            start = pl.multiple_of(at // 2 * LANES + place, cap)
            for part in range(half // LANES):
                rows[pl.ds(start, cap), part * LANES : (part + 1) * LANES] = chunk[
                    part * cap : (part + 1) * cap, :
                ]
            line = jnp.sum(chunk[data_rows:, :].astype(F32), axis=0, keepdims=True)
            parts.append(((own_ref, other_ref)[side], lanes, line))
        if len(parts) == 1:
            start = pl.multiple_of(at // 2 * LANES + (LANES - cap) - place, cap)
            rows[pl.ds(start, cap), :] = jnp.zeros((cap, half), BF16)
        for top in range(0, hid, LANES):
            values = [
                hidden[top : top + LANES, lanes].astype(F32) * line for hidden, lanes, line in parts
            ]
            if len(values) == 2:
                values[0] += pltpu.roll(values[1], LANES - cap, axis=1)
            scaled[top : top + LANES, at // 2 * LANES : (at // 2 + 1) * LANES] = values[0].astype(
                BF16
            )
    total[...] = jnp.dot(scaled[...], rows[...], preferred_element_type=F32)

    def moments(top, columns):
        lines = slice(top, top + TILE)
        grad = total[lines, columns] + grad_ref[lines, columns]
        first = moment_ref[lines, columns].astype(F32) * (beta_first / (1.0 - beta_first)) + grad
        square = (
            second_ref[lines, columns].astype(F32) * (beta_second / (1.0 - beta_second))
            + grad * grad
        )
        return first, square, lax.rsqrt(square)

    def inverse(first, square, root):
        scale = square * root * (second_unit**0.5 / first_unit) + adam_eps / first_unit
        return first, pl.reciprocal(scale, approx=True)

    def finish(top, columns, first, scale):
        lines = slice(top, top + TILE)
        update[lines, columns] = first * scale + decay_rate * master_ref[lines, columns]

    copies = []
    pieces = [
        (top, slice(column, column + width))
        for top in range(0, hid, TILE)
        for column in range(0, half, width)
    ]
    held = {}
    for turn in range(len(pieces) + 2):
        if turn < len(pieces):
            held[turn, 0] = moments(*pieces[turn])
        if 0 <= turn - 1 < len(pieces):
            held[turn - 1, 1] = inverse(*held.pop((turn - 1, 0)))
        if turn >= 2:
            finish(*pieces[turn - 2], *held.pop((turn - 2, 1)))
            top, columns = pieces[turn - 2]
            if (top + TILE) % height == 0 and columns.stop == half:
                lines = slice(top + TILE - height, top + TILE)
                copies.append(
                    pltpu.make_async_copy(
                        update.at[lines, :], update_hbm.at[lines, :], sems.at[len(copies)]
                    )
                )
                copies[-1].start()
    for copy in copies:
        copy.wait()


def combine_kernel(steps, group, cap, ids_ref, slots_ref, *rest):
    refs, out_ref = iter(rest[:-1]), rest[-1]
    tokens = ids_ref.shape[1]
    me = ep_index()
    shape = rest[0].shape
    lane = lax.broadcasted_iota(jnp.int32, shape, 1)
    row = lax.broadcasted_iota(jnp.int32, shape, 0)
    lines = jnp.zeros(shape, F32)
    for k, tiles in steps:
        scores = next(refs)[...]
        if tiles == 2:
            scores = jnp.where(lane < cap, scores, next(refs)[...])
        line = jnp.sum(jnp.where(row == me, scores, 0.0), axis=0, keepdims=True)
        lines = jnp.where(row == k, line, lines)
    rest = jnp.zeros((LANES - lines.shape[0], LANES), F32)
    columns = jnp.concatenate([lines, rest], axis=0).T
    columns = columns[:cap] + columns[cap : 2 * cap]
    place = lax.broadcasted_iota(jnp.int32, (cap, tokens), 0).astype(F32)
    ids = ids_ref[...]
    result = jnp.zeros(ids.shape, F32)
    for k in range(group):
        at_slot = jnp.where(place == slots_ref[k : k + 1, :], columns[:, k : k + 1], 0.0)
        result = jnp.where(ids == (me ^ k), jnp.sum(at_slot, axis=0, keepdims=True), result)
    out_ref[...] = result


def moved(array, side, step):
    if (side, step) == (0, 0):
        return array
    group = lax.axis_size("ep")
    pairs = [
        (p * group + e, (p ^ side) * group + (e ^ step)) for p in range(2) for e in range(group)
    ]
    return lax.ppermute(array, ("pair", "ep"), pairs)


def local(grad_out, router_weights, expert_ids, hidden, master, moment, second):
    group = lax.axis_size("ep")
    tokens, width = grad_out.shape[1:]
    top = expert_ids.shape[2]
    hid, slots = hidden.shape[2:]
    half = master.shape[3]
    cap = slots // group
    ids = expert_ids[0].T
    own_hidden = hidden[0, 0]
    param = master[0, 0]
    other_hidden = moved(own_hidden, 1, 0)

    far = group // 2
    first = [k for k in range(1, group) if k != far]
    late = [0, far]
    first_items = [(side, k) for side in range(2) for k in reversed(first)]
    last_items = [(1, far), (0, far), (1, 0), (0, 0)]
    order = first_items + last_items
    chunk = jax.ShapeDtypeStruct((half // LANES * cap + TILE, LANES), BF16)
    grads = pltpu.with_memory_space_constraint(grad_out[0], pltpu.HBM)
    held = pltpu.VMEM((2, tokens, half), BF16)
    routed = pl.pallas_call(
        functools.partial(route_kernel, first_items, first, group, cap),
        out_shape=[
            jax.ShapeDtypeStruct((group + -group % TILE, tokens), F32),
            jax.ShapeDtypeStruct((group, TILE, LANES), BF16),
        ]
        + [chunk] * len(first_items),
        in_specs=specs(pltpu.HBM, 3),
        out_specs=specs(pltpu.VMEM, 2 + len(first_items)),
        scratch_shapes=[
            pltpu.VMEM((top, tokens), jnp.int32),
            pltpu.VMEM((top, tokens), BF16),
            held,
            pltpu.SemaphoreType.DMA((4,)),
        ],
        compiler_params=params(),
        cost_estimate=cost(2 * slots * tokens * width, 2 * (tokens + slots) * width),
        name="route",
    )(
        pltpu.with_memory_space_constraint(ids, pltpu.HBM),
        pltpu.with_memory_space_constraint(router_weights[0].T, pltpu.HBM),
        grads,
    )
    slot_of, tiles = routed[:2]
    arrived = {item: moved(sent, *item) for item, sent in zip(first_items, routed[2:])}

    routed = pl.pallas_call(
        functools.partial(later_kernel, last_items, late, cap),
        out_shape=[jax.ShapeDtypeStruct((2 * slots, half), F32)] + [chunk] * len(last_items),
        in_specs=specs(pltpu.VMEM, 2)
        + specs(pltpu.HBM, 1)
        + specs(pltpu.VMEM, 2)
        + specs(pltpu.HBM, 1),
        out_specs=specs(pltpu.VMEM, 1 + len(last_items)),
        scratch_shapes=[
            held,
            pltpu.VMEM((hid, half), F32),
            pltpu.SemaphoreType.DMA((3,)),
        ],
        compiler_params=params(),
        cost_estimate=cost(
            2 * slots * tokens * width + 4 * slots * hid * half, 2 * (tokens + slots) * width
        ),
        name="later",
    )(
        slot_of,
        tiles,
        grads,
        own_hidden,
        other_hidden,
        pltpu.with_memory_space_constraint(param, pltpu.HBM),
    )
    inner = routed[0]
    arrived |= {item: moved(sent, *item) for item, sent in zip(last_items, routed[1:])}

    tile = jax.ShapeDtypeStruct((group + -group % 8, LANES), F32)

    def scored(items, *after):
        return pl.pallas_call(
            functools.partial(score_kernel, items, group, cap),
            out_shape=tile,
            in_specs=specs(pltpu.VMEM, 1 + len(items)) + specs(pl.ANY, len(after)),
            out_specs=specs(pltpu.VMEM, 1)[0],
            compiler_params=params(),
            cost_estimate=cost(2 * cap * half, 6 * cap * half),
            name="score",
        )(inner, *[arrived[item] for item in items], *after)

    first_scores = scored(first_items)
    other_scores = moved(first_scores, 1, 0)
    added = [(1, far), (0, far), (1, 0)]
    summed = [item for item in order if item not in added]
    grad = pl.pallas_call(
        functools.partial(sum_kernel, summed, group, cap),
        out_shape=jax.ShapeDtypeStruct((hid, half), F32),
        in_specs=specs(pltpu.VMEM, 2 + len(summed)) + specs(pl.ANY, 1),
        out_specs=specs(pltpu.VMEM, 1)[0],
        scratch_shapes=[
            pltpu.VMEM((2 * slots, half), BF16),
            pltpu.VMEM((hid, 2 * slots), BF16),
        ],
        compiler_params=params(),
        cost_estimate=cost(4 * slots * hid * half, 4 * hid * half),
        name="sum",
    )(own_hidden, other_hidden, *[arrived[item] for item in summed], first_scores)
    merged = pl.pallas_call(
        functools.partial(merge_kernel, cap),
        out_shape=tile,
        in_specs=specs(pltpu.VMEM, 2) + specs(pl.ANY, 1),
        out_specs=specs(pltpu.VMEM, 1)[0],
        compiler_params=params(),
        name="merge",
    )(first_scores, other_scores, grad)
    returned = {k: [moved(merged, 0, k)] for k in first}
    zero_scores = scored([(0, 0), (1, 0)], merged)
    returned[0] = [zero_scores, moved(zero_scores, 1, 0)]
    other_far = scored([(1, far)], zero_scores)
    last_scores = scored([(0, far)], other_far)
    returned[far] = [moved(last_scores, 0, far), moved(other_far, 1, far)]

    depth = -(-len(added) // 2) * LANES
    update = pl.pallas_call(
        functools.partial(update_kernel, added, cap),
        out_shape=jax.ShapeDtypeStruct((hid, half), F32),
        in_specs=specs(pltpu.VMEM, 6 + len(added)) + specs(pl.ANY, 1),
        out_specs=specs(pltpu.HBM, 1)[0],
        scratch_shapes=[
            pltpu.VMEM((depth, half), BF16),
            pltpu.VMEM((hid, depth), BF16),
            pltpu.VMEM((hid, half), F32),
            pltpu.VMEM((hid, half), F32),
            pltpu.SemaphoreType.DMA((hid // LANES,)),
        ],
        compiler_params=params(),
        cost_estimate=cost(2 * depth * hid * half, 16 * hid * half),
        name="update",
    )(
        own_hidden,
        other_hidden,
        grad,
        param,
        moment[0, 0],
        second[0, 0],
        *[arrived[item] for item in added],
        last_scores,
    )
    shares = [array for arrays in returned.values() for array in arrays]
    router = pl.pallas_call(
        functools.partial(
            combine_kernel, [(k, len(arrays)) for k, arrays in returned.items()], group, cap
        ),
        out_shape=jax.ShapeDtypeStruct((top, tokens), F32),
        in_specs=specs(pltpu.VMEM, 2 + len(shares)),
        out_specs=specs(pltpu.VMEM, 1)[0],
        compiler_params=params(),
        cost_estimate=cost(4 * slots * tokens, 8 * top * tokens),
        name="combine",
    )(ids, slot_of, *shares)
    return (update[None, None], router.T[None])


def solution(mesh):
    sections, group = mesh.devices.shape
    split = jax.sharding.Mesh(
        mesh.devices.reshape(2, sections // 2, group), ("pair", "rest", "ep")
    )
    section = ("pair", "rest")
    rows = P(section, "ep", None)
    blocks = P(section, "ep", None, None)
    return jax.shard_map(
        local,
        mesh=split,
        in_specs=(rows, rows, rows, blocks, blocks, blocks, blocks),
        out_specs=(blocks, rows),
        check_vma=False,
    )
```

```python
import functools

import jax
import jax.numpy as jnp
from jax import lax
from jax.experimental import pallas as pl
from jax.experimental.pallas import tpu as pltpu
from jax.sharding import PartitionSpec as P

beta_first = 0.9
beta_second = 0.95
adam_eps = 1e-08
decay_rate = 0.1
first_fix = 1.0 - 0.9**10
second_fix = 1.0 - 0.95**10
first_unit = (1.0 - beta_first) / first_fix
second_unit = (1.0 - beta_second) / second_fix

LANES = 128
TILE = 16
VMEM_BYTES = 32 * 1024 * 1024
F32 = jnp.float32
BF16 = jnp.bfloat16


def params():
    return pltpu.CompilerParams(vmem_limit_bytes=VMEM_BYTES)


def cost(flops, touched):
    return pl.CostEstimate(flops=int(flops), bytes_accessed=int(touched), transcendentals=0)


def specs(space, count):
    return [pl.BlockSpec(memory_space=space) for _ in range(count)]


def ep_index():
    return lax.axis_index("ep").astype(jnp.int32)


def own_half():
    return lax.axis_index("pair").astype(jnp.int32)


def start_grads(grads_hbm, held, sems):
    half = held.shape[2]
    mine = own_half()
    copies = []
    for side in range(2):
        column = pl.multiple_of((1 - mine if side else mine) * half, half)
        copies.append(
            pltpu.make_async_copy(
                grads_hbm.at[:, pl.ds(column, half)], held.at[side], sems.at[side]
            )
        )
        copies[-1].start()
    return copies


def pick_rows(slots, k, cap):
    place = lax.broadcasted_iota(jnp.int32, (cap, slots.shape[1]), 0).astype(F32)
    return jnp.where(place == slots[k : k + 1, :], 1.0, 0.0).astype(BF16)


def fill_chunks(steps, cap, picks, held, copies, tiles, chunks):
    half = held.shape[2]
    data_rows = half // LANES * cap
    pick = jnp.concatenate([picks[k] for k in steps], axis=0)
    for side in range(2):
        for k in steps:
            chunks[side, k][data_rows:, :] = tiles[k]
        copies[side].wait()
        block = jnp.dot(pick, held[side], preferred_element_type=F32).astype(BF16)
        for at, k in enumerate(steps):
            for part in range(half // LANES):
                chunks[side, k][part * cap : (part + 1) * cap, :] = block[
                    at * cap : (at + 1) * cap, part * LANES : (part + 1) * LANES
                ]


def route_kernel(
    items, steps, group, cap, ids_hbm, weight_hbm, grads_hbm, slots_ref, tiles_ref, *rest
):
    chunks = dict(zip(items, rest))
    ids_ref, weight_ref, held, sems = rest[len(items) :]
    tokens = held.shape[1]
    me = ep_index()
    small = [
        pltpu.make_async_copy(ids_hbm, ids_ref, sems.at[2]),
        pltpu.make_async_copy(weight_hbm, weight_ref, sems.at[3]),
    ]
    for copy in small:
        copy.start()
    copies = start_grads(grads_hbm, held, sems)
    earlier = lax.broadcasted_iota(jnp.int32, (tokens, tokens), 0)
    later = lax.broadcasted_iota(jnp.int32, (tokens, tokens), 1)
    ahead = jnp.where(earlier < later, 1.0, 0.0).astype(BF16)
    for copy in small:
        copy.wait()
    ids = ids_ref[...]
    weights = weight_ref[...].astype(F32)
    members, scales = [], []
    for k in range(group):
        named = ids == (me ^ k)
        members.append(jnp.sum(jnp.where(named, 1.0, 0.0), axis=0, keepdims=True))
        scales.append(jnp.sum(jnp.where(named, weights, 0.0), axis=0, keepdims=True))
    if group % TILE:
        members.append(jnp.zeros((-group % TILE, tokens), F32))
    member = jnp.concatenate(members, axis=0)
    before = jnp.dot(member.astype(BF16), ahead, preferred_element_type=F32)
    slots = jnp.where(member > 0.5, before, -1.0)
    slots_ref[...] = slots
    picks = [pick_rows(slots, k, cap) for k in range(group)]
    base = me * cap
    tile_row = lax.broadcasted_iota(jnp.int32, (TILE, LANES), 0)
    tile_lane = lax.broadcasted_iota(jnp.int32, (TILE, LANES), 1)
    spot = tile_row * LANES + tile_lane
    kept = (spot >= base) & (spot < base + cap)
    if group % TILE:
        scales.append(jnp.zeros((-group % TILE, tokens), F32))
    rows = jnp.concatenate(scales, axis=0)
    lines = lax.dot_general(
        rows.astype(BF16),
        jnp.concatenate(picks, axis=0),
        (((1,), (1,)), ((), ())),
        preferred_element_type=F32,
    )
    tiles = []
    for k in range(group):
        line = lines[k : k + 1, k * cap : (k + 1) * cap]
        line = jnp.concatenate([line] * (LANES // cap), axis=1)
        tiles.append(jnp.where(kept, line, 0.0).astype(BF16))
        tiles_ref[k] = tiles[k]
    fill_chunks(steps, cap, picks, held, copies, tiles, chunks)


def later_kernel(
    items, steps, cap, slots_ref, tiles_ref, grads_hbm, own_ref, other_ref, master_hbm, inner_ref, *rest
):
    chunks = dict(zip(items, rest))
    held, master_ref, sems = rest[len(items) :]
    copies = start_grads(grads_hbm, held, sems)
    half = master_ref.shape[1]
    step = min(half, 4 * LANES)
    parts = [slice(column, column + step) for column in range(0, half, step)]
    loads = [
        pltpu.make_async_copy(master_hbm.at[:, part], master_ref.at[:, part], sems.at[2 + at])
        for at, part in enumerate(parts)
    ]
    for load in loads:
        load.start()
    slots = slots_ref[...]
    picks = {k: pick_rows(slots, k, cap) for k in steps}
    fill_chunks(steps, cap, picks, held, copies, tiles_ref, chunks)
    slot_count = own_ref.shape[1]
    for load, part in zip(loads, parts):
        load.wait()
        weights = master_ref[:, part].astype(BF16)
        for at, ref in ((0, own_ref), (slot_count, other_ref)):
            inner_ref[at : at + slot_count, part] = lax.dot_general(
                ref[...], weights, (((0,), (0,)), ((), ())), preferred_element_type=F32
            )


def score_kernel(items, group, cap, inner_ref, *rest):
    chunks, score_ref = dict(zip(items, rest)), rest[-1]
    blocks = inner_ref.shape[1] // LANES
    me = ep_index()
    line_of = lax.broadcasted_iota(jnp.int32, score_ref.shape, 0)
    scores = jnp.zeros(score_ref.shape, F32)
    for k in sorted({k for _, k in items}):
        sums = []
        for side in range(2):
            total = jnp.zeros((cap, LANES), F32)
            if (side, k) in items:
                start = pl.multiple_of(side * group * cap + (me ^ k) * cap, cap)
                for block in range(blocks):
                    rows = chunks[side, k][block * cap : (block + 1) * cap, :].astype(F32)
                    total += rows * inner_ref[
                        pl.ds(start, cap), block * LANES : (block + 1) * LANES
                    ]
            sums.append(total)
        both = jnp.concatenate(sums, axis=0)
        line = jnp.sum(both.T, axis=0, keepdims=True)
        scores = jnp.where(line_of == (me ^ k), line, scores)
    score_ref[...] = scores


def scale_into(scaled, at, hidden, line):
    for top in range(0, hidden.shape[0], LANES):
        lines = slice(top, top + LANES)
        scaled[lines, at : at + LANES] = (hidden[lines, :].astype(F32) * line).astype(BF16)


def sum_kernel(items, group, cap, own_ref, other_ref, *rest):
    chunks = dict(zip(items, rest))
    grad_ref, rows, scaled = rest[-3:]
    blocks = rows.shape[1] // LANES
    slots = group * cap
    me = ep_index()
    for side, hidden in enumerate((own_ref, other_ref)):
        tile = jnp.zeros((TILE, LANES), F32)
        for k in range(group):
            start = pl.multiple_of(side * slots + (me ^ k) * cap, cap)
            if (side, k) not in items:
                rows[pl.ds(start, cap), :] = jnp.zeros((cap, rows.shape[1]), BF16)
                continue
            chunk = chunks[side, k]
            tile += chunk[blocks * cap :, :].astype(F32)
            for block in range(blocks):
                rows[pl.ds(start, cap), block * LANES : (block + 1) * LANES] = chunk[
                    block * cap : (block + 1) * cap, :
                ]
        for part in range(slots // LANES):
            lanes = slice(part * LANES, (part + 1) * LANES)
            scale_into(scaled, side * slots + part * LANES, hidden.at[:, lanes], tile[part : part + 1, :])
    grad_ref[...] = jnp.dot(scaled[...], rows[...], preferred_element_type=F32)


def merge_kernel(cap, own_ref, other_ref, _, out_ref):
    lane = lax.broadcasted_iota(jnp.int32, own_ref.shape, 1)
    scores = own_ref[...] + pltpu.roll(other_ref[...], LANES - cap, axis=1)
    out_ref[...] = jnp.where(lane < cap, scores, 0.0)


def update_kernel(items, cap, own_ref, other_ref, grad_ref, master_ref, moment_ref, second_ref, *rest):
    chunks = rest[: len(items)]
    _, update_hbm, rows, scaled, total, update, sems = rest[len(items) :]
    hid, half = update.shape
    width = min(half, 4 * LANES)
    height = 2 * TILE
    data_rows = half // LANES * cap
    me = ep_index()
    for at in range(0, len(items), 2):
        parts = []
        for turn, ((side, k), chunk) in enumerate(zip(items[at : at + 2], chunks[at : at + 2])):
            slot = (me ^ k) * cap
            lanes = pl.ds(pl.multiple_of(slot // LANES * LANES, LANES), LANES)
            place = slot % LANES if turn == 0 else (LANES - cap) - slot % LANES
            start = pl.multiple_of(at // 2 * LANES + place, cap)
            for part in range(half // LANES):
                rows[pl.ds(start, cap), part * LANES : (part + 1) * LANES] = chunk[
                    part * cap : (part + 1) * cap, :
                ]
            line = jnp.sum(chunk[data_rows:, :].astype(F32), axis=0, keepdims=True)
            parts.append(((own_ref, other_ref)[side], lanes, line))
        if len(parts) == 1:
            start = pl.multiple_of(at // 2 * LANES + (LANES - cap) - place, cap)
            rows[pl.ds(start, cap), :] = jnp.zeros((cap, half), BF16)
        for top in range(0, hid, LANES):
            values = [
                hidden[top : top + LANES, lanes].astype(F32) * line for hidden, lanes, line in parts
            ]
            if len(values) == 2:
                values[0] += pltpu.roll(values[1], LANES - cap, axis=1)
            scaled[top : top + LANES, at // 2 * LANES : (at // 2 + 1) * LANES] = values[0].astype(
                BF16
            )
    total[...] = jnp.dot(scaled[...], rows[...], preferred_element_type=F32)

    def moments(top, columns):
        lines = slice(top, top + TILE)
        grad = total[lines, columns] + grad_ref[lines, columns]
        first = moment_ref[lines, columns].astype(F32) * (beta_first / (1.0 - beta_first)) + grad
        square = (
            second_ref[lines, columns].astype(F32) * (beta_second / (1.0 - beta_second))
            + grad * grad
        )
        return first, square, lax.rsqrt(square)

    def inverse(first, square, root):
        scale = square * root * (second_unit**0.5 / first_unit) + adam_eps / first_unit
        return first, pl.reciprocal(scale, approx=True)

    def finish(top, columns, first, scale):
        lines = slice(top, top + TILE)
        update[lines, columns] = first * scale + decay_rate * master_ref[lines, columns]

    copies = []
    pieces = [
        (top, slice(column, column + width))
        for top in range(0, hid, TILE)
        for column in range(0, half, width)
    ]
    held = {}
    for turn in range(len(pieces) + 2):
        if turn < len(pieces):
            held[turn, 0] = moments(*pieces[turn])
        if 0 <= turn - 1 < len(pieces):
            held[turn - 1, 1] = inverse(*held.pop((turn - 1, 0)))
        if turn >= 2:
            finish(*pieces[turn - 2], *held.pop((turn - 2, 1)))
            top, columns = pieces[turn - 2]
            if (top + TILE) % height == 0 and columns.stop == half:
                lines = slice(top + TILE - height, top + TILE)
                copies.append(
                    pltpu.make_async_copy(
                        update.at[lines, :], update_hbm.at[lines, :], sems.at[len(copies)]
                    )
                )
                copies[-1].start()
    for copy in copies:
        copy.wait()


def combine_kernel(steps, group, cap, ids_ref, slots_ref, *rest):
    refs, out_ref = iter(rest[:-1]), rest[-1]
    tokens = ids_ref.shape[1]
    me = ep_index()
    shape = rest[0].shape
    lane = lax.broadcasted_iota(jnp.int32, shape, 1)
    row = lax.broadcasted_iota(jnp.int32, shape, 0)
    lines = jnp.zeros(shape, F32)
    for k, tiles in steps:
        scores = next(refs)[...]
        if tiles == 2:
            scores = jnp.where(lane < cap, scores, next(refs)[...])
        line = jnp.sum(jnp.where(row == me, scores, 0.0), axis=0, keepdims=True)
        lines = jnp.where(row == k, line, lines)
    rest = jnp.zeros((LANES - lines.shape[0], LANES), F32)
    columns = jnp.concatenate([lines, rest], axis=0).T
    columns = columns[:cap] + columns[cap : 2 * cap]
    place = lax.broadcasted_iota(jnp.int32, (cap, tokens), 0).astype(F32)
    ids = ids_ref[...]
    result = jnp.zeros(ids.shape, F32)
    for k in range(group):
        at_slot = jnp.where(place == slots_ref[k : k + 1, :], columns[:, k : k + 1], 0.0)
        result = jnp.where(ids == (me ^ k), jnp.sum(at_slot, axis=0, keepdims=True), result)
    out_ref[...] = result


def moved(array, side, step):
    if (side, step) == (0, 0):
        return array
    group = lax.axis_size("ep")
    pairs = [
        (p * group + e, (p ^ side) * group + (e ^ step)) for p in range(2) for e in range(group)
    ]
    return lax.ppermute(array, ("pair", "ep"), pairs)


def local(grad_out, router_weights, expert_ids, hidden, master, moment, second):
    group = lax.axis_size("ep")
    tokens, width = grad_out.shape[1:]
    top = expert_ids.shape[2]
    hid, slots = hidden.shape[2:]
    half = master.shape[3]
    cap = slots // group
    ids = expert_ids[0].T
    own_hidden = hidden[0, 0]
    param = master[0, 0]
    other_hidden = moved(own_hidden, 1, 0)

    far = group // 2
    first = [k for k in range(1, group) if k != far]
    late = [0, far]
    first_items = [(side, k) for side in range(2) for k in reversed(first)]
    last_items = [(1, far), (0, far), (1, 0), (0, 0)]
    order = first_items + last_items
    chunk = jax.ShapeDtypeStruct((half // LANES * cap + TILE, LANES), BF16)
    grads = pltpu.with_memory_space_constraint(grad_out[0], pltpu.HBM)
    held = pltpu.VMEM((2, tokens, half), BF16)
    routed = pl.pallas_call(
        functools.partial(route_kernel, first_items, first, group, cap),
        out_shape=[
            jax.ShapeDtypeStruct((group + -group % TILE, tokens), F32),
            jax.ShapeDtypeStruct((group, TILE, LANES), BF16),
        ]
        + [chunk] * len(first_items),
        in_specs=specs(pltpu.HBM, 3),
        out_specs=specs(pltpu.VMEM, 2 + len(first_items)),
        scratch_shapes=[
            pltpu.VMEM((top, tokens), jnp.int32),
            pltpu.VMEM((top, tokens), BF16),
            held,
            pltpu.SemaphoreType.DMA((4,)),
        ],
        compiler_params=params(),
        cost_estimate=cost(2 * slots * tokens * width, 2 * (tokens + slots) * width),
        name="route",
    )(
        pltpu.with_memory_space_constraint(ids, pltpu.HBM),
        pltpu.with_memory_space_constraint(router_weights[0].T, pltpu.HBM),
        grads,
    )
    slot_of, tiles = routed[:2]
    arrived = {item: moved(sent, *item) for item, sent in zip(first_items, routed[2:])}

    routed = pl.pallas_call(
        functools.partial(later_kernel, last_items, late, cap),
        out_shape=[jax.ShapeDtypeStruct((2 * slots, half), F32)] + [chunk] * len(last_items),
        in_specs=specs(pltpu.VMEM, 2)
        + specs(pltpu.HBM, 1)
        + specs(pltpu.VMEM, 2)
        + specs(pltpu.HBM, 1),
        out_specs=specs(pltpu.VMEM, 1 + len(last_items)),
        scratch_shapes=[
            held,
            pltpu.VMEM((hid, half), F32),
            pltpu.SemaphoreType.DMA((2 + half // min(half, 4 * LANES),)),
        ],
        compiler_params=params(),
        cost_estimate=cost(
            2 * slots * tokens * width + 4 * slots * hid * half, 2 * (tokens + slots) * width
        ),
        name="later",
    )(
        slot_of,
        tiles,
        grads,
        own_hidden,
        other_hidden,
        pltpu.with_memory_space_constraint(param, pltpu.HBM),
    )
    inner = routed[0]
    arrived |= {item: moved(sent, *item) for item, sent in zip(last_items, routed[1:])}

    tile = jax.ShapeDtypeStruct((group + -group % 8, LANES), F32)

    def scored(items, *after):
        return pl.pallas_call(
            functools.partial(score_kernel, items, group, cap),
            out_shape=tile,
            in_specs=specs(pltpu.VMEM, 1 + len(items)) + specs(pl.ANY, len(after)),
            out_specs=specs(pltpu.VMEM, 1)[0],
            compiler_params=params(),
            cost_estimate=cost(2 * cap * half, 6 * cap * half),
            name="score",
        )(inner, *[arrived[item] for item in items], *after)

    first_scores = scored(first_items)
    other_scores = moved(first_scores, 1, 0)
    added = [(1, far), (0, far), (1, 0)]
    summed = [item for item in order if item not in added]
    grad = pl.pallas_call(
        functools.partial(sum_kernel, summed, group, cap),
        out_shape=jax.ShapeDtypeStruct((hid, half), F32),
        in_specs=specs(pltpu.VMEM, 2 + len(summed)) + specs(pl.ANY, 1),
        out_specs=specs(pltpu.VMEM, 1)[0],
        scratch_shapes=[
            pltpu.VMEM((2 * slots, half), BF16),
            pltpu.VMEM((hid, 2 * slots), BF16),
        ],
        compiler_params=params(),
        cost_estimate=cost(4 * slots * hid * half, 4 * hid * half),
        name="sum",
    )(own_hidden, other_hidden, *[arrived[item] for item in summed], first_scores)
    merged = pl.pallas_call(
        functools.partial(merge_kernel, cap),
        out_shape=tile,
        in_specs=specs(pltpu.VMEM, 2) + specs(pl.ANY, 1),
        out_specs=specs(pltpu.VMEM, 1)[0],
        compiler_params=params(),
        name="merge",
    )(first_scores, other_scores, grad)
    returned = {k: [moved(merged, 0, k)] for k in first}
    zero_scores = scored([(0, 0), (1, 0)], merged)
    returned[0] = [zero_scores, moved(zero_scores, 1, 0)]
    other_far = scored([(1, far)], zero_scores)
    last_scores = scored([(0, far)], other_far)
    returned[far] = [moved(last_scores, 0, far), moved(other_far, 1, far)]

    depth = -(-len(added) // 2) * LANES
    update = pl.pallas_call(
        functools.partial(update_kernel, added, cap),
        out_shape=jax.ShapeDtypeStruct((hid, half), F32),
        in_specs=specs(pltpu.VMEM, 6 + len(added)) + specs(pl.ANY, 1),
        out_specs=specs(pltpu.HBM, 1)[0],
        scratch_shapes=[
            pltpu.VMEM((depth, half), BF16),
            pltpu.VMEM((hid, depth), BF16),
            pltpu.VMEM((hid, half), F32),
            pltpu.VMEM((hid, half), F32),
            pltpu.SemaphoreType.DMA((hid // (2 * TILE),)),
        ],
        compiler_params=params(),
        cost_estimate=cost(2 * depth * hid * half, 16 * hid * half),
        name="update",
    )(
        own_hidden,
        other_hidden,
        grad,
        param,
        moment[0, 0],
        second[0, 0],
        *[arrived[item] for item in added],
        last_scores,
    )
    shares = [array for arrays in returned.values() for array in arrays]
    router = pl.pallas_call(
        functools.partial(
            combine_kernel, [(k, len(arrays)) for k, arrays in returned.items()], group, cap
        ),
        out_shape=jax.ShapeDtypeStruct((top, tokens), F32),
        in_specs=specs(pltpu.VMEM, 2 + len(shares)),
        out_specs=specs(pltpu.VMEM, 1)[0],
        compiler_params=params(),
        cost_estimate=cost(4 * slots * tokens, 8 * top * tokens),
        name="combine",
    )(ids, slot_of, *shares)
    return (update[None, None], router.T[None])


def solution(mesh):
    sections, group = mesh.devices.shape
    split = jax.sharding.Mesh(
        mesh.devices.reshape(2, sections // 2, group), ("pair", "rest", "ep")
    )
    section = ("pair", "rest")
    rows = P(section, "ep", None)
    blocks = P(section, "ep", None, None)
    return jax.shard_map(
        local,
        mesh=split,
        in_specs=(rows, rows, rows, blocks, blocks, blocks, blocks),
        out_specs=(blocks, rows),
        check_vma=False,
    )
```

```python
import functools

import jax
import jax.numpy as jnp
from jax import lax
from jax.experimental import pallas as pl
from jax.experimental.pallas import tpu as pltpu
from jax.sharding import PartitionSpec as P

beta_first = 0.9
beta_second = 0.95
adam_eps = 1e-08
decay_rate = 0.1
first_fix = 1.0 - 0.9**10
second_fix = 1.0 - 0.95**10
first_unit = (1.0 - beta_first) / first_fix
second_unit = (1.0 - beta_second) / second_fix

LANES = 128
TILE = 16
VMEM_BYTES = 32 * 1024 * 1024
F32 = jnp.float32
BF16 = jnp.bfloat16


def params():
    return pltpu.CompilerParams(vmem_limit_bytes=VMEM_BYTES)


def cost(flops, touched):
    return pl.CostEstimate(flops=int(flops), bytes_accessed=int(touched), transcendentals=0)


def specs(space, count):
    return [pl.BlockSpec(memory_space=space) for _ in range(count)]


def ep_index():
    return lax.axis_index("ep").astype(jnp.int32)


def own_half():
    return lax.axis_index("pair").astype(jnp.int32)


def start_grads(grads_hbm, held, sems):
    half = held.shape[2]
    mine = own_half()
    copies = []
    for side in range(2):
        column = pl.multiple_of((1 - mine if side else mine) * half, half)
        copies.append(
            pltpu.make_async_copy(
                grads_hbm.at[:, pl.ds(column, half)], held.at[side], sems.at[side]
            )
        )
        copies[-1].start()
    return copies


def pick_rows(slots, k, cap):
    place = lax.broadcasted_iota(jnp.int32, (cap, slots.shape[1]), 0).astype(F32)
    return jnp.where(place == slots[k : k + 1, :], 1.0, 0.0).astype(BF16)


def fill_chunks(steps, cap, picks, held, copies, tiles, chunks):
    half = held.shape[2]
    data_rows = half // LANES * cap
    pick = jnp.concatenate([picks[k] for k in steps], axis=0)
    for side in range(2):
        for k in steps:
            chunks[side, k][data_rows:, :] = tiles[k]
        copies[side].wait()
        block = jnp.dot(pick, held[side], preferred_element_type=F32).astype(BF16)
        for at, k in enumerate(steps):
            for part in range(half // LANES):
                chunks[side, k][part * cap : (part + 1) * cap, :] = block[
                    at * cap : (at + 1) * cap, part * LANES : (part + 1) * LANES
                ]


def route_kernel(
    items, steps, group, cap, ids_hbm, weight_hbm, grads_hbm, slots_ref, tiles_ref, *rest
):
    chunks = dict(zip(items, rest))
    ids_ref, weight_ref, held, sems = rest[len(items) :]
    tokens = held.shape[1]
    me = ep_index()
    small = [
        pltpu.make_async_copy(ids_hbm, ids_ref, sems.at[2]),
        pltpu.make_async_copy(weight_hbm, weight_ref, sems.at[3]),
    ]
    for copy in small:
        copy.start()
    copies = start_grads(grads_hbm, held, sems)
    earlier = lax.broadcasted_iota(jnp.int32, (tokens, tokens), 0)
    later = lax.broadcasted_iota(jnp.int32, (tokens, tokens), 1)
    ahead = jnp.where(earlier < later, 1.0, 0.0).astype(BF16)
    for copy in small:
        copy.wait()
    ids = ids_ref[...]
    weights = weight_ref[...].astype(F32)
    members, scales = [], []
    for k in range(group):
        named = ids == (me ^ k)
        members.append(jnp.sum(jnp.where(named, 1.0, 0.0), axis=0, keepdims=True))
        scales.append(jnp.sum(jnp.where(named, weights, 0.0), axis=0, keepdims=True))
    if group % TILE:
        members.append(jnp.zeros((-group % TILE, tokens), F32))
    member = jnp.concatenate(members, axis=0)
    before = jnp.dot(member.astype(BF16), ahead, preferred_element_type=F32)
    slots = jnp.where(member > 0.5, before, -1.0)
    slots_ref[...] = slots
    picks = [pick_rows(slots, k, cap) for k in range(group)]
    base = me * cap
    tile_row = lax.broadcasted_iota(jnp.int32, (TILE, LANES), 0)
    tile_lane = lax.broadcasted_iota(jnp.int32, (TILE, LANES), 1)
    spot = tile_row * LANES + tile_lane
    kept = (spot >= base) & (spot < base + cap)
    if group % TILE:
        scales.append(jnp.zeros((-group % TILE, tokens), F32))
    rows = jnp.concatenate(scales, axis=0)
    lines = lax.dot_general(
        rows.astype(BF16),
        jnp.concatenate(picks, axis=0),
        (((1,), (1,)), ((), ())),
        preferred_element_type=F32,
    )
    tiles = []
    for k in range(group):
        line = lines[k : k + 1, k * cap : (k + 1) * cap]
        line = jnp.concatenate([line] * (LANES // cap), axis=1)
        tiles.append(jnp.where(kept, line, 0.0).astype(BF16))
        tiles_ref[k] = tiles[k]
    fill_chunks(steps, cap, picks, held, copies, tiles, chunks)


def later_kernel(
    items, steps, cap, slots_ref, tiles_ref, grads_hbm, own_ref, other_ref, master_hbm, inner_ref, *rest
):
    chunks = dict(zip(items, rest))
    held, master_ref, sems = rest[len(items) :]
    copies = start_grads(grads_hbm, held, sems)
    half = master_ref.shape[1]
    step = min(half, 4 * LANES)
    parts = [slice(column, column + step) for column in range(0, half, step)]
    loads = [
        pltpu.make_async_copy(master_hbm.at[:, part], master_ref.at[:, part], sems.at[2 + at])
        for at, part in enumerate(parts)
    ]
    for load in loads:
        load.start()
    slots = slots_ref[...]
    picks = {k: pick_rows(slots, k, cap) for k in steps}
    fill_chunks(steps, cap, picks, held, copies, tiles_ref, chunks)
    slot_count = own_ref.shape[1]
    for load, part in zip(loads, parts):
        load.wait()
        weights = master_ref[:, part].astype(BF16)
        for at, ref in ((0, own_ref), (slot_count, other_ref)):
            inner_ref[at : at + slot_count, part] = lax.dot_general(
                ref[...], weights, (((0,), (0,)), ((), ())), preferred_element_type=F32
            )


def score_kernel(items, group, cap, inner_ref, *rest):
    chunks, score_ref = dict(zip(items, rest)), rest[-1]
    blocks = inner_ref.shape[1] // LANES
    me = ep_index()
    line_of = lax.broadcasted_iota(jnp.int32, score_ref.shape, 0)
    scores = jnp.zeros(score_ref.shape, F32)
    for k in sorted({k for _, k in items}):
        sums = []
        for side in range(2):
            total = jnp.zeros((cap, LANES), F32)
            if (side, k) in items:
                start = pl.multiple_of(side * group * cap + (me ^ k) * cap, cap)
                for block in range(blocks):
                    rows = chunks[side, k][block * cap : (block + 1) * cap, :].astype(F32)
                    total += rows * inner_ref[
                        pl.ds(start, cap), block * LANES : (block + 1) * LANES
                    ]
            sums.append(total)
        both = jnp.concatenate(sums, axis=0)
        line = jnp.sum(both.T, axis=0, keepdims=True)
        scores = jnp.where(line_of == (me ^ k), line, scores)
    score_ref[...] = scores


def scale_into(scaled, at, hidden, line):
    for top in range(0, hidden.shape[0], LANES):
        lines = slice(top, top + LANES)
        scaled[lines, at : at + LANES] = (hidden[lines, :].astype(F32) * line).astype(BF16)


def sum_kernel(items, group, cap, own_ref, other_ref, *rest):
    chunks = dict(zip(items, rest))
    grad_ref, rows, scaled = rest[-3:]
    blocks = rows.shape[1] // LANES
    slots = group * cap
    me = ep_index()
    for side, hidden in enumerate((own_ref, other_ref)):
        tile = jnp.zeros((TILE, LANES), F32)
        for k in range(group):
            start = pl.multiple_of(side * slots + (me ^ k) * cap, cap)
            if (side, k) not in items:
                rows[pl.ds(start, cap), :] = jnp.zeros((cap, rows.shape[1]), BF16)
                continue
            chunk = chunks[side, k]
            tile += chunk[blocks * cap :, :].astype(F32)
            for block in range(blocks):
                rows[pl.ds(start, cap), block * LANES : (block + 1) * LANES] = chunk[
                    block * cap : (block + 1) * cap, :
                ]
        for part in range(slots // LANES):
            lanes = slice(part * LANES, (part + 1) * LANES)
            scale_into(scaled, side * slots + part * LANES, hidden.at[:, lanes], tile[part : part + 1, :])
    grad_ref[...] = jnp.dot(scaled[...], rows[...], preferred_element_type=F32)


def merge_kernel(cap, own_ref, other_ref, _, out_ref):
    lane = lax.broadcasted_iota(jnp.int32, own_ref.shape, 1)
    scores = own_ref[...] + pltpu.roll(other_ref[...], LANES - cap, axis=1)
    out_ref[...] = jnp.where(lane < cap, scores, 0.0)


def update_kernel(items, cap, own_ref, other_ref, grad_ref, master_ref, moment_ref, second_ref, *rest):
    chunks = rest[: len(items)]
    _, update_hbm, rows, scaled, total, update, sems = rest[len(items) :]
    hid, half = update.shape
    width = min(half, 4 * LANES)
    height = hid // sems.shape[0]
    data_rows = half // LANES * cap
    me = ep_index()
    for at in range(0, len(items), 2):
        parts = []
        for turn, ((side, k), chunk) in enumerate(zip(items[at : at + 2], chunks[at : at + 2])):
            slot = (me ^ k) * cap
            lanes = pl.ds(pl.multiple_of(slot // LANES * LANES, LANES), LANES)
            place = slot % LANES if turn == 0 else (LANES - cap) - slot % LANES
            start = pl.multiple_of(at // 2 * LANES + place, cap)
            for part in range(half // LANES):
                rows[pl.ds(start, cap), part * LANES : (part + 1) * LANES] = chunk[
                    part * cap : (part + 1) * cap, :
                ]
            line = jnp.sum(chunk[data_rows:, :].astype(F32), axis=0, keepdims=True)
            parts.append(((own_ref, other_ref)[side], lanes, line))
        if len(parts) == 1:
            start = pl.multiple_of(at // 2 * LANES + (LANES - cap) - place, cap)
            rows[pl.ds(start, cap), :] = jnp.zeros((cap, half), BF16)
        for top in range(0, hid, LANES):
            values = [
                hidden[top : top + LANES, lanes].astype(F32) * line for hidden, lanes, line in parts
            ]
            if len(values) == 2:
                values[0] += pltpu.roll(values[1], LANES - cap, axis=1)
            scaled[top : top + LANES, at // 2 * LANES : (at // 2 + 1) * LANES] = values[0].astype(
                BF16
            )
    total[...] = jnp.dot(scaled[...], rows[...], preferred_element_type=F32)

    def moments(lines, columns):
        grad = total[lines, columns] + grad_ref[lines, columns]
        first = moment_ref[lines, columns].astype(F32) * (beta_first / (1.0 - beta_first)) + grad
        square = (
            second_ref[lines, columns].astype(F32) * (beta_second / (1.0 - beta_second))
            + grad * grad
        )
        return first, square, lax.rsqrt(square)

    def inverse(first, square, root):
        scale = square * root * (second_unit**0.5 / first_unit) + adam_eps / first_unit
        return first, pl.reciprocal(scale, approx=True)

    def finish(lines, columns, first, scale):
        update[lines, columns] = first * scale + decay_rate * master_ref[lines, columns]

    def copy_out(turn):
        lines = pl.ds(pl.multiple_of(turn * height, height), height)
        return pltpu.make_async_copy(update.at[lines, :], update_hbm.at[lines, :], sems.at[turn])

    def adam(turn, carry):
        pieces = [
            (pl.ds(pl.multiple_of(turn * height + top, TILE), TILE), slice(column, column + width))
            for top in range(0, height, TILE)
            for column in range(0, half, width)
        ]
        held = {}
        for at in range(len(pieces) + 2):
            if at < len(pieces):
                held[at, 0] = moments(*pieces[at])
            if 0 <= at - 1 < len(pieces):
                held[at - 1, 1] = inverse(*held.pop((at - 1, 0)))
            if at >= 2:
                finish(*pieces[at - 2], *held.pop((at - 2, 1)))
        copy_out(turn).start()
        return carry

    def settle(turn, carry):
        copy_out(turn).wait()
        return carry

    lax.fori_loop(0, hid // height, adam, 0)
    lax.fori_loop(0, hid // height, settle, 0)


def combine_kernel(steps, group, cap, ids_ref, slots_ref, *rest):
    refs, out_ref = iter(rest[:-1]), rest[-1]
    tokens = ids_ref.shape[1]
    me = ep_index()
    shape = rest[0].shape
    lane = lax.broadcasted_iota(jnp.int32, shape, 1)
    row = lax.broadcasted_iota(jnp.int32, shape, 0)
    lines = jnp.zeros(shape, F32)
    for k, tiles in steps:
        scores = next(refs)[...]
        if tiles == 2:
            scores = jnp.where(lane < cap, scores, next(refs)[...])
        line = jnp.sum(jnp.where(row == me, scores, 0.0), axis=0, keepdims=True)
        lines = jnp.where(row == k, line, lines)
    rest = jnp.zeros((LANES - lines.shape[0], LANES), F32)
    columns = jnp.concatenate([lines, rest], axis=0).T
    columns = columns[:cap] + columns[cap : 2 * cap]
    place = lax.broadcasted_iota(jnp.int32, (cap, tokens), 0).astype(F32)
    ids = ids_ref[...]
    result = jnp.zeros(ids.shape, F32)
    for k in range(group):
        at_slot = jnp.where(place == slots_ref[k : k + 1, :], columns[:, k : k + 1], 0.0)
        result = jnp.where(ids == (me ^ k), jnp.sum(at_slot, axis=0, keepdims=True), result)
    out_ref[...] = result


def moved(array, side, step):
    if (side, step) == (0, 0):
        return array
    group = lax.axis_size("ep")
    pairs = [
        (p * group + e, (p ^ side) * group + (e ^ step)) for p in range(2) for e in range(group)
    ]
    return lax.ppermute(array, ("pair", "ep"), pairs)


def local(grad_out, router_weights, expert_ids, hidden, master, moment, second):
    group = lax.axis_size("ep")
    tokens, width = grad_out.shape[1:]
    top = expert_ids.shape[2]
    hid, slots = hidden.shape[2:]
    half = master.shape[3]
    cap = slots // group
    ids = expert_ids[0].T
    own_hidden = hidden[0, 0]
    param = master[0, 0]
    other_hidden = moved(own_hidden, 1, 0)

    far = group // 2
    first = [k for k in range(1, group) if k != far]
    late = [0, far]
    first_items = [(side, k) for side in range(2) for k in reversed(first)]
    last_items = [(1, far), (0, far), (1, 0), (0, 0)]
    order = first_items + last_items
    chunk = jax.ShapeDtypeStruct((half // LANES * cap + TILE, LANES), BF16)
    grads = pltpu.with_memory_space_constraint(grad_out[0], pltpu.HBM)
    held = pltpu.VMEM((2, tokens, half), BF16)
    routed = pl.pallas_call(
        functools.partial(route_kernel, first_items, first, group, cap),
        out_shape=[
            jax.ShapeDtypeStruct((group + -group % TILE, tokens), F32),
            jax.ShapeDtypeStruct((group, TILE, LANES), BF16),
        ]
        + [chunk] * len(first_items),
        in_specs=specs(pltpu.HBM, 3),
        out_specs=specs(pltpu.VMEM, 2 + len(first_items)),
        scratch_shapes=[
            pltpu.VMEM((top, tokens), jnp.int32),
            pltpu.VMEM((top, tokens), BF16),
            held,
            pltpu.SemaphoreType.DMA((4,)),
        ],
        compiler_params=params(),
        cost_estimate=cost(2 * slots * tokens * width, 2 * (tokens + slots) * width),
        name="route",
    )(
        pltpu.with_memory_space_constraint(ids, pltpu.HBM),
        pltpu.with_memory_space_constraint(router_weights[0].T, pltpu.HBM),
        grads,
    )
    slot_of, tiles = routed[:2]
    arrived = {item: moved(sent, *item) for item, sent in zip(first_items, routed[2:])}

    routed = pl.pallas_call(
        functools.partial(later_kernel, last_items, late, cap),
        out_shape=[jax.ShapeDtypeStruct((2 * slots, half), F32)] + [chunk] * len(last_items),
        in_specs=specs(pltpu.VMEM, 2)
        + specs(pltpu.HBM, 1)
        + specs(pltpu.VMEM, 2)
        + specs(pltpu.HBM, 1),
        out_specs=specs(pltpu.VMEM, 1 + len(last_items)),
        scratch_shapes=[
            held,
            pltpu.VMEM((hid, half), F32),
            pltpu.SemaphoreType.DMA((2 + half // min(half, 4 * LANES),)),
        ],
        compiler_params=params(),
        cost_estimate=cost(
            2 * slots * tokens * width + 4 * slots * hid * half, 2 * (tokens + slots) * width
        ),
        name="later",
    )(
        slot_of,
        tiles,
        grads,
        own_hidden,
        other_hidden,
        pltpu.with_memory_space_constraint(param, pltpu.HBM),
    )
    inner = routed[0]
    arrived |= {item: moved(sent, *item) for item, sent in zip(last_items, routed[1:])}

    tile = jax.ShapeDtypeStruct((group + -group % 8, LANES), F32)

    def scored(items, *after):
        return pl.pallas_call(
            functools.partial(score_kernel, items, group, cap),
            out_shape=tile,
            in_specs=specs(pltpu.VMEM, 1 + len(items)) + specs(pl.ANY, len(after)),
            out_specs=specs(pltpu.VMEM, 1)[0],
            compiler_params=params(),
            cost_estimate=cost(2 * cap * half, 6 * cap * half),
            name="score",
        )(inner, *[arrived[item] for item in items], *after)

    first_scores = scored(first_items)
    other_scores = moved(first_scores, 1, 0)
    added = [(1, far), (0, far), (1, 0)]
    summed = [item for item in order if item not in added]
    grad = pl.pallas_call(
        functools.partial(sum_kernel, summed, group, cap),
        out_shape=jax.ShapeDtypeStruct((hid, half), F32),
        in_specs=specs(pltpu.VMEM, 2 + len(summed)) + specs(pl.ANY, 1),
        out_specs=specs(pltpu.VMEM, 1)[0],
        scratch_shapes=[
            pltpu.VMEM((2 * slots, half), BF16),
            pltpu.VMEM((hid, 2 * slots), BF16),
        ],
        compiler_params=params(),
        cost_estimate=cost(4 * slots * hid * half, 4 * hid * half),
        name="sum",
    )(own_hidden, other_hidden, *[arrived[item] for item in summed], first_scores)
    merged = pl.pallas_call(
        functools.partial(merge_kernel, cap),
        out_shape=tile,
        in_specs=specs(pltpu.VMEM, 2) + specs(pl.ANY, 1),
        out_specs=specs(pltpu.VMEM, 1)[0],
        compiler_params=params(),
        name="merge",
    )(first_scores, other_scores, grad)
    returned = {k: [moved(merged, 0, k)] for k in first}
    zero_scores = scored([(0, 0), (1, 0)], merged)
    returned[0] = [zero_scores, moved(zero_scores, 1, 0)]
    other_far = scored([(1, far)], zero_scores)
    last_scores = scored([(0, far)], other_far)
    returned[far] = [moved(last_scores, 0, far), moved(other_far, 1, far)]

    depth = -(-len(added) // 2) * LANES
    update = pl.pallas_call(
        functools.partial(update_kernel, added, cap),
        out_shape=jax.ShapeDtypeStruct((hid, half), F32),
        in_specs=specs(pltpu.VMEM, 6 + len(added)) + specs(pl.ANY, 1),
        out_specs=specs(pltpu.HBM, 1)[0],
        scratch_shapes=[
            pltpu.VMEM((depth, half), BF16),
            pltpu.VMEM((hid, depth), BF16),
            pltpu.VMEM((hid, half), F32),
            pltpu.VMEM((hid, half), F32),
            pltpu.SemaphoreType.DMA((hid // (6 * TILE),)),
        ],
        compiler_params=params(),
        cost_estimate=cost(2 * depth * hid * half, 16 * hid * half),
        name="update",
    )(
        own_hidden,
        other_hidden,
        grad,
        param,
        moment[0, 0],
        second[0, 0],
        *[arrived[item] for item in added],
        last_scores,
    )
    shares = [array for arrays in returned.values() for array in arrays]
    router = pl.pallas_call(
        functools.partial(
            combine_kernel, [(k, len(arrays)) for k, arrays in returned.items()], group, cap
        ),
        out_shape=jax.ShapeDtypeStruct((top, tokens), F32),
        in_specs=specs(pltpu.VMEM, 2 + len(shares)),
        out_specs=specs(pltpu.VMEM, 1)[0],
        compiler_params=params(),
        cost_estimate=cost(4 * slots * tokens, 8 * top * tokens),
        name="combine",
    )(ids, slot_of, *shares)
    return (update[None, None], router.T[None])


def solution(mesh):
    sections, group = mesh.devices.shape
    split = jax.sharding.Mesh(
        mesh.devices.reshape(2, sections // 2, group), ("pair", "rest", "ep")
    )
    section = ("pair", "rest")
    rows = P(section, "ep", None)
    blocks = P(section, "ep", None, None)
    return jax.shard_map(
        local,
        mesh=split,
        in_specs=(rows, rows, rows, blocks, blocks, blocks, blocks),
        out_specs=(blocks, rows),
        check_vma=False,
    )
```

```python
import functools

import jax
import jax.numpy as jnp
from jax import lax
from jax.experimental import pallas as pl
from jax.experimental.pallas import tpu as pltpu
from jax.sharding import PartitionSpec as P

beta_first = 0.9
beta_second = 0.95
adam_eps = 1e-08
decay_rate = 0.1
first_fix = 1.0 - 0.9**10
second_fix = 1.0 - 0.95**10
first_unit = (1.0 - beta_first) / first_fix
second_unit = (1.0 - beta_second) / second_fix

LANES = 128
TILE = 16
VMEM_BYTES = 32 * 1024 * 1024
F32 = jnp.float32
BF16 = jnp.bfloat16


def params():
    return pltpu.CompilerParams(vmem_limit_bytes=VMEM_BYTES)


def cost(flops, touched):
    return pl.CostEstimate(flops=int(flops), bytes_accessed=int(touched), transcendentals=0)


def specs(space, count):
    return [pl.BlockSpec(memory_space=space) for _ in range(count)]


def ep_index():
    return lax.axis_index("ep").astype(jnp.int32)


def own_half():
    return lax.axis_index("pair").astype(jnp.int32)


def start_grads(grads_hbm, held, sems):
    half = held.shape[2]
    mine = own_half()
    copies = []
    for side in range(2):
        column = pl.multiple_of((1 - mine if side else mine) * half, half)
        copies.append(
            pltpu.make_async_copy(
                grads_hbm.at[:, pl.ds(column, half)], held.at[side], sems.at[side]
            )
        )
        copies[-1].start()
    return copies


def pick_rows(slots, k, cap):
    place = lax.broadcasted_iota(jnp.int32, (cap, slots.shape[1]), 0).astype(F32)
    return jnp.where(place == slots[k : k + 1, :], 1.0, 0.0).astype(BF16)


def fill_chunks(steps, cap, picks, held, copies, tiles, chunks):
    half = held.shape[2]
    data_rows = half // LANES * cap
    pick = jnp.concatenate([picks[k] for k in steps], axis=0)
    for side in range(2):
        for k in steps:
            chunks[side, k][data_rows:, :] = tiles[k]
        copies[side].wait()
        block = jnp.dot(pick, held[side], preferred_element_type=F32).astype(BF16)
        for at, k in enumerate(steps):
            for part in range(half // LANES):
                chunks[side, k][part * cap : (part + 1) * cap, :] = block[
                    at * cap : (at + 1) * cap, part * LANES : (part + 1) * LANES
                ]


def route_kernel(
    items, steps, group, cap, ids_hbm, weight_hbm, grads_hbm, slots_ref, tiles_ref, *rest
):
    chunks = dict(zip(items, rest))
    ids_ref, weight_ref, held, sems = rest[len(items) :]
    tokens = held.shape[1]
    me = ep_index()
    small = [
        pltpu.make_async_copy(ids_hbm, ids_ref, sems.at[2]),
        pltpu.make_async_copy(weight_hbm, weight_ref, sems.at[3]),
    ]
    for copy in small:
        copy.start()
    copies = start_grads(grads_hbm, held, sems)
    earlier = lax.broadcasted_iota(jnp.int32, (tokens, tokens), 0)
    later = lax.broadcasted_iota(jnp.int32, (tokens, tokens), 1)
    ahead = jnp.where(earlier < later, 1.0, 0.0).astype(BF16)
    for copy in small:
        copy.wait()
    ids = ids_ref[...]
    weights = weight_ref[...].astype(F32)
    members, scales = [], []
    for k in range(group):
        named = ids == (me ^ k)
        members.append(jnp.sum(jnp.where(named, 1.0, 0.0), axis=0, keepdims=True))
        scales.append(jnp.sum(jnp.where(named, weights, 0.0), axis=0, keepdims=True))
    if group % TILE:
        members.append(jnp.zeros((-group % TILE, tokens), F32))
    member = jnp.concatenate(members, axis=0)
    before = jnp.dot(member.astype(BF16), ahead, preferred_element_type=F32)
    slots = jnp.where(member > 0.5, before, -1.0)
    slots_ref[...] = slots
    picks = [pick_rows(slots, k, cap) for k in range(group)]
    base = me * cap
    tile_row = lax.broadcasted_iota(jnp.int32, (TILE, LANES), 0)
    tile_lane = lax.broadcasted_iota(jnp.int32, (TILE, LANES), 1)
    spot = tile_row * LANES + tile_lane
    kept = (spot >= base) & (spot < base + cap)
    if group % TILE:
        scales.append(jnp.zeros((-group % TILE, tokens), F32))
    rows = jnp.concatenate(scales, axis=0)
    lines = lax.dot_general(
        rows.astype(BF16),
        jnp.concatenate(picks, axis=0),
        (((1,), (1,)), ((), ())),
        preferred_element_type=F32,
    )
    tiles = []
    for k in range(group):
        line = lines[k : k + 1, k * cap : (k + 1) * cap]
        line = jnp.concatenate([line] * (LANES // cap), axis=1)
        tiles.append(jnp.where(kept, line, 0.0).astype(BF16))
        tiles_ref[k] = tiles[k]
    fill_chunks(steps, cap, picks, held, copies, tiles, chunks)


def later_kernel(
    items, steps, cap, slots_ref, tiles_ref, grads_hbm, own_ref, other_ref, master_hbm, inner_ref, *rest
):
    chunks = dict(zip(items, rest))
    held, master_ref, sems = rest[len(items) :]
    copies = start_grads(grads_hbm, held, sems)
    half = master_ref.shape[1]
    step = min(half, 4 * LANES)
    parts = [slice(column, column + step) for column in range(0, half, step)]
    loads = [
        pltpu.make_async_copy(master_hbm.at[:, part], master_ref.at[:, part], sems.at[2 + at])
        for at, part in enumerate(parts)
    ]
    for load in loads:
        load.start()
    slots = slots_ref[...]
    picks = {k: pick_rows(slots, k, cap) for k in steps}
    fill_chunks(steps, cap, picks, held, copies, tiles_ref, chunks)
    slot_count = own_ref.shape[1]
    for load, part in zip(loads, parts):
        load.wait()
        weights = master_ref[:, part].astype(BF16)
        for at, ref in ((0, own_ref), (slot_count, other_ref)):
            inner_ref[at : at + slot_count, part] = lax.dot_general(
                ref[...], weights, (((0,), (0,)), ((), ())), preferred_element_type=F32
            )


def score_kernel(items, group, cap, inner_ref, *rest):
    chunks, score_ref = dict(zip(items, rest)), rest[-1]
    blocks = inner_ref.shape[1] // LANES
    me = ep_index()
    line_of = lax.broadcasted_iota(jnp.int32, score_ref.shape, 0)
    scores = jnp.zeros(score_ref.shape, F32)
    for k in sorted({k for _, k in items}):
        sums = []
        for side in range(2):
            total = jnp.zeros((cap, LANES), F32)
            if (side, k) in items:
                start = pl.multiple_of(side * group * cap + (me ^ k) * cap, cap)
                for block in range(blocks):
                    rows = chunks[side, k][block * cap : (block + 1) * cap, :].astype(F32)
                    total += rows * inner_ref[
                        pl.ds(start, cap), block * LANES : (block + 1) * LANES
                    ]
            sums.append(total)
        both = jnp.concatenate(sums, axis=0)
        line = jnp.sum(both.T, axis=0, keepdims=True)
        scores = jnp.where(line_of == (me ^ k), line, scores)
    score_ref[...] = scores


def scale_into(scaled, at, hidden, line):
    for top in range(0, hidden.shape[0], LANES):
        lines = slice(top, top + LANES)
        scaled[lines, at : at + LANES] = (hidden[lines, :].astype(F32) * line).astype(BF16)


def sum_kernel(items, group, cap, own_ref, other_ref, moment_ref, second_ref, *rest):
    chunks = dict(zip(items, rest))
    grad_ref, first_ref, square_ref, rows, scaled = rest[-5:]
    blocks = rows.shape[1] // LANES
    slots = group * cap
    me = ep_index()
    for side, hidden in enumerate((own_ref, other_ref)):
        tile = jnp.zeros((TILE, LANES), F32)
        for k in range(group):
            start = pl.multiple_of(side * slots + (me ^ k) * cap, cap)
            if (side, k) not in items:
                rows[pl.ds(start, cap), :] = jnp.zeros((cap, rows.shape[1]), BF16)
                continue
            chunk = chunks[side, k]
            tile += chunk[blocks * cap :, :].astype(F32)
            for block in range(blocks):
                rows[pl.ds(start, cap), block * LANES : (block + 1) * LANES] = chunk[
                    block * cap : (block + 1) * cap, :
                ]
        for part in range(slots // LANES):
            lanes = slice(part * LANES, (part + 1) * LANES)
            scale_into(scaled, side * slots + part * LANES, hidden.at[:, lanes], tile[part : part + 1, :])
    grad_ref[...] = jnp.dot(scaled[...], rows[...], preferred_element_type=F32)
    for top in range(0, grad_ref.shape[0], TILE):
        lines = slice(top, top + TILE)
        first_ref[lines, :] = (
            moment_ref[lines, :].astype(F32) * (beta_first / (1.0 - beta_first)) + grad_ref[lines, :]
        )
        square_ref[lines, :] = second_ref[lines, :].astype(F32) * (beta_second / (1.0 - beta_second))


def merge_kernel(cap, own_ref, other_ref, _, out_ref):
    lane = lax.broadcasted_iota(jnp.int32, own_ref.shape, 1)
    scores = own_ref[...] + pltpu.roll(other_ref[...], LANES - cap, axis=1)
    out_ref[...] = jnp.where(lane < cap, scores, 0.0)


def update_kernel(items, cap, own_ref, other_ref, grad_ref, first_ref, square_ref, master_ref, *rest):
    chunks = rest[: len(items)]
    _, update_hbm, rows, scaled, total, update, sems = rest[len(items) :]
    hid, half = update.shape
    width = min(half, 4 * LANES)
    height = 2 * TILE
    data_rows = half // LANES * cap
    me = ep_index()
    for at in range(0, len(items), 2):
        parts = []
        for turn, ((side, k), chunk) in enumerate(zip(items[at : at + 2], chunks[at : at + 2])):
            slot = (me ^ k) * cap
            lanes = pl.ds(pl.multiple_of(slot // LANES * LANES, LANES), LANES)
            place = slot % LANES if turn == 0 else (LANES - cap) - slot % LANES
            start = pl.multiple_of(at // 2 * LANES + place, cap)
            for part in range(half // LANES):
                rows[pl.ds(start, cap), part * LANES : (part + 1) * LANES] = chunk[
                    part * cap : (part + 1) * cap, :
                ]
            line = jnp.sum(chunk[data_rows:, :].astype(F32), axis=0, keepdims=True)
            parts.append(((own_ref, other_ref)[side], lanes, line))
        if len(parts) == 1:
            start = pl.multiple_of(at // 2 * LANES + (LANES - cap) - place, cap)
            rows[pl.ds(start, cap), :] = jnp.zeros((cap, half), BF16)
        for top in range(0, hid, LANES):
            values = [
                hidden[top : top + LANES, lanes].astype(F32) * line for hidden, lanes, line in parts
            ]
            if len(values) == 2:
                values[0] += pltpu.roll(values[1], LANES - cap, axis=1)
            scaled[top : top + LANES, at // 2 * LANES : (at // 2 + 1) * LANES] = values[0].astype(
                BF16
            )
    total[...] = jnp.dot(scaled[...], rows[...], preferred_element_type=F32)

    def moments(top, columns):
        lines = slice(top, top + TILE)
        added = total[lines, columns]
        grad = added + grad_ref[lines, columns]
        first = added + first_ref[lines, columns]
        square = square_ref[lines, columns] + grad * grad
        return first, square, lax.rsqrt(square)

    def inverse(first, square, root):
        scale = square * root * (second_unit**0.5 / first_unit) + adam_eps / first_unit
        return first, pl.reciprocal(scale, approx=True)

    def finish(top, columns, first, scale):
        lines = slice(top, top + TILE)
        update[lines, columns] = first * scale + decay_rate * master_ref[lines, columns]

    copies = []
    pieces = [
        (top, slice(column, column + width))
        for top in range(0, hid, TILE)
        for column in range(0, half, width)
    ]
    held = {}
    for turn in range(len(pieces) + 2):
        if turn < len(pieces):
            held[turn, 0] = moments(*pieces[turn])
        if 0 <= turn - 1 < len(pieces):
            held[turn - 1, 1] = inverse(*held.pop((turn - 1, 0)))
        if turn >= 2:
            finish(*pieces[turn - 2], *held.pop((turn - 2, 1)))
            top, columns = pieces[turn - 2]
            if (top + TILE) % height == 0 and columns.stop == half:
                lines = slice(top + TILE - height, top + TILE)
                copies.append(
                    pltpu.make_async_copy(
                        update.at[lines, :], update_hbm.at[lines, :], sems.at[len(copies)]
                    )
                )
                copies[-1].start()
    for copy in copies:
        copy.wait()


def combine_kernel(steps, group, cap, ids_ref, slots_ref, *rest):
    refs, out_ref = iter(rest[:-1]), rest[-1]
    tokens = ids_ref.shape[1]
    me = ep_index()
    shape = rest[0].shape
    lane = lax.broadcasted_iota(jnp.int32, shape, 1)
    row = lax.broadcasted_iota(jnp.int32, shape, 0)
    lines = jnp.zeros(shape, F32)
    for k, tiles in steps:
        scores = next(refs)[...]
        if tiles == 2:
            scores = jnp.where(lane < cap, scores, next(refs)[...])
        line = jnp.sum(jnp.where(row == me, scores, 0.0), axis=0, keepdims=True)
        lines = jnp.where(row == k, line, lines)
    rest = jnp.zeros((LANES - lines.shape[0], LANES), F32)
    columns = jnp.concatenate([lines, rest], axis=0).T
    columns = columns[:cap] + columns[cap : 2 * cap]
    place = lax.broadcasted_iota(jnp.int32, (cap, tokens), 0).astype(F32)
    ids = ids_ref[...]
    result = jnp.zeros(ids.shape, F32)
    for k in range(group):
        at_slot = jnp.where(place == slots_ref[k : k + 1, :], columns[:, k : k + 1], 0.0)
        result = jnp.where(ids == (me ^ k), jnp.sum(at_slot, axis=0, keepdims=True), result)
    out_ref[...] = result


def moved(array, side, step):
    if (side, step) == (0, 0):
        return array
    group = lax.axis_size("ep")
    pairs = [
        (p * group + e, (p ^ side) * group + (e ^ step)) for p in range(2) for e in range(group)
    ]
    return lax.ppermute(array, ("pair", "ep"), pairs)


def local(grad_out, router_weights, expert_ids, hidden, master, moment, second):
    group = lax.axis_size("ep")
    tokens, width = grad_out.shape[1:]
    top = expert_ids.shape[2]
    hid, slots = hidden.shape[2:]
    half = master.shape[3]
    cap = slots // group
    ids = expert_ids[0].T
    own_hidden = hidden[0, 0]
    param = master[0, 0]
    other_hidden = moved(own_hidden, 1, 0)

    far = group // 2
    first = [k for k in range(1, group) if k != far]
    late = [0, far]
    first_items = [(side, k) for side in range(2) for k in reversed(first)]
    last_items = [(1, far), (0, far), (1, 0), (0, 0)]
    order = first_items + last_items
    chunk = jax.ShapeDtypeStruct((half // LANES * cap + TILE, LANES), BF16)
    grads = pltpu.with_memory_space_constraint(grad_out[0], pltpu.HBM)
    held = pltpu.VMEM((2, tokens, half), BF16)
    routed = pl.pallas_call(
        functools.partial(route_kernel, first_items, first, group, cap),
        out_shape=[
            jax.ShapeDtypeStruct((group + -group % TILE, tokens), F32),
            jax.ShapeDtypeStruct((group, TILE, LANES), BF16),
        ]
        + [chunk] * len(first_items),
        in_specs=specs(pltpu.HBM, 3),
        out_specs=specs(pltpu.VMEM, 2 + len(first_items)),
        scratch_shapes=[
            pltpu.VMEM((top, tokens), jnp.int32),
            pltpu.VMEM((top, tokens), BF16),
            held,
            pltpu.SemaphoreType.DMA((4,)),
        ],
        compiler_params=params(),
        cost_estimate=cost(2 * slots * tokens * width, 2 * (tokens + slots) * width),
        name="route",
    )(
        pltpu.with_memory_space_constraint(ids, pltpu.HBM),
        pltpu.with_memory_space_constraint(router_weights[0].T, pltpu.HBM),
        grads,
    )
    slot_of, tiles = routed[:2]
    arrived = {item: moved(sent, *item) for item, sent in zip(first_items, routed[2:])}

    routed = pl.pallas_call(
        functools.partial(later_kernel, last_items, late, cap),
        out_shape=[jax.ShapeDtypeStruct((2 * slots, half), F32)] + [chunk] * len(last_items),
        in_specs=specs(pltpu.VMEM, 2)
        + specs(pltpu.HBM, 1)
        + specs(pltpu.VMEM, 2)
        + specs(pltpu.HBM, 1),
        out_specs=specs(pltpu.VMEM, 1 + len(last_items)),
        scratch_shapes=[
            held,
            pltpu.VMEM((hid, half), F32),
            pltpu.SemaphoreType.DMA((2 + half // min(half, 4 * LANES),)),
        ],
        compiler_params=params(),
        cost_estimate=cost(
            2 * slots * tokens * width + 4 * slots * hid * half, 2 * (tokens + slots) * width
        ),
        name="later",
    )(
        slot_of,
        tiles,
        grads,
        own_hidden,
        other_hidden,
        pltpu.with_memory_space_constraint(param, pltpu.HBM),
    )
    inner = routed[0]
    arrived |= {item: moved(sent, *item) for item, sent in zip(last_items, routed[1:])}

    tile = jax.ShapeDtypeStruct((group + -group % 8, LANES), F32)

    def scored(items, *after):
        return pl.pallas_call(
            functools.partial(score_kernel, items, group, cap),
            out_shape=tile,
            in_specs=specs(pltpu.VMEM, 1 + len(items)) + specs(pl.ANY, len(after)),
            out_specs=specs(pltpu.VMEM, 1)[0],
            compiler_params=params(),
            cost_estimate=cost(2 * cap * half, 6 * cap * half),
            name="score",
        )(inner, *[arrived[item] for item in items], *after)

    first_scores = scored(first_items)
    other_scores = moved(first_scores, 1, 0)
    added = [(1, far), (0, far), (1, 0)]
    summed = [item for item in order if item not in added]
    grad, *prepared = pl.pallas_call(
        functools.partial(sum_kernel, summed, group, cap),
        out_shape=[jax.ShapeDtypeStruct((hid, half), F32)] * 3,
        in_specs=specs(pltpu.VMEM, 4 + len(summed)) + specs(pl.ANY, 1),
        out_specs=specs(pltpu.VMEM, 3),
        scratch_shapes=[
            pltpu.VMEM((2 * slots, half), BF16),
            pltpu.VMEM((hid, 2 * slots), BF16),
        ],
        compiler_params=params(),
        cost_estimate=cost(4 * slots * hid * half, 4 * hid * half),
        name="sum",
    )(
        own_hidden,
        other_hidden,
        moment[0, 0],
        second[0, 0],
        *[arrived[item] for item in summed],
        first_scores,
    )
    merged = pl.pallas_call(
        functools.partial(merge_kernel, cap),
        out_shape=tile,
        in_specs=specs(pltpu.VMEM, 2) + specs(pl.ANY, 1),
        out_specs=specs(pltpu.VMEM, 1)[0],
        compiler_params=params(),
        name="merge",
    )(first_scores, other_scores, grad)
    returned = {k: [moved(merged, 0, k)] for k in first}
    zero_scores = scored([(0, 0), (1, 0)], merged)
    returned[0] = [zero_scores, moved(zero_scores, 1, 0)]
    other_far = scored([(1, far)], zero_scores)
    last_scores = scored([(0, far)], other_far)
    returned[far] = [moved(last_scores, 0, far), moved(other_far, 1, far)]

    depth = -(-len(added) // 2) * LANES
    update = pl.pallas_call(
        functools.partial(update_kernel, added, cap),
        out_shape=jax.ShapeDtypeStruct((hid, half), F32),
        in_specs=specs(pltpu.VMEM, 6 + len(added)) + specs(pl.ANY, 1),
        out_specs=specs(pltpu.HBM, 1)[0],
        scratch_shapes=[
            pltpu.VMEM((depth, half), BF16),
            pltpu.VMEM((hid, depth), BF16),
            pltpu.VMEM((hid, half), F32),
            pltpu.VMEM((hid, half), F32),
            pltpu.SemaphoreType.DMA((hid // (2 * TILE),)),
        ],
        compiler_params=params(),
        cost_estimate=cost(2 * depth * hid * half, 16 * hid * half),
        name="update",
    )(
        own_hidden,
        other_hidden,
        grad,
        *prepared,
        param,
        *[arrived[item] for item in added],
        last_scores,
    )
    shares = [array for arrays in returned.values() for array in arrays]
    router = pl.pallas_call(
        functools.partial(
            combine_kernel, [(k, len(arrays)) for k, arrays in returned.items()], group, cap
        ),
        out_shape=jax.ShapeDtypeStruct((top, tokens), F32),
        in_specs=specs(pltpu.VMEM, 2 + len(shares)),
        out_specs=specs(pltpu.VMEM, 1)[0],
        compiler_params=params(),
        cost_estimate=cost(4 * slots * tokens, 8 * top * tokens),
        name="combine",
    )(ids, slot_of, *shares)
    return (update[None, None], router.T[None])


def solution(mesh):
    sections, group = mesh.devices.shape
    split = jax.sharding.Mesh(
        mesh.devices.reshape(2, sections // 2, group), ("pair", "rest", "ep")
    )
    section = ("pair", "rest")
    rows = P(section, "ep", None)
    blocks = P(section, "ep", None, None)
    return jax.shard_map(
        local,
        mesh=split,
        in_specs=(rows, rows, rows, blocks, blocks, blocks, blocks),
        out_specs=(blocks, rows),
        check_vma=False,
    )
```

```python
import functools

import jax
import jax.numpy as jnp
from jax import lax
from jax.experimental import pallas as pl
from jax.experimental.pallas import tpu as pltpu
from jax.sharding import PartitionSpec as P

beta_first = 0.9
beta_second = 0.95
adam_eps = 1e-08
decay_rate = 0.1
first_fix = 1.0 - 0.9**10
second_fix = 1.0 - 0.95**10
first_unit = (1.0 - beta_first) / first_fix
second_unit = (1.0 - beta_second) / second_fix

LANES = 128
TILE = 16
PARTS = 4
VMEM_BYTES = 32 * 1024 * 1024
F32 = jnp.float32
BF16 = jnp.bfloat16


def params():
    return pltpu.CompilerParams(vmem_limit_bytes=VMEM_BYTES)


def cost(flops, touched):
    return pl.CostEstimate(flops=int(flops), bytes_accessed=int(touched), transcendentals=0)


def specs(space, count):
    return [pl.BlockSpec(memory_space=space) for _ in range(count)]


def ep_index():
    return lax.axis_index("ep").astype(jnp.int32)


def own_half():
    return lax.axis_index("pair").astype(jnp.int32)


def start_grads(grads_hbm, held, sems):
    tokens, half = held.shape[1:]
    step = tokens // PARTS
    mine = own_half()
    copies = []
    for side in range(2):
        column = pl.multiple_of((1 - mine if side else mine) * half, half)
        copies.append([])
        for part in range(PARTS):
            lines = slice(part * step, (part + 1) * step)
            copy = pltpu.make_async_copy(
                grads_hbm.at[lines, pl.ds(column, half)],
                held.at[side, lines],
                sems.at[side * PARTS + part],
            )
            copy.start()
            copies[side].append(copy)
    return copies


def pick_rows(slots, k, cap):
    place = lax.broadcasted_iota(jnp.int32, (cap, slots.shape[1]), 0).astype(F32)
    return jnp.where(place == slots[k : k + 1, :], 1.0, 0.0).astype(BF16)


def fill_chunks(steps, cap, picks, held, copies, tiles, chunks):
    half = held.shape[2]
    data_rows = half // LANES * cap
    pick = jnp.concatenate([picks[k] for k in steps], axis=0)
    for side in range(2):
        for k in steps:
            chunks[side, k][data_rows:, :] = tiles[k]
        for copy in copies[side]:
            copy.wait()
        block = jnp.dot(pick, held[side], preferred_element_type=F32).astype(BF16)
        for at, k in enumerate(steps):
            for part in range(half // LANES):
                chunks[side, k][part * cap : (part + 1) * cap, :] = block[
                    at * cap : (at + 1) * cap, part * LANES : (part + 1) * LANES
                ]


def route_kernel(
    items, steps, group, cap, ids_hbm, weight_hbm, grads_hbm, slots_ref, tiles_ref, *rest
):
    chunks = dict(zip(items, rest))
    ids_ref, weight_ref, held, sems = rest[len(items) :]
    tokens = held.shape[1]
    me = ep_index()
    small = [
        pltpu.make_async_copy(ids_hbm, ids_ref, sems.at[2 * PARTS]),
        pltpu.make_async_copy(weight_hbm, weight_ref, sems.at[2 * PARTS + 1]),
    ]
    for copy in small:
        copy.start()
    copies = start_grads(grads_hbm, held, sems)
    earlier = lax.broadcasted_iota(jnp.int32, (tokens, tokens), 0)
    later = lax.broadcasted_iota(jnp.int32, (tokens, tokens), 1)
    ahead = jnp.where(earlier < later, 1.0, 0.0).astype(BF16)
    for copy in small:
        copy.wait()
    ids = ids_ref[...]
    weights = weight_ref[...].astype(F32)
    members, scales = [], []
    for k in range(group):
        named = ids == (me ^ k)
        members.append(jnp.sum(jnp.where(named, 1.0, 0.0), axis=0, keepdims=True))
        scales.append(jnp.sum(jnp.where(named, weights, 0.0), axis=0, keepdims=True))
    if group % TILE:
        members.append(jnp.zeros((-group % TILE, tokens), F32))
    member = jnp.concatenate(members, axis=0)
    before = jnp.dot(member.astype(BF16), ahead, preferred_element_type=F32)
    slots = jnp.where(member > 0.5, before, -1.0)
    slots_ref[...] = slots
    picks = [pick_rows(slots, k, cap) for k in range(group)]
    base = me * cap
    tile_row = lax.broadcasted_iota(jnp.int32, (TILE, LANES), 0)
    tile_lane = lax.broadcasted_iota(jnp.int32, (TILE, LANES), 1)
    spot = tile_row * LANES + tile_lane
    kept = (spot >= base) & (spot < base + cap)
    if group % TILE:
        scales.append(jnp.zeros((-group % TILE, tokens), F32))
    rows = jnp.concatenate(scales, axis=0)
    lines = lax.dot_general(
        rows.astype(BF16),
        jnp.concatenate(picks, axis=0),
        (((1,), (1,)), ((), ())),
        preferred_element_type=F32,
    )
    tiles = []
    for k in range(group):
        line = lines[k : k + 1, k * cap : (k + 1) * cap]
        line = jnp.concatenate([line] * (LANES // cap), axis=1)
        tiles.append(jnp.where(kept, line, 0.0).astype(BF16))
        tiles_ref[k] = tiles[k]
    fill_chunks(steps, cap, picks, held, copies, tiles, chunks)


def later_kernel(
    items, steps, cap, slots_ref, tiles_ref, grads_hbm, own_ref, other_ref, master_hbm, inner_ref, *rest
):
    chunks = dict(zip(items, rest))
    held, master_ref, sems = rest[len(items) :]
    copies = start_grads(grads_hbm, held, sems)
    half = master_ref.shape[1]
    step = min(half, 4 * LANES)
    parts = [slice(column, column + step) for column in range(0, half, step)]
    loads = [
        pltpu.make_async_copy(master_hbm.at[:, part], master_ref.at[:, part], sems.at[2 * PARTS + at])
        for at, part in enumerate(parts)
    ]
    for load in loads:
        load.start()
    slots = slots_ref[...]
    picks = {k: pick_rows(slots, k, cap) for k in steps}
    fill_chunks(steps, cap, picks, held, copies, tiles_ref, chunks)
    slot_count = own_ref.shape[1]
    for load, part in zip(loads, parts):
        load.wait()
        weights = master_ref[:, part].astype(BF16)
        for at, ref in ((0, own_ref), (slot_count, other_ref)):
            inner_ref[at : at + slot_count, part] = lax.dot_general(
                ref[...], weights, (((0,), (0,)), ((), ())), preferred_element_type=F32
            )


def score_kernel(items, group, cap, inner_ref, *rest):
    chunks, score_ref = dict(zip(items, rest)), rest[-1]
    blocks = inner_ref.shape[1] // LANES
    me = ep_index()
    line_of = lax.broadcasted_iota(jnp.int32, score_ref.shape, 0)
    scores = jnp.zeros(score_ref.shape, F32)
    for k in sorted({k for _, k in items}):
        sums = []
        for side in range(2):
            total = jnp.zeros((cap, LANES), F32)
            if (side, k) in items:
                start = pl.multiple_of(side * group * cap + (me ^ k) * cap, cap)
                for block in range(blocks):
                    rows = chunks[side, k][block * cap : (block + 1) * cap, :].astype(F32)
                    total += rows * inner_ref[
                        pl.ds(start, cap), block * LANES : (block + 1) * LANES
                    ]
            sums.append(total)
        both = jnp.concatenate(sums, axis=0)
        line = jnp.sum(both.T, axis=0, keepdims=True)
        scores = jnp.where(line_of == (me ^ k), line, scores)
    score_ref[...] = scores


def scale_into(scaled, at, hidden, line):
    for top in range(0, hidden.shape[0], LANES):
        lines = slice(top, top + LANES)
        scaled[lines, at : at + LANES] = (hidden[lines, :].astype(F32) * line).astype(BF16)


def sum_kernel(items, group, cap, own_ref, other_ref, *rest):
    chunks = dict(zip(items, rest))
    grad_ref, rows, scaled = rest[-3:]
    blocks = rows.shape[1] // LANES
    slots = group * cap
    me = ep_index()
    for side, hidden in enumerate((own_ref, other_ref)):
        tile = jnp.zeros((TILE, LANES), F32)
        for k in range(group):
            start = pl.multiple_of(side * slots + (me ^ k) * cap, cap)
            if (side, k) not in items:
                rows[pl.ds(start, cap), :] = jnp.zeros((cap, rows.shape[1]), BF16)
                continue
            chunk = chunks[side, k]
            tile += chunk[blocks * cap :, :].astype(F32)
            for block in range(blocks):
                rows[pl.ds(start, cap), block * LANES : (block + 1) * LANES] = chunk[
                    block * cap : (block + 1) * cap, :
                ]
        for part in range(slots // LANES):
            lanes = slice(part * LANES, (part + 1) * LANES)
            scale_into(scaled, side * slots + part * LANES, hidden.at[:, lanes], tile[part : part + 1, :])
    grad_ref[...] = jnp.dot(scaled[...], rows[...], preferred_element_type=F32)


def merge_kernel(cap, own_ref, other_ref, _, out_ref):
    lane = lax.broadcasted_iota(jnp.int32, own_ref.shape, 1)
    scores = own_ref[...] + pltpu.roll(other_ref[...], LANES - cap, axis=1)
    out_ref[...] = jnp.where(lane < cap, scores, 0.0)


def update_kernel(items, cap, own_ref, other_ref, grad_ref, master_ref, moment_ref, second_ref, *rest):
    chunks = rest[: len(items)]
    _, update_hbm, rows, scaled, total, update, sems = rest[len(items) :]
    hid, half = update.shape
    width = min(half, 4 * LANES)
    height = 2 * TILE
    data_rows = half // LANES * cap
    me = ep_index()
    for at in range(0, len(items), 2):
        parts = []
        for turn, ((side, k), chunk) in enumerate(zip(items[at : at + 2], chunks[at : at + 2])):
            slot = (me ^ k) * cap
            lanes = pl.ds(pl.multiple_of(slot // LANES * LANES, LANES), LANES)
            place = slot % LANES if turn == 0 else (LANES - cap) - slot % LANES
            start = pl.multiple_of(at // 2 * LANES + place, cap)
            for part in range(half // LANES):
                rows[pl.ds(start, cap), part * LANES : (part + 1) * LANES] = chunk[
                    part * cap : (part + 1) * cap, :
                ]
            line = jnp.sum(chunk[data_rows:, :].astype(F32), axis=0, keepdims=True)
            parts.append(((own_ref, other_ref)[side], lanes, line))
        if len(parts) == 1:
            start = pl.multiple_of(at // 2 * LANES + (LANES - cap) - place, cap)
            rows[pl.ds(start, cap), :] = jnp.zeros((cap, half), BF16)
        for top in range(0, hid, LANES):
            values = [
                hidden[top : top + LANES, lanes].astype(F32) * line for hidden, lanes, line in parts
            ]
            if len(values) == 2:
                values[0] += pltpu.roll(values[1], LANES - cap, axis=1)
            scaled[top : top + LANES, at // 2 * LANES : (at // 2 + 1) * LANES] = values[0].astype(
                BF16
            )
    total[...] = jnp.dot(scaled[...], rows[...], preferred_element_type=F32)

    def moments(top, columns):
        lines = slice(top, top + TILE)
        grad = total[lines, columns] + grad_ref[lines, columns]
        first = moment_ref[lines, columns].astype(F32) * (beta_first / (1.0 - beta_first)) + grad
        square = (
            second_ref[lines, columns].astype(F32) * (beta_second / (1.0 - beta_second))
            + grad * grad
        )
        return first, square, lax.rsqrt(square)

    def inverse(first, square, root):
        scale = square * root * (second_unit**0.5 / first_unit) + adam_eps / first_unit
        return first, pl.reciprocal(scale, approx=True)

    def finish(top, columns, first, scale):
        lines = slice(top, top + TILE)
        update[lines, columns] = first * scale + decay_rate * master_ref[lines, columns]

    copies = []
    pieces = [
        (top, slice(column, column + width))
        for top in range(0, hid, TILE)
        for column in range(0, half, width)
    ]
    held = {}
    for turn in range(len(pieces) + 2):
        if turn < len(pieces):
            held[turn, 0] = moments(*pieces[turn])
        if 0 <= turn - 1 < len(pieces):
            held[turn - 1, 1] = inverse(*held.pop((turn - 1, 0)))
        if turn >= 2:
            finish(*pieces[turn - 2], *held.pop((turn - 2, 1)))
            top, columns = pieces[turn - 2]
            if (top + TILE) % height == 0 and columns.stop == half:
                lines = slice(top + TILE - height, top + TILE)
                copies.append(
                    pltpu.make_async_copy(
                        update.at[lines, :], update_hbm.at[lines, :], sems.at[len(copies)]
                    )
                )
                copies[-1].start()
    for copy in copies:
        copy.wait()


def combine_kernel(steps, group, cap, ids_ref, slots_ref, *rest):
    refs, out_ref = iter(rest[:-1]), rest[-1]
    tokens = ids_ref.shape[1]
    me = ep_index()
    shape = rest[0].shape
    lane = lax.broadcasted_iota(jnp.int32, shape, 1)
    row = lax.broadcasted_iota(jnp.int32, shape, 0)
    lines = jnp.zeros(shape, F32)
    for k, tiles in steps:
        scores = next(refs)[...]
        if tiles == 2:
            scores = jnp.where(lane < cap, scores, next(refs)[...])
        line = jnp.sum(jnp.where(row == me, scores, 0.0), axis=0, keepdims=True)
        lines = jnp.where(row == k, line, lines)
    rest = jnp.zeros((LANES - lines.shape[0], LANES), F32)
    columns = jnp.concatenate([lines, rest], axis=0).T
    columns = columns[:cap] + columns[cap : 2 * cap]
    place = lax.broadcasted_iota(jnp.int32, (cap, tokens), 0).astype(F32)
    ids = ids_ref[...]
    result = jnp.zeros(ids.shape, F32)
    for k in range(group):
        at_slot = jnp.where(place == slots_ref[k : k + 1, :], columns[:, k : k + 1], 0.0)
        result = jnp.where(ids == (me ^ k), jnp.sum(at_slot, axis=0, keepdims=True), result)
    out_ref[...] = result


def moved(array, side, step):
    if (side, step) == (0, 0):
        return array
    group = lax.axis_size("ep")
    pairs = [
        (p * group + e, (p ^ side) * group + (e ^ step)) for p in range(2) for e in range(group)
    ]
    return lax.ppermute(array, ("pair", "ep"), pairs)


def local(grad_out, router_weights, expert_ids, hidden, master, moment, second):
    group = lax.axis_size("ep")
    tokens, width = grad_out.shape[1:]
    top = expert_ids.shape[2]
    hid, slots = hidden.shape[2:]
    half = master.shape[3]
    cap = slots // group
    ids = expert_ids[0].T
    own_hidden = hidden[0, 0]
    param = master[0, 0]
    other_hidden = moved(own_hidden, 1, 0)

    far = group // 2
    first = [k for k in range(1, group) if k != far]
    late = [0, far]
    first_items = [(side, k) for side in range(2) for k in reversed(first)]
    last_items = [(1, far), (0, far), (1, 0), (0, 0)]
    order = first_items + last_items
    chunk = jax.ShapeDtypeStruct((half // LANES * cap + TILE, LANES), BF16)
    grads = pltpu.with_memory_space_constraint(grad_out[0], pltpu.HBM)
    held = pltpu.VMEM((2, tokens, half), BF16)
    routed = pl.pallas_call(
        functools.partial(route_kernel, first_items, first, group, cap),
        out_shape=[
            jax.ShapeDtypeStruct((group + -group % TILE, tokens), F32),
            jax.ShapeDtypeStruct((group, TILE, LANES), BF16),
        ]
        + [chunk] * len(first_items),
        in_specs=specs(pltpu.HBM, 3),
        out_specs=specs(pltpu.VMEM, 2 + len(first_items)),
        scratch_shapes=[
            pltpu.VMEM((top, tokens), jnp.int32),
            pltpu.VMEM((top, tokens), BF16),
            held,
            pltpu.SemaphoreType.DMA((2 * PARTS + 2,)),
        ],
        compiler_params=params(),
        cost_estimate=cost(2 * slots * tokens * width, 2 * (tokens + slots) * width),
        name="route",
    )(
        pltpu.with_memory_space_constraint(ids, pltpu.HBM),
        pltpu.with_memory_space_constraint(router_weights[0].T, pltpu.HBM),
        grads,
    )
    slot_of, tiles = routed[:2]
    arrived = {item: moved(sent, *item) for item, sent in zip(first_items, routed[2:])}

    routed = pl.pallas_call(
        functools.partial(later_kernel, last_items, late, cap),
        out_shape=[jax.ShapeDtypeStruct((2 * slots, half), F32)] + [chunk] * len(last_items),
        in_specs=specs(pltpu.VMEM, 2)
        + specs(pltpu.HBM, 1)
        + specs(pltpu.VMEM, 2)
        + specs(pltpu.HBM, 1),
        out_specs=specs(pltpu.VMEM, 1 + len(last_items)),
        scratch_shapes=[
            held,
            pltpu.VMEM((hid, half), F32),
            pltpu.SemaphoreType.DMA((2 * PARTS + half // min(half, 4 * LANES),)),
        ],
        compiler_params=params(),
        cost_estimate=cost(
            2 * slots * tokens * width + 4 * slots * hid * half, 2 * (tokens + slots) * width
        ),
        name="later",
    )(
        slot_of,
        tiles,
        grads,
        own_hidden,
        other_hidden,
        pltpu.with_memory_space_constraint(param, pltpu.HBM),
    )
    inner = routed[0]
    arrived |= {item: moved(sent, *item) for item, sent in zip(last_items, routed[1:])}

    tile = jax.ShapeDtypeStruct((group + -group % 8, LANES), F32)

    def scored(items, *after):
        return pl.pallas_call(
            functools.partial(score_kernel, items, group, cap),
            out_shape=tile,
            in_specs=specs(pltpu.VMEM, 1 + len(items)) + specs(pl.ANY, len(after)),
            out_specs=specs(pltpu.VMEM, 1)[0],
            compiler_params=params(),
            cost_estimate=cost(2 * cap * half, 6 * cap * half),
            name="score",
        )(inner, *[arrived[item] for item in items], *after)

    first_scores = scored(first_items)
    other_scores = moved(first_scores, 1, 0)
    added = [(1, far), (0, far), (1, 0)]
    summed = [item for item in order if item not in added]
    grad = pl.pallas_call(
        functools.partial(sum_kernel, summed, group, cap),
        out_shape=jax.ShapeDtypeStruct((hid, half), F32),
        in_specs=specs(pltpu.VMEM, 2 + len(summed)) + specs(pl.ANY, 1),
        out_specs=specs(pltpu.VMEM, 1)[0],
        scratch_shapes=[
            pltpu.VMEM((2 * slots, half), BF16),
            pltpu.VMEM((hid, 2 * slots), BF16),
        ],
        compiler_params=params(),
        cost_estimate=cost(4 * slots * hid * half, 4 * hid * half),
        name="sum",
    )(own_hidden, other_hidden, *[arrived[item] for item in summed], first_scores)
    merged = pl.pallas_call(
        functools.partial(merge_kernel, cap),
        out_shape=tile,
        in_specs=specs(pltpu.VMEM, 2) + specs(pl.ANY, 1),
        out_specs=specs(pltpu.VMEM, 1)[0],
        compiler_params=params(),
        name="merge",
    )(first_scores, other_scores, grad)
    returned = {k: [moved(merged, 0, k)] for k in first}
    zero_scores = scored([(0, 0), (1, 0)], merged)
    returned[0] = [zero_scores, moved(zero_scores, 1, 0)]
    other_far = scored([(1, far)], zero_scores)
    last_scores = scored([(0, far)], other_far)
    returned[far] = [moved(last_scores, 0, far), moved(other_far, 1, far)]

    depth = -(-len(added) // 2) * LANES
    update = pl.pallas_call(
        functools.partial(update_kernel, added, cap),
        out_shape=jax.ShapeDtypeStruct((hid, half), F32),
        in_specs=specs(pltpu.VMEM, 6 + len(added)) + specs(pl.ANY, 1),
        out_specs=specs(pltpu.HBM, 1)[0],
        scratch_shapes=[
            pltpu.VMEM((depth, half), BF16),
            pltpu.VMEM((hid, depth), BF16),
            pltpu.VMEM((hid, half), F32),
            pltpu.VMEM((hid, half), F32),
            pltpu.SemaphoreType.DMA((hid // (2 * TILE),)),
        ],
        compiler_params=params(),
        cost_estimate=cost(2 * depth * hid * half, 16 * hid * half),
        name="update",
    )(
        own_hidden,
        other_hidden,
        grad,
        param,
        moment[0, 0],
        second[0, 0],
        *[arrived[item] for item in added],
        last_scores,
    )
    shares = [array for arrays in returned.values() for array in arrays]
    router = pl.pallas_call(
        functools.partial(
            combine_kernel, [(k, len(arrays)) for k, arrays in returned.items()], group, cap
        ),
        out_shape=jax.ShapeDtypeStruct((top, tokens), F32),
        in_specs=specs(pltpu.VMEM, 2 + len(shares)),
        out_specs=specs(pltpu.VMEM, 1)[0],
        compiler_params=params(),
        cost_estimate=cost(4 * slots * tokens, 8 * top * tokens),
        name="combine",
    )(ids, slot_of, *shares)
    return (update[None, None], router.T[None])


def solution(mesh):
    sections, group = mesh.devices.shape
    split = jax.sharding.Mesh(
        mesh.devices.reshape(2, sections // 2, group), ("pair", "rest", "ep")
    )
    section = ("pair", "rest")
    rows = P(section, "ep", None)
    blocks = P(section, "ep", None, None)
    return jax.shard_map(
        local,
        mesh=split,
        in_specs=(rows, rows, rows, blocks, blocks, blocks, blocks),
        out_specs=(blocks, rows),
        check_vma=False,
    )
```

```python
import functools

import jax
import jax.numpy as jnp
from jax import lax
from jax.experimental import pallas as pl
from jax.experimental.pallas import tpu as pltpu
from jax.sharding import PartitionSpec as P

beta_first = 0.9
beta_second = 0.95
adam_eps = 1e-08
decay_rate = 0.1
first_fix = 1.0 - 0.9**10
second_fix = 1.0 - 0.95**10
first_unit = (1.0 - beta_first) / first_fix
second_unit = (1.0 - beta_second) / second_fix

LANES = 128
TILE = 16
VMEM_BYTES = 32 * 1024 * 1024
F32 = jnp.float32
BF16 = jnp.bfloat16


def params():
    return pltpu.CompilerParams(vmem_limit_bytes=VMEM_BYTES)


def cost(flops, touched):
    return pl.CostEstimate(flops=int(flops), bytes_accessed=int(touched), transcendentals=0)


def specs(space, count):
    return [pl.BlockSpec(memory_space=space) for _ in range(count)]


def ep_index():
    return lax.axis_index("ep").astype(jnp.int32)


def own_half():
    return lax.axis_index("pair").astype(jnp.int32)


def start_grads(grads_hbm, held, sems):
    half = held.shape[2]
    mine = own_half()
    copies = []
    for side in range(2):
        column = pl.multiple_of((1 - mine if side else mine) * half, half)
        copies.append(
            pltpu.make_async_copy(
                grads_hbm.at[:, pl.ds(column, half)], held.at[side], sems.at[side]
            )
        )
        copies[-1].start()
    return copies


def pick_rows(slots, k, cap):
    place = lax.broadcasted_iota(jnp.int32, (cap, slots.shape[1]), 0).astype(F32)
    return jnp.where(place == slots[k : k + 1, :], 1.0, 0.0).astype(BF16)


def fill_chunks(steps, cap, picks, held, copies, tiles, chunks, ready=False):
    half = held.shape[2]
    data_rows = half // LANES * cap
    pick = jnp.concatenate([picks[k] for k in steps], axis=0)
    for side in range(2):
        if side > 0 or not ready:
            copies[side].wait()
        for k in steps:
            chunks[side, k][data_rows:, :] = tiles[k]
        block = jnp.dot(pick, held[side], preferred_element_type=F32).astype(BF16)
        for at, k in enumerate(steps):
            for part in range(half // LANES):
                chunks[side, k][part * cap : (part + 1) * cap, :] = block[
                    at * cap : (at + 1) * cap, part * LANES : (part + 1) * LANES
                ]


def route_kernel(
    items, steps, group, cap, ids_hbm, weight_hbm, grads_hbm, slots_ref, tiles_ref, *rest
):
    chunks = dict(zip(items, rest))
    ids_ref, weight_ref, held, sems = rest[len(items) :]
    tokens = held.shape[1]
    me = ep_index()
    small = [
        pltpu.make_async_copy(ids_hbm, ids_ref, sems.at[2]),
        pltpu.make_async_copy(weight_hbm, weight_ref, sems.at[3]),
    ]
    for copy in small:
        copy.start()
    copies = start_grads(grads_hbm, held, sems)
    earlier = lax.broadcasted_iota(jnp.int32, (tokens, tokens), 0)
    later = lax.broadcasted_iota(jnp.int32, (tokens, tokens), 1)
    ahead = jnp.where(earlier < later, 1.0, 0.0).astype(BF16)
    for copy in small:
        copy.wait()
    ids = ids_ref[...]
    weights = weight_ref[...].astype(F32)
    members, scales = [], []
    for k in range(group):
        named = ids == (me ^ k)
        members.append(jnp.sum(jnp.where(named, 1.0, 0.0), axis=0, keepdims=True))
        scales.append(jnp.sum(jnp.where(named, weights, 0.0), axis=0, keepdims=True))
    if group % TILE:
        members.append(jnp.zeros((-group % TILE, tokens), F32))
    member = jnp.concatenate(members, axis=0)
    before = jnp.dot(member.astype(BF16), ahead, preferred_element_type=F32)
    slots = jnp.where(member > 0.5, before, -1.0)
    slots_ref[...] = slots
    copies[0].wait()
    picks = [pick_rows(slots, k, cap) for k in range(group)]
    base = me * cap
    tile_row = lax.broadcasted_iota(jnp.int32, (TILE, LANES), 0)
    tile_lane = lax.broadcasted_iota(jnp.int32, (TILE, LANES), 1)
    spot = tile_row * LANES + tile_lane
    kept = (spot >= base) & (spot < base + cap)
    if group % TILE:
        scales.append(jnp.zeros((-group % TILE, tokens), F32))
    rows = jnp.concatenate(scales, axis=0)
    lines = lax.dot_general(
        rows.astype(BF16),
        jnp.concatenate(picks, axis=0),
        (((1,), (1,)), ((), ())),
        preferred_element_type=F32,
    )
    tiles = []
    for k in range(group):
        line = lines[k : k + 1, k * cap : (k + 1) * cap]
        line = jnp.concatenate([line] * (LANES // cap), axis=1)
        tiles.append(jnp.where(kept, line, 0.0).astype(BF16))
        tiles_ref[k] = tiles[k]
    fill_chunks(steps, cap, picks, held, copies, tiles, chunks, ready=True)


def later_kernel(
    items, steps, cap, slots_ref, tiles_ref, grads_hbm, own_ref, other_ref, master_hbm, inner_ref, *rest
):
    chunks = dict(zip(items, rest))
    held, master_ref, sems = rest[len(items) :]
    copies = start_grads(grads_hbm, held, sems)
    half = master_ref.shape[1]
    step = min(half, 4 * LANES)
    parts = [slice(column, column + step) for column in range(0, half, step)]
    loads = [
        pltpu.make_async_copy(master_hbm.at[:, part], master_ref.at[:, part], sems.at[2 + at])
        for at, part in enumerate(parts)
    ]
    for load in loads:
        load.start()
    slots = slots_ref[...]
    picks = {k: pick_rows(slots, k, cap) for k in steps}
    fill_chunks(steps, cap, picks, held, copies, tiles_ref, chunks)
    slot_count = own_ref.shape[1]
    for load, part in zip(loads, parts):
        load.wait()
        weights = master_ref[:, part].astype(BF16)
        for at, ref in ((0, own_ref), (slot_count, other_ref)):
            inner_ref[at : at + slot_count, part] = lax.dot_general(
                ref[...], weights, (((0,), (0,)), ((), ())), preferred_element_type=F32
            )


def score_kernel(items, group, cap, inner_ref, *rest):
    chunks, score_ref = dict(zip(items, rest)), rest[-1]
    blocks = inner_ref.shape[1] // LANES
    me = ep_index()
    line_of = lax.broadcasted_iota(jnp.int32, score_ref.shape, 0)
    scores = jnp.zeros(score_ref.shape, F32)
    for k in sorted({k for _, k in items}):
        sums = []
        for side in range(2):
            total = jnp.zeros((cap, LANES), F32)
            if (side, k) in items:
                start = pl.multiple_of(side * group * cap + (me ^ k) * cap, cap)
                for block in range(blocks):
                    rows = chunks[side, k][block * cap : (block + 1) * cap, :].astype(F32)
                    total += rows * inner_ref[
                        pl.ds(start, cap), block * LANES : (block + 1) * LANES
                    ]
            sums.append(total)
        both = jnp.concatenate(sums, axis=0)
        line = jnp.sum(both.T, axis=0, keepdims=True)
        scores = jnp.where(line_of == (me ^ k), line, scores)
    score_ref[...] = scores


def scale_into(scaled, at, hidden, line):
    for top in range(0, hidden.shape[0], LANES):
        lines = slice(top, top + LANES)
        scaled[lines, at : at + LANES] = (hidden[lines, :].astype(F32) * line).astype(BF16)


def sum_kernel(items, group, cap, own_ref, other_ref, *rest):
    chunks = dict(zip(items, rest))
    grad_ref, rows, scaled = rest[-3:]
    blocks = rows.shape[1] // LANES
    slots = group * cap
    me = ep_index()
    for side, hidden in enumerate((own_ref, other_ref)):
        tile = jnp.zeros((TILE, LANES), F32)
        for k in range(group):
            start = pl.multiple_of(side * slots + (me ^ k) * cap, cap)
            if (side, k) not in items:
                rows[pl.ds(start, cap), :] = jnp.zeros((cap, rows.shape[1]), BF16)
                continue
            chunk = chunks[side, k]
            tile += chunk[blocks * cap :, :].astype(F32)
            for block in range(blocks):
                rows[pl.ds(start, cap), block * LANES : (block + 1) * LANES] = chunk[
                    block * cap : (block + 1) * cap, :
                ]
        for part in range(slots // LANES):
            lanes = slice(part * LANES, (part + 1) * LANES)
            scale_into(scaled, side * slots + part * LANES, hidden.at[:, lanes], tile[part : part + 1, :])
    grad_ref[...] = jnp.dot(scaled[...], rows[...], preferred_element_type=F32)


def merge_kernel(cap, own_ref, other_ref, _, out_ref):
    lane = lax.broadcasted_iota(jnp.int32, own_ref.shape, 1)
    scores = own_ref[...] + pltpu.roll(other_ref[...], LANES - cap, axis=1)
    out_ref[...] = jnp.where(lane < cap, scores, 0.0)


def update_kernel(items, cap, own_ref, other_ref, grad_ref, master_ref, moment_ref, second_ref, *rest):
    chunks = rest[: len(items)]
    _, update_hbm, rows, scaled, total, update, sems = rest[len(items) :]
    hid, half = update.shape
    width = min(half, 4 * LANES)
    height = 2 * TILE
    data_rows = half // LANES * cap
    me = ep_index()
    for at in range(0, len(items), 2):
        parts = []
        for turn, ((side, k), chunk) in enumerate(zip(items[at : at + 2], chunks[at : at + 2])):
            slot = (me ^ k) * cap
            lanes = pl.ds(pl.multiple_of(slot // LANES * LANES, LANES), LANES)
            place = slot % LANES if turn == 0 else (LANES - cap) - slot % LANES
            start = pl.multiple_of(at // 2 * LANES + place, cap)
            for part in range(half // LANES):
                rows[pl.ds(start, cap), part * LANES : (part + 1) * LANES] = chunk[
                    part * cap : (part + 1) * cap, :
                ]
            line = jnp.sum(chunk[data_rows:, :].astype(F32), axis=0, keepdims=True)
            parts.append(((own_ref, other_ref)[side], lanes, line))
        if len(parts) == 1:
            start = pl.multiple_of(at // 2 * LANES + (LANES - cap) - place, cap)
            rows[pl.ds(start, cap), :] = jnp.zeros((cap, half), BF16)
        for top in range(0, hid, LANES):
            values = [
                hidden[top : top + LANES, lanes].astype(F32) * line for hidden, lanes, line in parts
            ]
            if len(values) == 2:
                values[0] += pltpu.roll(values[1], LANES - cap, axis=1)
            scaled[top : top + LANES, at // 2 * LANES : (at // 2 + 1) * LANES] = values[0].astype(
                BF16
            )
    total[...] = jnp.dot(scaled[...], rows[...], preferred_element_type=F32)

    def moments(top, columns):
        lines = slice(top, top + TILE)
        grad = total[lines, columns] + grad_ref[lines, columns]
        first = moment_ref[lines, columns].astype(F32) * (beta_first / (1.0 - beta_first)) + grad
        square = (
            second_ref[lines, columns].astype(F32) * (beta_second / (1.0 - beta_second))
            + grad * grad
        )
        return first, square, lax.rsqrt(square)

    def inverse(first, square, root):
        scale = square * root * (second_unit**0.5 / first_unit) + adam_eps / first_unit
        return first, pl.reciprocal(scale, approx=True)

    def finish(top, columns, first, scale):
        lines = slice(top, top + TILE)
        update[lines, columns] = first * scale + decay_rate * master_ref[lines, columns]

    copies = []
    pieces = [
        (top, slice(column, column + width))
        for top in range(0, hid, TILE)
        for column in range(0, half, width)
    ]
    held = {}
    for turn in range(len(pieces) + 2):
        if turn < len(pieces):
            held[turn, 0] = moments(*pieces[turn])
        if 0 <= turn - 1 < len(pieces):
            held[turn - 1, 1] = inverse(*held.pop((turn - 1, 0)))
        if turn >= 2:
            finish(*pieces[turn - 2], *held.pop((turn - 2, 1)))
            top, columns = pieces[turn - 2]
            if (top + TILE) % height == 0 and columns.stop == half:
                lines = slice(top + TILE - height, top + TILE)
                copies.append(
                    pltpu.make_async_copy(
                        update.at[lines, :], update_hbm.at[lines, :], sems.at[len(copies)]
                    )
                )
                copies[-1].start()
    for copy in copies:
        copy.wait()


def combine_kernel(steps, group, cap, ids_ref, slots_ref, *rest):
    refs, out_ref = iter(rest[:-1]), rest[-1]
    tokens = ids_ref.shape[1]
    me = ep_index()
    shape = rest[0].shape
    lane = lax.broadcasted_iota(jnp.int32, shape, 1)
    row = lax.broadcasted_iota(jnp.int32, shape, 0)
    lines = jnp.zeros(shape, F32)
    for k, tiles in steps:
        scores = next(refs)[...]
        if tiles == 2:
            scores = jnp.where(lane < cap, scores, next(refs)[...])
        line = jnp.sum(jnp.where(row == me, scores, 0.0), axis=0, keepdims=True)
        lines = jnp.where(row == k, line, lines)
    rest = jnp.zeros((LANES - lines.shape[0], LANES), F32)
    columns = jnp.concatenate([lines, rest], axis=0).T
    columns = columns[:cap] + columns[cap : 2 * cap]
    place = lax.broadcasted_iota(jnp.int32, (cap, tokens), 0).astype(F32)
    ids = ids_ref[...]
    result = jnp.zeros(ids.shape, F32)
    for k in range(group):
        at_slot = jnp.where(place == slots_ref[k : k + 1, :], columns[:, k : k + 1], 0.0)
        result = jnp.where(ids == (me ^ k), jnp.sum(at_slot, axis=0, keepdims=True), result)
    out_ref[...] = result


def moved(array, side, step):
    if (side, step) == (0, 0):
        return array
    group = lax.axis_size("ep")
    pairs = [
        (p * group + e, (p ^ side) * group + (e ^ step)) for p in range(2) for e in range(group)
    ]
    return lax.ppermute(array, ("pair", "ep"), pairs)


def local(grad_out, router_weights, expert_ids, hidden, master, moment, second):
    group = lax.axis_size("ep")
    tokens, width = grad_out.shape[1:]
    top = expert_ids.shape[2]
    hid, slots = hidden.shape[2:]
    half = master.shape[3]
    cap = slots // group
    ids = expert_ids[0].T
    own_hidden = hidden[0, 0]
    param = master[0, 0]
    other_hidden = moved(own_hidden, 1, 0)

    far = group // 2
    first = [k for k in range(1, group) if k != far]
    late = [0, far]
    first_items = [(side, k) for side in range(2) for k in reversed(first)]
    last_items = [(1, far), (0, far), (1, 0), (0, 0)]
    order = first_items + last_items
    chunk = jax.ShapeDtypeStruct((half // LANES * cap + TILE, LANES), BF16)
    grads = pltpu.with_memory_space_constraint(grad_out[0], pltpu.HBM)
    held = pltpu.VMEM((2, tokens, half), BF16)
    routed = pl.pallas_call(
        functools.partial(route_kernel, first_items, first, group, cap),
        out_shape=[
            jax.ShapeDtypeStruct((group + -group % TILE, tokens), F32),
            jax.ShapeDtypeStruct((group, TILE, LANES), BF16),
        ]
        + [chunk] * len(first_items),
        in_specs=specs(pltpu.HBM, 3),
        out_specs=specs(pltpu.VMEM, 2 + len(first_items)),
        scratch_shapes=[
            pltpu.VMEM((top, tokens), jnp.int32),
            pltpu.VMEM((top, tokens), BF16),
            held,
            pltpu.SemaphoreType.DMA((4,)),
        ],
        compiler_params=params(),
        cost_estimate=cost(2 * slots * tokens * width, 2 * (tokens + slots) * width),
        name="route",
    )(
        pltpu.with_memory_space_constraint(ids, pltpu.HBM),
        pltpu.with_memory_space_constraint(router_weights[0].T, pltpu.HBM),
        grads,
    )
    slot_of, tiles = routed[:2]
    arrived = {item: moved(sent, *item) for item, sent in zip(first_items, routed[2:])}

    routed = pl.pallas_call(
        functools.partial(later_kernel, last_items, late, cap),
        out_shape=[jax.ShapeDtypeStruct((2 * slots, half), F32)] + [chunk] * len(last_items),
        in_specs=specs(pltpu.VMEM, 2)
        + specs(pltpu.HBM, 1)
        + specs(pltpu.VMEM, 2)
        + specs(pltpu.HBM, 1),
        out_specs=specs(pltpu.VMEM, 1 + len(last_items)),
        scratch_shapes=[
            held,
            pltpu.VMEM((hid, half), F32),
            pltpu.SemaphoreType.DMA((2 + half // min(half, 4 * LANES),)),
        ],
        compiler_params=params(),
        cost_estimate=cost(
            2 * slots * tokens * width + 4 * slots * hid * half, 2 * (tokens + slots) * width
        ),
        name="later",
    )(
        slot_of,
        tiles,
        grads,
        own_hidden,
        other_hidden,
        pltpu.with_memory_space_constraint(param, pltpu.HBM),
    )
    inner = routed[0]
    arrived |= {item: moved(sent, *item) for item, sent in zip(last_items, routed[1:])}

    tile = jax.ShapeDtypeStruct((group + -group % 8, LANES), F32)

    def scored(items, *after):
        return pl.pallas_call(
            functools.partial(score_kernel, items, group, cap),
            out_shape=tile,
            in_specs=specs(pltpu.VMEM, 1 + len(items)) + specs(pl.ANY, len(after)),
            out_specs=specs(pltpu.VMEM, 1)[0],
            compiler_params=params(),
            cost_estimate=cost(2 * cap * half, 6 * cap * half),
            name="score",
        )(inner, *[arrived[item] for item in items], *after)

    first_scores = scored(first_items)
    other_scores = moved(first_scores, 1, 0)
    added = [(1, far), (0, far), (1, 0)]
    summed = [item for item in order if item not in added]
    grad = pl.pallas_call(
        functools.partial(sum_kernel, summed, group, cap),
        out_shape=jax.ShapeDtypeStruct((hid, half), F32),
        in_specs=specs(pltpu.VMEM, 2 + len(summed)) + specs(pl.ANY, 1),
        out_specs=specs(pltpu.VMEM, 1)[0],
        scratch_shapes=[
            pltpu.VMEM((2 * slots, half), BF16),
            pltpu.VMEM((hid, 2 * slots), BF16),
        ],
        compiler_params=params(),
        cost_estimate=cost(4 * slots * hid * half, 4 * hid * half),
        name="sum",
    )(own_hidden, other_hidden, *[arrived[item] for item in summed], first_scores)
    merged = pl.pallas_call(
        functools.partial(merge_kernel, cap),
        out_shape=tile,
        in_specs=specs(pltpu.VMEM, 2) + specs(pl.ANY, 1),
        out_specs=specs(pltpu.VMEM, 1)[0],
        compiler_params=params(),
        name="merge",
    )(first_scores, other_scores, grad)
    returned = {k: [moved(merged, 0, k)] for k in first}
    zero_scores = scored([(0, 0), (1, 0)], merged)
    returned[0] = [zero_scores, moved(zero_scores, 1, 0)]
    other_far = scored([(1, far)], zero_scores)
    last_scores = scored([(0, far)], other_far)
    returned[far] = [moved(last_scores, 0, far), moved(other_far, 1, far)]

    depth = -(-len(added) // 2) * LANES
    update = pl.pallas_call(
        functools.partial(update_kernel, added, cap),
        out_shape=jax.ShapeDtypeStruct((hid, half), F32),
        in_specs=specs(pltpu.VMEM, 6 + len(added)) + specs(pl.ANY, 1),
        out_specs=specs(pltpu.HBM, 1)[0],
        scratch_shapes=[
            pltpu.VMEM((depth, half), BF16),
            pltpu.VMEM((hid, depth), BF16),
            pltpu.VMEM((hid, half), F32),
            pltpu.VMEM((hid, half), F32),
            pltpu.SemaphoreType.DMA((hid // (2 * TILE),)),
        ],
        compiler_params=params(),
        cost_estimate=cost(2 * depth * hid * half, 16 * hid * half),
        name="update",
    )(
        own_hidden,
        other_hidden,
        grad,
        param,
        moment[0, 0],
        second[0, 0],
        *[arrived[item] for item in added],
        last_scores,
    )
    shares = [array for arrays in returned.values() for array in arrays]
    router = pl.pallas_call(
        functools.partial(
            combine_kernel, [(k, len(arrays)) for k, arrays in returned.items()], group, cap
        ),
        out_shape=jax.ShapeDtypeStruct((top, tokens), F32),
        in_specs=specs(pltpu.VMEM, 2 + len(shares)),
        out_specs=specs(pltpu.VMEM, 1)[0],
        compiler_params=params(),
        cost_estimate=cost(4 * slots * tokens, 8 * top * tokens),
        name="combine",
    )(ids, slot_of, *shares)
    return (update[None, None], router.T[None])


def solution(mesh):
    sections, group = mesh.devices.shape
    split = jax.sharding.Mesh(
        mesh.devices.reshape(2, sections // 2, group), ("pair", "rest", "ep")
    )
    section = ("pair", "rest")
    rows = P(section, "ep", None)
    blocks = P(section, "ep", None, None)
    return jax.shard_map(
        local,
        mesh=split,
        in_specs=(rows, rows, rows, blocks, blocks, blocks, blocks),
        out_specs=(blocks, rows),
        check_vma=False,
    )
```

```python
import functools

import jax
import jax.numpy as jnp
from jax import lax
from jax.experimental import pallas as pl
from jax.experimental.pallas import tpu as pltpu
from jax.sharding import PartitionSpec as P

beta_first = 0.9
beta_second = 0.95
adam_eps = 1e-08
decay_rate = 0.1
first_fix = 1.0 - 0.9**10
second_fix = 1.0 - 0.95**10
first_unit = (1.0 - beta_first) / first_fix
second_unit = (1.0 - beta_second) / second_fix

LANES = 128
TILE = 16
VMEM_BYTES = 32 * 1024 * 1024
F32 = jnp.float32
BF16 = jnp.bfloat16


def params():
    return pltpu.CompilerParams(vmem_limit_bytes=VMEM_BYTES)


def cost(flops, touched):
    return pl.CostEstimate(flops=int(flops), bytes_accessed=int(touched), transcendentals=0)


def specs(space, count):
    return [pl.BlockSpec(memory_space=space) for _ in range(count)]


def ep_index():
    return lax.axis_index("ep").astype(jnp.int32)


def own_half():
    return lax.axis_index("pair").astype(jnp.int32)


def start_grads(grads_hbm, held, sems):
    half = held.shape[2]
    mine = own_half()
    copies = []
    for side in range(2):
        column = pl.multiple_of((1 - mine if side else mine) * half, half)
        copies.append(
            pltpu.make_async_copy(
                grads_hbm.at[:, pl.ds(column, half)], held.at[side], sems.at[side]
            )
        )
        copies[-1].start()
    return copies


def pick_rows(slots, k, cap):
    place = lax.broadcasted_iota(jnp.int32, (cap, slots.shape[1]), 0).astype(F32)
    return jnp.where(place == slots[k : k + 1, :], 1.0, 0.0).astype(BF16)


def fill_chunks(steps, cap, picks, held, copies, tiles, chunks):
    half = held.shape[2]
    data_rows = half // LANES * cap
    pick = jnp.concatenate([picks[k] for k in steps], axis=0)
    for side in range(2):
        for k in steps:
            chunks[side, k][data_rows:, :] = tiles[k]
        copies[side].wait()
        block = jnp.dot(pick, held[side], preferred_element_type=F32).astype(BF16)
        for at, k in enumerate(steps):
            for part in range(half // LANES):
                chunks[side, k][part * cap : (part + 1) * cap, :] = block[
                    at * cap : (at + 1) * cap, part * LANES : (part + 1) * LANES
                ]


def route_kernel(
    items, steps, group, cap, ids_hbm, weight_hbm, grads_hbm, slots_ref, tiles_ref, *rest
):
    chunks = dict(zip(items, rest))
    ids_ref, weight_ref, held, sems = rest[len(items) :]
    tokens = held.shape[1]
    me = ep_index()
    small = [
        pltpu.make_async_copy(ids_hbm, ids_ref, sems.at[2]),
        pltpu.make_async_copy(weight_hbm, weight_ref, sems.at[3]),
    ]
    for copy in small:
        copy.start()
    copies = start_grads(grads_hbm, held, sems)
    earlier = lax.broadcasted_iota(jnp.int32, (tokens, tokens), 0)
    later = lax.broadcasted_iota(jnp.int32, (tokens, tokens), 1)
    ahead = jnp.where(earlier < later, 1.0, 0.0).astype(BF16)
    for copy in small:
        copy.wait()
    ids = ids_ref[...]
    weights = weight_ref[...].astype(F32)
    members, scales = [], []
    for k in range(group):
        named = ids == (me ^ k)
        members.append(jnp.sum(jnp.where(named, 1.0, 0.0), axis=0, keepdims=True))
        scales.append(jnp.sum(jnp.where(named, weights, 0.0), axis=0, keepdims=True))
    if group % TILE:
        members.append(jnp.zeros((-group % TILE, tokens), F32))
    member = jnp.concatenate(members, axis=0)
    before = jnp.dot(member.astype(BF16), ahead, preferred_element_type=F32)
    slots = jnp.where(member > 0.5, before, -1.0)
    slots_ref[...] = slots
    picks = [pick_rows(slots, k, cap) for k in range(group)]
    base = me * cap
    tile_row = lax.broadcasted_iota(jnp.int32, (TILE, LANES), 0)
    tile_lane = lax.broadcasted_iota(jnp.int32, (TILE, LANES), 1)
    spot = tile_row * LANES + tile_lane
    kept = (spot >= base) & (spot < base + cap)
    if group % TILE:
        scales.append(jnp.zeros((-group % TILE, tokens), F32))
    rows = jnp.concatenate(scales, axis=0)
    lines = lax.dot_general(
        rows.astype(BF16),
        jnp.concatenate(picks, axis=0),
        (((1,), (1,)), ((), ())),
        preferred_element_type=F32,
    )
    tiles = []
    for k in range(group):
        line = lines[k : k + 1, k * cap : (k + 1) * cap]
        line = jnp.concatenate([line] * (LANES // cap), axis=1)
        tiles.append(jnp.where(kept, line, 0.0).astype(BF16))
        tiles_ref[k] = tiles[k]
    fill_chunks(steps, cap, picks, held, copies, tiles, chunks)


def later_kernel(
    items, steps, cap, slots_ref, tiles_ref, grads_hbm, own_ref, other_ref, master_hbm, inner_ref, *rest
):
    chunks = dict(zip(items, rest))
    held, master_ref, sems = rest[len(items) :]
    copies = start_grads(grads_hbm, held, sems)
    half = master_ref.shape[1]
    step = min(half, 4 * LANES)
    parts = [slice(column, column + step) for column in range(0, half, step)]
    loads = [
        pltpu.make_async_copy(master_hbm.at[:, part], master_ref.at[:, part], sems.at[2 + at])
        for at, part in enumerate(parts)
    ]
    for load in loads:
        load.start()
    slots = slots_ref[...]
    picks = {k: pick_rows(slots, k, cap) for k in steps}
    fill_chunks(steps, cap, picks, held, copies, tiles_ref, chunks)
    slot_count = own_ref.shape[1]
    for load, part in zip(loads, parts):
        load.wait()
        weights = master_ref[:, part].astype(BF16)
        for at, ref in ((0, own_ref), (slot_count, other_ref)):
            inner_ref[at : at + slot_count, part] = lax.dot_general(
                ref[...], weights, (((0,), (0,)), ((), ())), preferred_element_type=F32
            )


def score_kernel(items, group, cap, inner_ref, *rest):
    chunks, score_ref = dict(zip(items, rest)), rest[-1]
    blocks = inner_ref.shape[1] // LANES
    me = ep_index()
    line_of = lax.broadcasted_iota(jnp.int32, score_ref.shape, 0)
    scores = jnp.zeros(score_ref.shape, F32)
    for k in sorted({k for _, k in items}):
        sums = []
        for side in range(2):
            total = jnp.zeros((cap, LANES), F32)
            if (side, k) in items:
                start = pl.multiple_of(side * group * cap + (me ^ k) * cap, cap)
                for block in range(blocks):
                    rows = chunks[side, k][block * cap : (block + 1) * cap, :].astype(F32)
                    total += rows * inner_ref[
                        pl.ds(start, cap), block * LANES : (block + 1) * LANES
                    ]
            sums.append(total)
        both = jnp.concatenate(sums, axis=0)
        line = jnp.sum(both.T, axis=0, keepdims=True)
        scores = jnp.where(line_of == (me ^ k), line, scores)
    score_ref[...] = scores


def scale_into(scaled, at, hidden, line):
    for top in range(0, hidden.shape[0], LANES):
        lines = slice(top, top + LANES)
        scaled[lines, at : at + LANES] = (hidden[lines, :].astype(F32) * line).astype(BF16)


def sum_kernel(items, group, cap, own_ref, other_ref, *rest):
    chunks = dict(zip(items, rest))
    grad_ref, rows, scaled = rest[-3:]
    blocks = rows.shape[1] // LANES
    slots = group * cap
    me = ep_index()
    for side, hidden in enumerate((own_ref, other_ref)):
        tile = jnp.zeros((TILE, LANES), F32)
        for k in range(group):
            start = pl.multiple_of(side * slots + (me ^ k) * cap, cap)
            if (side, k) not in items:
                rows[pl.ds(start, cap), :] = jnp.zeros((cap, rows.shape[1]), BF16)
                continue
            chunk = chunks[side, k]
            tile += chunk[blocks * cap :, :].astype(F32)
            for block in range(blocks):
                rows[pl.ds(start, cap), block * LANES : (block + 1) * LANES] = chunk[
                    block * cap : (block + 1) * cap, :
                ]
        for part in range(slots // LANES):
            lanes = slice(part * LANES, (part + 1) * LANES)
            scale_into(scaled, side * slots + part * LANES, hidden.at[:, lanes], tile[part : part + 1, :])
    grad_ref[...] = jnp.dot(scaled[...], rows[...], preferred_element_type=F32)


def merge_kernel(cap, own_ref, other_ref, _, out_ref):
    lane = lax.broadcasted_iota(jnp.int32, own_ref.shape, 1)
    scores = own_ref[...] + pltpu.roll(other_ref[...], LANES - cap, axis=1)
    out_ref[...] = jnp.where(lane < cap, scores, 0.0)


def update_kernel(items, cap, own_ref, other_ref, grad_ref, master_ref, moment_ref, second_ref, *rest):
    chunks = rest[: len(items)]
    _, update_hbm, tail_ref, rows, scaled, total, update, sems = rest[len(items) :]
    hid, half = total.shape
    cut = update.shape[0]
    width = min(half, 4 * LANES)
    height = 2 * TILE
    data_rows = half // LANES * cap
    me = ep_index()
    for at in range(0, len(items), 2):
        parts = []
        for turn, ((side, k), chunk) in enumerate(zip(items[at : at + 2], chunks[at : at + 2])):
            slot = (me ^ k) * cap
            lanes = pl.ds(pl.multiple_of(slot // LANES * LANES, LANES), LANES)
            place = slot % LANES if turn == 0 else (LANES - cap) - slot % LANES
            start = pl.multiple_of(at // 2 * LANES + place, cap)
            for part in range(half // LANES):
                rows[pl.ds(start, cap), part * LANES : (part + 1) * LANES] = chunk[
                    part * cap : (part + 1) * cap, :
                ]
            line = jnp.sum(chunk[data_rows:, :].astype(F32), axis=0, keepdims=True)
            parts.append(((own_ref, other_ref)[side], lanes, line))
        if len(parts) == 1:
            start = pl.multiple_of(at // 2 * LANES + (LANES - cap) - place, cap)
            rows[pl.ds(start, cap), :] = jnp.zeros((cap, half), BF16)
        for top in range(0, hid, LANES):
            values = [
                hidden[top : top + LANES, lanes].astype(F32) * line for hidden, lanes, line in parts
            ]
            if len(values) == 2:
                values[0] += pltpu.roll(values[1], LANES - cap, axis=1)
            scaled[top : top + LANES, at // 2 * LANES : (at // 2 + 1) * LANES] = values[0].astype(
                BF16
            )
    total[...] = jnp.dot(scaled[...], rows[...], preferred_element_type=F32)

    def moments(top, columns):
        lines = slice(top, top + TILE)
        grad = total[lines, columns] + grad_ref[lines, columns]
        first = moment_ref[lines, columns].astype(F32) * (beta_first / (1.0 - beta_first)) + grad
        square = (
            second_ref[lines, columns].astype(F32) * (beta_second / (1.0 - beta_second))
            + grad * grad
        )
        return first, square, lax.rsqrt(square)

    def inverse(first, square, root):
        scale = square * root * (second_unit**0.5 / first_unit) + adam_eps / first_unit
        return first, pl.reciprocal(scale, approx=True)

    def finish(top, columns, first, scale):
        out, place = (update, top) if top < cut else (tail_ref, top - cut)
        out[place : place + TILE, columns] = (
            first * scale + decay_rate * master_ref[top : top + TILE, columns]
        )

    copies = []
    pieces = [
        (top, slice(column, column + width))
        for top in range(0, hid, TILE)
        for column in range(0, half, width)
    ]
    held = {}
    for turn in range(len(pieces) + 2):
        if turn < len(pieces):
            held[turn, 0] = moments(*pieces[turn])
        if 0 <= turn - 1 < len(pieces):
            held[turn - 1, 1] = inverse(*held.pop((turn - 1, 0)))
        if turn >= 2:
            finish(*pieces[turn - 2], *held.pop((turn - 2, 1)))
            top, columns = pieces[turn - 2]
            if top < cut and (top + TILE) % height == 0 and columns.stop == half:
                lines = slice(top + TILE - height, top + TILE)
                copies.append(
                    pltpu.make_async_copy(
                        update.at[lines, :], update_hbm.at[lines, :], sems.at[len(copies)]
                    )
                )
                copies[-1].start()
    for copy in copies:
        copy.wait()


def combine_kernel(steps, group, cap, _, tail_ref, ids_ref, slots_ref, *rest):
    refs, (out_ref, update_hbm, sem) = iter(rest[:-3]), rest[-3:]
    cut = update_hbm.shape[0] - tail_ref.shape[0]
    copy = pltpu.make_async_copy(tail_ref, update_hbm.at[cut:, :], sem)
    copy.start()
    tokens = ids_ref.shape[1]
    me = ep_index()
    shape = rest[0].shape
    lane = lax.broadcasted_iota(jnp.int32, shape, 1)
    row = lax.broadcasted_iota(jnp.int32, shape, 0)
    lines = jnp.zeros(shape, F32)
    for k, tiles in steps:
        scores = next(refs)[...]
        if tiles == 2:
            scores = jnp.where(lane < cap, scores, next(refs)[...])
        line = jnp.sum(jnp.where(row == me, scores, 0.0), axis=0, keepdims=True)
        lines = jnp.where(row == k, line, lines)
    rest = jnp.zeros((LANES - lines.shape[0], LANES), F32)
    columns = jnp.concatenate([lines, rest], axis=0).T
    columns = columns[:cap] + columns[cap : 2 * cap]
    place = lax.broadcasted_iota(jnp.int32, (cap, tokens), 0).astype(F32)
    ids = ids_ref[...]
    result = jnp.zeros(ids.shape, F32)
    for k in range(group):
        at_slot = jnp.where(place == slots_ref[k : k + 1, :], columns[:, k : k + 1], 0.0)
        result = jnp.where(ids == (me ^ k), jnp.sum(at_slot, axis=0, keepdims=True), result)
    out_ref[...] = result
    copy.wait()


def moved(array, side, step):
    if (side, step) == (0, 0):
        return array
    group = lax.axis_size("ep")
    pairs = [
        (p * group + e, (p ^ side) * group + (e ^ step)) for p in range(2) for e in range(group)
    ]
    return lax.ppermute(array, ("pair", "ep"), pairs)


def local(grad_out, router_weights, expert_ids, hidden, master, moment, second):
    group = lax.axis_size("ep")
    tokens, width = grad_out.shape[1:]
    top = expert_ids.shape[2]
    hid, slots = hidden.shape[2:]
    half = master.shape[3]
    cap = slots // group
    ids = expert_ids[0].T
    own_hidden = hidden[0, 0]
    param = master[0, 0]
    other_hidden = moved(own_hidden, 1, 0)

    far = group // 2
    first = [k for k in range(1, group) if k != far]
    late = [0, far]
    first_items = [(side, k) for side in range(2) for k in reversed(first)]
    last_items = [(1, far), (0, far), (1, 0), (0, 0)]
    order = first_items + last_items
    chunk = jax.ShapeDtypeStruct((half // LANES * cap + TILE, LANES), BF16)
    grads = pltpu.with_memory_space_constraint(grad_out[0], pltpu.HBM)
    held = pltpu.VMEM((2, tokens, half), BF16)
    routed = pl.pallas_call(
        functools.partial(route_kernel, first_items, first, group, cap),
        out_shape=[
            jax.ShapeDtypeStruct((group + -group % TILE, tokens), F32),
            jax.ShapeDtypeStruct((group, TILE, LANES), BF16),
        ]
        + [chunk] * len(first_items),
        in_specs=specs(pltpu.HBM, 3),
        out_specs=specs(pltpu.VMEM, 2 + len(first_items)),
        scratch_shapes=[
            pltpu.VMEM((top, tokens), jnp.int32),
            pltpu.VMEM((top, tokens), BF16),
            held,
            pltpu.SemaphoreType.DMA((4,)),
        ],
        compiler_params=params(),
        cost_estimate=cost(2 * slots * tokens * width, 2 * (tokens + slots) * width),
        name="route",
    )(
        pltpu.with_memory_space_constraint(ids, pltpu.HBM),
        pltpu.with_memory_space_constraint(router_weights[0].T, pltpu.HBM),
        grads,
    )
    slot_of, tiles = routed[:2]
    arrived = {item: moved(sent, *item) for item, sent in zip(first_items, routed[2:])}

    routed = pl.pallas_call(
        functools.partial(later_kernel, last_items, late, cap),
        out_shape=[jax.ShapeDtypeStruct((2 * slots, half), F32)] + [chunk] * len(last_items),
        in_specs=specs(pltpu.VMEM, 2)
        + specs(pltpu.HBM, 1)
        + specs(pltpu.VMEM, 2)
        + specs(pltpu.HBM, 1),
        out_specs=specs(pltpu.VMEM, 1 + len(last_items)),
        scratch_shapes=[
            held,
            pltpu.VMEM((hid, half), F32),
            pltpu.SemaphoreType.DMA((2 + half // min(half, 4 * LANES),)),
        ],
        compiler_params=params(),
        cost_estimate=cost(
            2 * slots * tokens * width + 4 * slots * hid * half, 2 * (tokens + slots) * width
        ),
        name="later",
    )(
        slot_of,
        tiles,
        grads,
        own_hidden,
        other_hidden,
        pltpu.with_memory_space_constraint(param, pltpu.HBM),
    )
    inner = routed[0]
    arrived |= {item: moved(sent, *item) for item, sent in zip(last_items, routed[1:])}

    tile = jax.ShapeDtypeStruct((group + -group % 8, LANES), F32)

    def scored(items, *after):
        return pl.pallas_call(
            functools.partial(score_kernel, items, group, cap),
            out_shape=tile,
            in_specs=specs(pltpu.VMEM, 1 + len(items)) + specs(pl.ANY, len(after)),
            out_specs=specs(pltpu.VMEM, 1)[0],
            compiler_params=params(),
            cost_estimate=cost(2 * cap * half, 6 * cap * half),
            name="score",
        )(inner, *[arrived[item] for item in items], *after)

    first_scores = scored(first_items)
    other_scores = moved(first_scores, 1, 0)
    added = [(1, far), (0, far), (1, 0)]
    summed = [item for item in order if item not in added]
    grad = pl.pallas_call(
        functools.partial(sum_kernel, summed, group, cap),
        out_shape=jax.ShapeDtypeStruct((hid, half), F32),
        in_specs=specs(pltpu.VMEM, 2 + len(summed)) + specs(pl.ANY, 1),
        out_specs=specs(pltpu.VMEM, 1)[0],
        scratch_shapes=[
            pltpu.VMEM((2 * slots, half), BF16),
            pltpu.VMEM((hid, 2 * slots), BF16),
        ],
        compiler_params=params(),
        cost_estimate=cost(4 * slots * hid * half, 4 * hid * half),
        name="sum",
    )(own_hidden, other_hidden, *[arrived[item] for item in summed], first_scores)
    merged = pl.pallas_call(
        functools.partial(merge_kernel, cap),
        out_shape=tile,
        in_specs=specs(pltpu.VMEM, 2) + specs(pl.ANY, 1),
        out_specs=specs(pltpu.VMEM, 1)[0],
        compiler_params=params(),
        name="merge",
    )(first_scores, other_scores, grad)
    returned = {k: [moved(merged, 0, k)] for k in first}
    zero_scores = scored([(0, 0), (1, 0)], merged)
    returned[0] = [zero_scores, moved(zero_scores, 1, 0)]
    other_far = scored([(1, far)], zero_scores)
    last_scores = scored([(0, far)], other_far)
    returned[far] = [moved(last_scores, 0, far), moved(other_far, 1, far)]

    depth = -(-len(added) // 2) * LANES
    kept = 2 * LANES if hid > 2 * LANES else hid // 2
    update, tail = pl.pallas_call(
        functools.partial(update_kernel, added, cap),
        out_shape=[
            jax.ShapeDtypeStruct((hid, half), F32),
            jax.ShapeDtypeStruct((kept, half), F32),
        ],
        in_specs=specs(pltpu.VMEM, 6 + len(added)) + specs(pl.ANY, 1),
        out_specs=specs(pltpu.HBM, 1) + specs(pltpu.VMEM, 1),
        scratch_shapes=[
            pltpu.VMEM((depth, half), BF16),
            pltpu.VMEM((hid, depth), BF16),
            pltpu.VMEM((hid, half), F32),
            pltpu.VMEM((hid - kept, half), F32),
            pltpu.SemaphoreType.DMA((hid // (2 * TILE),)),
        ],
        compiler_params=params(),
        cost_estimate=cost(2 * depth * hid * half, 16 * hid * half),
        name="update",
    )(
        own_hidden,
        other_hidden,
        grad,
        param,
        moment[0, 0],
        second[0, 0],
        *[arrived[item] for item in added],
        last_scores,
    )
    shares = [array for arrays in returned.values() for array in arrays]
    router, update = pl.pallas_call(
        functools.partial(
            combine_kernel, [(k, len(arrays)) for k, arrays in returned.items()], group, cap
        ),
        out_shape=[
            jax.ShapeDtypeStruct((top, tokens), F32),
            jax.ShapeDtypeStruct((hid, half), F32),
        ],
        in_specs=specs(pltpu.HBM, 1) + specs(pltpu.VMEM, 3 + len(shares)),
        out_specs=specs(pltpu.VMEM, 1) + specs(pltpu.HBM, 1),
        input_output_aliases={0: 1},
        scratch_shapes=[pltpu.SemaphoreType.DMA],
        compiler_params=params(),
        cost_estimate=cost(4 * slots * tokens, 8 * top * tokens),
        name="combine",
    )(update, tail, ids, slot_of, *shares)
    return (update[None, None], router.T[None])


def solution(mesh):
    sections, group = mesh.devices.shape
    split = jax.sharding.Mesh(
        mesh.devices.reshape(2, sections // 2, group), ("pair", "rest", "ep")
    )
    section = ("pair", "rest")
    rows = P(section, "ep", None)
    blocks = P(section, "ep", None, None)
    return jax.shard_map(
        local,
        mesh=split,
        in_specs=(rows, rows, rows, blocks, blocks, blocks, blocks),
        out_specs=(blocks, rows),
        check_vma=False,
    )
```

```python
import functools

import jax
import jax.numpy as jnp
from jax import lax
from jax.experimental import pallas as pl
from jax.experimental.pallas import tpu as pltpu
from jax.sharding import PartitionSpec as P

beta_first = 0.9
beta_second = 0.95
adam_eps = 1e-08
decay_rate = 0.1
first_fix = 1.0 - 0.9**10
second_fix = 1.0 - 0.95**10
first_unit = (1.0 - beta_first) / first_fix
second_unit = (1.0 - beta_second) / second_fix

LANES = 128
TILE = 16
VMEM_BYTES = 32 * 1024 * 1024
F32 = jnp.float32
BF16 = jnp.bfloat16


def params():
    return pltpu.CompilerParams(vmem_limit_bytes=VMEM_BYTES)


def cost(flops, touched):
    return pl.CostEstimate(flops=int(flops), bytes_accessed=int(touched), transcendentals=0)


def specs(space, count):
    return [pl.BlockSpec(memory_space=space) for _ in range(count)]


def ep_index():
    return lax.axis_index("ep").astype(jnp.int32)


def own_half():
    return lax.axis_index("pair").astype(jnp.int32)


def start_grads(grads_hbm, held, sems):
    half = held.shape[2]
    mine = own_half()
    copies = []
    for side in range(2):
        column = pl.multiple_of((1 - mine if side else mine) * half, half)
        copies.append(
            pltpu.make_async_copy(
                grads_hbm.at[:, pl.ds(column, half)], held.at[side], sems.at[side]
            )
        )
        copies[-1].start()
    return copies


def pick_rows(slots, k, cap):
    place = lax.broadcasted_iota(jnp.int32, (cap, slots.shape[1]), 0).astype(F32)
    return jnp.where(place == slots[k : k + 1, :], 1.0, 0.0).astype(BF16)


def fill_chunks(steps, cap, picks, held, copies, tiles, chunks):
    half = held.shape[2]
    data_rows = half // LANES * cap
    pick = jnp.concatenate([picks[k] for k in steps], axis=0)
    for side in range(2):
        for k in steps:
            chunks[side, k][data_rows:, :] = tiles[k]
        copies[side].wait()
        block = jnp.dot(pick, held[side], preferred_element_type=F32).astype(BF16)
        for at, k in enumerate(steps):
            for part in range(half // LANES):
                chunks[side, k][part * cap : (part + 1) * cap, :] = block[
                    at * cap : (at + 1) * cap, part * LANES : (part + 1) * LANES
                ]


def route_kernel(
    items, steps, group, cap, ids_hbm, weight_hbm, grads_hbm, slots_ref, tiles_ref, *rest
):
    chunks = dict(zip(items, rest))
    ids_ref, weight_ref, held, sems = rest[len(items) :]
    tokens = held.shape[1]
    me = ep_index()
    small = [
        pltpu.make_async_copy(ids_hbm, ids_ref, sems.at[2]),
        pltpu.make_async_copy(weight_hbm, weight_ref, sems.at[3]),
    ]
    for copy in small:
        copy.start()
    copies = start_grads(grads_hbm, held, sems)
    earlier = lax.broadcasted_iota(jnp.int32, (tokens, tokens), 0)
    later = lax.broadcasted_iota(jnp.int32, (tokens, tokens), 1)
    ahead = jnp.where(earlier < later, 1.0, 0.0).astype(BF16)
    for copy in small:
        copy.wait()
    ids = ids_ref[...]
    weights = weight_ref[...].astype(F32)
    members, scales = [], []
    for k in range(group):
        named = ids == (me ^ k)
        members.append(jnp.sum(jnp.where(named, 1.0, 0.0), axis=0, keepdims=True))
        scales.append(jnp.sum(jnp.where(named, weights, 0.0), axis=0, keepdims=True))
    if group % TILE:
        members.append(jnp.zeros((-group % TILE, tokens), F32))
    member = jnp.concatenate(members, axis=0)
    before = jnp.dot(member.astype(BF16), ahead, preferred_element_type=F32)
    slots = jnp.where(member > 0.5, before, -1.0)
    slots_ref[...] = slots
    picks = [pick_rows(slots, k, cap) for k in range(group)]
    base = me * cap
    tile_row = lax.broadcasted_iota(jnp.int32, (TILE, LANES), 0)
    tile_lane = lax.broadcasted_iota(jnp.int32, (TILE, LANES), 1)
    spot = tile_row * LANES + tile_lane
    kept = (spot >= base) & (spot < base + cap)
    if group % TILE:
        scales.append(jnp.zeros((-group % TILE, tokens), F32))
    rows = jnp.concatenate(scales, axis=0)
    lines = lax.dot_general(
        rows.astype(BF16),
        jnp.concatenate(picks, axis=0),
        (((1,), (1,)), ((), ())),
        preferred_element_type=F32,
    )
    tiles = []
    for k in range(group):
        line = lines[k : k + 1, k * cap : (k + 1) * cap]
        line = jnp.concatenate([line] * (LANES // cap), axis=1)
        tiles.append(jnp.where(kept, line, 0.0).astype(BF16))
        tiles_ref[k] = tiles[k]
    fill_chunks(steps, cap, picks, held, copies, tiles, chunks)


def later_kernel(
    items, steps, cap, slots_ref, tiles_ref, grads_hbm, own_ref, other_ref, master_hbm, inner_ref, *rest
):
    chunks = dict(zip(items, rest))
    held, master_ref, sems = rest[len(items) :]
    copies = start_grads(grads_hbm, held, sems)
    half = master_ref.shape[1]
    step = min(half, 4 * LANES)
    parts = [slice(column, column + step) for column in range(0, half, step)]
    loads = [
        pltpu.make_async_copy(master_hbm.at[:, part], master_ref.at[:, part], sems.at[2 + at])
        for at, part in enumerate(parts)
    ]
    for load in loads:
        load.start()
    slots = slots_ref[...]
    picks = {k: pick_rows(slots, k, cap) for k in steps}
    fill_chunks(steps, cap, picks, held, copies, tiles_ref, chunks)
    slot_count = own_ref.shape[1]
    for load, part in zip(loads, parts):
        load.wait()
        weights = master_ref[:, part].astype(BF16)
        for at, ref in ((0, own_ref), (slot_count, other_ref)):
            inner_ref[at : at + slot_count, part] = lax.dot_general(
                ref[...], weights, (((0,), (0,)), ((), ())), preferred_element_type=F32
            )


def score_kernel(items, group, cap, inner_ref, *rest):
    chunks, score_ref = dict(zip(items, rest)), rest[-1]
    blocks = inner_ref.shape[1] // LANES
    me = ep_index()
    line_of = lax.broadcasted_iota(jnp.int32, score_ref.shape, 0)
    scores = jnp.zeros(score_ref.shape, F32)
    for k in sorted({k for _, k in items}):
        sums = []
        for side in range(2):
            total = jnp.zeros((cap, LANES), F32)
            if (side, k) in items:
                start = pl.multiple_of(side * group * cap + (me ^ k) * cap, cap)
                for block in range(blocks):
                    rows = chunks[side, k][block * cap : (block + 1) * cap, :].astype(F32)
                    total += rows * inner_ref[
                        pl.ds(start, cap), block * LANES : (block + 1) * LANES
                    ]
            sums.append(total)
        both = jnp.concatenate(sums, axis=0)
        line = jnp.sum(both.T, axis=0, keepdims=True)
        scores = jnp.where(line_of == (me ^ k), line, scores)
    score_ref[...] = scores


def scale_into(scaled, at, hidden, line):
    for top in range(0, hidden.shape[0], LANES):
        lines = slice(top, top + LANES)
        scaled[lines, at : at + LANES] = (hidden[lines, :].astype(F32) * line).astype(BF16)


def sum_kernel(items, group, cap, own_ref, other_ref, *rest):
    chunks = dict(zip(items, rest))
    grad_ref, rows, scaled = rest[-3:]
    blocks = rows.shape[1] // LANES
    slots = group * cap
    me = ep_index()
    for side, hidden in enumerate((own_ref, other_ref)):
        tile = jnp.zeros((TILE, LANES), F32)
        for k in range(group):
            start = pl.multiple_of(side * slots + (me ^ k) * cap, cap)
            if (side, k) not in items:
                rows[pl.ds(start, cap), :] = jnp.zeros((cap, rows.shape[1]), BF16)
                continue
            chunk = chunks[side, k]
            tile += chunk[blocks * cap :, :].astype(F32)
            for block in range(blocks):
                rows[pl.ds(start, cap), block * LANES : (block + 1) * LANES] = chunk[
                    block * cap : (block + 1) * cap, :
                ]
        for part in range(slots // LANES):
            lanes = slice(part * LANES, (part + 1) * LANES)
            scale_into(scaled, side * slots + part * LANES, hidden.at[:, lanes], tile[part : part + 1, :])
    grad_ref[...] = jnp.dot(scaled[...], rows[...], preferred_element_type=F32)


def merge_kernel(cap, own_ref, other_ref, _, out_ref):
    lane = lax.broadcasted_iota(jnp.int32, own_ref.shape, 1)
    scores = own_ref[...] + pltpu.roll(other_ref[...], LANES - cap, axis=1)
    out_ref[...] = jnp.where(lane < cap, scores, 0.0)


def update_kernel(items, cap, own_ref, other_ref, grad_ref, master_ref, moment_ref, second_ref, *rest):
    chunks = rest[: len(items)]
    _, update_hbm, rows, scaled, total, update, sems = rest[len(items) :]
    hid, half = update.shape
    width = min(half, 4 * LANES)
    height = 2 * TILE
    data_rows = half // LANES * cap
    me = ep_index()
    for at in range(0, len(items), 2):
        parts = []
        for turn, ((side, k), chunk) in enumerate(zip(items[at : at + 2], chunks[at : at + 2])):
            slot = (me ^ k) * cap
            lanes = pl.ds(pl.multiple_of(slot // LANES * LANES, LANES), LANES)
            place = slot % LANES if turn == 0 else (LANES - cap) - slot % LANES
            start = pl.multiple_of(at // 2 * LANES + place, cap)
            for part in range(half // LANES):
                rows[pl.ds(start, cap), part * LANES : (part + 1) * LANES] = chunk[
                    part * cap : (part + 1) * cap, :
                ]
            line = jnp.sum(chunk[data_rows:, :].astype(F32), axis=0, keepdims=True)
            parts.append(((own_ref, other_ref)[side], lanes, line))
        if len(parts) == 1:
            start = pl.multiple_of(at // 2 * LANES + (LANES - cap) - place, cap)
            rows[pl.ds(start, cap), :] = jnp.zeros((cap, half), BF16)
        for top in range(0, hid, LANES):
            values = [
                hidden[top : top + LANES, lanes].astype(F32) * line for hidden, lanes, line in parts
            ]
            if len(values) == 2:
                values[0] += pltpu.roll(values[1], LANES - cap, axis=1)
            scaled[top : top + LANES, at // 2 * LANES : (at // 2 + 1) * LANES] = values[0].astype(
                BF16
            )
    total[...] = jnp.dot(scaled[...], rows[...], preferred_element_type=F32)

    def moments(top, columns):
        lines = slice(top, top + TILE)
        grad = total[lines, columns] + grad_ref[lines, columns]
        unit = first_unit / second_unit**0.5
        first = moment_ref[lines, columns].astype(F32) * (
            unit * beta_first / (1.0 - beta_first)
        ) + grad * unit
        square = (
            second_ref[lines, columns].astype(F32) * (beta_second / (1.0 - beta_second))
            + grad * grad
        )
        return first, square, lax.rsqrt(square)

    def inverse(first, square, root):
        below = square * root + adam_eps / second_unit**0.5
        return first, root * (2.0 - below * root)

    def finish(top, columns, first, scale):
        lines = slice(top, top + TILE)
        update[lines, columns] = first * scale + decay_rate * master_ref[lines, columns]

    copies = []
    pieces = [
        (top, slice(column, column + width))
        for top in range(0, hid, TILE)
        for column in range(0, half, width)
    ]
    held = {}
    for turn in range(len(pieces) + 2):
        if turn < len(pieces):
            held[turn, 0] = moments(*pieces[turn])
        if 0 <= turn - 1 < len(pieces):
            held[turn - 1, 1] = inverse(*held.pop((turn - 1, 0)))
        if turn >= 2:
            finish(*pieces[turn - 2], *held.pop((turn - 2, 1)))
            top, columns = pieces[turn - 2]
            if (top + TILE) % height == 0 and columns.stop == half:
                lines = slice(top + TILE - height, top + TILE)
                copies.append(
                    pltpu.make_async_copy(
                        update.at[lines, :], update_hbm.at[lines, :], sems.at[len(copies)]
                    )
                )
                copies[-1].start()
    for copy in copies:
        copy.wait()


def combine_kernel(steps, group, cap, ids_ref, slots_ref, *rest):
    refs, out_ref = iter(rest[:-1]), rest[-1]
    tokens = ids_ref.shape[1]
    me = ep_index()
    shape = rest[0].shape
    lane = lax.broadcasted_iota(jnp.int32, shape, 1)
    row = lax.broadcasted_iota(jnp.int32, shape, 0)
    lines = jnp.zeros(shape, F32)
    for k, tiles in steps:
        scores = next(refs)[...]
        if tiles == 2:
            scores = jnp.where(lane < cap, scores, next(refs)[...])
        line = jnp.sum(jnp.where(row == me, scores, 0.0), axis=0, keepdims=True)
        lines = jnp.where(row == k, line, lines)
    rest = jnp.zeros((LANES - lines.shape[0], LANES), F32)
    columns = jnp.concatenate([lines, rest], axis=0).T
    columns = columns[:cap] + columns[cap : 2 * cap]
    place = lax.broadcasted_iota(jnp.int32, (cap, tokens), 0).astype(F32)
    ids = ids_ref[...]
    result = jnp.zeros(ids.shape, F32)
    for k in range(group):
        at_slot = jnp.where(place == slots_ref[k : k + 1, :], columns[:, k : k + 1], 0.0)
        result = jnp.where(ids == (me ^ k), jnp.sum(at_slot, axis=0, keepdims=True), result)
    out_ref[...] = result


def moved(array, side, step):
    if (side, step) == (0, 0):
        return array
    group = lax.axis_size("ep")
    pairs = [
        (p * group + e, (p ^ side) * group + (e ^ step)) for p in range(2) for e in range(group)
    ]
    return lax.ppermute(array, ("pair", "ep"), pairs)


def local(grad_out, router_weights, expert_ids, hidden, master, moment, second):
    group = lax.axis_size("ep")
    tokens, width = grad_out.shape[1:]
    top = expert_ids.shape[2]
    hid, slots = hidden.shape[2:]
    half = master.shape[3]
    cap = slots // group
    ids = expert_ids[0].T
    own_hidden = hidden[0, 0]
    param = master[0, 0]
    other_hidden = moved(own_hidden, 1, 0)

    far = group // 2
    first = [k for k in range(1, group) if k != far]
    late = [0, far]
    first_items = [(side, k) for side in range(2) for k in reversed(first)]
    last_items = [(1, far), (0, far), (1, 0), (0, 0)]
    order = first_items + last_items
    chunk = jax.ShapeDtypeStruct((half // LANES * cap + TILE, LANES), BF16)
    grads = pltpu.with_memory_space_constraint(grad_out[0], pltpu.HBM)
    held = pltpu.VMEM((2, tokens, half), BF16)
    routed = pl.pallas_call(
        functools.partial(route_kernel, first_items, first, group, cap),
        out_shape=[
            jax.ShapeDtypeStruct((group + -group % TILE, tokens), F32),
            jax.ShapeDtypeStruct((group, TILE, LANES), BF16),
        ]
        + [chunk] * len(first_items),
        in_specs=specs(pltpu.HBM, 3),
        out_specs=specs(pltpu.VMEM, 2 + len(first_items)),
        scratch_shapes=[
            pltpu.VMEM((top, tokens), jnp.int32),
            pltpu.VMEM((top, tokens), BF16),
            held,
            pltpu.SemaphoreType.DMA((4,)),
        ],
        compiler_params=params(),
        cost_estimate=cost(2 * slots * tokens * width, 2 * (tokens + slots) * width),
        name="route",
    )(
        pltpu.with_memory_space_constraint(ids, pltpu.HBM),
        pltpu.with_memory_space_constraint(router_weights[0].T, pltpu.HBM),
        grads,
    )
    slot_of, tiles = routed[:2]
    arrived = {item: moved(sent, *item) for item, sent in zip(first_items, routed[2:])}

    routed = pl.pallas_call(
        functools.partial(later_kernel, last_items, late, cap),
        out_shape=[jax.ShapeDtypeStruct((2 * slots, half), F32)] + [chunk] * len(last_items),
        in_specs=specs(pltpu.VMEM, 2)
        + specs(pltpu.HBM, 1)
        + specs(pltpu.VMEM, 2)
        + specs(pltpu.HBM, 1),
        out_specs=specs(pltpu.VMEM, 1 + len(last_items)),
        scratch_shapes=[
            held,
            pltpu.VMEM((hid, half), F32),
            pltpu.SemaphoreType.DMA((2 + half // min(half, 4 * LANES),)),
        ],
        compiler_params=params(),
        cost_estimate=cost(
            2 * slots * tokens * width + 4 * slots * hid * half, 2 * (tokens + slots) * width
        ),
        name="later",
    )(
        slot_of,
        tiles,
        grads,
        own_hidden,
        other_hidden,
        pltpu.with_memory_space_constraint(param, pltpu.HBM),
    )
    inner = routed[0]
    arrived |= {item: moved(sent, *item) for item, sent in zip(last_items, routed[1:])}

    tile = jax.ShapeDtypeStruct((group + -group % 8, LANES), F32)

    def scored(items, *after):
        return pl.pallas_call(
            functools.partial(score_kernel, items, group, cap),
            out_shape=tile,
            in_specs=specs(pltpu.VMEM, 1 + len(items)) + specs(pl.ANY, len(after)),
            out_specs=specs(pltpu.VMEM, 1)[0],
            compiler_params=params(),
            cost_estimate=cost(2 * cap * half, 6 * cap * half),
            name="score",
        )(inner, *[arrived[item] for item in items], *after)

    first_scores = scored(first_items)
    other_scores = moved(first_scores, 1, 0)
    added = [(1, far), (0, far), (1, 0)]
    summed = [item for item in order if item not in added]
    grad = pl.pallas_call(
        functools.partial(sum_kernel, summed, group, cap),
        out_shape=jax.ShapeDtypeStruct((hid, half), F32),
        in_specs=specs(pltpu.VMEM, 2 + len(summed)) + specs(pl.ANY, 1),
        out_specs=specs(pltpu.VMEM, 1)[0],
        scratch_shapes=[
            pltpu.VMEM((2 * slots, half), BF16),
            pltpu.VMEM((hid, 2 * slots), BF16),
        ],
        compiler_params=params(),
        cost_estimate=cost(4 * slots * hid * half, 4 * hid * half),
        name="sum",
    )(own_hidden, other_hidden, *[arrived[item] for item in summed], first_scores)
    merged = pl.pallas_call(
        functools.partial(merge_kernel, cap),
        out_shape=tile,
        in_specs=specs(pltpu.VMEM, 2) + specs(pl.ANY, 1),
        out_specs=specs(pltpu.VMEM, 1)[0],
        compiler_params=params(),
        name="merge",
    )(first_scores, other_scores, grad)
    returned = {k: [moved(merged, 0, k)] for k in first}
    zero_scores = scored([(0, 0), (1, 0)], merged)
    returned[0] = [zero_scores, moved(zero_scores, 1, 0)]
    other_far = scored([(1, far)], zero_scores)
    last_scores = scored([(0, far)], other_far)
    returned[far] = [moved(last_scores, 0, far), moved(other_far, 1, far)]

    depth = -(-len(added) // 2) * LANES
    update = pl.pallas_call(
        functools.partial(update_kernel, added, cap),
        out_shape=jax.ShapeDtypeStruct((hid, half), F32),
        in_specs=specs(pltpu.VMEM, 6 + len(added)) + specs(pl.ANY, 1),
        out_specs=specs(pltpu.HBM, 1)[0],
        scratch_shapes=[
            pltpu.VMEM((depth, half), BF16),
            pltpu.VMEM((hid, depth), BF16),
            pltpu.VMEM((hid, half), F32),
            pltpu.VMEM((hid, half), F32),
            pltpu.SemaphoreType.DMA((hid // (2 * TILE),)),
        ],
        compiler_params=params(),
        cost_estimate=cost(2 * depth * hid * half, 16 * hid * half),
        name="update",
    )(
        own_hidden,
        other_hidden,
        grad,
        param,
        moment[0, 0],
        second[0, 0],
        *[arrived[item] for item in added],
        last_scores,
    )
    shares = [array for arrays in returned.values() for array in arrays]
    router = pl.pallas_call(
        functools.partial(
            combine_kernel, [(k, len(arrays)) for k, arrays in returned.items()], group, cap
        ),
        out_shape=jax.ShapeDtypeStruct((top, tokens), F32),
        in_specs=specs(pltpu.VMEM, 2 + len(shares)),
        out_specs=specs(pltpu.VMEM, 1)[0],
        compiler_params=params(),
        cost_estimate=cost(4 * slots * tokens, 8 * top * tokens),
        name="combine",
    )(ids, slot_of, *shares)
    return (update[None, None], router.T[None])


def solution(mesh):
    sections, group = mesh.devices.shape
    split = jax.sharding.Mesh(
        mesh.devices.reshape(2, sections // 2, group), ("pair", "rest", "ep")
    )
    section = ("pair", "rest")
    rows = P(section, "ep", None)
    blocks = P(section, "ep", None, None)
    return jax.shard_map(
        local,
        mesh=split,
        in_specs=(rows, rows, rows, blocks, blocks, blocks, blocks),
        out_specs=(blocks, rows),
        check_vma=False,
    )
```

```python
import functools

import jax
import jax.numpy as jnp
from jax import lax
from jax.experimental import pallas as pl
from jax.experimental.pallas import tpu as pltpu
from jax.sharding import PartitionSpec as P

beta_first = 0.9
beta_second = 0.95
adam_eps = 1e-08
decay_rate = 0.1
first_fix = 1.0 - 0.9**10
second_fix = 1.0 - 0.95**10
first_unit = (1.0 - beta_first) / first_fix
second_unit = (1.0 - beta_second) / second_fix

LANES = 128
TILE = 16
VMEM_BYTES = 32 * 1024 * 1024
F32 = jnp.float32
BF16 = jnp.bfloat16


def params():
    return pltpu.CompilerParams(vmem_limit_bytes=VMEM_BYTES)


def cost(flops, touched):
    return pl.CostEstimate(flops=int(flops), bytes_accessed=int(touched), transcendentals=0)


def specs(space, count):
    return [pl.BlockSpec(memory_space=space) for _ in range(count)]


def ep_index():
    return lax.axis_index("ep").astype(jnp.int32)


def own_half():
    return lax.axis_index("pair").astype(jnp.int32)


def start_grads(grads_hbm, held, sems):
    half = held.shape[2]
    mine = own_half()
    copies = []
    for side in range(2):
        column = pl.multiple_of((1 - mine if side else mine) * half, half)
        copies.append(
            pltpu.make_async_copy(
                grads_hbm.at[:, pl.ds(column, half)], held.at[side], sems.at[side]
            )
        )
        copies[-1].start()
    return copies


def pick_rows(slots, k, cap):
    place = lax.broadcasted_iota(jnp.int32, (cap, slots.shape[1]), 0).astype(F32)
    return jnp.where(place == slots[k : k + 1, :], 1.0, 0.0).astype(BF16)


def fill_chunks(steps, cap, picks, held, copies, tiles, chunks):
    half = held.shape[2]
    data_rows = half // LANES * cap
    pick = jnp.concatenate([picks[k] for k in steps], axis=0)
    for side in range(2):
        for k in steps:
            chunks[side, k][data_rows:, :] = tiles[k]
        copies[side].wait()
        block = jnp.dot(pick, held[side], preferred_element_type=F32).astype(BF16)
        for at, k in enumerate(steps):
            for part in range(half // LANES):
                chunks[side, k][part * cap : (part + 1) * cap, :] = block[
                    at * cap : (at + 1) * cap, part * LANES : (part + 1) * LANES
                ]


def route_kernel(
    items, steps, group, cap, ids_hbm, weight_ref, grads_hbm, slots_ref, tiles_ref, *rest
):
    chunks = dict(zip(items, rest))
    ids_ref, held, sems = rest[len(items) :]
    tokens = held.shape[1]
    me = ep_index()
    small = pltpu.make_async_copy(ids_hbm, ids_ref, sems.at[2])
    small.start()
    copies = start_grads(grads_hbm, held, sems)
    earlier = lax.broadcasted_iota(jnp.int32, (tokens, tokens), 0)
    later = lax.broadcasted_iota(jnp.int32, (tokens, tokens), 1)
    ahead = jnp.where(earlier < later, 1.0, 0.0).astype(BF16)
    small.wait()
    ids = ids_ref[...]
    weights = weight_ref[...].astype(F32)
    members, scales = [], []
    for k in range(group):
        named = ids == (me ^ k)
        members.append(jnp.sum(jnp.where(named, 1.0, 0.0), axis=0, keepdims=True))
        scales.append(jnp.sum(jnp.where(named, weights, 0.0), axis=0, keepdims=True))
    if group % TILE:
        members.append(jnp.zeros((-group % TILE, tokens), F32))
    member = jnp.concatenate(members, axis=0)
    before = jnp.dot(member.astype(BF16), ahead, preferred_element_type=F32)
    slots = jnp.where(member > 0.5, before, -1.0)
    slots_ref[...] = slots
    picks = [pick_rows(slots, k, cap) for k in range(group)]
    base = me * cap
    tile_row = lax.broadcasted_iota(jnp.int32, (TILE, LANES), 0)
    tile_lane = lax.broadcasted_iota(jnp.int32, (TILE, LANES), 1)
    spot = tile_row * LANES + tile_lane
    kept = (spot >= base) & (spot < base + cap)
    if group % TILE:
        scales.append(jnp.zeros((-group % TILE, tokens), F32))
    rows = jnp.concatenate(scales, axis=0)
    lines = lax.dot_general(
        rows.astype(BF16),
        jnp.concatenate(picks, axis=0),
        (((1,), (1,)), ((), ())),
        preferred_element_type=F32,
    )
    tiles = []
    for k in range(group):
        line = lines[k : k + 1, k * cap : (k + 1) * cap]
        line = jnp.concatenate([line] * (LANES // cap), axis=1)
        tiles.append(jnp.where(kept, line, 0.0).astype(BF16))
        tiles_ref[k] = tiles[k]
    fill_chunks(steps, cap, picks, held, copies, tiles, chunks)


def later_kernel(
    items, steps, cap, slots_ref, tiles_ref, grads_hbm, own_ref, other_ref, master_hbm, inner_ref, *rest
):
    chunks = dict(zip(items, rest))
    held, master_ref, sems = rest[len(items) :]
    copies = start_grads(grads_hbm, held, sems)
    half = master_ref.shape[1]
    step = min(half, 4 * LANES)
    parts = [slice(column, column + step) for column in range(0, half, step)]
    loads = [
        pltpu.make_async_copy(master_hbm.at[:, part], master_ref.at[:, part], sems.at[2 + at])
        for at, part in enumerate(parts)
    ]
    for load in loads:
        load.start()
    slots = slots_ref[...]
    picks = {k: pick_rows(slots, k, cap) for k in steps}
    fill_chunks(steps, cap, picks, held, copies, tiles_ref, chunks)
    slot_count = own_ref.shape[1]
    for load, part in zip(loads, parts):
        load.wait()
        weights = master_ref[:, part].astype(BF16)
        for at, ref in ((0, own_ref), (slot_count, other_ref)):
            inner_ref[at : at + slot_count, part] = lax.dot_general(
                ref[...], weights, (((0,), (0,)), ((), ())), preferred_element_type=F32
            )


def score_kernel(items, group, cap, inner_ref, *rest):
    chunks, score_ref = dict(zip(items, rest)), rest[-1]
    blocks = inner_ref.shape[1] // LANES
    me = ep_index()
    line_of = lax.broadcasted_iota(jnp.int32, score_ref.shape, 0)
    scores = jnp.zeros(score_ref.shape, F32)
    for k in sorted({k for _, k in items}):
        sums = []
        for side in range(2):
            total = jnp.zeros((cap, LANES), F32)
            if (side, k) in items:
                start = pl.multiple_of(side * group * cap + (me ^ k) * cap, cap)
                for block in range(blocks):
                    rows = chunks[side, k][block * cap : (block + 1) * cap, :].astype(F32)
                    total += rows * inner_ref[
                        pl.ds(start, cap), block * LANES : (block + 1) * LANES
                    ]
            sums.append(total)
        both = jnp.concatenate(sums, axis=0)
        line = jnp.sum(both.T, axis=0, keepdims=True)
        scores = jnp.where(line_of == (me ^ k), line, scores)
    score_ref[...] = scores


def scale_into(scaled, at, hidden, line):
    for top in range(0, hidden.shape[0], LANES):
        lines = slice(top, top + LANES)
        scaled[lines, at : at + LANES] = (hidden[lines, :].astype(F32) * line).astype(BF16)


def sum_kernel(items, group, cap, own_ref, other_ref, *rest):
    chunks = dict(zip(items, rest))
    grad_ref, rows, scaled = rest[-3:]
    blocks = rows.shape[1] // LANES
    slots = group * cap
    me = ep_index()
    for side, hidden in enumerate((own_ref, other_ref)):
        tile = jnp.zeros((TILE, LANES), F32)
        for k in range(group):
            start = pl.multiple_of(side * slots + (me ^ k) * cap, cap)
            if (side, k) not in items:
                rows[pl.ds(start, cap), :] = jnp.zeros((cap, rows.shape[1]), BF16)
                continue
            chunk = chunks[side, k]
            tile += chunk[blocks * cap :, :].astype(F32)
            for block in range(blocks):
                rows[pl.ds(start, cap), block * LANES : (block + 1) * LANES] = chunk[
                    block * cap : (block + 1) * cap, :
                ]
        for part in range(slots // LANES):
            lanes = slice(part * LANES, (part + 1) * LANES)
            scale_into(scaled, side * slots + part * LANES, hidden.at[:, lanes], tile[part : part + 1, :])
    grad_ref[...] = jnp.dot(scaled[...], rows[...], preferred_element_type=F32)


def merge_kernel(cap, own_ref, other_ref, _, out_ref):
    lane = lax.broadcasted_iota(jnp.int32, own_ref.shape, 1)
    scores = own_ref[...] + pltpu.roll(other_ref[...], LANES - cap, axis=1)
    out_ref[...] = jnp.where(lane < cap, scores, 0.0)


def update_kernel(items, cap, own_ref, other_ref, grad_ref, master_ref, moment_ref, second_ref, *rest):
    chunks = rest[: len(items)]
    _, update_hbm, rows, scaled, total, update, sems = rest[len(items) :]
    hid, half = update.shape
    width = min(half, 4 * LANES)
    height = 2 * TILE
    data_rows = half // LANES * cap
    me = ep_index()
    for at in range(0, len(items), 2):
        parts = []
        for turn, ((side, k), chunk) in enumerate(zip(items[at : at + 2], chunks[at : at + 2])):
            slot = (me ^ k) * cap
            lanes = pl.ds(pl.multiple_of(slot // LANES * LANES, LANES), LANES)
            place = slot % LANES if turn == 0 else (LANES - cap) - slot % LANES
            start = pl.multiple_of(at // 2 * LANES + place, cap)
            for part in range(half // LANES):
                rows[pl.ds(start, cap), part * LANES : (part + 1) * LANES] = chunk[
                    part * cap : (part + 1) * cap, :
                ]
            line = jnp.sum(chunk[data_rows:, :].astype(F32), axis=0, keepdims=True)
            parts.append(((own_ref, other_ref)[side], lanes, line))
        if len(parts) == 1:
            start = pl.multiple_of(at // 2 * LANES + (LANES - cap) - place, cap)
            rows[pl.ds(start, cap), :] = jnp.zeros((cap, half), BF16)
        for top in range(0, hid, LANES):
            values = [
                hidden[top : top + LANES, lanes].astype(F32) * line for hidden, lanes, line in parts
            ]
            if len(values) == 2:
                values[0] += pltpu.roll(values[1], LANES - cap, axis=1)
            scaled[top : top + LANES, at // 2 * LANES : (at // 2 + 1) * LANES] = values[0].astype(
                BF16
            )
    total[...] = jnp.dot(scaled[...], rows[...], preferred_element_type=F32)

    def moments(top, columns):
        lines = slice(top, top + TILE)
        grad = total[lines, columns] + grad_ref[lines, columns]
        first = moment_ref[lines, columns].astype(F32) * (beta_first / (1.0 - beta_first)) + grad
        square = (
            second_ref[lines, columns].astype(F32) * (beta_second / (1.0 - beta_second))
            + grad * grad
        )
        return first, square, lax.rsqrt(square)

    def inverse(first, square, root):
        scale = square * root * (second_unit**0.5 / first_unit) + adam_eps / first_unit
        return first, pl.reciprocal(scale, approx=True)

    def finish(top, columns, first, scale):
        lines = slice(top, top + TILE)
        update[lines, columns] = first * scale + decay_rate * master_ref[lines, columns]

    copies = []
    pieces = [
        (top, slice(column, column + width))
        for top in range(0, hid, TILE)
        for column in range(0, half, width)
    ]
    held = {}
    for turn in range(len(pieces) + 2):
        if turn < len(pieces):
            held[turn, 0] = moments(*pieces[turn])
        if 0 <= turn - 1 < len(pieces):
            held[turn - 1, 1] = inverse(*held.pop((turn - 1, 0)))
        if turn >= 2:
            finish(*pieces[turn - 2], *held.pop((turn - 2, 1)))
            top, columns = pieces[turn - 2]
            if (top + TILE) % height == 0 and columns.stop == half:
                lines = slice(top + TILE - height, top + TILE)
                copies.append(
                    pltpu.make_async_copy(
                        update.at[lines, :], update_hbm.at[lines, :], sems.at[len(copies)]
                    )
                )
                copies[-1].start()
    for copy in copies:
        copy.wait()


def combine_kernel(steps, group, cap, ids_ref, slots_ref, *rest):
    refs, out_ref = iter(rest[:-1]), rest[-1]
    tokens = ids_ref.shape[1]
    me = ep_index()
    shape = rest[0].shape
    lane = lax.broadcasted_iota(jnp.int32, shape, 1)
    row = lax.broadcasted_iota(jnp.int32, shape, 0)
    lines = jnp.zeros(shape, F32)
    for k, tiles in steps:
        scores = next(refs)[...]
        if tiles == 2:
            scores = jnp.where(lane < cap, scores, next(refs)[...])
        line = jnp.sum(jnp.where(row == me, scores, 0.0), axis=0, keepdims=True)
        lines = jnp.where(row == k, line, lines)
    rest = jnp.zeros((LANES - lines.shape[0], LANES), F32)
    columns = jnp.concatenate([lines, rest], axis=0).T
    columns = columns[:cap] + columns[cap : 2 * cap]
    place = lax.broadcasted_iota(jnp.int32, (cap, tokens), 0).astype(F32)
    ids = ids_ref[...]
    result = jnp.zeros(ids.shape, F32)
    for k in range(group):
        at_slot = jnp.where(place == slots_ref[k : k + 1, :], columns[:, k : k + 1], 0.0)
        result = jnp.where(ids == (me ^ k), jnp.sum(at_slot, axis=0, keepdims=True), result)
    out_ref[...] = result


def moved(array, side, step):
    if (side, step) == (0, 0):
        return array
    group = lax.axis_size("ep")
    pairs = [
        (p * group + e, (p ^ side) * group + (e ^ step)) for p in range(2) for e in range(group)
    ]
    return lax.ppermute(array, ("pair", "ep"), pairs)


def local(grad_out, router_weights, expert_ids, hidden, master, moment, second):
    group = lax.axis_size("ep")
    tokens, width = grad_out.shape[1:]
    top = expert_ids.shape[2]
    hid, slots = hidden.shape[2:]
    half = master.shape[3]
    cap = slots // group
    ids = expert_ids[0].T
    own_hidden = hidden[0, 0]
    param = master[0, 0]
    other_hidden = moved(own_hidden, 1, 0)

    far = group // 2
    first = [k for k in range(1, group) if k != far]
    late = [0, far]
    first_items = [(side, k) for side in range(2) for k in reversed(first)]
    last_items = [(1, far), (0, far), (1, 0), (0, 0)]
    order = first_items + last_items
    chunk = jax.ShapeDtypeStruct((half // LANES * cap + TILE, LANES), BF16)
    grads = pltpu.with_memory_space_constraint(grad_out[0], pltpu.HBM)
    held = pltpu.VMEM((2, tokens, half), BF16)
    routed = pl.pallas_call(
        functools.partial(route_kernel, first_items, first, group, cap),
        out_shape=[
            jax.ShapeDtypeStruct((group + -group % TILE, tokens), F32),
            jax.ShapeDtypeStruct((group, TILE, LANES), BF16),
        ]
        + [chunk] * len(first_items),
        in_specs=specs(pltpu.HBM, 1) + specs(pltpu.VMEM, 1) + specs(pltpu.HBM, 1),
        out_specs=specs(pltpu.VMEM, 2 + len(first_items)),
        scratch_shapes=[
            pltpu.VMEM((top, tokens), jnp.int32),
            held,
            pltpu.SemaphoreType.DMA((3,)),
        ],
        compiler_params=params(),
        cost_estimate=cost(2 * slots * tokens * width, 2 * (tokens + slots) * width),
        name="route",
    )(
        pltpu.with_memory_space_constraint(ids, pltpu.HBM),
        router_weights[0].T,
        grads,
    )
    slot_of, tiles = routed[:2]
    arrived = {item: moved(sent, *item) for item, sent in zip(first_items, routed[2:])}

    routed = pl.pallas_call(
        functools.partial(later_kernel, last_items, late, cap),
        out_shape=[jax.ShapeDtypeStruct((2 * slots, half), F32)] + [chunk] * len(last_items),
        in_specs=specs(pltpu.VMEM, 2)
        + specs(pltpu.HBM, 1)
        + specs(pltpu.VMEM, 2)
        + specs(pltpu.HBM, 1),
        out_specs=specs(pltpu.VMEM, 1 + len(last_items)),
        scratch_shapes=[
            held,
            pltpu.VMEM((hid, half), F32),
            pltpu.SemaphoreType.DMA((2 + half // min(half, 4 * LANES),)),
        ],
        compiler_params=params(),
        cost_estimate=cost(
            2 * slots * tokens * width + 4 * slots * hid * half, 2 * (tokens + slots) * width
        ),
        name="later",
    )(
        slot_of,
        tiles,
        grads,
        own_hidden,
        other_hidden,
        pltpu.with_memory_space_constraint(param, pltpu.HBM),
    )
    inner = routed[0]
    arrived |= {item: moved(sent, *item) for item, sent in zip(last_items, routed[1:])}

    tile = jax.ShapeDtypeStruct((group + -group % 8, LANES), F32)

    def scored(items, *after):
        return pl.pallas_call(
            functools.partial(score_kernel, items, group, cap),
            out_shape=tile,
            in_specs=specs(pltpu.VMEM, 1 + len(items)) + specs(pl.ANY, len(after)),
            out_specs=specs(pltpu.VMEM, 1)[0],
            compiler_params=params(),
            cost_estimate=cost(2 * cap * half, 6 * cap * half),
            name="score",
        )(inner, *[arrived[item] for item in items], *after)

    first_scores = scored(first_items)
    other_scores = moved(first_scores, 1, 0)
    added = [(1, far), (0, far), (1, 0)]
    summed = [item for item in order if item not in added]
    grad = pl.pallas_call(
        functools.partial(sum_kernel, summed, group, cap),
        out_shape=jax.ShapeDtypeStruct((hid, half), F32),
        in_specs=specs(pltpu.VMEM, 2 + len(summed)) + specs(pl.ANY, 1),
        out_specs=specs(pltpu.VMEM, 1)[0],
        scratch_shapes=[
            pltpu.VMEM((2 * slots, half), BF16),
            pltpu.VMEM((hid, 2 * slots), BF16),
        ],
        compiler_params=params(),
        cost_estimate=cost(4 * slots * hid * half, 4 * hid * half),
        name="sum",
    )(own_hidden, other_hidden, *[arrived[item] for item in summed], first_scores)
    merged = pl.pallas_call(
        functools.partial(merge_kernel, cap),
        out_shape=tile,
        in_specs=specs(pltpu.VMEM, 2) + specs(pl.ANY, 1),
        out_specs=specs(pltpu.VMEM, 1)[0],
        compiler_params=params(),
        name="merge",
    )(first_scores, other_scores, grad)
    returned = {k: [moved(merged, 0, k)] for k in first}
    zero_scores = scored([(0, 0), (1, 0)], merged)
    returned[0] = [zero_scores, moved(zero_scores, 1, 0)]
    other_far = scored([(1, far)], zero_scores)
    last_scores = scored([(0, far)], other_far)
    returned[far] = [moved(last_scores, 0, far), moved(other_far, 1, far)]

    depth = -(-len(added) // 2) * LANES
    update = pl.pallas_call(
        functools.partial(update_kernel, added, cap),
        out_shape=jax.ShapeDtypeStruct((hid, half), F32),
        in_specs=specs(pltpu.VMEM, 6 + len(added)) + specs(pl.ANY, 1),
        out_specs=specs(pltpu.HBM, 1)[0],
        scratch_shapes=[
            pltpu.VMEM((depth, half), BF16),
            pltpu.VMEM((hid, depth), BF16),
            pltpu.VMEM((hid, half), F32),
            pltpu.VMEM((hid, half), F32),
            pltpu.SemaphoreType.DMA((hid // (2 * TILE),)),
        ],
        compiler_params=params(),
        cost_estimate=cost(2 * depth * hid * half, 16 * hid * half),
        name="update",
    )(
        own_hidden,
        other_hidden,
        grad,
        param,
        moment[0, 0],
        second[0, 0],
        *[arrived[item] for item in added],
        last_scores,
    )
    shares = [array for arrays in returned.values() for array in arrays]
    router = pl.pallas_call(
        functools.partial(
            combine_kernel, [(k, len(arrays)) for k, arrays in returned.items()], group, cap
        ),
        out_shape=jax.ShapeDtypeStruct((top, tokens), F32),
        in_specs=specs(pltpu.VMEM, 2 + len(shares)),
        out_specs=specs(pltpu.VMEM, 1)[0],
        compiler_params=params(),
        cost_estimate=cost(4 * slots * tokens, 8 * top * tokens),
        name="combine",
    )(ids, slot_of, *shares)
    return (update[None, None], router.T[None])


def solution(mesh):
    sections, group = mesh.devices.shape
    split = jax.sharding.Mesh(
        mesh.devices.reshape(2, sections // 2, group), ("pair", "rest", "ep")
    )
    section = ("pair", "rest")
    rows = P(section, "ep", None)
    blocks = P(section, "ep", None, None)
    return jax.shard_map(
        local,
        mesh=split,
        in_specs=(rows, rows, rows, blocks, blocks, blocks, blocks),
        out_specs=(blocks, rows),
        check_vma=False,
    )
```

```python
import functools

import jax
import jax.numpy as jnp
from jax import lax
from jax.experimental import pallas as pl
from jax.experimental.pallas import tpu as pltpu
from jax.sharding import PartitionSpec as P

beta_first = 0.9
beta_second = 0.95
adam_eps = 1e-08
decay_rate = 0.1
first_fix = 1.0 - 0.9**10
second_fix = 1.0 - 0.95**10
first_unit = (1.0 - beta_first) / first_fix
second_unit = (1.0 - beta_second) / second_fix

LANES = 128
TILE = 16
VMEM_BYTES = 32 * 1024 * 1024
F32 = jnp.float32
BF16 = jnp.bfloat16


def params():
    return pltpu.CompilerParams(vmem_limit_bytes=VMEM_BYTES)


def cost(flops, touched):
    return pl.CostEstimate(flops=int(flops), bytes_accessed=int(touched), transcendentals=0)


def specs(space, count):
    return [pl.BlockSpec(memory_space=space) for _ in range(count)]


def ep_index():
    return lax.axis_index("ep").astype(jnp.int32)


def own_half():
    return lax.axis_index("pair").astype(jnp.int32)


def start_grads(grads_hbm, held, sems):
    half = held.shape[2]
    mine = own_half()
    copies = []
    for side in range(2):
        column = pl.multiple_of((1 - mine if side else mine) * half, half)
        copies.append(
            pltpu.make_async_copy(
                grads_hbm.at[:, pl.ds(column, half)], held.at[side], sems.at[side]
            )
        )
        copies[-1].start()
    return copies


def pick_rows(slots, k, cap):
    place = lax.broadcasted_iota(jnp.int32, (cap, slots.shape[1]), 0).astype(F32)
    return jnp.where(place == slots[k : k + 1, :], 1.0, 0.0).astype(BF16)


def fill_chunks(steps, cap, picks, held, copies, tiles, chunks):
    half = held.shape[2]
    data_rows = half // LANES * cap
    pick = jnp.concatenate([picks[k] for k in steps], axis=0)
    for side in range(2):
        for k in steps:
            chunks[side, k][data_rows:, :] = tiles[k]
        copies[side].wait()
        block = jnp.dot(pick, held[side], preferred_element_type=F32).astype(BF16)
        for at, k in enumerate(steps):
            for part in range(half // LANES):
                chunks[side, k][part * cap : (part + 1) * cap, :] = block[
                    at * cap : (at + 1) * cap, part * LANES : (part + 1) * LANES
                ]


def route_kernel(
    items, steps, group, cap, ids_hbm, weight_hbm, grads_hbm, slots_ref, tiles_ref, *rest
):
    chunks = dict(zip(items, rest))
    ids_ref, weight_ref, held, sems = rest[len(items) :]
    tokens = held.shape[1]
    me = ep_index()
    small = [
        pltpu.make_async_copy(ids_hbm, ids_ref, sems.at[2]),
        pltpu.make_async_copy(weight_hbm, weight_ref, sems.at[3]),
    ]
    for copy in small:
        copy.start()
    copies = start_grads(grads_hbm, held, sems)
    earlier = lax.broadcasted_iota(jnp.int32, (tokens, tokens), 0)
    later = lax.broadcasted_iota(jnp.int32, (tokens, tokens), 1)
    ahead = jnp.where(earlier < later, 1.0, 0.0).astype(BF16)
    for copy in small:
        copy.wait()
    ids = ids_ref[...]
    weights = weight_ref[...].astype(F32)
    members, scales = [], []
    for k in range(group):
        named = ids == (me ^ k)
        members.append(jnp.sum(jnp.where(named, 1.0, 0.0), axis=0, keepdims=True))
        scales.append(jnp.sum(jnp.where(named, weights, 0.0), axis=0, keepdims=True))
    if group % TILE:
        members.append(jnp.zeros((-group % TILE, tokens), F32))
    member = jnp.concatenate(members, axis=0)
    before = jnp.dot(member.astype(BF16), ahead, preferred_element_type=F32)
    slots = jnp.where(member > 0.5, before, -1.0)
    slots_ref[...] = slots
    picks = [pick_rows(slots, k, cap) for k in range(group)]
    base = me * cap
    tile_row = lax.broadcasted_iota(jnp.int32, (TILE, LANES), 0)
    tile_lane = lax.broadcasted_iota(jnp.int32, (TILE, LANES), 1)
    spot = tile_row * LANES + tile_lane
    kept = (spot >= base) & (spot < base + cap)
    if group % TILE:
        scales.append(jnp.zeros((-group % TILE, tokens), F32))
    rows = jnp.concatenate(scales, axis=0)
    lines = lax.dot_general(
        rows.astype(BF16),
        jnp.concatenate(picks, axis=0),
        (((1,), (1,)), ((), ())),
        preferred_element_type=F32,
    )
    tiles = []
    for k in range(group):
        line = lines[k : k + 1, k * cap : (k + 1) * cap]
        line = jnp.concatenate([line] * (LANES // cap), axis=1)
        tiles.append(jnp.where(kept, line, 0.0).astype(BF16))
        tiles_ref[k] = tiles[k]
    fill_chunks(steps, cap, picks, held, copies, tiles, chunks)


def later_kernel(
    items, steps, cap, slots_ref, tiles_ref, grads_hbm, own_ref, other_ref, master_hbm, inner_ref, *rest
):
    chunks = dict(zip(items, rest))
    held, master_ref, sems = rest[len(items) :]
    copies = start_grads(grads_hbm, held, sems)
    half = master_ref.shape[1]
    step = min(half, 4 * LANES)
    parts = [slice(column, column + step) for column in range(0, half, step)]
    loads = [
        pltpu.make_async_copy(master_hbm.at[:, part], master_ref.at[:, part], sems.at[2 + at])
        for at, part in enumerate(parts)
    ]
    for load in loads:
        load.start()
    slots = slots_ref[...]
    picks = {k: pick_rows(slots, k, cap) for k in steps}
    fill_chunks(steps, cap, picks, held, copies, tiles_ref, chunks)
    slot_count = own_ref.shape[1]
    for load, part in zip(loads, parts):
        load.wait()
        weights = master_ref[:, part].astype(BF16)
        for at, ref in ((0, own_ref), (slot_count, other_ref)):
            inner_ref[at : at + slot_count, part] = lax.dot_general(
                ref[...], weights, (((0,), (0,)), ((), ())), preferred_element_type=F32
            )


def score_kernel(items, group, cap, inner_ref, *rest):
    chunks, score_ref = dict(zip(items, rest)), rest[-1]
    blocks = inner_ref.shape[1] // LANES
    me = ep_index()
    line_of = lax.broadcasted_iota(jnp.int32, score_ref.shape, 0)
    scores = jnp.zeros(score_ref.shape, F32)
    for k in sorted({k for _, k in items}):
        sums = []
        for side in range(2):
            total = jnp.zeros((cap, LANES), F32)
            if (side, k) in items:
                start = pl.multiple_of(side * group * cap + (me ^ k) * cap, cap)
                for block in range(blocks):
                    rows = chunks[side, k][block * cap : (block + 1) * cap, :].astype(F32)
                    total += rows * inner_ref[
                        pl.ds(start, cap), block * LANES : (block + 1) * LANES
                    ]
            sums.append(total)
        both = jnp.concatenate(sums, axis=0)
        line = jnp.sum(both.T, axis=0, keepdims=True)
        scores = jnp.where(line_of == (me ^ k), line, scores)
    score_ref[...] = scores


def scale_into(scaled, at, hidden, line):
    for top in range(0, hidden.shape[0], LANES):
        lines = slice(top, top + LANES)
        scaled[lines, at : at + LANES] = (hidden[lines, :].astype(F32) * line).astype(BF16)


def sum_kernel(items, group, cap, own_ref, other_ref, *rest):
    chunks = dict(zip(items, rest))
    grad_ref, rows, scaled = rest[-3:]
    blocks = rows.shape[1] // LANES
    slots = group * cap
    me = ep_index()
    for side, hidden in enumerate((own_ref, other_ref)):
        tile = jnp.zeros((TILE, LANES), F32)
        for k in range(group):
            start = pl.multiple_of(side * slots + (me ^ k) * cap, cap)
            if (side, k) not in items:
                rows[pl.ds(start, cap), :] = jnp.zeros((cap, rows.shape[1]), BF16)
                continue
            chunk = chunks[side, k]
            tile += chunk[blocks * cap :, :].astype(F32)
            for block in range(blocks):
                rows[pl.ds(start, cap), block * LANES : (block + 1) * LANES] = chunk[
                    block * cap : (block + 1) * cap, :
                ]
        for part in range(slots // LANES):
            lanes = slice(part * LANES, (part + 1) * LANES)
            scale_into(scaled, side * slots + part * LANES, hidden.at[:, lanes], tile[part : part + 1, :])
    grad_ref[...] = jnp.dot(scaled[...], rows[...], preferred_element_type=F32)


def merge_kernel(cap, own_ref, other_ref, _, out_ref):
    lane = lax.broadcasted_iota(jnp.int32, own_ref.shape, 1)
    scores = own_ref[...] + pltpu.roll(other_ref[...], LANES - cap, axis=1)
    out_ref[...] = jnp.where(lane < cap, scores, 0.0)


def update_kernel(items, cap, own_ref, other_ref, grad_ref, master_ref, moment_ref, second_ref, *rest):
    chunks = rest[: len(items)]
    _, update_hbm, rows, scaled, total, update, sems = rest[len(items) :]
    hid, half = update.shape
    width = min(half, 2 * LANES)
    height = 2 * TILE
    data_rows = half // LANES * cap
    me = ep_index()
    for at in range(0, len(items), 2):
        parts = []
        for turn, ((side, k), chunk) in enumerate(zip(items[at : at + 2], chunks[at : at + 2])):
            slot = (me ^ k) * cap
            lanes = pl.ds(pl.multiple_of(slot // LANES * LANES, LANES), LANES)
            place = slot % LANES if turn == 0 else (LANES - cap) - slot % LANES
            start = pl.multiple_of(at // 2 * LANES + place, cap)
            for part in range(half // LANES):
                rows[pl.ds(start, cap), part * LANES : (part + 1) * LANES] = chunk[
                    part * cap : (part + 1) * cap, :
                ]
            line = jnp.sum(chunk[data_rows:, :].astype(F32), axis=0, keepdims=True)
            parts.append(((own_ref, other_ref)[side], lanes, line))
        if len(parts) == 1:
            start = pl.multiple_of(at // 2 * LANES + (LANES - cap) - place, cap)
            rows[pl.ds(start, cap), :] = jnp.zeros((cap, half), BF16)
        for top in range(0, hid, LANES):
            values = [
                hidden[top : top + LANES, lanes].astype(F32) * line for hidden, lanes, line in parts
            ]
            if len(values) == 2:
                values[0] += pltpu.roll(values[1], LANES - cap, axis=1)
            scaled[top : top + LANES, at // 2 * LANES : (at // 2 + 1) * LANES] = values[0].astype(
                BF16
            )
    total[...] = jnp.dot(scaled[...], rows[...], preferred_element_type=F32)

    def moments(top, columns):
        lines = slice(top, top + TILE)
        grad = total[lines, columns] + grad_ref[lines, columns]
        first = moment_ref[lines, columns].astype(F32) * (beta_first / (1.0 - beta_first)) + grad
        square = (
            second_ref[lines, columns].astype(F32) * (beta_second / (1.0 - beta_second))
            + grad * grad
        )
        return first, square, lax.rsqrt(square)

    def inverse(first, square, root):
        scale = square * root * (second_unit**0.5 / first_unit) + adam_eps / first_unit
        return first, pl.reciprocal(scale, approx=True)

    def finish(top, columns, first, scale):
        lines = slice(top, top + TILE)
        update[lines, columns] = first * scale + decay_rate * master_ref[lines, columns]

    copies = []
    pieces = [
        (top, slice(column, column + width))
        for top in range(0, hid, TILE)
        for column in range(0, half, width)
    ]
    held = {}
    for turn in range(len(pieces) + 2):
        if turn < len(pieces):
            held[turn, 0] = moments(*pieces[turn])
        if 0 <= turn - 1 < len(pieces):
            held[turn - 1, 1] = inverse(*held.pop((turn - 1, 0)))
        if turn >= 2:
            finish(*pieces[turn - 2], *held.pop((turn - 2, 1)))
            top, columns = pieces[turn - 2]
            if (top + TILE) % height == 0 and columns.stop == half:
                lines = slice(top + TILE - height, top + TILE)
                copies.append(
                    pltpu.make_async_copy(
                        update.at[lines, :], update_hbm.at[lines, :], sems.at[len(copies)]
                    )
                )
                copies[-1].start()
    for copy in copies:
        copy.wait()


def combine_kernel(steps, group, cap, ids_ref, slots_ref, *rest):
    refs, out_ref = iter(rest[:-1]), rest[-1]
    tokens = ids_ref.shape[1]
    me = ep_index()
    shape = rest[0].shape
    lane = lax.broadcasted_iota(jnp.int32, shape, 1)
    row = lax.broadcasted_iota(jnp.int32, shape, 0)
    lines = jnp.zeros(shape, F32)
    for k, tiles in steps:
        scores = next(refs)[...]
        if tiles == 2:
            scores = jnp.where(lane < cap, scores, next(refs)[...])
        line = jnp.sum(jnp.where(row == me, scores, 0.0), axis=0, keepdims=True)
        lines = jnp.where(row == k, line, lines)
    rest = jnp.zeros((LANES - lines.shape[0], LANES), F32)
    columns = jnp.concatenate([lines, rest], axis=0).T
    columns = columns[:cap] + columns[cap : 2 * cap]
    place = lax.broadcasted_iota(jnp.int32, (cap, tokens), 0).astype(F32)
    ids = ids_ref[...]
    result = jnp.zeros(ids.shape, F32)
    for k in range(group):
        at_slot = jnp.where(place == slots_ref[k : k + 1, :], columns[:, k : k + 1], 0.0)
        result = jnp.where(ids == (me ^ k), jnp.sum(at_slot, axis=0, keepdims=True), result)
    out_ref[...] = result


def moved(array, side, step):
    if (side, step) == (0, 0):
        return array
    group = lax.axis_size("ep")
    pairs = [
        (p * group + e, (p ^ side) * group + (e ^ step)) for p in range(2) for e in range(group)
    ]
    return lax.ppermute(array, ("pair", "ep"), pairs)


def local(grad_out, router_weights, expert_ids, hidden, master, moment, second):
    group = lax.axis_size("ep")
    tokens, width = grad_out.shape[1:]
    top = expert_ids.shape[2]
    hid, slots = hidden.shape[2:]
    half = master.shape[3]
    cap = slots // group
    ids = expert_ids[0].T
    own_hidden = hidden[0, 0]
    param = master[0, 0]
    other_hidden = moved(own_hidden, 1, 0)

    far = group // 2
    first = [k for k in range(1, group) if k != far]
    late = [0, far]
    first_items = [(side, k) for side in range(2) for k in reversed(first)]
    last_items = [(1, far), (0, far), (1, 0), (0, 0)]
    order = first_items + last_items
    chunk = jax.ShapeDtypeStruct((half // LANES * cap + TILE, LANES), BF16)
    grads = pltpu.with_memory_space_constraint(grad_out[0], pltpu.HBM)
    held = pltpu.VMEM((2, tokens, half), BF16)
    routed = pl.pallas_call(
        functools.partial(route_kernel, first_items, first, group, cap),
        out_shape=[
            jax.ShapeDtypeStruct((group + -group % TILE, tokens), F32),
            jax.ShapeDtypeStruct((group, TILE, LANES), BF16),
        ]
        + [chunk] * len(first_items),
        in_specs=specs(pltpu.HBM, 3),
        out_specs=specs(pltpu.VMEM, 2 + len(first_items)),
        scratch_shapes=[
            pltpu.VMEM((top, tokens), jnp.int32),
            pltpu.VMEM((top, tokens), BF16),
            held,
            pltpu.SemaphoreType.DMA((4,)),
        ],
        compiler_params=params(),
        cost_estimate=cost(2 * slots * tokens * width, 2 * (tokens + slots) * width),
        name="route",
    )(
        pltpu.with_memory_space_constraint(ids, pltpu.HBM),
        pltpu.with_memory_space_constraint(router_weights[0].T, pltpu.HBM),
        grads,
    )
    slot_of, tiles = routed[:2]
    arrived = {item: moved(sent, *item) for item, sent in zip(first_items, routed[2:])}

    routed = pl.pallas_call(
        functools.partial(later_kernel, last_items, late, cap),
        out_shape=[jax.ShapeDtypeStruct((2 * slots, half), F32)] + [chunk] * len(last_items),
        in_specs=specs(pltpu.VMEM, 2)
        + specs(pltpu.HBM, 1)
        + specs(pltpu.VMEM, 2)
        + specs(pltpu.HBM, 1),
        out_specs=specs(pltpu.VMEM, 1 + len(last_items)),
        scratch_shapes=[
            held,
            pltpu.VMEM((hid, half), F32),
            pltpu.SemaphoreType.DMA((2 + half // min(half, 4 * LANES),)),
        ],
        compiler_params=params(),
        cost_estimate=cost(
            2 * slots * tokens * width + 4 * slots * hid * half, 2 * (tokens + slots) * width
        ),
        name="later",
    )(
        slot_of,
        tiles,
        grads,
        own_hidden,
        other_hidden,
        pltpu.with_memory_space_constraint(param, pltpu.HBM),
    )
    inner = routed[0]
    arrived |= {item: moved(sent, *item) for item, sent in zip(last_items, routed[1:])}

    tile = jax.ShapeDtypeStruct((group + -group % 8, LANES), F32)

    def scored(items, *after):
        return pl.pallas_call(
            functools.partial(score_kernel, items, group, cap),
            out_shape=tile,
            in_specs=specs(pltpu.VMEM, 1 + len(items)) + specs(pl.ANY, len(after)),
            out_specs=specs(pltpu.VMEM, 1)[0],
            compiler_params=params(),
            cost_estimate=cost(2 * cap * half, 6 * cap * half),
            name="score",
        )(inner, *[arrived[item] for item in items], *after)

    first_scores = scored(first_items)
    other_scores = moved(first_scores, 1, 0)
    added = [(1, far), (0, far), (1, 0)]
    summed = [item for item in order if item not in added]
    grad = pl.pallas_call(
        functools.partial(sum_kernel, summed, group, cap),
        out_shape=jax.ShapeDtypeStruct((hid, half), F32),
        in_specs=specs(pltpu.VMEM, 2 + len(summed)) + specs(pl.ANY, 1),
        out_specs=specs(pltpu.VMEM, 1)[0],
        scratch_shapes=[
            pltpu.VMEM((2 * slots, half), BF16),
            pltpu.VMEM((hid, 2 * slots), BF16),
        ],
        compiler_params=params(),
        cost_estimate=cost(4 * slots * hid * half, 4 * hid * half),
        name="sum",
    )(own_hidden, other_hidden, *[arrived[item] for item in summed], first_scores)
    merged = pl.pallas_call(
        functools.partial(merge_kernel, cap),
        out_shape=tile,
        in_specs=specs(pltpu.VMEM, 2) + specs(pl.ANY, 1),
        out_specs=specs(pltpu.VMEM, 1)[0],
        compiler_params=params(),
        name="merge",
    )(first_scores, other_scores, grad)
    returned = {k: [moved(merged, 0, k)] for k in first}
    zero_scores = scored([(0, 0), (1, 0)], merged)
    returned[0] = [zero_scores, moved(zero_scores, 1, 0)]
    other_far = scored([(1, far)], zero_scores)
    last_scores = scored([(0, far)], other_far)
    returned[far] = [moved(last_scores, 0, far), moved(other_far, 1, far)]

    depth = -(-len(added) // 2) * LANES
    update = pl.pallas_call(
        functools.partial(update_kernel, added, cap),
        out_shape=jax.ShapeDtypeStruct((hid, half), F32),
        in_specs=specs(pltpu.VMEM, 6 + len(added)) + specs(pl.ANY, 1),
        out_specs=specs(pltpu.HBM, 1)[0],
        scratch_shapes=[
            pltpu.VMEM((depth, half), BF16),
            pltpu.VMEM((hid, depth), BF16),
            pltpu.VMEM((hid, half), F32),
            pltpu.VMEM((hid, half), F32),
            pltpu.SemaphoreType.DMA((hid // (2 * TILE),)),
        ],
        compiler_params=params(),
        cost_estimate=cost(2 * depth * hid * half, 16 * hid * half),
        name="update",
    )(
        own_hidden,
        other_hidden,
        grad,
        param,
        moment[0, 0],
        second[0, 0],
        *[arrived[item] for item in added],
        last_scores,
    )
    shares = [array for arrays in returned.values() for array in arrays]
    router = pl.pallas_call(
        functools.partial(
            combine_kernel, [(k, len(arrays)) for k, arrays in returned.items()], group, cap
        ),
        out_shape=jax.ShapeDtypeStruct((top, tokens), F32),
        in_specs=specs(pltpu.VMEM, 2 + len(shares)),
        out_specs=specs(pltpu.VMEM, 1)[0],
        compiler_params=params(),
        cost_estimate=cost(4 * slots * tokens, 8 * top * tokens),
        name="combine",
    )(ids, slot_of, *shares)
    return (update[None, None], router.T[None])


def solution(mesh):
    sections, group = mesh.devices.shape
    split = jax.sharding.Mesh(
        mesh.devices.reshape(2, sections // 2, group), ("pair", "rest", "ep")
    )
    section = ("pair", "rest")
    rows = P(section, "ep", None)
    blocks = P(section, "ep", None, None)
    return jax.shard_map(
        local,
        mesh=split,
        in_specs=(rows, rows, rows, blocks, blocks, blocks, blocks),
        out_specs=(blocks, rows),
        check_vma=False,
    )
```
